32 devices in a mesh: ctx: 8 (over z, y), head: 4 (over x, core).
Axes of the slice: x: 2, y: 2, z: 4, core: 2. Of those that a mesh axis runs over, the one named last changes fastest.
Arguments:
- queries: bfloat16 [8, 512, 3072], P('ctx', None, 'head'), may hold values from -5 to 5
- key_rows: bfloat16 [8, 512, 3072], P('ctx', None, 'head'), may hold values from -5 to 5
- value_rows: bfloat16 [8, 512, 3072], P('ctx', None, 'head'), may hold values from -6 to 6
- out_grad: bfloat16 [8, 512, 3072], P('ctx', None, 'head'), may hold values from -6 to 6
- head_kind: int32 [24], replicated, may hold values from 0 to 1, as said below
- frame_band: int32 [24], replicated, may hold values from 1 to 7, as said below
Outputs:
- attended: bfloat16 [8, 512, 3072], P('ctx', None, 'head')
- query_grad: bfloat16 [8, 512, 3072], P('ctx', None, 'head')
- key_grad: bfloat16 [8, 512, 3072], P('ctx', None, 'head')
- value_grad: bfloat16 [8, 512, 3072], P('ctx', None, 'head')
The draws below stay inside these ranges and needn't reach their ends.
Inputs may be any that keep to these rules, and one draw needn't show every extreme that they name: `head_kind`: exactly 8 entries are 1. `frame_band`: entries of spatial heads are not used; some temporal head has the value 8 - 1.
All inputs are finite; a program needn't handle non-finite values.
Results may differ from the reference program's by a relative error of at most 0.024.
Values may be sent and summed in bfloat16 or wider, within the bound.
No kernel may reach another device: no remote copies, remote signals or barrier semaphores. Data moves between devices by JAX's collectives and lax.ppermute only.
A program may use at most 64 MiB of HBM per device.

```python
import jax
import jax.numpy as jnp
from jax import lax

DH = 128
HEADS = 24
NSPATIAL = 8
POS = 512
FRAMES = 8


def draw_queries(key, part):
    shape = (FRAMES, POS, HEADS * DH)
    values = jax.random.truncated_normal(jax.random.fold_in(key, 1), -5.0, 5.0, shape, jnp.float32)
    return values.astype(jnp.bfloat16)


def draw_key_rows(key, part):
    shape = (FRAMES, POS, HEADS * DH)
    values = jax.random.truncated_normal(jax.random.fold_in(key, 2), -5.0, 5.0, shape, jnp.float32)
    return values.astype(jnp.bfloat16)


def head_order(key):
    return jax.random.permutation(jax.random.fold_in(key, 11), jnp.arange(HEADS, dtype=jnp.int32))


def draw_head_kind(key, part):
    return (head_order(key) < NSPATIAL).astype(jnp.int32)


def draw_frame_band(key, part):
    order = head_order(key)
    band_draw = jax.random.randint(jax.random.fold_in(key, 12), (HEADS,), 1, FRAMES, dtype=jnp.int32)
    return jnp.where(order == HEADS - 1, FRAMES - 1, band_draw).astype(jnp.int32)


def level_of(own_key, shape, split, low, high):
    factor_of, own = 1.0, jax.random.fold_in(own_key, 6)
    for dim, shards_of in split:
        steps = jnp.exp(jax.random.uniform(jax.random.fold_in(own, dim), (shards_of,), jnp.float32, low / len(split), high / len(split)))
        factor_of = factor_of * jnp.repeat(steps, shape[dim] // shards_of).reshape([-1 if axis == dim else 1 for axis in range(len(shape))])
    return factor_of


def centred(key, extent, scale, limit, split=(), held_as=jnp.bfloat16):
    entries = jax.random.normal(key, extent, jnp.float32) * scale
    if len(split) > 0:
        entries = level_of(key, extent, split, -0.22, 0.18) * entries
    return jnp.clip(entries, min=-limit, max=limit).astype(held_as)


def setup_inputs(seed: int = 0) -> dict:
    splits = jax.random.split(jax.random.key(seed), 7)
    return {
        "queries": draw_queries(jax.random.fold_in(splits[6], 71), 0),
        "key_rows": draw_key_rows(jax.random.fold_in(splits[6], 71), 0),
        "value_rows": centred(splits[2], (FRAMES, POS, HEADS * DH), 1.0, 6.0, ((0, 8), (2, 4))),
        "out_grad": centred(splits[3], (FRAMES, POS, HEADS * DH), 1.0, 6.0, ((0, 8), (2, 4))),
        "head_kind": draw_head_kind(jax.random.fold_in(splits[6], 71), 0),
        "frame_band": draw_frame_band(jax.random.fold_in(splits[6], 71), 0),
    }


def log_sum(scores):
    top_value = jnp.max(scores, axis=-1, keepdims=True)
    return top_value + jnp.log(jnp.sum(jnp.exp(scores - top_value), axis=-1, keepdims=True))


def spatial_frames(q_head, k_head, v_head, g_head, band_value):
    scaling = DH ** -0.5

    def one_frame(frame):
        earlier = jnp.maximum(frame - 1, 0)
        key_pair = jnp.concatenate([k_head[earlier], k_head[frame]], axis=0)
        value_pair = jnp.concatenate([v_head[earlier], v_head[frame]], axis=0)
        q_frame = q_head[frame]
        g_frame = g_head[frame]
        has_prior = jnp.broadcast_to(frame > 0, (POS,))
        valid = jnp.concatenate([has_prior, jnp.ones((POS,), dtype=bool)])[None, :]
        score = jnp.dot(q_frame, key_pair.T, preferred_element_type=jnp.float32) * scaling
        score = jnp.where(valid, score, -jnp.inf)
        weight = jnp.exp(score - log_sum(score))
        prob = weight.astype(jnp.bfloat16)
        attended = jnp.dot(prob, value_pair, preferred_element_type=jnp.float32).astype(jnp.bfloat16)
        delta = jnp.sum(g_frame.astype(jnp.float32) * attended.astype(jnp.float32), axis=-1, keepdims=True)
        dprob = jnp.dot(g_frame, value_pair.T, preferred_element_type=jnp.float32)
        dscore = (weight * (dprob - delta) * scaling).astype(jnp.bfloat16)
        q_grad = jnp.dot(dscore, key_pair, preferred_element_type=jnp.float32).astype(jnp.bfloat16)
        k_grad = jnp.dot(dscore.T, q_frame, preferred_element_type=jnp.float32)
        v_grad = jnp.dot(prob.T, g_frame, preferred_element_type=jnp.float32)
        return attended, q_grad, k_grad[POS:], k_grad[:POS], v_grad[POS:], v_grad[:POS]

    attended, q_grad, k_own, k_prior, v_own, v_prior = lax.map(one_frame, jnp.arange(FRAMES, dtype=jnp.int32))
    tail_rows = jnp.zeros((1, POS, DH), jnp.float32)
    k_grad = (k_own + jnp.concatenate([k_prior[1:], tail_rows], axis=0)).astype(jnp.bfloat16)
    v_grad = (v_own + jnp.concatenate([v_prior[1:], tail_rows], axis=0)).astype(jnp.bfloat16)
    return attended, q_grad, k_grad, v_grad


def temporal_frames(q_head, k_head, v_head, g_head, band_value):
    scaling = DH ** -0.5
    q_float = q_head.astype(jnp.float32)
    k_float = k_head.astype(jnp.float32)
    v_float = v_head.astype(jnp.float32)
    g_float = g_head.astype(jnp.float32)
    score = jnp.einsum("fpd,gpd->pfg", q_float, k_float) * scaling
    frame_ids = jnp.arange(FRAMES, dtype=jnp.int32)
    allowed = jnp.abs(frame_ids[:, None] - frame_ids[None, :]) <= band_value
    score = jnp.where(allowed[None], score, -jnp.inf)
    weight = jnp.exp(score - log_sum(score))
    prob = weight.astype(jnp.bfloat16)
    attended = jnp.einsum("pfg,gpd->fpd", prob.astype(jnp.float32), v_float).astype(jnp.bfloat16)
    delta = jnp.sum(g_float * attended.astype(jnp.float32), axis=-1)
    dprob = jnp.einsum("fpd,gpd->pfg", g_float, v_float)
    dscore = (weight * (dprob - delta.T[:, :, None]) * scaling).astype(jnp.bfloat16)
    dscore_float = dscore.astype(jnp.float32)
    q_grad = jnp.einsum("pfg,gpd->fpd", dscore_float, k_float).astype(jnp.bfloat16)
    k_grad = jnp.einsum("pfg,fpd->gpd", dscore_float, q_float).astype(jnp.bfloat16)
    v_grad = jnp.einsum("pfg,fpd->gpd", prob.astype(jnp.float32), g_float).astype(jnp.bfloat16)
    return attended, q_grad, k_grad, v_grad


def split_heads(rows):
    return jnp.transpose(rows.reshape(FRAMES, POS, HEADS, DH), (2, 0, 1, 3))


def join_heads(rows):
    return jnp.transpose(rows, (1, 2, 0, 3)).reshape(FRAMES, POS, HEADS * DH)


def reference(queries, key_rows, value_rows, out_grad, head_kind, frame_band):
    stacked = (split_heads(queries), split_heads(key_rows), split_heads(value_rows), split_heads(out_grad), head_kind, frame_band)

    def one_head(item):
        q_head, k_head, v_head, g_head, kind_value, band_value = item
        return lax.cond(kind_value == 1, spatial_frames, temporal_frames, q_head, k_head, v_head, g_head, band_value)

    results = lax.map(one_head, stacked)
    return join_heads(results[0]), join_heads(results[1]), join_heads(results[2]), join_heads(results[3])
```

```python
import functools

import jax
import jax.numpy as jnp
from jax import lax
from jax.experimental import pallas as pl
from jax.experimental.pallas import tpu as pltpu
from jax.sharding import PartitionSpec as P

DH = 128
SCALE = DH ** (-0.5)
SPATIAL, TEMPORAL = 1, 0
MASKED = -1e30
F32 = jnp.float32
BF16 = jnp.bfloat16


def head_at(kind_ref, heads, kind, slot):
    found, seen = jnp.int32(0), jnp.int32(0)
    for head in range(heads):
        hit = kind_ref[head] == kind
        found = jnp.where(jnp.logical_and(hit, seen == slot), jnp.int32(head), found)
        seen = seen + hit.astype(jnp.int32)
    return found


def dot_nt(a, b):
    return lax.dot_general(a, b, (((1,), (1,)), ((), ())), preferred_element_type=F32)


def dot_nn(a, b):
    return lax.dot_general(a, b, (((1,), (0,)), ((), ())), preferred_element_type=F32)


def dot_tn(a, b):
    return lax.dot_general(a, b, (((0,), (0,)), ((), ())), preferred_element_type=F32)


def params(mib=32):
    return pltpu.CompilerParams(
        dimension_semantics=("arbitrary",), vmem_limit_bytes=mib * 1024 * 1024
    )


def cost(flops, moved):
    return pl.CostEstimate(flops=int(flops), bytes_accessed=int(moved), transcendentals=0)


def column_spec(count, heads, kind):
    return pl.BlockSpec((count, DH), lambda i, kind_ref: (0, head_at(kind_ref, heads, kind, i)))


def pack_temporal(kinds, arrays, frames, slots, heads):
    count = arrays[0].shape[0]
    rows = count // frames
    shape = (frames, len(arrays), slots, rows, DH)

    def kernel(kind_ref, *refs):
        out_ref = refs[-1]
        for place, ref in enumerate(refs[:-1]):
            out_ref[:, place, 0] = ref[...].reshape(frames, rows, DH)

    return pl.pallas_call(
        kernel,
        out_shape=jax.ShapeDtypeStruct(shape, BF16),
        grid_spec=pltpu.PrefetchScalarGridSpec(
            num_scalar_prefetch=1,
            grid=(slots,),
            in_specs=[column_spec(count, heads, TEMPORAL)] * len(arrays),
            out_specs=pl.BlockSpec(
                (frames, len(arrays), 1, rows, DH), lambda i, kind_ref: (0, 0, i, 0, 0)
            ),
        ),
        compiler_params=params(),
        cost_estimate=cost(0, 4 * len(arrays) * slots * count * DH),
        name="pack_temporal",
    )(kinds, *arrays)


def pack_spatial(kinds, arrays, slots, heads):
    count = arrays[0].shape[0]
    shape = (slots, len(arrays), count, DH)

    def kernel(kind_ref, *refs):
        out_ref = refs[-1]
        for place, ref in enumerate(refs[:-1]):
            out_ref[0, place] = ref[...]

    return pl.pallas_call(
        kernel,
        out_shape=jax.ShapeDtypeStruct(shape, BF16),
        grid_spec=pltpu.PrefetchScalarGridSpec(
            num_scalar_prefetch=1,
            grid=(slots,),
            in_specs=[column_spec(count, heads, SPATIAL)] * len(arrays),
            out_specs=pl.BlockSpec(
                (1, len(arrays), count, DH), lambda i, kind_ref: (i, 0, 0, 0)
            ),
        ),
        compiler_params=params(),
        cost_estimate=cost(0, 4 * len(arrays) * slots * count * DH),
        name="pack_spatial",
    )(kinds, *arrays)


def temporal(kinds, bands, rows_in, heads):
    frames, _, slots, rows, _ = rows_in.shape
    group = min(rows, max(16, 256 // frames))
    size = frames * group

    def kernel(kind_ref, band_ref, in_ref, out_ref):
        band = band_ref[head_at(kind_ref, heads, TEMPORAL, pl.program_id(0))]
        row = lax.broadcasted_iota(jnp.int32, (size, size), 0)
        col = lax.broadcasted_iota(jnp.int32, (size, size), 1)
        same = lax.rem(row, group) == lax.rem(col, group)
        near = jnp.abs(lax.div(row, group) - lax.div(col, group)) <= band
        allowed = jnp.logical_and(same, near)
        for start in range(0, rows, group):
            part = slice(start, start + group)
            q, k, v, g = (in_ref[:, place, 0, part].reshape(size, DH) for place in range(4))
            score = jnp.where(allowed, dot_nt(q, k) * SCALE, MASKED)
            raised = jnp.exp(score - jnp.max(score, axis=1, keepdims=True))
            weight = raised / jnp.sum(raised, axis=1, keepdims=True)
            prob = weight.astype(BF16)
            attended = dot_nn(prob, v).astype(BF16)
            delta = jnp.sum(g.astype(F32) * attended.astype(F32), axis=1, keepdims=True)
            dscore = (weight * (dot_nt(g, v) - delta) * SCALE).astype(BF16)
            out_ref[:, 0, 0, part] = attended.reshape(frames, group, DH)
            out_ref[:, 1, 0, part] = dot_nn(dscore, k).astype(BF16).reshape(frames, group, DH)
            out_ref[:, 2, 0, part] = dot_tn(dscore, q).astype(BF16).reshape(frames, group, DH)
            out_ref[:, 3, 0, part] = dot_tn(prob, g).astype(BF16).reshape(frames, group, DH)

    spec = pl.BlockSpec(
        (frames, 4, 1, rows, DH), lambda i, kind_ref, band_ref: (0, 0, i, 0, 0)
    )
    return pl.pallas_call(
        kernel,
        out_shape=jax.ShapeDtypeStruct(rows_in.shape, BF16),
        grid_spec=pltpu.PrefetchScalarGridSpec(
            num_scalar_prefetch=2, grid=(slots,), in_specs=[spec], out_specs=spec
        ),
        compiler_params=params(),
        cost_estimate=cost(12 * slots * rows * frames * size * DH, 4 * rows_in.size),
        name="temporal",
    )(kinds, bands, rows_in)


def unpack_temporal(kinds, rows_in, filled, heads):
    frames, _, slots, rows, _ = rows_in.shape
    count = frames * rows
    held = () if filled is None else filled

    def kernel(kind_ref, in_ref, *refs):
        for place, ref in enumerate(refs[len(held) :]):
            ref[...] = in_ref[:, place, 0].reshape(count, DH)

    return pl.pallas_call(
        kernel,
        out_shape=[jax.ShapeDtypeStruct((count, heads * DH), BF16)] * 4,
        grid_spec=pltpu.PrefetchScalarGridSpec(
            num_scalar_prefetch=1,
            grid=(slots,),
            in_specs=[
                pl.BlockSpec((frames, 4, 1, rows, DH), lambda i, kind_ref: (0, 0, i, 0, 0))
            ]
            + [pl.BlockSpec(memory_space=pl.ANY)] * len(held),
            out_specs=[column_spec(count, heads, TEMPORAL)] * 4,
        ),
        input_output_aliases={2 + place: place for place in range(len(held))},
        compiler_params=params(),
        cost_estimate=cost(0, 4 * rows_in.size),
        name="unpack_temporal",
    )(kinds, rows_in, *held)


def spatial(kinds, frame, arrays, prior, heads):
    count = arrays[0].shape[0]
    slots = prior.shape[0]
    chunk = 256

    def kernel(
        kind_ref, frame_ref, q_ref, k_ref, v_ref, g_ref, prior_ref,
        out_ref, qgrad_ref, own_ref, send_ref,
    ):
        has_prior = frame_ref[0] > 0
        k, v = k_ref[...], v_ref[...]
        k_prior, v_prior = prior_ref[0, 0], prior_ref[0, 1]
        k_own = v_own = k_send = v_send = None
        for start in range(0, count, chunk):
            part = slice(start, start + chunk)
            q, g = q_ref[part], g_ref[part]
            own = dot_nt(q, k) * SCALE
            before = jnp.where(has_prior, dot_nt(q, k_prior) * SCALE, MASKED)
            top = jnp.maximum(
                jnp.max(own, axis=1, keepdims=True), jnp.max(before, axis=1, keepdims=True)
            )
            own, before = jnp.exp(own - top), jnp.exp(before - top)
            total = jnp.sum(own, axis=1, keepdims=True) + jnp.sum(before, axis=1, keepdims=True)
            inverse = 1.0 / total
            own, before = own * inverse, before * inverse
            own_prob, before_prob = own.astype(BF16), before.astype(BF16)
            attended = (dot_nn(own_prob, v) + dot_nn(before_prob, v_prior)).astype(BF16)
            delta = jnp.sum(g.astype(F32) * attended.astype(F32), axis=1, keepdims=True)
            own_ds = (own * (dot_nt(g, v) - delta) * SCALE).astype(BF16)
            before_ds = (before * (dot_nt(g, v_prior) - delta) * SCALE).astype(BF16)
            out_ref[part] = attended
            qgrad_ref[part] = (dot_nn(own_ds, k) + dot_nn(before_ds, k_prior)).astype(BF16)
            terms = (
                dot_tn(own_ds, q), dot_tn(own_prob, g), dot_tn(before_ds, q), dot_tn(before_prob, g)
            )
            if start == 0:
                k_own, v_own, k_send, v_send = terms
            else:
                k_own, v_own = k_own + terms[0], v_own + terms[1]
                k_send, v_send = k_send + terms[2], v_send + terms[3]
        own_ref[0, 0], own_ref[0, 1] = k_own, v_own
        send_ref[0, 0], send_ref[0, 1] = k_send.astype(BF16), v_send.astype(BF16)

    columns = pl.BlockSpec(
        (count, DH), lambda i, kind_ref, frame_ref: (0, head_at(kind_ref, heads, SPATIAL, i))
    )
    pair = pl.BlockSpec((1, 2, count, DH), lambda i, kind_ref, frame_ref: (i, 0, 0, 0))
    whole = jax.ShapeDtypeStruct((count, heads * DH), BF16)
    return pl.pallas_call(
        kernel,
        out_shape=[
            whole,
            whole,
            jax.ShapeDtypeStruct(prior.shape, F32),
            jax.ShapeDtypeStruct(prior.shape, BF16),
        ],
        grid_spec=pltpu.PrefetchScalarGridSpec(
            num_scalar_prefetch=2,
            grid=(slots,),
            in_specs=[columns] * 4 + [pair],
            out_specs=[columns, columns, pair, pair],
        ),
        compiler_params=params(48),
        cost_estimate=cost(24 * slots * count * count * DH, 12 * 2 * slots * count * DH),
        name="spatial",
    )(kinds, frame, *arrays, prior)


def add_spatial(kinds, own, back, heads):
    slots, _, count, _ = own.shape

    def kernel(kind_ref, own_ref, back_ref, k_ref, v_ref):
        k_ref[...] = (own_ref[0, 0] + back_ref[0, 0].astype(F32)).astype(BF16)
        v_ref[...] = (own_ref[0, 1] + back_ref[0, 1].astype(F32)).astype(BF16)

    pair = pl.BlockSpec((1, 2, count, DH), lambda i, kind_ref: (i, 0, 0, 0))
    return pl.pallas_call(
        kernel,
        out_shape=[jax.ShapeDtypeStruct((count, heads * DH), BF16)] * 2,
        grid_spec=pltpu.PrefetchScalarGridSpec(
            num_scalar_prefetch=1,
            grid=(slots,),
            in_specs=[pair, pair],
            out_specs=[column_spec(count, heads, SPATIAL)] * 2,
        ),
        compiler_params=params(),
        cost_estimate=cost(0, 8 * own.size),
        name="add_spatial",
    )(kinds, own, back)


def passed_along(array, axis, by):
    length = lax.axis_size(axis)
    pairs = [(i, i + by) for i in range(length) if 0 <= i + by < length]
    return lax.ppermute(array, axis, pairs)


def branch(slots, heads, frames, kinds, bands, frame, q, k, v, g):
    exchange = functools.partial(
        lax.all_to_all, axis_name="ctx", split_axis=0, concat_axis=0, tiled=True
    )
    filled = None
    if slots > 0:
        packed = pack_temporal(kinds, (q, k, v, g), frames, slots, heads)
        framed = exchange(packed)
    if slots < heads:
        prior = passed_along(pack_spatial(kinds, (k, v), heads - slots, heads), "ctx", 1)
        attended, qgrad, own, send = spatial(kinds, frame, (q, k, v, g), prior, heads)
        back = passed_along(send, "ctx", -1)
        filled = (attended, qgrad, *add_spatial(kinds, own, back, heads))
    if slots > 0:
        returned = exchange(temporal(kinds, bands, framed, heads))
        filled = unpack_temporal(kinds, returned, filled, heads)
    return tuple(filled)


def body(queries, key_rows, value_rows, out_grad, head_kind, frame_band):
    frames = lax.axis_size("ctx")
    heads = queries.shape[2] // DH
    first = lax.axis_index("head") * heads
    kinds = lax.dynamic_slice_in_dim(head_kind, first, heads)
    bands = lax.dynamic_slice_in_dim(frame_band, first, heads)
    frame = lax.axis_index("ctx").astype(jnp.int32).reshape(1)
    slots = jnp.sum((kinds == TEMPORAL).astype(jnp.int32))
    outs = lax.switch(
        slots,
        [functools.partial(branch, n, heads, frames) for n in range(heads + 1)],
        kinds, bands, frame, queries[0], key_rows[0], value_rows[0], out_grad[0],
    )
    return tuple(out[None] for out in outs)


def solution(mesh):
    rows = P("ctx", None, "head")
    return jax.shard_map(
        body,
        mesh=mesh,
        in_specs=(rows, rows, rows, rows, P(), P()),
        out_specs=(rows, rows, rows, rows),
        check_vma=False,
    )
```

```python
import functools

import jax
import jax.numpy as jnp
from jax import lax
from jax.experimental import pallas as pl
from jax.experimental.pallas import tpu as pltpu
from jax.sharding import PartitionSpec as P

DH = 128
SCALE = DH ** (-0.5)
SPATIAL, TEMPORAL = 1, 0
MASKED = -1e30
F32 = jnp.float32
BF16 = jnp.bfloat16
MIB = 1024 * 1024


def head_at(kind_ref, heads, kind, slot):
    found, seen = jnp.int32(0), jnp.int32(0)
    for head in range(heads):
        hit = kind_ref[head] == kind
        found = jnp.where(jnp.logical_and(hit, seen == slot), jnp.int32(head), found)
        seen = seen + hit.astype(jnp.int32)
    return found


def dot_nt(a, b):
    return lax.dot_general(a, b, (((1,), (1,)), ((), ())), preferred_element_type=F32)


def dot_nn(a, b):
    return lax.dot_general(a, b, (((1,), (0,)), ((), ())), preferred_element_type=F32)


def dot_tn(a, b):
    return lax.dot_general(a, b, (((0,), (0,)), ((), ())), preferred_element_type=F32)


def params(mib=32):
    return pltpu.CompilerParams(
        dimension_semantics=("arbitrary",), vmem_limit_bytes=mib * MIB
    )


def cost(flops, moved):
    return pl.CostEstimate(flops=int(flops), bytes_accessed=int(moved), transcendentals=0)


def column_spec(count, heads, kind):
    return pl.BlockSpec((count, DH), lambda i, kind_ref: (0, head_at(kind_ref, heads, kind, i)))


def head_columns(kind_ref, heads, kind, slot):
    return pl.ds(pl.multiple_of(head_at(kind_ref, heads, kind, slot) * DH, DH), DH)


def copy_all(pairs, sems):
    copies = [pltpu.make_async_copy(*pair, sems.at[i]) for i, pair in enumerate(pairs)]
    for copy in copies:
        copy.start()
    for copy in copies:
        copy.wait()


def pack(kinds, arrays, slots, heads):
    frames, rows, _ = arrays[0].shape
    others = heads - slots
    shapes = []
    if slots > 0:
        shapes.append(jax.ShapeDtypeStruct((frames, 4, slots, rows, DH), BF16))
    if others > 0:
        shapes.append(jax.ShapeDtypeStruct((others, 2, frames, rows, DH), BF16))

    def kernel(kind_ref, *refs):
        ins, outs, sems = refs[:4], refs[4:-1], refs[-1]
        pairs = []
        for slot in range(others):
            cols = head_columns(kind_ref, heads, SPATIAL, slot)
            for place, ref in enumerate(ins[1:3]):
                pairs.append((ref.at[:, :, cols], outs[-1].at[slot, place]))
        for slot in range(slots):
            cols = head_columns(kind_ref, heads, TEMPORAL, slot)
            for place, ref in enumerate(ins):
                pairs.append((ref.at[:, :, cols], outs[0].at[:, place, slot]))
        copy_all(pairs, sems)

    outs = pl.pallas_call(
        kernel,
        out_shape=shapes,
        in_specs=[pl.BlockSpec(memory_space=pltpu.SMEM)] + [pl.BlockSpec(memory_space=pl.ANY)] * 4,
        out_specs=[pl.BlockSpec(memory_space=pl.ANY)] * len(shapes),
        scratch_shapes=[pltpu.SemaphoreType.DMA((4 * slots + 2 * others,))],
        compiler_params=pltpu.CompilerParams(vmem_limit_bytes=MIB),
        cost_estimate=cost(0, 4 * (4 * slots + 2 * others) * frames * rows * DH),
        name="pack",
    )(kinds, *arrays)
    return (outs[0] if slots > 0 else None), (outs[-1] if others > 0 else None)


def temporal(kinds, bands, rows_in, heads):
    frames, _, slots, rows, _ = rows_in.shape
    group = 16
    size = frames * group

    def kernel(kind_ref, band_ref, in_ref, out_ref):
        band = band_ref[head_at(kind_ref, heads, TEMPORAL, pl.program_id(0))]
        row = lax.broadcasted_iota(jnp.int32, (size, size), 0)
        col = lax.broadcasted_iota(jnp.int32, (size, size), 1)
        same = lax.rem(row, group) == lax.rem(col, group)
        near = jnp.abs(lax.div(row, group) - lax.div(col, group)) <= band
        allowed = jnp.logical_and(same, near)
        parts = [slice(start, start + group) for start in range(0, rows, group)]
        qs, ks, vs, gs = (
            [in_ref[:, place, 0, part].reshape(size, DH) for part in parts] for place in range(4)
        )
        scores = [jnp.where(allowed, dot_nt(q, k) * SCALE, MASKED) for q, k in zip(qs, ks)]
        dprobs = [dot_nt(g, v) for g, v in zip(gs, vs)]
        raised = [jnp.exp(x - jnp.max(x, axis=1, keepdims=True)) for x in scores]
        weights = [x * (1.0 / jnp.sum(x, axis=1, keepdims=True)) for x in raised]
        probs = [x.astype(BF16) for x in weights]
        attended = [dot_nn(x, v).astype(BF16) for x, v in zip(probs, vs)]
        deltas = [
            jnp.sum(g.astype(F32) * x.astype(F32), axis=1, keepdims=True)
            for g, x in zip(gs, attended)
        ]
        dscores = [
            (w * (dp - delta) * SCALE).astype(BF16)
            for w, dp, delta in zip(weights, dprobs, deltas)
        ]
        results = (
            attended,
            [dot_nn(x, k).astype(BF16) for x, k in zip(dscores, ks)],
            [dot_tn(x, q).astype(BF16) for x, q in zip(dscores, qs)],
            [dot_tn(x, g).astype(BF16) for x, g in zip(probs, gs)],
        )
        for place, result in enumerate(results):
            for part, value in zip(parts, result):
                out_ref[:, place, 0, part] = value.reshape(frames, group, DH)

    spec = pl.BlockSpec(
        (frames, 4, 1, rows, DH), lambda i, kind_ref, band_ref: (0, 0, i, 0, 0)
    )
    return pl.pallas_call(
        kernel,
        out_shape=jax.ShapeDtypeStruct(rows_in.shape, BF16),
        grid_spec=pltpu.PrefetchScalarGridSpec(
            num_scalar_prefetch=2, grid=(slots,), in_specs=[spec], out_specs=spec
        ),
        compiler_params=params(),
        cost_estimate=cost(12 * slots * rows * frames * size * DH, 4 * rows_in.size),
        name="temporal",
    )(kinds, bands, rows_in)


def unpack(kinds, rows_in, filled, heads):
    frames, _, slots, rows, _ = rows_in.shape

    def kernel(kind_ref, in_ref, *refs):
        outs, sems = refs[-5:-1], refs[-1]
        pairs = []
        for slot in range(slots):
            cols = head_columns(kind_ref, heads, TEMPORAL, slot)
            for place, ref in enumerate(outs):
                pairs.append((in_ref.at[:, place, slot], ref.at[:, :, cols]))
        copy_all(pairs, sems)

    return pl.pallas_call(
        kernel,
        out_shape=[jax.ShapeDtypeStruct((frames, rows, heads * DH), BF16)] * 4,
        in_specs=[pl.BlockSpec(memory_space=pltpu.SMEM)]
        + [pl.BlockSpec(memory_space=pl.ANY)] * (1 + len(filled)),
        out_specs=[pl.BlockSpec(memory_space=pl.ANY)] * 4,
        scratch_shapes=[pltpu.SemaphoreType.DMA((4 * slots,))],
        input_output_aliases={2 + place: place for place in range(len(filled))},
        compiler_params=pltpu.CompilerParams(vmem_limit_bytes=MIB),
        cost_estimate=cost(0, 4 * rows_in.size),
        name="unpack",
    )(kinds, rows_in, *filled)


def spatial(kinds, frame, arrays, prior, heads):
    count = arrays[0].shape[0]
    slots = prior.shape[0]
    chunk = 256

    def kernel(
        kind_ref, frame_ref, q_ref, k_ref, v_ref, g_ref, prior_ref,
        out_ref, qgrad_ref, own_ref, send_ref,
    ):
        has_prior = frame_ref[0] > 0
        k, v = k_ref[...], v_ref[...]
        k_prior, v_prior = prior_ref[0, 0], prior_ref[0, 1]
        k_own = v_own = k_send = v_send = None
        for start in range(0, count, chunk):
            part = slice(start, start + chunk)
            q, g = q_ref[part], g_ref[part]
            own = dot_nt(q, k) * SCALE
            before = jnp.where(has_prior, dot_nt(q, k_prior) * SCALE, MASKED)
            top = jnp.maximum(
                jnp.max(own, axis=1, keepdims=True), jnp.max(before, axis=1, keepdims=True)
            )
            own, before = jnp.exp(own - top), jnp.exp(before - top)
            total = jnp.sum(own, axis=1, keepdims=True) + jnp.sum(before, axis=1, keepdims=True)
            inverse = 1.0 / total
            own, before = own * inverse, before * inverse
            own_prob, before_prob = own.astype(BF16), before.astype(BF16)
            attended = (dot_nn(own_prob, v) + dot_nn(before_prob, v_prior)).astype(BF16)
            delta = jnp.sum(g.astype(F32) * attended.astype(F32), axis=1, keepdims=True)
            own_ds = (own * (dot_nt(g, v) - delta) * SCALE).astype(BF16)
            before_ds = (before * (dot_nt(g, v_prior) - delta) * SCALE).astype(BF16)
            out_ref[part] = attended
            qgrad_ref[part] = (dot_nn(own_ds, k) + dot_nn(before_ds, k_prior)).astype(BF16)
            terms = (
                dot_tn(own_ds, q), dot_tn(own_prob, g), dot_tn(before_ds, q), dot_tn(before_prob, g)
            )
            if start == 0:
                k_own, v_own, k_send, v_send = terms
            else:
                k_own, v_own = k_own + terms[0], v_own + terms[1]
                k_send, v_send = k_send + terms[2], v_send + terms[3]
        own_ref[0, 0], own_ref[0, 1] = k_own, v_own
        send_ref[0, 0], send_ref[0, 1] = k_send.astype(BF16), v_send.astype(BF16)

    columns = pl.BlockSpec(
        (count, DH), lambda i, kind_ref, frame_ref: (0, head_at(kind_ref, heads, SPATIAL, i))
    )
    pair = pl.BlockSpec((1, 2, count, DH), lambda i, kind_ref, frame_ref: (i, 0, 0, 0))
    whole = jax.ShapeDtypeStruct((count, heads * DH), BF16)
    return pl.pallas_call(
        kernel,
        out_shape=[
            whole,
            whole,
            jax.ShapeDtypeStruct(prior.shape, F32),
            jax.ShapeDtypeStruct(prior.shape, BF16),
        ],
        grid_spec=pltpu.PrefetchScalarGridSpec(
            num_scalar_prefetch=2,
            grid=(slots,),
            in_specs=[columns] * 4 + [pair],
            out_specs=[columns, columns, pair, pair],
        ),
        compiler_params=params(48),
        cost_estimate=cost(24 * slots * count * count * DH, 12 * 2 * slots * count * DH),
        name="spatial",
    )(kinds, frame, *arrays, prior)


def add_spatial(kinds, own, back, heads):
    slots, _, count, _ = own.shape

    def kernel(kind_ref, own_ref, back_ref, k_ref, v_ref):
        k_ref[...] = (own_ref[0, 0] + back_ref[0, 0].astype(F32)).astype(BF16)
        v_ref[...] = (own_ref[0, 1] + back_ref[0, 1].astype(F32)).astype(BF16)

    pair = pl.BlockSpec((1, 2, count, DH), lambda i, kind_ref: (i, 0, 0, 0))
    return pl.pallas_call(
        kernel,
        out_shape=[jax.ShapeDtypeStruct((count, heads * DH), BF16)] * 2,
        grid_spec=pltpu.PrefetchScalarGridSpec(
            num_scalar_prefetch=1,
            grid=(slots,),
            in_specs=[pair, pair],
            out_specs=[column_spec(count, heads, SPATIAL)] * 2,
        ),
        compiler_params=params(),
        cost_estimate=cost(0, 8 * own.size),
        name="add_spatial",
    )(kinds, own, back)


def passed_along(array, axis, by):
    length = lax.axis_size(axis)
    pairs = [(i, i + by) for i in range(length) if 0 <= i + by < length]
    return lax.ppermute(array, axis, pairs)


def branch(slots, heads, kinds, bands, frame, q, k, v, g):
    frames, rows, width = q.shape
    count = frames * rows
    exchange = functools.partial(
        lax.all_to_all, axis_name="ctx", split_axis=0, concat_axis=0, tiled=True
    )
    packed, pairs = pack(kinds, (q, k, v, g), slots, heads)
    filled = ()
    if slots > 0:
        framed = exchange(packed)
    if slots < heads:
        prior = passed_along(pairs, "ctx", 1).reshape(heads - slots, 2, count, DH)
        flat = [x.reshape(count, width) for x in (q, k, v, g)]
        attended, qgrad, own, send = spatial(kinds, frame, flat, prior, heads)
        if slots > 0:
            framed, send = lax.optimization_barrier((framed, send))
        back = passed_along(send, "ctx", -1)
        filled = (attended, qgrad, *add_spatial(kinds, own, back, heads))
        filled = tuple(x.reshape(q.shape) for x in filled)
    if slots > 0:
        returned = exchange(temporal(kinds, bands, framed, heads))
        filled = unpack(kinds, returned, filled, heads)
    return tuple(filled)


def body(queries, key_rows, value_rows, out_grad, head_kind, frame_band):
    frames = lax.axis_size("ctx")
    heads = queries.shape[2] // DH
    first = lax.axis_index("head") * heads
    kinds = lax.dynamic_slice_in_dim(head_kind, first, heads)
    bands = lax.dynamic_slice_in_dim(frame_band, first, heads)
    frame = lax.axis_index("ctx").astype(jnp.int32).reshape(1)
    count = queries.shape[1]
    arrays = [
        x.reshape(frames, count // frames, heads * DH)
        for x in (queries, key_rows, value_rows, out_grad)
    ]
    slots = jnp.sum((kinds == TEMPORAL).astype(jnp.int32))
    outs = lax.switch(
        slots,
        [functools.partial(branch, n, heads) for n in range(heads + 1)],
        kinds, bands, frame, *arrays,
    )
    return tuple(out.reshape(queries.shape) for out in outs)


def solution(mesh):
    rows = P("ctx", None, "head")
    return jax.shard_map(
        body,
        mesh=mesh,
        in_specs=(rows, rows, rows, rows, P(), P()),
        out_specs=(rows, rows, rows, rows),
        check_vma=False,
    )
```

```python
import functools

import jax
import jax.numpy as jnp
from jax import lax
from jax.experimental import pallas as pl
from jax.experimental.pallas import tpu as pltpu
from jax.sharding import PartitionSpec as P

DH = 128
SCALE = DH ** (-0.5)
SPATIAL, TEMPORAL = 1, 0
MASKED = -1e30
F32 = jnp.float32
BF16 = jnp.bfloat16
MIB = 1024 * 1024


def head_at(kind_ref, heads, kind, slot):
    found, seen = jnp.int32(0), jnp.int32(0)
    for head in range(heads):
        hit = kind_ref[head] == kind
        found = jnp.where(jnp.logical_and(hit, seen == slot), jnp.int32(head), found)
        seen = seen + hit.astype(jnp.int32)
    return found


def dot_nt(a, b):
    return lax.dot_general(a, b, (((1,), (1,)), ((), ())), preferred_element_type=F32)


def dot_nn(a, b):
    return lax.dot_general(a, b, (((1,), (0,)), ((), ())), preferred_element_type=F32)


def dot_tn(a, b):
    return lax.dot_general(a, b, (((0,), (0,)), ((), ())), preferred_element_type=F32)


def params(mib=32):
    return pltpu.CompilerParams(
        dimension_semantics=("arbitrary",), vmem_limit_bytes=mib * MIB
    )


def cost(flops, moved):
    return pl.CostEstimate(flops=int(flops), bytes_accessed=int(moved), transcendentals=0)


def column_spec(count, heads, kind):
    return pl.BlockSpec((count, DH), lambda i, kind_ref: (0, head_at(kind_ref, heads, kind, i)))


def head_columns(kind_ref, heads, kind, slot):
    return pl.ds(pl.multiple_of(head_at(kind_ref, heads, kind, slot) * DH, DH), DH)


def staged_copies(triples, in_sems, out_sems):
    loads = [pltpu.make_async_copy(x, y, in_sems.at[i]) for i, (x, y, _) in enumerate(triples)]
    stores = [pltpu.make_async_copy(y, z, out_sems.at[i]) for i, (_, y, z) in enumerate(triples)]
    for load in loads:
        load.start()
    for load, store in zip(loads, stores):
        load.wait()
        store.start()
    for store in stores:
        store.wait()


def moving_params(staged):
    return pltpu.CompilerParams(vmem_limit_bytes=2 * staged + 4 * MIB)


def pack_spatial(kinds, arrays, slots, heads):
    frames, rows, _ = arrays[0].shape
    count = len(arrays)
    total = slots * count

    def kernel(kind_ref, *refs):
        ins, (out, stage, in_sems, out_sems) = refs[:count], refs[count:]
        triples = []
        for slot in range(slots):
            cols = head_columns(kind_ref, heads, SPATIAL, slot)
            for place, ref in enumerate(ins):
                triples.append(
                    (ref.at[:, :, cols], stage.at[slot, place], out.at[slot, place])
                )
        staged_copies(triples, in_sems, out_sems)

    shape = (slots, count, frames, rows, DH)
    return pl.pallas_call(
        kernel,
        out_shape=jax.ShapeDtypeStruct(shape, BF16),
        in_specs=[pl.BlockSpec(memory_space=pltpu.SMEM)]
        + [pl.BlockSpec(memory_space=pl.ANY)] * count,
        out_specs=pl.BlockSpec(memory_space=pltpu.HBM),
        scratch_shapes=[
            pltpu.VMEM(shape, BF16),
            pltpu.SemaphoreType.DMA((total,)),
            pltpu.SemaphoreType.DMA((total,)),
        ],
        compiler_params=moving_params(2 * total * frames * rows * DH),
        cost_estimate=cost(0, 4 * total * frames * rows * DH),
        name="pack_spatial",
    )(kinds, *arrays)


def pack_temporal(kinds, arrays, slots, heads, after):
    frames, rows, _ = arrays[0].shape
    total = 4 * slots
    extra = 0 if after is None else 1

    def kernel(kind_ref, *refs):
        ins, (out, stage, in_sems, out_sems) = refs[:4], refs[4 + extra :]
        triples = []
        for slot in range(slots):
            cols = head_columns(kind_ref, heads, TEMPORAL, slot)
            for place, ref in enumerate(ins):
                triples.append(
                    (ref.at[:, :, cols], stage.at[slot, place], out.at[:, place, slot])
                )
        staged_copies(triples, in_sems, out_sems)

    return pl.pallas_call(
        kernel,
        out_shape=jax.ShapeDtypeStruct((frames, 4, slots, rows, DH), BF16),
        in_specs=[pl.BlockSpec(memory_space=pltpu.SMEM)]
        + [pl.BlockSpec(memory_space=pl.ANY)] * (4 + extra),
        out_specs=pl.BlockSpec(memory_space=pltpu.HBM),
        scratch_shapes=[
            pltpu.VMEM((slots, 4, frames, rows, DH), BF16),
            pltpu.SemaphoreType.DMA((total,)),
            pltpu.SemaphoreType.DMA((total,)),
        ],
        compiler_params=moving_params(2 * total * frames * rows * DH),
        cost_estimate=cost(0, 4 * total * frames * rows * DH),
        name="pack_temporal",
    )(kinds, *arrays, *([] if after is None else [after]))


def temporal(kinds, bands, rows_in, heads):
    frames, _, slots, rows, _ = rows_in.shape
    group = 16
    size = frames * group

    def kernel(kind_ref, band_ref, rows_ref, result_ref, held, made, in_sems, out_sems):
        def load(slot):
            return pltpu.make_async_copy(rows_ref.at[:, :, slot], held.at[slot], in_sems.at[slot])

        def store(slot):
            return pltpu.make_async_copy(
                made.at[slot], result_ref.at[:, :, slot], out_sems.at[slot]
            )

        for slot in range(slots):
            load(slot).start()

        @pl.loop(0, slots)
        def _(slot):
            load(slot).wait()
            one_head(kind_ref, band_ref, slot, held.at[slot], made.at[slot])
            store(slot).start()

        for slot in range(slots):
            store(slot).wait()

    def one_head(kind_ref, band_ref, slot, in_ref, out_ref):
        band = band_ref[head_at(kind_ref, heads, TEMPORAL, slot)]
        row = lax.broadcasted_iota(jnp.int32, (size, size), 0)
        col = lax.broadcasted_iota(jnp.int32, (size, size), 1)
        same = lax.rem(row, group) == lax.rem(col, group)
        near = jnp.abs(lax.div(row, group) - lax.div(col, group)) <= band
        allowed = jnp.logical_and(same, near)
        parts = [slice(start, start + group) for start in range(0, rows, group)]
        qs, ks, vs, gs = (
            [in_ref[:, place, part].reshape(size, DH) for part in parts] for place in range(4)
        )
        scores = [jnp.where(allowed, dot_nt(q, k) * SCALE, MASKED) for q, k in zip(qs, ks)]
        dprobs = [dot_nt(g, v) for g, v in zip(gs, vs)]
        raised = [jnp.exp(x - jnp.max(x, axis=1, keepdims=True)) for x in scores]
        weights = [x * (1.0 / jnp.sum(x, axis=1, keepdims=True)) for x in raised]
        probs = [x.astype(BF16) for x in weights]
        attended = [dot_nn(x, v).astype(BF16) for x, v in zip(probs, vs)]
        deltas = [
            jnp.sum(g.astype(F32) * x.astype(F32), axis=1, keepdims=True)
            for g, x in zip(gs, attended)
        ]
        dscores = [
            (w * (dp - delta) * SCALE).astype(BF16)
            for w, dp, delta in zip(weights, dprobs, deltas)
        ]
        results = (
            attended,
            [dot_nn(x, k).astype(BF16) for x, k in zip(dscores, ks)],
            [dot_tn(x, q).astype(BF16) for x, q in zip(dscores, qs)],
            [dot_tn(x, g).astype(BF16) for x, g in zip(probs, gs)],
        )
        for place, result in enumerate(results):
            for part, value in zip(parts, result):
                out_ref[:, place, part] = value.reshape(frames, group, DH)

    block = (slots, frames, 4, rows, DH)
    return pl.pallas_call(
        kernel,
        out_shape=jax.ShapeDtypeStruct(rows_in.shape, BF16),
        in_specs=[pl.BlockSpec(memory_space=pltpu.SMEM)] * 2
        + [pl.BlockSpec(memory_space=pl.ANY)],
        out_specs=pl.BlockSpec(memory_space=pltpu.HBM),
        scratch_shapes=[
            pltpu.VMEM(block, BF16),
            pltpu.VMEM(block, BF16),
            pltpu.SemaphoreType.DMA((slots,)),
            pltpu.SemaphoreType.DMA((slots,)),
        ],
        compiler_params=pltpu.CompilerParams(vmem_limit_bytes=48 * MIB),
        cost_estimate=cost(12 * slots * rows * frames * size * DH, 4 * rows_in.size),
        name="temporal",
    )(kinds, bands, rows_in)


def unpack(kinds, rows_in, filled, heads):
    frames, _, slots, rows, _ = rows_in.shape

    def kernel(kind_ref, in_ref, *refs):
        outs, (stage, in_sems, out_sems) = refs[-7:-3], refs[-3:]
        triples = []
        for slot in range(slots):
            cols = head_columns(kind_ref, heads, TEMPORAL, slot)
            for place, ref in enumerate(outs):
                triples.append(
                    (in_ref.at[:, place, slot], stage.at[slot, place], ref.at[:, :, cols])
                )
        staged_copies(triples, in_sems, out_sems)

    return pl.pallas_call(
        kernel,
        out_shape=[jax.ShapeDtypeStruct((frames, rows, heads * DH), BF16)] * 4,
        in_specs=[pl.BlockSpec(memory_space=pltpu.SMEM)]
        + [pl.BlockSpec(memory_space=pl.ANY)] * (1 + len(filled)),
        out_specs=[pl.BlockSpec(memory_space=pltpu.HBM)] * 4,
        scratch_shapes=[
            pltpu.VMEM((slots, 4, frames, rows, DH), BF16),
            pltpu.SemaphoreType.DMA((4 * slots,)),
            pltpu.SemaphoreType.DMA((4 * slots,)),
        ],
        input_output_aliases={2 + place: place for place in range(len(filled))},
        compiler_params=moving_params(2 * rows_in.size),
        cost_estimate=cost(0, 4 * rows_in.size),
        name="unpack",
    )(kinds, rows_in, *filled)


def spatial(kinds, frame, arrays, prior, heads):
    count = arrays[0].shape[0]
    slots = prior.shape[0]
    chunk = 256

    def kernel(
        kind_ref, frame_ref, q_ref, k_ref, v_ref, g_ref, prior_ref,
        out_ref, qgrad_ref, own_ref, send_ref,
    ):
        has_prior = frame_ref[0] > 0
        k, v = k_ref[...], v_ref[...]
        k_prior, v_prior = prior_ref[0, 0], prior_ref[0, 1]
        k_own = v_own = k_send = v_send = None
        for start in range(0, count, chunk):
            part = slice(start, start + chunk)
            q, g = q_ref[part], g_ref[part]
            own = dot_nt(q, k) * SCALE
            before = jnp.where(has_prior, dot_nt(q, k_prior) * SCALE, MASKED)
            top = jnp.maximum(
                jnp.max(own, axis=1, keepdims=True), jnp.max(before, axis=1, keepdims=True)
            )
            own, before = jnp.exp(own - top), jnp.exp(before - top)
            total = jnp.sum(own, axis=1, keepdims=True) + jnp.sum(before, axis=1, keepdims=True)
            inverse = 1.0 / total
            own, before = own * inverse, before * inverse
            own_prob, before_prob = own.astype(BF16), before.astype(BF16)
            attended = (dot_nn(own_prob, v) + dot_nn(before_prob, v_prior)).astype(BF16)
            delta = jnp.sum(g.astype(F32) * attended.astype(F32), axis=1, keepdims=True)
            own_ds = (own * (dot_nt(g, v) - delta) * SCALE).astype(BF16)
            before_ds = (before * (dot_nt(g, v_prior) - delta) * SCALE).astype(BF16)
            out_ref[part] = attended
            qgrad_ref[part] = (dot_nn(own_ds, k) + dot_nn(before_ds, k_prior)).astype(BF16)
            terms = (
                dot_tn(own_ds, q), dot_tn(own_prob, g), dot_tn(before_ds, q), dot_tn(before_prob, g)
            )
            if start == 0:
                k_own, v_own, k_send, v_send = terms
            else:
                k_own, v_own = k_own + terms[0], v_own + terms[1]
                k_send, v_send = k_send + terms[2], v_send + terms[3]
        own_ref[0, 0], own_ref[0, 1] = k_own, v_own
        send_ref[0, 0], send_ref[0, 1] = k_send.astype(BF16), v_send.astype(BF16)

    columns = pl.BlockSpec(
        (count, DH), lambda i, kind_ref, frame_ref: (0, head_at(kind_ref, heads, SPATIAL, i))
    )
    pair = pl.BlockSpec((1, 2, count, DH), lambda i, kind_ref, frame_ref: (i, 0, 0, 0))
    whole = jax.ShapeDtypeStruct((count, heads * DH), BF16)
    return pl.pallas_call(
        kernel,
        out_shape=[
            whole,
            whole,
            jax.ShapeDtypeStruct(prior.shape, F32),
            jax.ShapeDtypeStruct(prior.shape, BF16),
        ],
        grid_spec=pltpu.PrefetchScalarGridSpec(
            num_scalar_prefetch=2,
            grid=(slots,),
            in_specs=[columns] * 4 + [pair],
            out_specs=[columns, columns, pair, pair],
        ),
        compiler_params=params(60),
        cost_estimate=cost(24 * slots * count * count * DH, 12 * 2 * slots * count * DH),
        name="spatial",
    )(kinds, frame, *arrays, prior)


def add_spatial(kinds, own, back, heads):
    slots, _, count, _ = own.shape

    def kernel(kind_ref, own_ref, back_ref, k_ref, v_ref):
        k_ref[...] = (own_ref[0, 0] + back_ref[0, 0].astype(F32)).astype(BF16)
        v_ref[...] = (own_ref[0, 1] + back_ref[0, 1].astype(F32)).astype(BF16)

    pair = pl.BlockSpec((1, 2, count, DH), lambda i, kind_ref: (i, 0, 0, 0))
    return pl.pallas_call(
        kernel,
        out_shape=[jax.ShapeDtypeStruct((count, heads * DH), BF16)] * 2,
        grid_spec=pltpu.PrefetchScalarGridSpec(
            num_scalar_prefetch=1,
            grid=(slots,),
            in_specs=[pair, pair],
            out_specs=[column_spec(count, heads, SPATIAL)] * 2,
        ),
        compiler_params=params(),
        cost_estimate=cost(0, 8 * own.size),
        name="add_spatial",
    )(kinds, own, back)


def passed_along(array, axis, by):
    length = lax.axis_size(axis)
    pairs = [(i, i + by) for i in range(length) if 0 <= i + by < length]
    return lax.ppermute(array, axis, pairs)


def branch(slots, heads, kinds, bands, frame, q, k, v, g):
    frames, rows, width = q.shape
    count = frames * rows
    exchange = functools.partial(
        lax.all_to_all, axis_name="ctx", split_axis=0, concat_axis=0, tiled=True
    )
    filled, pairs = (), None
    if slots < heads:
        pairs = pack_spatial(kinds, (k, v), heads - slots, heads)
    if slots > 0:
        framed = exchange(pack_temporal(kinds, (q, k, v, g), slots, heads, pairs))
    if slots < heads:
        prior = passed_along(pairs, "ctx", 1).reshape(heads - slots, 2, count, DH)
        flat = [x.reshape(count, width) for x in (q, k, v, g)]
        attended, qgrad, own, send = spatial(kinds, frame, flat, prior, heads)
        if slots > 0:
            framed, _ = lax.optimization_barrier((framed, send))
        back = passed_along(send, "ctx", -1)
        filled = (attended, qgrad, *add_spatial(kinds, own, back, heads))
        filled = tuple(x.reshape(q.shape) for x in filled)
    if slots > 0:
        returned = exchange(temporal(kinds, bands, framed, heads))
        filled = unpack(kinds, returned, filled, heads)
    return tuple(filled)


def body(queries, key_rows, value_rows, out_grad, head_kind, frame_band):
    frames = lax.axis_size("ctx")
    heads = queries.shape[2] // DH
    first = lax.axis_index("head") * heads
    kinds = lax.dynamic_slice_in_dim(head_kind, first, heads)
    bands = lax.dynamic_slice_in_dim(frame_band, first, heads)
    frame = lax.axis_index("ctx").astype(jnp.int32).reshape(1)
    count = queries.shape[1]
    arrays = [
        x.reshape(frames, count // frames, heads * DH)
        for x in (queries, key_rows, value_rows, out_grad)
    ]
    slots = jnp.sum((kinds == TEMPORAL).astype(jnp.int32))
    outs = lax.switch(
        slots,
        [functools.partial(branch, n, heads) for n in range(heads + 1)],
        kinds, bands, frame, *arrays,
    )
    return tuple(out.reshape(queries.shape) for out in outs)


def solution(mesh):
    rows = P("ctx", None, "head")
    return jax.shard_map(
        body,
        mesh=mesh,
        in_specs=(rows, rows, rows, rows, P(), P()),
        out_specs=(rows, rows, rows, rows),
        check_vma=False,
    )
```

```python
import functools

import jax
import jax.numpy as jnp
from jax import lax
from jax.experimental import pallas as pl
from jax.experimental.pallas import tpu as pltpu
from jax.sharding import PartitionSpec as P

DH = 128
SCALE = DH ** (-0.5)
SPATIAL, TEMPORAL = 1, 0
MASKED = -1e30
F32 = jnp.float32
BF16 = jnp.bfloat16
MIB = 1024 * 1024


def head_at(kind_ref, first_ref, heads, kind, slot):
    found, seen = jnp.int32(0), jnp.int32(0)
    for head in range(heads):
        hit = kind_ref[first_ref[0] + head] == kind
        found = jnp.where(jnp.logical_and(hit, seen == slot), jnp.int32(head), found)
        seen = seen + hit.astype(jnp.int32)
    return found


def dot_nt(a, b):
    return lax.dot_general(a, b, (((1,), (1,)), ((), ())), preferred_element_type=F32)


def dot_nn(a, b):
    return lax.dot_general(a, b, (((1,), (0,)), ((), ())), preferred_element_type=F32)


def dot_tn(a, b):
    return lax.dot_general(a, b, (((0,), (0,)), ((), ())), preferred_element_type=F32)


def params(mib=32):
    return pltpu.CompilerParams(
        dimension_semantics=("arbitrary",), vmem_limit_bytes=mib * MIB
    )


def cost(flops, moved):
    return pl.CostEstimate(flops=int(flops), bytes_accessed=int(moved), transcendentals=0)


def column_spec(count, heads, kind):
    return pl.BlockSpec((count, DH), lambda i, *refs: (0, head_at(*refs[:2], heads, kind, i)))


def head_columns(kind_ref, first_ref, heads, kind, slot):
    return pl.ds(pl.multiple_of(head_at(kind_ref, first_ref, heads, kind, slot) * DH, DH), DH)


def staged_copies(triples, in_sems, out_sems):
    loads = [pltpu.make_async_copy(x, y, in_sems.at[i]) for i, (x, y, _) in enumerate(triples)]
    stores = [pltpu.make_async_copy(y, z, out_sems.at[i]) for i, (_, y, z) in enumerate(triples)]
    for load in loads:
        load.start()
    for load, store in zip(loads, stores):
        load.wait()
        store.start()
    for store in stores:
        store.wait()


def whole_params():
    return pltpu.CompilerParams(vmem_limit_bytes=62 * MIB)


def pack_spatial(kinds, first, arrays, slots, heads):
    frames, rows, _ = arrays[0].shape
    count = len(arrays)
    total = slots * count

    def kernel(kind_ref, first_ref, *refs):
        ins, outs = refs[:count], refs[count:-3]
        stage, in_sems, out_sems = refs[-3:]
        triples = []
        for slot in range(slots):
            cols = head_columns(kind_ref, first_ref, heads, SPATIAL, slot)
            for place, ref in enumerate(ins):
                target = outs[place // 2].at[slot, place % 2]
                triples.append((ref.at[:, :, cols], stage.at[slot, place], target))
        staged_copies(triples, in_sems, out_sems)

    pair = jax.ShapeDtypeStruct((slots, 2, frames, rows, DH), BF16)
    return pl.pallas_call(
        kernel,
        out_shape=[pair] * (count // 2),
        in_specs=[pl.BlockSpec(memory_space=pltpu.SMEM)] * 2
        + [pl.BlockSpec(memory_space=pl.ANY)] * count,
        out_specs=[pl.BlockSpec(memory_space=pl.ANY)] * (count // 2),
        scratch_shapes=[
            pltpu.VMEM((slots, count, frames, rows, DH), BF16),
            pltpu.SemaphoreType.DMA((total,)),
            pltpu.SemaphoreType.DMA((total,)),
        ],
        compiler_params=whole_params(),
        cost_estimate=cost(0, 4 * total * frames * rows * DH),
        name="pack_spatial",
    )(kinds, first, *arrays)


def pack_temporal(kinds, first, arrays, slots, heads):
    frames, rows, _ = arrays[0].shape
    total = 4 * slots

    def kernel(kind_ref, first_ref, *refs):
        ins, (out, stage, in_sems, out_sems) = refs[:4], refs[4:]
        triples = []
        for slot in range(slots):
            cols = head_columns(kind_ref, first_ref, heads, TEMPORAL, slot)
            for place, ref in enumerate(ins):
                triples.append(
                    (ref.at[:, :, cols], stage.at[slot, place], out.at[:, place, slot])
                )
        staged_copies(triples, in_sems, out_sems)

    return pl.pallas_call(
        kernel,
        out_shape=jax.ShapeDtypeStruct((frames, 4, slots, rows, DH), BF16),
        in_specs=[pl.BlockSpec(memory_space=pltpu.SMEM)] * 2
        + [pl.BlockSpec(memory_space=pl.ANY)] * 4,
        out_specs=pl.BlockSpec(memory_space=pl.ANY),
        scratch_shapes=[
            pltpu.VMEM((slots, 4, frames, rows, DH), BF16),
            pltpu.SemaphoreType.DMA((total,)),
            pltpu.SemaphoreType.DMA((total,)),
        ],
        compiler_params=whole_params(),
        cost_estimate=cost(0, 4 * total * frames * rows * DH),
        name="pack_temporal",
    )(kinds, first, *arrays)


def temporal(kinds, first, bands, rows_in, heads):
    frames, _, slots, rows, _ = rows_in.shape
    group = 16
    size = frames * group

    def kernel(kind_ref, first_ref, band_ref, rows_ref, result_ref, held, made, in_sems, out_sems):
        def load(slot):
            return pltpu.make_async_copy(rows_ref.at[:, :, slot], held.at[slot], in_sems.at[slot])

        def store(slot):
            return pltpu.make_async_copy(
                made.at[slot], result_ref.at[:, :, slot], out_sems.at[slot]
            )

        for slot in range(slots):
            load(slot).start()

        @pl.loop(0, slots)
        def _(slot):
            load(slot).wait()
            one_head(kind_ref, first_ref, band_ref, slot, held.at[slot], made.at[slot])
            store(slot).start()

        for slot in range(slots):
            store(slot).wait()

    def one_head(kind_ref, first_ref, band_ref, slot, in_ref, out_ref):
        band = band_ref[first_ref[0] + head_at(kind_ref, first_ref, heads, TEMPORAL, slot)]
        row = lax.broadcasted_iota(jnp.int32, (size, size), 0)
        col = lax.broadcasted_iota(jnp.int32, (size, size), 1)
        same = lax.rem(row, group) == lax.rem(col, group)
        near = jnp.abs(lax.div(row, group) - lax.div(col, group)) <= band
        allowed = jnp.logical_and(same, near)
        parts = [slice(start, start + group) for start in range(0, rows, group)]
        qs, ks, vs, gs = (
            [in_ref[:, place, part].reshape(size, DH) for part in parts] for place in range(4)
        )
        scores = [jnp.where(allowed, dot_nt(q, k) * SCALE, MASKED) for q, k in zip(qs, ks)]
        dprobs = [dot_nt(g, v) for g, v in zip(gs, vs)]
        raised = [jnp.exp(x - jnp.max(x, axis=1, keepdims=True)) for x in scores]
        weights = [x * (1.0 / jnp.sum(x, axis=1, keepdims=True)) for x in raised]
        probs = [x.astype(BF16) for x in weights]
        attended = [dot_nn(x, v).astype(BF16) for x, v in zip(probs, vs)]
        deltas = [
            jnp.sum(g.astype(F32) * x.astype(F32), axis=1, keepdims=True)
            for g, x in zip(gs, attended)
        ]
        dscores = [
            (w * (dp - delta) * SCALE).astype(BF16)
            for w, dp, delta in zip(weights, dprobs, deltas)
        ]
        results = (
            attended,
            [dot_nn(x, k).astype(BF16) for x, k in zip(dscores, ks)],
            [dot_tn(x, q).astype(BF16) for x, q in zip(dscores, qs)],
            [dot_tn(x, g).astype(BF16) for x, g in zip(probs, gs)],
        )
        for place, result in enumerate(results):
            for part, value in zip(parts, result):
                out_ref[:, place, part] = value.reshape(frames, group, DH)

    block = (slots, frames, 4, rows, DH)
    return pl.pallas_call(
        kernel,
        out_shape=jax.ShapeDtypeStruct(rows_in.shape, BF16),
        in_specs=[pl.BlockSpec(memory_space=pltpu.SMEM)] * 3
        + [pl.BlockSpec(memory_space=pl.ANY)],
        out_specs=pl.BlockSpec(memory_space=pl.ANY),
        scratch_shapes=[
            pltpu.VMEM(block, BF16),
            pltpu.VMEM(block, BF16),
            pltpu.SemaphoreType.DMA((slots,)),
            pltpu.SemaphoreType.DMA((slots,)),
        ],
        compiler_params=whole_params(),
        cost_estimate=cost(12 * slots * rows * frames * size * DH, 4 * rows_in.size),
        name="temporal",
    )(kinds, first, bands, rows_in)


def unpack(kinds, first, rows_in, filled, heads):
    frames, _, slots, rows, _ = rows_in.shape

    def kernel(kind_ref, first_ref, in_ref, *refs):
        outs, (stage, in_sems, out_sems) = refs[-7:-3], refs[-3:]
        triples = []
        for slot in range(slots):
            cols = head_columns(kind_ref, first_ref, heads, TEMPORAL, slot)
            for place, ref in enumerate(outs):
                triples.append(
                    (in_ref.at[:, place, slot], stage.at[slot, place], ref.at[:, :, cols])
                )
        staged_copies(triples, in_sems, out_sems)

    return pl.pallas_call(
        kernel,
        out_shape=[jax.ShapeDtypeStruct((frames, rows, heads * DH), BF16)] * 4,
        in_specs=[pl.BlockSpec(memory_space=pltpu.SMEM)] * 2
        + [pl.BlockSpec(memory_space=pl.ANY)] * (1 + len(filled)),
        out_specs=[pl.BlockSpec(memory_space=pl.ANY)] * 4,
        scratch_shapes=[
            pltpu.VMEM((slots, 4, frames, rows, DH), BF16),
            pltpu.SemaphoreType.DMA((4 * slots,)),
            pltpu.SemaphoreType.DMA((4 * slots,)),
        ],
        input_output_aliases={3 + place: place for place in range(len(filled))},
        compiler_params=whole_params(),
        cost_estimate=cost(0, 4 * rows_in.size),
        name="unpack",
    )(kinds, first, rows_in, *filled)


def spatial(kinds, first, frame, arrays, prior, heads):
    count = arrays[0].shape[0]
    slots = prior.shape[0]
    chunk = min(count, 256)

    def kernel(
        kind_ref, first_ref, frame_ref, q_ref, k_ref, v_ref, g_ref, prior_ref,
        out_ref, qgrad_ref, own_ref, stats_ref,
    ):
        has_prior = frame_ref[0] > 0
        k, v = k_ref[...], v_ref[...]
        k_prior, v_prior = prior_ref[0, 0], prior_ref[0, 1]
        k_own = v_own = None
        for start in range(0, count, chunk):
            part = slice(start, start + chunk)
            q, g = q_ref[part], g_ref[part]
            own = dot_nt(q, k) * SCALE
            before = jnp.where(has_prior, dot_nt(q, k_prior) * SCALE, MASKED)
            top = jnp.maximum(
                jnp.max(own, axis=1, keepdims=True), jnp.max(before, axis=1, keepdims=True)
            )
            own, before = jnp.exp(own - top), jnp.exp(before - top)
            total = jnp.sum(own, axis=1, keepdims=True) + jnp.sum(before, axis=1, keepdims=True)
            inverse = 1.0 / total
            own, before = own * inverse, before * inverse
            own_prob, before_prob = own.astype(BF16), before.astype(BF16)
            attended = (dot_nn(own_prob, v) + dot_nn(before_prob, v_prior)).astype(BF16)
            delta = jnp.sum(g.astype(F32) * attended.astype(F32), axis=1, keepdims=True)
            own_ds = (own * (dot_nt(g, v) - delta) * SCALE).astype(BF16)
            before_ds = (before * (dot_nt(g, v_prior) - delta) * SCALE).astype(BF16)
            out_ref[part] = attended
            qgrad_ref[part] = (dot_nn(own_ds, k) + dot_nn(before_ds, k_prior)).astype(BF16)
            k_term, v_term = dot_tn(own_ds, q), dot_tn(own_prob, g)
            k_own = k_term if start == 0 else k_own + k_term
            v_own = v_term if start == 0 else v_own + v_term
            lane = lax.broadcasted_iota(jnp.int32, (chunk, DH), 1)
            stats = jnp.where(lane == 0, top + jnp.log(total), delta)
            stats_ref[0, :, part] = stats.T[:2]
        own_ref[0, 0], own_ref[0, 1] = k_own, v_own

    columns = column_spec(count, heads, SPATIAL)
    pair = pl.BlockSpec((1, 2, count, DH), lambda i, *refs: (i, 0, 0, 0))
    whole = jax.ShapeDtypeStruct((count, heads * DH), BF16)
    return pl.pallas_call(
        kernel,
        out_shape=[
            whole,
            whole,
            jax.ShapeDtypeStruct(prior.shape, F32),
            jax.ShapeDtypeStruct((slots, 2, count), F32),
        ],
        grid_spec=pltpu.PrefetchScalarGridSpec(
            num_scalar_prefetch=3,
            grid=(slots,),
            in_specs=[columns] * 4 + [pair],
            out_specs=[
                columns, columns, pair, pl.BlockSpec((1, 2, count), lambda i, *refs: (i, 0, 0))
            ],
        ),
        compiler_params=params(60),
        cost_estimate=cost(20 * slots * count * count * DH, 16 * slots * count * DH),
        name="spatial",
    )(kinds, first, frame, *arrays, prior)


def spatial_next(kinds, first, k, v, following, stats, own, heads):
    slots, _, count, _ = own.shape
    chunk = min(count, 256)

    def kernel(
        kind_ref, first_ref, k_ref, v_ref, next_ref, stats_ref, own_ref, kgrad_ref, vgrad_ref
    ):
        q, g = next_ref[0, 0], next_ref[0, 1]
        lse, delta = stats_ref[0, 0:1], stats_ref[0, 1:2]
        for start in range(0, count, chunk):
            part = slice(start, start + chunk)
            weight = jnp.exp(dot_nt(k_ref[part], q) * SCALE - lse)
            dscore = (weight * (dot_nt(v_ref[part], g) - delta) * SCALE).astype(BF16)
            kgrad_ref[part] = (own_ref[0, 0, part] + dot_nn(dscore, q)).astype(BF16)
            vgrad_ref[part] = (own_ref[0, 1, part] + dot_nn(weight.astype(BF16), g)).astype(BF16)

    columns = column_spec(count, heads, SPATIAL)
    pair = pl.BlockSpec((1, 2, count, DH), lambda i, *refs: (i, 0, 0, 0))
    return pl.pallas_call(
        kernel,
        out_shape=[jax.ShapeDtypeStruct((count, heads * DH), BF16)] * 2,
        grid_spec=pltpu.PrefetchScalarGridSpec(
            num_scalar_prefetch=2,
            grid=(slots,),
            in_specs=[columns, columns, pair]
            + [pl.BlockSpec((1, 2, count), lambda i, *refs: (i, 0, 0)), pair],
            out_specs=[columns] * 2,
        ),
        compiler_params=params(60),
        cost_estimate=cost(8 * slots * count * count * DH, 20 * slots * count * DH),
        name="spatial_next",
    )(kinds, first, k, v, following, stats, own)


def passed_along(array, axis, by):
    length = lax.axis_size(axis)
    pairs = [(i, i + by) for i in range(length) if 0 <= i + by < length]
    return lax.ppermute(array, axis, pairs)


def branch(slots, heads, kinds, bands, first, frame, q, k, v, g):
    frames, rows, width = q.shape
    count = frames * rows
    others = heads - slots
    exchange = functools.partial(
        lax.all_to_all, axis_name="ctx", split_axis=0, concat_axis=0, tiled=True
    )
    filled = ()
    if slots > 0:
        framed = exchange(pack_temporal(kinds, first, (q, k, v, g), slots, heads))
    if others > 0:
        ahead, back = pack_spatial(kinds, first, (k, v, q, g), others, heads)
        if slots > 0:
            framed, ahead, back = lax.optimization_barrier((framed, ahead, back))
        prior, following = passed_along(ahead, "ctx", 1), passed_along(back, "ctx", -1)
    if slots > 0:
        results = temporal(kinds, first, bands, framed, heads)
        if others > 0:
            results, prior, following = lax.optimization_barrier((results, prior, following))
        returned = exchange(results)
    if others > 0:
        prior, following = (x.reshape(others, 2, count, DH) for x in (prior, following))
        flat = [x.reshape(count, width) for x in (q, k, v, g)]
        attended, qgrad, own, stats = spatial(kinds, first, frame, flat, prior, heads)
        stats = passed_along(stats, "ctx", -1)
        grads = spatial_next(kinds, first, flat[1], flat[2], following, stats, own, heads)
        filled = tuple(x.reshape(q.shape) for x in (attended, qgrad, *grads))
    if slots > 0:
        filled = unpack(kinds, first, returned, filled, heads)
    return tuple(filled)


def body(queries, key_rows, value_rows, out_grad, head_kind, frame_band):
    frames = lax.axis_size("ctx")
    count = queries.shape[1]
    heads = queries.shape[2] // DH
    first = lax.axis_index("head").astype(jnp.int32) * heads
    frame = lax.axis_index("ctx").astype(jnp.int32)
    kinds = lax.dynamic_slice_in_dim(head_kind, first, heads)
    slots = jnp.sum((kinds == TEMPORAL).astype(jnp.int32))
    arrays = [
        x.reshape(frames, count // frames, heads * DH)
        for x in (queries, key_rows, value_rows, out_grad)
    ]
    outs = lax.switch(
        slots,
        [functools.partial(branch, n, heads) for n in range(heads + 1)],
        head_kind, frame_band, first.reshape(1), frame.reshape(1), *arrays,
    )
    return tuple(out.reshape(queries.shape) for out in outs)


def solution(mesh):
    rows = P("ctx", None, "head")
    return jax.shard_map(
        body,
        mesh=mesh,
        in_specs=(rows, rows, rows, rows, P(), P()),
        out_specs=(rows, rows, rows, rows),
        check_vma=False,
    )
```

```python
import functools

import jax
import jax.numpy as jnp
from jax import lax
from jax.experimental import pallas as pl
from jax.experimental.pallas import tpu as pltpu
from jax.sharding import PartitionSpec as P

DH = 128
SCALE = DH ** (-0.5)
SPATIAL, TEMPORAL = 1, 0
MASKED = -1e30
F32 = jnp.float32
BF16 = jnp.bfloat16
MIB = 1024 * 1024


def head_at(kind_ref, first_ref, heads, kind, slot):
    found, seen = jnp.int32(0), jnp.int32(0)
    for head in range(heads):
        hit = kind_ref[first_ref[0] + head] == kind
        found = jnp.where(jnp.logical_and(hit, seen == slot), jnp.int32(head), found)
        seen = seen + hit.astype(jnp.int32)
    return found


def dot_nt(a, b):
    return lax.dot_general(a, b, (((1,), (1,)), ((), ())), preferred_element_type=F32)


def dot_nn(a, b):
    return lax.dot_general(a, b, (((1,), (0,)), ((), ())), preferred_element_type=F32)


def dot_tn(a, b):
    return lax.dot_general(a, b, (((0,), (0,)), ((), ())), preferred_element_type=F32)


def params(mib=32):
    return pltpu.CompilerParams(
        dimension_semantics=("arbitrary",), vmem_limit_bytes=mib * MIB
    )


def cost(flops, moved):
    return pl.CostEstimate(flops=int(flops), bytes_accessed=int(moved), transcendentals=0)


def column_spec(count, heads, kind):
    return pl.BlockSpec((count, DH), lambda i, *refs: (0, head_at(*refs[:2], heads, kind, i)))


def head_columns(kind_ref, first_ref, heads, kind, slot):
    return pl.ds(pl.multiple_of(head_at(kind_ref, first_ref, heads, kind, slot) * DH, DH), DH)


def staged_copies(triples, in_sems, out_sems):
    loads = [pltpu.make_async_copy(x, y, in_sems.at[i]) for i, (x, y, _) in enumerate(triples)]
    stores = [pltpu.make_async_copy(y, z, out_sems.at[i]) for i, (_, y, z) in enumerate(triples)]
    for load in loads:
        load.start()
    for load, store in zip(loads, stores):
        load.wait()
        store.start()
    for store in stores:
        store.wait()


def whole_params():
    return pltpu.CompilerParams(vmem_limit_bytes=62 * MIB)


def pack_spatial(kinds, first, arrays, slots, heads):
    frames, rows, _ = arrays[0].shape
    count = len(arrays)
    total = slots * count

    def kernel(kind_ref, first_ref, *refs):
        ins, outs = refs[:count], refs[count:-3]
        stage, in_sems, out_sems = refs[-3:]
        triples = []
        for slot in range(slots):
            cols = head_columns(kind_ref, first_ref, heads, SPATIAL, slot)
            for place, ref in enumerate(ins):
                target = outs[place // 2].at[slot, place % 2]
                triples.append((ref.at[:, :, cols], stage.at[slot, place], target))
        staged_copies(triples, in_sems, out_sems)

    pair = jax.ShapeDtypeStruct((slots, 2, frames, rows, DH), BF16)
    return pl.pallas_call(
        kernel,
        out_shape=[pair] * (count // 2),
        in_specs=[pl.BlockSpec(memory_space=pltpu.SMEM)] * 2
        + [pl.BlockSpec(memory_space=pl.ANY)] * count,
        out_specs=[pl.BlockSpec(memory_space=pl.ANY)] * (count // 2),
        scratch_shapes=[
            pltpu.VMEM((slots, count, frames, rows, DH), BF16),
            pltpu.SemaphoreType.DMA((total,)),
            pltpu.SemaphoreType.DMA((total,)),
        ],
        compiler_params=whole_params(),
        cost_estimate=cost(0, 4 * total * frames * rows * DH),
        name="pack_spatial",
    )(kinds, first, *arrays)


def pack_temporal(kinds, first, arrays, span, heads):
    frames, rows, _ = arrays[0].shape
    low, slots = span[0], span[1] - span[0]
    total = 4 * slots

    def kernel(kind_ref, first_ref, *refs):
        ins, (out, stage, in_sems, out_sems) = refs[:4], refs[4:]
        triples = []
        for slot in range(slots):
            cols = head_columns(kind_ref, first_ref, heads, TEMPORAL, low + slot)
            for place, ref in enumerate(ins):
                triples.append(
                    (ref.at[:, :, cols], stage.at[slot, place], out.at[:, place, slot])
                )
        staged_copies(triples, in_sems, out_sems)

    return pl.pallas_call(
        kernel,
        out_shape=jax.ShapeDtypeStruct((frames, 4, slots, rows, DH), BF16),
        in_specs=[pl.BlockSpec(memory_space=pltpu.SMEM)] * 2
        + [pl.BlockSpec(memory_space=pl.ANY)] * 4,
        out_specs=pl.BlockSpec(memory_space=pl.ANY),
        scratch_shapes=[
            pltpu.VMEM((slots, 4, frames, rows, DH), BF16),
            pltpu.SemaphoreType.DMA((total,)),
            pltpu.SemaphoreType.DMA((total,)),
        ],
        compiler_params=whole_params(),
        cost_estimate=cost(0, 4 * total * frames * rows * DH),
        name="pack_temporal",
    )(kinds, first, *arrays)


def temporal(kinds, first, bands, rows_in, low, heads):
    frames, _, slots, rows, _ = rows_in.shape
    group = 16
    size = frames * group

    def kernel(kind_ref, first_ref, band_ref, rows_ref, result_ref, held, made, in_sems, out_sems):
        def load(slot):
            return pltpu.make_async_copy(rows_ref.at[:, :, slot], held.at[slot], in_sems.at[slot])

        def store(slot):
            return pltpu.make_async_copy(
                made.at[slot], result_ref.at[:, :, slot], out_sems.at[slot]
            )

        for slot in range(slots):
            load(slot).start()

        @pl.loop(0, slots)
        def _(slot):
            load(slot).wait()
            one_head(kind_ref, first_ref, band_ref, slot, held.at[slot], made.at[slot])
            store(slot).start()

        for slot in range(slots):
            store(slot).wait()

    def one_head(kind_ref, first_ref, band_ref, slot, in_ref, out_ref):
        band = band_ref[first_ref[0] + head_at(kind_ref, first_ref, heads, TEMPORAL, low + slot)]
        row = lax.broadcasted_iota(jnp.int32, (size, size), 0)
        col = lax.broadcasted_iota(jnp.int32, (size, size), 1)
        same = lax.rem(row, group) == lax.rem(col, group)
        near = jnp.abs(lax.div(row, group) - lax.div(col, group)) <= band
        allowed = jnp.logical_and(same, near)
        parts = [slice(start, start + group) for start in range(0, rows, group)]
        qs, ks, vs, gs = (
            [in_ref[:, place, part].reshape(size, DH) for part in parts] for place in range(4)
        )
        scores = [jnp.where(allowed, dot_nt(q, k) * SCALE, MASKED) for q, k in zip(qs, ks)]
        dprobs = [dot_nt(g, v) for g, v in zip(gs, vs)]
        raised = [jnp.exp(x - jnp.max(x, axis=1, keepdims=True)) for x in scores]
        weights = [x * (1.0 / jnp.sum(x, axis=1, keepdims=True)) for x in raised]
        probs = [x.astype(BF16) for x in weights]
        attended = [dot_nn(x, v).astype(BF16) for x, v in zip(probs, vs)]
        deltas = [
            jnp.sum(g.astype(F32) * x.astype(F32), axis=1, keepdims=True)
            for g, x in zip(gs, attended)
        ]
        dscores = [
            (w * (dp - delta) * SCALE).astype(BF16)
            for w, dp, delta in zip(weights, dprobs, deltas)
        ]
        results = (
            attended,
            [dot_nn(x, k).astype(BF16) for x, k in zip(dscores, ks)],
            [dot_tn(x, q).astype(BF16) for x, q in zip(dscores, qs)],
            [dot_tn(x, g).astype(BF16) for x, g in zip(probs, gs)],
        )
        for place, result in enumerate(results):
            for part, value in zip(parts, result):
                out_ref[:, place, part] = value.reshape(frames, group, DH)

    block = (slots, frames, 4, rows, DH)
    return pl.pallas_call(
        kernel,
        out_shape=jax.ShapeDtypeStruct(rows_in.shape, BF16),
        in_specs=[pl.BlockSpec(memory_space=pltpu.SMEM)] * 3
        + [pl.BlockSpec(memory_space=pl.ANY)],
        out_specs=pl.BlockSpec(memory_space=pl.ANY),
        scratch_shapes=[
            pltpu.VMEM(block, BF16),
            pltpu.VMEM(block, BF16),
            pltpu.SemaphoreType.DMA((slots,)),
            pltpu.SemaphoreType.DMA((slots,)),
        ],
        compiler_params=whole_params(),
        cost_estimate=cost(12 * slots * rows * frames * size * DH, 4 * rows_in.size),
        name="temporal",
    )(kinds, first, bands, rows_in)


def unpack(kinds, first, rows_in, low, filled, heads):
    frames, _, slots, rows, _ = rows_in.shape

    def kernel(kind_ref, first_ref, in_ref, *refs):
        outs, (stage, in_sems, out_sems) = refs[-7:-3], refs[-3:]
        triples = []
        for slot in range(slots):
            cols = head_columns(kind_ref, first_ref, heads, TEMPORAL, low + slot)
            for place, ref in enumerate(outs):
                triples.append(
                    (in_ref.at[:, place, slot], stage.at[slot, place], ref.at[:, :, cols])
                )
        staged_copies(triples, in_sems, out_sems)

    return pl.pallas_call(
        kernel,
        out_shape=[jax.ShapeDtypeStruct((frames, rows, heads * DH), BF16)] * 4,
        in_specs=[pl.BlockSpec(memory_space=pltpu.SMEM)] * 2
        + [pl.BlockSpec(memory_space=pl.ANY)] * (1 + len(filled)),
        out_specs=[pl.BlockSpec(memory_space=pl.ANY)] * 4,
        scratch_shapes=[
            pltpu.VMEM((slots, 4, frames, rows, DH), BF16),
            pltpu.SemaphoreType.DMA((4 * slots,)),
            pltpu.SemaphoreType.DMA((4 * slots,)),
        ],
        input_output_aliases={3 + place: place for place in range(len(filled))},
        compiler_params=whole_params(),
        cost_estimate=cost(0, 4 * rows_in.size),
        name="unpack",
    )(kinds, first, rows_in, *filled)


def spatial(kinds, first, frame, arrays, prior, heads):
    count = arrays[0].shape[0]
    slots = prior.shape[0]
    chunk = min(count, 256)

    def kernel(
        kind_ref, first_ref, frame_ref, q_ref, k_ref, v_ref, g_ref, prior_ref,
        out_ref, qgrad_ref, own_ref, stats_ref,
    ):
        has_prior = frame_ref[0] > 0
        k, v = k_ref[...], v_ref[...]
        k_prior, v_prior = prior_ref[0, 0], prior_ref[0, 1]
        k_own = v_own = None
        for start in range(0, count, chunk):
            part = slice(start, start + chunk)
            q, g = q_ref[part], g_ref[part]
            own = dot_nt(q, k) * SCALE
            before = jnp.where(has_prior, dot_nt(q, k_prior) * SCALE, MASKED)
            top = jnp.maximum(
                jnp.max(own, axis=1, keepdims=True), jnp.max(before, axis=1, keepdims=True)
            )
            own, before = jnp.exp(own - top), jnp.exp(before - top)
            total = jnp.sum(own, axis=1, keepdims=True) + jnp.sum(before, axis=1, keepdims=True)
            inverse = 1.0 / total
            own, before = own * inverse, before * inverse
            own_prob, before_prob = own.astype(BF16), before.astype(BF16)
            attended = (dot_nn(own_prob, v) + dot_nn(before_prob, v_prior)).astype(BF16)
            delta = jnp.sum(g.astype(F32) * attended.astype(F32), axis=1, keepdims=True)
            own_ds = (own * (dot_nt(g, v) - delta) * SCALE).astype(BF16)
            before_ds = (before * (dot_nt(g, v_prior) - delta) * SCALE).astype(BF16)
            out_ref[part] = attended
            qgrad_ref[part] = (dot_nn(own_ds, k) + dot_nn(before_ds, k_prior)).astype(BF16)
            k_term, v_term = dot_tn(own_ds, q), dot_tn(own_prob, g)
            k_own = k_term if start == 0 else k_own + k_term
            v_own = v_term if start == 0 else v_own + v_term
            lane = lax.broadcasted_iota(jnp.int32, (chunk, DH), 1)
            stats = jnp.where(lane == 0, top + jnp.log(total), delta)
            stats_ref[0, :, part] = stats.T[:2]
        own_ref[0, 0], own_ref[0, 1] = k_own, v_own

    columns = column_spec(count, heads, SPATIAL)
    pair = pl.BlockSpec((1, 2, count, DH), lambda i, *refs: (i, 0, 0, 0))
    whole = jax.ShapeDtypeStruct((count, heads * DH), BF16)
    return pl.pallas_call(
        kernel,
        out_shape=[
            whole,
            whole,
            jax.ShapeDtypeStruct(prior.shape, F32),
            jax.ShapeDtypeStruct((slots, 2, count), F32),
        ],
        grid_spec=pltpu.PrefetchScalarGridSpec(
            num_scalar_prefetch=3,
            grid=(slots,),
            in_specs=[columns] * 4 + [pair],
            out_specs=[
                columns, columns, pair, pl.BlockSpec((1, 2, count), lambda i, *refs: (i, 0, 0))
            ],
        ),
        compiler_params=params(60),
        cost_estimate=cost(20 * slots * count * count * DH, 16 * slots * count * DH),
        name="spatial",
    )(kinds, first, frame, *arrays, prior)


def spatial_next(kinds, first, k, v, following, stats, own, heads):
    slots, _, count, _ = own.shape
    chunk = min(count, 256)

    def kernel(
        kind_ref, first_ref, k_ref, v_ref, next_ref, stats_ref, own_ref, kgrad_ref, vgrad_ref
    ):
        q, g = next_ref[0, 0], next_ref[0, 1]
        lse, delta = stats_ref[0, 0:1], stats_ref[0, 1:2]
        for start in range(0, count, chunk):
            part = slice(start, start + chunk)
            weight = jnp.exp(dot_nt(k_ref[part], q) * SCALE - lse)
            dscore = (weight * (dot_nt(v_ref[part], g) - delta) * SCALE).astype(BF16)
            kgrad_ref[part] = (own_ref[0, 0, part] + dot_nn(dscore, q)).astype(BF16)
            vgrad_ref[part] = (own_ref[0, 1, part] + dot_nn(weight.astype(BF16), g)).astype(BF16)

    columns = column_spec(count, heads, SPATIAL)
    pair = pl.BlockSpec((1, 2, count, DH), lambda i, *refs: (i, 0, 0, 0))
    return pl.pallas_call(
        kernel,
        out_shape=[jax.ShapeDtypeStruct((count, heads * DH), BF16)] * 2,
        grid_spec=pltpu.PrefetchScalarGridSpec(
            num_scalar_prefetch=2,
            grid=(slots,),
            in_specs=[columns, columns, pair]
            + [pl.BlockSpec((1, 2, count), lambda i, *refs: (i, 0, 0)), pair],
            out_specs=[columns] * 2,
        ),
        compiler_params=params(60),
        cost_estimate=cost(8 * slots * count * count * DH, 20 * slots * count * DH),
        name="spatial_next",
    )(kinds, first, k, v, following, stats, own)


def passed_along(array, axis, by):
    length = lax.axis_size(axis)
    pairs = [(i, i + by) for i in range(length) if 0 <= i + by < length]
    return lax.ppermute(array, axis, pairs)


def behind(arrays, *others):
    return lax.optimization_barrier((tuple(arrays), others))[0]


def chunks_of(slots):
    half = slots // 2
    return [span for span in ((0, half), (half, slots)) if span[1] > span[0]]


def branch(slots, heads, kinds, bands, first, frame, q, k, v, g):
    frames, rows, width = q.shape
    count = frames * rows
    others = heads - slots
    spans = chunks_of(slots)
    exchange = functools.partial(
        lax.all_to_all, axis_name="ctx", split_axis=0, concat_axis=0, tiled=True
    )
    framed, returned = [], []
    for span in spans:
        packed = pack_temporal(kinds, first, (q, k, v, g), span, heads)
        if framed:
            (packed,) = behind([packed], *framed)
        framed.append(exchange(packed))
    if others > 0:
        sent = pack_spatial(kinds, first, (k, v, q, g), others, heads)
        ahead, back = behind(sent, *framed[:1])
        arrived = [passed_along(ahead, "ctx", 1), passed_along(back, "ctx", -1)]
        arrived = behind(arrived, *framed)
        prior, following = (x.reshape(others, 2, count, DH) for x in arrived)
        flat = [x.reshape(count, width) for x in (q, k, v, g)]
        attended, qgrad, own, stats = spatial(kinds, first, frame, flat, prior, heads)
        stats = passed_along(stats, "ctx", -1)
    for place, span in enumerate(spans):
        results = temporal(kinds, first, bands, framed[place], span[0], heads)
        if place == 0:
            (results,) = behind([results], *framed)
        elif others > 0:
            (results,) = behind([results], stats, *returned)
        returned.append(exchange(results))
    filled = ()
    if others > 0:
        grads = spatial_next(kinds, first, flat[1], flat[2], following, stats, own, heads)
        filled = tuple(x.reshape(q.shape) for x in (attended, qgrad, *grads))
    for span, rows_in in zip(spans, returned):
        filled = unpack(kinds, first, rows_in, span[0], filled, heads)
    return tuple(filled)


def body(queries, key_rows, value_rows, out_grad, head_kind, frame_band):
    frames = lax.axis_size("ctx")
    count = queries.shape[1]
    heads = queries.shape[2] // DH
    first = lax.axis_index("head").astype(jnp.int32) * heads
    frame = lax.axis_index("ctx").astype(jnp.int32)
    kinds = lax.dynamic_slice_in_dim(head_kind, first, heads)
    slots = jnp.sum((kinds == TEMPORAL).astype(jnp.int32))
    arrays = [
        x.reshape(frames, count // frames, heads * DH)
        for x in (queries, key_rows, value_rows, out_grad)
    ]
    outs = lax.switch(
        slots,
        [functools.partial(branch, n, heads) for n in range(heads + 1)],
        head_kind, frame_band, first.reshape(1), frame.reshape(1), *arrays,
    )
    return tuple(out.reshape(queries.shape) for out in outs)


def solution(mesh):
    rows = P("ctx", None, "head")
    return jax.shard_map(
        body,
        mesh=mesh,
        in_specs=(rows, rows, rows, rows, P(), P()),
        out_specs=(rows, rows, rows, rows),
        check_vma=False,
    )
```

```python
import functools

import jax
import jax.numpy as jnp
from jax import lax
from jax.experimental import pallas as pl
from jax.experimental.pallas import tpu as pltpu
from jax.sharding import PartitionSpec as P

DH = 128
SCALE = DH ** (-0.5)
SPATIAL, TEMPORAL = 1, 0
MASKED = -1e30
F32 = jnp.float32
BF16 = jnp.bfloat16
MIB = 1024 * 1024


def head_at(kind_ref, first_ref, heads, kind, slot):
    found, seen = jnp.int32(0), jnp.int32(0)
    for head in range(heads):
        hit = kind_ref[first_ref[0] + head] == kind
        found = jnp.where(jnp.logical_and(hit, seen == slot), jnp.int32(head), found)
        seen = seen + hit.astype(jnp.int32)
    return found


def dot_nt(a, b):
    return lax.dot_general(a, b, (((1,), (1,)), ((), ())), preferred_element_type=F32)


def dot_nn(a, b):
    return lax.dot_general(a, b, (((1,), (0,)), ((), ())), preferred_element_type=F32)


def dot_tn(a, b):
    return lax.dot_general(a, b, (((0,), (0,)), ((), ())), preferred_element_type=F32)


def params(mib=32):
    return pltpu.CompilerParams(
        dimension_semantics=("arbitrary",), vmem_limit_bytes=mib * MIB
    )


def cost(flops, moved):
    return pl.CostEstimate(flops=int(flops), bytes_accessed=int(moved), transcendentals=0)


def column_spec(count, heads, kind):
    return pl.BlockSpec((count, DH), lambda i, *refs: (0, head_at(*refs[:2], heads, kind, i)))


def head_columns(kind_ref, first_ref, heads, kind, slot):
    return pl.ds(pl.multiple_of(head_at(kind_ref, first_ref, heads, kind, slot) * DH, DH), DH)


def staged_copies(triples, in_sems, out_sems):
    loads = [pltpu.make_async_copy(x, y, in_sems.at[i]) for i, (x, y, _) in enumerate(triples)]
    stores = [pltpu.make_async_copy(y, z, out_sems.at[i]) for i, (_, y, z) in enumerate(triples)]
    for load in loads:
        load.start()
    for load, store in zip(loads, stores):
        load.wait()
        store.start()
    for store in stores:
        store.wait()


def whole_params():
    return pltpu.CompilerParams(vmem_limit_bytes=62 * MIB)


def pack_spatial(kinds, first, arrays, slots, heads):
    frames, rows, _ = arrays[0].shape
    count = len(arrays)
    total = slots * count

    def kernel(kind_ref, first_ref, *refs):
        ins, outs = refs[:count], refs[count:-3]
        stage, in_sems, out_sems = refs[-3:]
        triples = []
        for slot in range(slots):
            cols = head_columns(kind_ref, first_ref, heads, SPATIAL, slot)
            for place, ref in enumerate(ins):
                target = outs[place // 2].at[slot, place % 2]
                triples.append((ref.at[:, :, cols], stage.at[slot, place], target))
        staged_copies(triples, in_sems, out_sems)

    pair = jax.ShapeDtypeStruct((slots, 2, frames, rows, DH), BF16)
    return pl.pallas_call(
        kernel,
        out_shape=[pair] * (count // 2),
        in_specs=[pl.BlockSpec(memory_space=pltpu.SMEM)] * 2
        + [pl.BlockSpec(memory_space=pl.ANY)] * count,
        out_specs=[pl.BlockSpec(memory_space=pl.ANY)] * (count // 2),
        scratch_shapes=[
            pltpu.VMEM((slots, count, frames, rows, DH), BF16),
            pltpu.SemaphoreType.DMA((total,)),
            pltpu.SemaphoreType.DMA((total,)),
        ],
        compiler_params=whole_params(),
        cost_estimate=cost(0, 4 * total * frames * rows * DH),
        name="pack_spatial",
    )(kinds, first, *arrays)


def pack_temporal(kinds, first, arrays, slots, heads):
    frames, rows, _ = arrays[0].shape
    total = 4 * slots

    def kernel(kind_ref, first_ref, *refs):
        ins, (out, stage, in_sems, out_sems) = refs[:4], refs[4:]
        triples = []
        for slot in range(slots):
            cols = head_columns(kind_ref, first_ref, heads, TEMPORAL, slot)
            for place, ref in enumerate(ins):
                triples.append(
                    (ref.at[:, :, cols], stage.at[slot, place], out.at[:, place, slot])
                )
        staged_copies(triples, in_sems, out_sems)

    return pl.pallas_call(
        kernel,
        out_shape=jax.ShapeDtypeStruct((frames, 4, slots, rows, DH), BF16),
        in_specs=[pl.BlockSpec(memory_space=pltpu.SMEM)] * 2
        + [pl.BlockSpec(memory_space=pl.ANY)] * 4,
        out_specs=pl.BlockSpec(memory_space=pl.ANY),
        scratch_shapes=[
            pltpu.VMEM((slots, 4, frames, rows, DH), BF16),
            pltpu.SemaphoreType.DMA((total,)),
            pltpu.SemaphoreType.DMA((total,)),
        ],
        compiler_params=whole_params(),
        cost_estimate=cost(0, 4 * total * frames * rows * DH),
        name="pack_temporal",
    )(kinds, first, *arrays)


def temporal(kinds, first, bands, rows_in, heads):
    frames, _, slots, rows, _ = rows_in.shape
    group = 16
    size = frames * group

    def kernel(kind_ref, first_ref, band_ref, rows_ref, result_ref, held, made, in_sems, out_sems):
        def load(slot):
            return pltpu.make_async_copy(rows_ref.at[:, :, slot], held.at[slot], in_sems.at[slot])

        def store(slot):
            return pltpu.make_async_copy(
                made.at[slot], result_ref.at[:, :, slot], out_sems.at[slot]
            )

        for slot in range(slots):
            load(slot).start()

        @pl.loop(0, slots)
        def _(slot):
            load(slot).wait()
            one_head(kind_ref, first_ref, band_ref, slot, held.at[slot], made.at[slot])
            store(slot).start()

        for slot in range(slots):
            store(slot).wait()

    def one_head(kind_ref, first_ref, band_ref, slot, in_ref, out_ref):
        band = band_ref[first_ref[0] + head_at(kind_ref, first_ref, heads, TEMPORAL, slot)]
        row = lax.broadcasted_iota(jnp.int32, (size, size), 0)
        col = lax.broadcasted_iota(jnp.int32, (size, size), 1)
        same = lax.rem(row, group) == lax.rem(col, group)
        near = jnp.abs(lax.div(row, group) - lax.div(col, group)) <= band
        allowed = jnp.logical_and(same, near)
        parts = [slice(start, start + group) for start in range(0, rows, group)]
        qs, ks, vs, gs = (
            [in_ref[:, place, part].reshape(size, DH) for part in parts] for place in range(4)
        )
        scores = [jnp.where(allowed, dot_nt(q, k) * SCALE, MASKED) for q, k in zip(qs, ks)]
        dprobs = [dot_nt(g, v) for g, v in zip(gs, vs)]
        raised = [jnp.exp(x - jnp.max(x, axis=1, keepdims=True)) for x in scores]
        weights = [x * (1.0 / jnp.sum(x, axis=1, keepdims=True)) for x in raised]
        probs = [x.astype(BF16) for x in weights]
        attended = [dot_nn(x, v).astype(BF16) for x, v in zip(probs, vs)]
        deltas = [
            jnp.sum(g.astype(F32) * x.astype(F32), axis=1, keepdims=True)
            for g, x in zip(gs, attended)
        ]
        dscores = [
            (w * (dp - delta) * SCALE).astype(BF16)
            for w, dp, delta in zip(weights, dprobs, deltas)
        ]
        results = (
            attended,
            [dot_nn(x, k).astype(BF16) for x, k in zip(dscores, ks)],
            [dot_tn(x, q).astype(BF16) for x, q in zip(dscores, qs)],
            [dot_tn(x, g).astype(BF16) for x, g in zip(probs, gs)],
        )
        for place, result in enumerate(results):
            for part, value in zip(parts, result):
                out_ref[:, place, part] = value.reshape(frames, group, DH)

    block = (slots, frames, 4, rows, DH)
    return pl.pallas_call(
        kernel,
        out_shape=jax.ShapeDtypeStruct(rows_in.shape, BF16),
        in_specs=[pl.BlockSpec(memory_space=pltpu.SMEM)] * 3
        + [pl.BlockSpec(memory_space=pl.ANY)],
        out_specs=pl.BlockSpec(memory_space=pl.ANY),
        scratch_shapes=[
            pltpu.VMEM(block, BF16),
            pltpu.VMEM(block, BF16),
            pltpu.SemaphoreType.DMA((slots,)),
            pltpu.SemaphoreType.DMA((slots,)),
        ],
        compiler_params=whole_params(),
        cost_estimate=cost(12 * slots * rows * frames * size * DH, 4 * rows_in.size),
        name="temporal",
    )(kinds, first, bands, rows_in)


def unpack(kinds, first, rows_in, filled, heads):
    frames, _, slots, rows, _ = rows_in.shape
    count = frames * rows
    held = len(filled)

    def kernel(kind_ref, first_ref, in_ref, *refs):
        for place, ref in enumerate(refs[held:]):
            ref[...] = in_ref[:, place, 0].reshape(count, DH)

    block = pl.BlockSpec((frames, 4, 1, rows, DH), lambda i, *refs: (0, 0, i, 0, 0))
    return pl.pallas_call(
        kernel,
        out_shape=[jax.ShapeDtypeStruct((count, heads * DH), BF16)] * 4,
        grid_spec=pltpu.PrefetchScalarGridSpec(
            num_scalar_prefetch=2,
            grid=(slots,),
            in_specs=[block] + [pl.BlockSpec(memory_space=pl.ANY)] * held,
            out_specs=[column_spec(count, heads, TEMPORAL)] * 4,
        ),
        input_output_aliases={3 + place: place for place in range(held)},
        compiler_params=params(),
        cost_estimate=cost(0, 4 * rows_in.size),
        name="unpack",
    )(kinds, first, rows_in, *filled)


def spatial(kinds, first, frame, arrays, prior, heads):
    count = arrays[0].shape[0]
    slots = prior.shape[0]
    chunk = min(count, 256)

    def kernel(
        kind_ref, first_ref, frame_ref, q_ref, k_ref, v_ref, g_ref, prior_ref,
        out_ref, qgrad_ref, own_ref, stats_ref,
    ):
        has_prior = frame_ref[0] > 0
        k, v = k_ref[...], v_ref[...]
        k_prior, v_prior = prior_ref[0, 0], prior_ref[0, 1]
        own_ref[...] = jnp.zeros_like(own_ref)

        @pl.loop(0, count // chunk)
        def _(step):
            part = pl.ds(pl.multiple_of(step * chunk, chunk), chunk)
            q, g = q_ref[part], g_ref[part]
            own = dot_nt(q, k) * SCALE
            before = jnp.where(has_prior, dot_nt(q, k_prior) * SCALE, MASKED)
            top = jnp.maximum(
                jnp.max(own, axis=1, keepdims=True), jnp.max(before, axis=1, keepdims=True)
            )
            own, before = jnp.exp(own - top), jnp.exp(before - top)
            total = jnp.sum(own, axis=1, keepdims=True) + jnp.sum(before, axis=1, keepdims=True)
            inverse = 1.0 / total
            own, before = own * inverse, before * inverse
            own_prob, before_prob = own.astype(BF16), before.astype(BF16)
            attended = (dot_nn(own_prob, v) + dot_nn(before_prob, v_prior)).astype(BF16)
            delta = jnp.sum(g.astype(F32) * attended.astype(F32), axis=1, keepdims=True)
            own_ds = (own * (dot_nt(g, v) - delta) * SCALE).astype(BF16)
            before_ds = (before * (dot_nt(g, v_prior) - delta) * SCALE).astype(BF16)
            out_ref[part] = attended
            qgrad_ref[part] = (dot_nn(own_ds, k) + dot_nn(before_ds, k_prior)).astype(BF16)
            own_ref[0, 0] += dot_tn(own_ds, q)
            own_ref[0, 1] += dot_tn(own_prob, g)
            lane = lax.broadcasted_iota(jnp.int32, (chunk, DH), 1)
            stats = jnp.where(lane == 0, top + jnp.log(total), delta)
            stats_ref[0, :, part] = stats.T[:2]

    columns = column_spec(count, heads, SPATIAL)
    pair = pl.BlockSpec((1, 2, count, DH), lambda i, *refs: (i, 0, 0, 0))
    whole = jax.ShapeDtypeStruct((count, heads * DH), BF16)
    return pl.pallas_call(
        kernel,
        out_shape=[
            whole,
            whole,
            jax.ShapeDtypeStruct(prior.shape, F32),
            jax.ShapeDtypeStruct((slots, 2, count), F32),
        ],
        grid_spec=pltpu.PrefetchScalarGridSpec(
            num_scalar_prefetch=3,
            grid=(slots,),
            in_specs=[columns] * 4 + [pair],
            out_specs=[
                columns, columns, pair, pl.BlockSpec((1, 2, count), lambda i, *refs: (i, 0, 0))
            ],
        ),
        compiler_params=params(60),
        cost_estimate=cost(20 * slots * count * count * DH, 16 * slots * count * DH),
        name="spatial",
    )(kinds, first, frame, *arrays, prior)


def spatial_next(kinds, first, frame, k, v, following, stats, own, heads):
    slots, _, count, _ = own.shape
    frames = stats.shape[0]
    chunk = min(count, 256)

    def kernel(
        kind_ref, first_ref, frame_ref, k_ref, v_ref, next_ref, stats_ref, own_ref,
        kgrad_ref, vgrad_ref,
    ):
        q, g = next_ref[0, 0], next_ref[0, 1]
        has_next = frame_ref[0] < frames - 1
        lse = jnp.where(has_next, stats_ref[0, 0, 0:1], 0.0)
        delta = jnp.where(has_next, stats_ref[0, 0, 1:2], 0.0)

        @pl.loop(0, count // chunk)
        def _(step):
            part = pl.ds(pl.multiple_of(step * chunk, chunk), chunk)
            weight = jnp.exp(dot_nt(k_ref[part], q) * SCALE - lse)
            dscore = (weight * (dot_nt(v_ref[part], g) - delta) * SCALE).astype(BF16)
            kgrad_ref[part] = (own_ref[0, 0, part] + dot_nn(dscore, q)).astype(BF16)
            vgrad_ref[part] = (own_ref[0, 1, part] + dot_nn(weight.astype(BF16), g)).astype(BF16)

    columns = column_spec(count, heads, SPATIAL)
    pair = pl.BlockSpec((1, 2, count, DH), lambda i, *refs: (i, 0, 0, 0))
    after = pl.BlockSpec(
        (1, 1, 2, count), lambda i, *refs: (jnp.minimum(refs[2][0] + 1, frames - 1), i, 0, 0)
    )
    return pl.pallas_call(
        kernel,
        out_shape=[jax.ShapeDtypeStruct((count, heads * DH), BF16)] * 2,
        grid_spec=pltpu.PrefetchScalarGridSpec(
            num_scalar_prefetch=3,
            grid=(slots,),
            in_specs=[columns, columns, pair, after, pair],
            out_specs=[columns] * 2,
        ),
        compiler_params=params(),
        cost_estimate=cost(8 * slots * count * count * DH, 20 * slots * count * DH),
        name="spatial_next",
    )(kinds, first, frame, k, v, following, stats, own)


def passed_along(array, axis, by):
    length = lax.axis_size(axis)
    pairs = [(i, i + by) for i in range(length) if 0 <= i + by < length]
    return lax.ppermute(array, axis, pairs)


def behind(arrays, *others):
    return lax.optimization_barrier((tuple(arrays), others))[0]


def branch(slots, heads, kinds, bands, first, frame, q, k, v, g):
    frames, rows, width = q.shape
    count = frames * rows
    others = heads - slots
    exchange = functools.partial(
        lax.all_to_all, axis_name="ctx", split_axis=0, concat_axis=0, tiled=True
    )
    filled = ()
    if slots > 0:
        framed = exchange(pack_temporal(kinds, first, (q, k, v, g), slots, heads))
        results = temporal(kinds, first, bands, framed, heads)
        returned = exchange(results)
    if others > 0:
        ahead, back = pack_spatial(kinds, first, (k, v, q, g), others, heads)
        arrived = [passed_along(ahead, "ctx", 1), passed_along(back, "ctx", -1)]
        if slots > 0:
            arrived = behind(arrived, results)
        prior, following = (x.reshape(others, 2, count, DH) for x in arrived)
        flat = [x.reshape(count, width) for x in (q, k, v, g)]
        attended, qgrad, own, stats = spatial(kinds, first, frame, flat, prior, heads)
        stats = lax.all_gather(stats, "ctx")
        grads = spatial_next(kinds, first, frame, flat[1], flat[2], following, stats, own, heads)
        filled = (attended, qgrad, *grads)
    if slots > 0:
        filled = unpack(kinds, first, returned, filled, heads)
    return tuple(filled)


def body(queries, key_rows, value_rows, out_grad, head_kind, frame_band):
    frames = lax.axis_size("ctx")
    count = queries.shape[1]
    heads = queries.shape[2] // DH
    first = lax.axis_index("head").astype(jnp.int32) * heads
    frame = lax.axis_index("ctx").astype(jnp.int32)
    kinds = lax.dynamic_slice_in_dim(head_kind, first, heads)
    slots = jnp.sum((kinds == TEMPORAL).astype(jnp.int32))
    arrays = [
        x.reshape(frames, count // frames, heads * DH)
        for x in (queries, key_rows, value_rows, out_grad)
    ]
    outs = lax.switch(
        slots,
        [functools.partial(branch, n, heads) for n in range(heads + 1)],
        head_kind, frame_band, first.reshape(1), frame.reshape(1), *arrays,
    )
    return tuple(out.reshape(queries.shape) for out in outs)


def solution(mesh):
    rows = P("ctx", None, "head")
    return jax.shard_map(
        body,
        mesh=mesh,
        in_specs=(rows, rows, rows, rows, P(), P()),
        out_specs=(rows, rows, rows, rows),
        check_vma=False,
    )
```

```python
import functools

import jax
import jax.numpy as jnp
from jax import lax
from jax.experimental import pallas as pl
from jax.experimental.pallas import tpu as pltpu
from jax.sharding import PartitionSpec as P

DH = 128
SCALE = DH ** (-0.5)
SPATIAL, TEMPORAL = 1, 0
MASKED = -1e30
F32 = jnp.float32
BF16 = jnp.bfloat16
MIB = 1024 * 1024


def head_at(kind_ref, first_ref, heads, kind, slot):
    found, seen = jnp.int32(0), jnp.int32(0)
    for head in range(heads):
        hit = kind_ref[first_ref[0] + head] == kind
        found = jnp.where(jnp.logical_and(hit, seen == slot), jnp.int32(head), found)
        seen = seen + hit.astype(jnp.int32)
    return found


def dot_nt(a, b):
    return lax.dot_general(a, b, (((1,), (1,)), ((), ())), preferred_element_type=F32)


def dot_nn(a, b):
    return lax.dot_general(a, b, (((1,), (0,)), ((), ())), preferred_element_type=F32)


def dot_tn(a, b):
    return lax.dot_general(a, b, (((0,), (0,)), ((), ())), preferred_element_type=F32)


def params(mib=32, grid=True):
    return pltpu.CompilerParams(
        dimension_semantics=("arbitrary",) if grid else None, vmem_limit_bytes=mib * MIB
    )


def cost(flops, moved):
    return pl.CostEstimate(flops=int(flops), bytes_accessed=int(moved), transcendentals=0)


def column_spec(count, heads, kind):
    return pl.BlockSpec((count, DH), lambda i, *refs: (0, head_at(*refs[:2], heads, kind, i)))


def head_columns(kind_ref, first_ref, heads, kind, slot):
    return pl.ds(pl.multiple_of(head_at(kind_ref, first_ref, heads, kind, slot) * DH, DH), DH)


def staged_copies(triples, in_sems, out_sems):
    loads = [pltpu.make_async_copy(x, y, in_sems.at[i]) for i, (x, y, _) in enumerate(triples)]
    stores = [pltpu.make_async_copy(y, z, out_sems.at[i]) for i, (_, y, z) in enumerate(triples)]
    for load in loads:
        load.start()
    for load, store in zip(loads, stores):
        load.wait()
        store.start()
    for store in stores:
        store.wait()


def whole_params():
    return pltpu.CompilerParams(vmem_limit_bytes=62 * MIB)


def pack_spatial(kinds, first, arrays, slots, heads, after):
    frames, rows, _ = arrays[0].shape
    count = len(arrays)
    total = slots * count

    def kernel(kind_ref, first_ref, *refs):
        ins, outs = refs[:count], refs[-3 - count : -3]
        stage, in_sems, out_sems = refs[-3:]
        triples = []
        for slot in range(slots):
            cols = head_columns(kind_ref, first_ref, heads, SPATIAL, slot)
            for place, (ref, out) in enumerate(zip(ins, outs)):
                triples.append((ref.at[:, :, cols], stage.at[slot, place], out.at[slot]))
        staged_copies(triples, in_sems, out_sems)

    return pl.pallas_call(
        kernel,
        out_shape=[jax.ShapeDtypeStruct((slots, frames, rows, DH), BF16)] * count,
        in_specs=[pl.BlockSpec(memory_space=pltpu.SMEM)] * 2
        + [pl.BlockSpec(memory_space=pl.ANY)] * (count + len(after)),
        out_specs=[pl.BlockSpec(memory_space=pl.ANY)] * count,
        scratch_shapes=[
            pltpu.VMEM((slots, count, frames, rows, DH), BF16),
            pltpu.SemaphoreType.DMA((total,)),
            pltpu.SemaphoreType.DMA((total,)),
        ],
        compiler_params=whole_params(),
        cost_estimate=cost(0, 4 * total * frames * rows * DH),
        name="pack_spatial",
    )(kinds, first, *arrays, *after)


def pack_temporal(kinds, first, arrays, slots, heads):
    frames, rows, _ = arrays[0].shape
    total = 4 * slots

    def kernel(kind_ref, first_ref, *refs):
        ins, (out, stage, in_sems, out_sems) = refs[:4], refs[4:]
        triples = []
        for slot in range(slots):
            cols = head_columns(kind_ref, first_ref, heads, TEMPORAL, slot)
            for place, ref in enumerate(ins):
                triples.append(
                    (ref.at[:, :, cols], stage.at[slot, place], out.at[:, place, slot])
                )
        staged_copies(triples, in_sems, out_sems)

    return pl.pallas_call(
        kernel,
        out_shape=jax.ShapeDtypeStruct((frames, 4, slots, rows, DH), BF16),
        in_specs=[pl.BlockSpec(memory_space=pltpu.SMEM)] * 2
        + [pl.BlockSpec(memory_space=pl.ANY)] * 4,
        out_specs=pl.BlockSpec(memory_space=pl.ANY),
        scratch_shapes=[
            pltpu.VMEM((slots, 4, frames, rows, DH), BF16),
            pltpu.SemaphoreType.DMA((total,)),
            pltpu.SemaphoreType.DMA((total,)),
        ],
        compiler_params=whole_params(),
        cost_estimate=cost(0, 4 * total * frames * rows * DH),
        name="pack_temporal",
    )(kinds, first, *arrays)


def temporal(kinds, first, bands, rows_in, heads):
    frames, _, slots, rows, _ = rows_in.shape
    group = 16
    size = frames * group

    def kernel(kind_ref, first_ref, band_ref, rows_ref, result_ref, held, made, in_sems, out_sems):
        def load(slot):
            return pltpu.make_async_copy(rows_ref.at[:, :, slot], held.at[slot], in_sems.at[slot])

        def store(slot):
            return pltpu.make_async_copy(
                made.at[slot], result_ref.at[:, :, slot], out_sems.at[slot]
            )

        for slot in range(slots):
            load(slot).start()

        @pl.loop(0, slots)
        def _(slot):
            load(slot).wait()
            one_head(kind_ref, first_ref, band_ref, slot, held.at[slot], made.at[slot])
            store(slot).start()

        for slot in range(slots):
            store(slot).wait()

    def one_head(kind_ref, first_ref, band_ref, slot, in_ref, out_ref):
        band = band_ref[first_ref[0] + head_at(kind_ref, first_ref, heads, TEMPORAL, slot)]
        row = lax.broadcasted_iota(jnp.int32, (size, size), 0)
        col = lax.broadcasted_iota(jnp.int32, (size, size), 1)
        same = lax.rem(row, group) == lax.rem(col, group)
        near = jnp.abs(lax.div(row, group) - lax.div(col, group)) <= band
        allowed = jnp.logical_and(same, near)
        parts = [slice(start, start + group) for start in range(0, rows, group)]
        qs, ks, vs, gs = (
            [in_ref[:, place, part].reshape(size, DH) for part in parts] for place in range(4)
        )
        scores = [jnp.where(allowed, dot_nt(q, k) * SCALE, MASKED) for q, k in zip(qs, ks)]
        dprobs = [dot_nt(g, v) for g, v in zip(gs, vs)]
        raised = [jnp.exp(x - jnp.max(x, axis=1, keepdims=True)) for x in scores]
        weights = [x * (1.0 / jnp.sum(x, axis=1, keepdims=True)) for x in raised]
        probs = [x.astype(BF16) for x in weights]
        attended = [dot_nn(x, v).astype(BF16) for x, v in zip(probs, vs)]
        deltas = [
            jnp.sum(g.astype(F32) * x.astype(F32), axis=1, keepdims=True)
            for g, x in zip(gs, attended)
        ]
        dscores = [
            (w * (dp - delta) * SCALE).astype(BF16)
            for w, dp, delta in zip(weights, dprobs, deltas)
        ]
        results = (
            attended,
            [dot_nn(x, k).astype(BF16) for x, k in zip(dscores, ks)],
            [dot_tn(x, q).astype(BF16) for x, q in zip(dscores, qs)],
            [dot_tn(x, g).astype(BF16) for x, g in zip(probs, gs)],
        )
        for place, result in enumerate(results):
            for part, value in zip(parts, result):
                out_ref[:, place, part] = value.reshape(frames, group, DH)

    block = (slots, frames, 4, rows, DH)
    return pl.pallas_call(
        kernel,
        out_shape=jax.ShapeDtypeStruct(rows_in.shape, BF16),
        in_specs=[pl.BlockSpec(memory_space=pltpu.SMEM)] * 3
        + [pl.BlockSpec(memory_space=pl.ANY)],
        out_specs=pl.BlockSpec(memory_space=pl.ANY),
        scratch_shapes=[
            pltpu.VMEM(block, BF16),
            pltpu.VMEM(block, BF16),
            pltpu.SemaphoreType.DMA((slots,)),
            pltpu.SemaphoreType.DMA((slots,)),
        ],
        compiler_params=whole_params(),
        cost_estimate=cost(1e10, 4 * rows_in.size),
        name="temporal",
    )(kinds, first, bands, rows_in)


def spatial(kinds, first, frame, arrays, k_prior, v_prior, heads):
    count = arrays[0].shape[0]
    slots = k_prior.shape[0]
    chunk = min(count, 256)

    def kernel(
        kind_ref, first_ref, frame_ref, q_ref, k_ref, v_ref, g_ref, k_prior_ref, v_prior_ref,
        out_ref, qgrad_ref, own_ref, stats_ref,
    ):
        has_prior = frame_ref[0] > 0
        k, v = k_ref[...], v_ref[...]
        k_prior, v_prior = k_prior_ref[0], v_prior_ref[0]
        own_ref[...] = jnp.zeros_like(own_ref)

        @pl.loop(0, count // chunk)
        def _(step):
            part = pl.ds(pl.multiple_of(step * chunk, chunk), chunk)
            q, g = q_ref[part], g_ref[part]
            own = dot_nt(q, k) * SCALE
            before = jnp.where(has_prior, dot_nt(q, k_prior) * SCALE, MASKED)
            top = jnp.maximum(
                jnp.max(own, axis=1, keepdims=True), jnp.max(before, axis=1, keepdims=True)
            )
            own, before = jnp.exp(own - top), jnp.exp(before - top)
            total = jnp.sum(own, axis=1, keepdims=True) + jnp.sum(before, axis=1, keepdims=True)
            inverse = 1.0 / total
            own, before = own * inverse, before * inverse
            own_prob, before_prob = own.astype(BF16), before.astype(BF16)
            attended = (dot_nn(own_prob, v) + dot_nn(before_prob, v_prior)).astype(BF16)
            delta = jnp.sum(g.astype(F32) * attended.astype(F32), axis=1, keepdims=True)
            own_ds = (own * (dot_nt(g, v) - delta) * SCALE).astype(BF16)
            before_ds = (before * (dot_nt(g, v_prior) - delta) * SCALE).astype(BF16)
            out_ref[part] = attended
            qgrad_ref[part] = (dot_nn(own_ds, k) + dot_nn(before_ds, k_prior)).astype(BF16)
            own_ref[0, 0] += dot_tn(own_ds, q)
            own_ref[0, 1] += dot_tn(own_prob, g)
            lane = lax.broadcasted_iota(jnp.int32, (chunk, DH), 1)
            stats = jnp.where(lane == 0, top + jnp.log(total), delta)
            stats_ref[0, :, part] = stats.T[:2]

    columns = column_spec(count, heads, SPATIAL)
    single = pl.BlockSpec((1, count, DH), lambda i, *refs: (i, 0, 0))
    pair = pl.BlockSpec((1, 2, count, DH), lambda i, *refs: (i, 0, 0, 0))
    whole = jax.ShapeDtypeStruct((count, heads * DH), BF16)
    return pl.pallas_call(
        kernel,
        out_shape=[
            whole,
            whole,
            jax.ShapeDtypeStruct((slots, 2, count, DH), F32),
            jax.ShapeDtypeStruct((slots, 2, count), F32),
        ],
        grid_spec=pltpu.PrefetchScalarGridSpec(
            num_scalar_prefetch=3,
            grid=(slots,),
            in_specs=[columns] * 4 + [single] * 2,
            out_specs=[
                columns, columns, pair, pl.BlockSpec((1, 2, count), lambda i, *refs: (i, 0, 0))
            ],
        ),
        compiler_params=params(60),
        cost_estimate=cost(2e11, 16 * slots * count * DH),
        name="spatial",
    )(kinds, first, frame, *arrays, k_prior, v_prior)


def finish(kinds, first, frame, rows_in, filled, k, v, following, stats, own, heads):
    count = k.shape[0]
    slots = 0 if rows_in is None else rows_in.shape[2]
    others = heads - slots
    chunk = min(count, 256)
    ins = ([] if rows_in is None else [rows_in]) + ([*filled, k, v, *following, stats, own] if others else [])
    scratch = []
    if slots:
        frames, _, _, rows, _ = rows_in.shape
        scratch += [pltpu.VMEM((slots, 4, frames, rows, DH), BF16)]
        scratch += [pltpu.SemaphoreType.DMA((4 * slots,))] * 2
    if others:
        scratch += [pltpu.VMEM((others, 4, count, DH), BF16), pltpu.VMEM((others, 2, count, DH), F32)]
        scratch += [pltpu.VMEM((others, 2, count), F32), pltpu.VMEM((others, 2, count, DH), BF16)]
        scratch += [pltpu.SemaphoreType.DMA((8 * others,))]

    def kernel(kind_ref, first_ref, *refs):
        refs = list(refs)
        in_refs, out_refs, temps = refs[: len(ins)], refs[len(ins) : len(ins) + 4], refs[len(ins) + 4 :]
        loads, stores, next_loads, next_stores = [], [], [], []
        if slots:
            stage, in_sems, out_sems = temps[:3]
            for slot in range(slots):
                cols = head_columns(kind_ref, first_ref, heads, TEMPORAL, slot)
                for place, out in enumerate(out_refs):
                    at = 4 * slot + place
                    held = stage.at[slot, place]
                    loads.append(
                        pltpu.make_async_copy(in_refs[0].at[:, place, slot], held, in_sems.at[at])
                    )
                    stores.append(
                        pltpu.make_async_copy(
                            held.reshape(count, DH), out.at[:, cols], out_sems.at[at]
                        )
                    )
        if others:
            rows_ref, own_ref, stats_ref, made_ref, sems = temps[-5:]
            k_in, v_in, q_in, g_in, stats_in, own_in = in_refs[-6:]
            for slot in range(others):
                cols = head_columns(kind_ref, first_ref, heads, SPATIAL, slot)
                pairs = [
                    (k_in.at[:, cols], rows_ref.at[slot, 0]),
                    (v_in.at[:, cols], rows_ref.at[slot, 1]),
                    (q_in.at[slot], rows_ref.at[slot, 2]),
                    (g_in.at[slot], rows_ref.at[slot, 3]),
                    (stats_in.at[slot], stats_ref.at[slot]),
                    (own_in.at[slot], own_ref.at[slot]),
                ]
                next_loads += [
                    pltpu.make_async_copy(x, y, sems.at[8 * slot + i])
                    for i, (x, y) in enumerate(pairs)
                ]
                next_stores += [
                    pltpu.make_async_copy(
                        made_ref.at[slot, i], out_refs[2 + i].at[:, cols], sems.at[8 * slot + 6 + i]
                    )
                    for i in range(2)
                ]
        for copy in next_loads + loads:
            copy.start()
        for load, store in zip(loads, stores):
            load.wait()
            store.start()
        for copy in next_loads:
            copy.wait()
        if others:

            @pl.loop(0, others)
            def _(slot):
                q, g = rows_ref[slot, 2], rows_ref[slot, 3]
                lse, delta = stats_ref[slot, 0:1], stats_ref[slot, 1:2]

                @pl.loop(0, count // chunk)
                def _(step):
                    part = pl.ds(pl.multiple_of(step * chunk, chunk), chunk)
                    weight = jnp.exp(dot_nt(rows_ref[slot, 0, part], q) * SCALE - lse)
                    dprob = dot_nt(rows_ref[slot, 1, part], g)
                    dscore = (weight * (dprob - delta) * SCALE).astype(BF16)
                    made_ref[slot, 0, part] = (own_ref[slot, 0, part] + dot_nn(dscore, q)).astype(BF16)
                    made_ref[slot, 1, part] = (
                        own_ref[slot, 1, part] + dot_nn(weight.astype(BF16), g)
                    ).astype(BF16)

        for copy in next_stores:
            copy.start()
        for copy in stores + next_stores:
            copy.wait()

    place = 2 + (1 if slots else 0)
    return pl.pallas_call(
        kernel,
        out_shape=[jax.ShapeDtypeStruct((count, heads * DH), BF16)] * 4,
        in_specs=[pl.BlockSpec(memory_space=pltpu.SMEM)] * 2
        + [pl.BlockSpec(memory_space=pl.ANY)] * len(ins),
        out_specs=[pl.BlockSpec(memory_space=pl.ANY)] * 4,
        scratch_shapes=scratch,
        input_output_aliases={place: 0, place + 1: 1} if others else {},
        compiler_params=params(32, grid=False),
        cost_estimate=cost(8 * others * count * count * DH, 16 * heads * count * DH),
        name="finish",
    )(kinds, first, *ins)


def passed_along(array, axis, by):
    length = lax.axis_size(axis)
    pairs = [(i, i + by) for i in range(length) if 0 <= i + by < length]
    return lax.ppermute(array, axis, pairs)


def behind(arrays, *others):
    return lax.optimization_barrier((tuple(arrays), others))[0]


def branch(slots, heads, kinds, bands, first, frame, q, k, v, g):
    frames, rows, width = q.shape
    count = frames * rows
    others = heads - slots
    exchange = functools.partial(
        lax.all_to_all, axis_name="ctx", split_axis=0, concat_axis=0, tiled=True
    )
    flat = [x.reshape(count, width) for x in (q, k, v, g)]
    returned = filled = following = stats = own = None
    packed = []
    if slots > 0:
        packed = [pack_temporal(kinds, first, (q, k, v, g), slots, heads)]
        framed = exchange(*packed)
        results = temporal(kinds, first, bands, framed, heads)
        returned = exchange(results)
    if others > 0:
        sent = pack_spatial(kinds, first, (k, v, q, g), others, heads, packed)
        arrived = [passed_along(x, "ctx", by) for x, by in zip(sent, (1, 1, -1, -1))]
        if slots > 0:
            arrived = behind(arrived, results)
        arrived = [x.reshape(others, count, DH) for x in arrived]
        *filled, own, stats = spatial(kinds, first, frame, flat, *arrived[:2], heads)
        following, stats = arrived[2:], passed_along(stats, "ctx", -1)
    return finish(
        kinds, first, frame, returned, filled, *flat[1:3], following, stats, own, heads
    )


def body(queries, key_rows, value_rows, out_grad, head_kind, frame_band):
    frames = lax.axis_size("ctx")
    count = queries.shape[1]
    heads = queries.shape[2] // DH
    first = lax.axis_index("head").astype(jnp.int32) * heads
    frame = lax.axis_index("ctx").astype(jnp.int32)
    kinds = lax.dynamic_slice_in_dim(head_kind, first, heads)
    slots = jnp.sum((kinds == TEMPORAL).astype(jnp.int32))
    arrays = [
        x.reshape(frames, count // frames, heads * DH)
        for x in (queries, key_rows, value_rows, out_grad)
    ]
    outs = lax.switch(
        slots,
        [functools.partial(branch, n, heads) for n in range(heads + 1)],
        head_kind, frame_band, first.reshape(1), frame.reshape(1), *arrays,
    )
    return tuple(out.reshape(queries.shape) for out in outs)


def solution(mesh):
    rows = P("ctx", None, "head")
    return jax.shard_map(
        body,
        mesh=mesh,
        in_specs=(rows, rows, rows, rows, P(), P()),
        out_specs=(rows, rows, rows, rows),
        check_vma=False,
    )
```

```python
import functools
import math

import jax
import jax.numpy as jnp
from jax import lax
from jax.experimental import pallas as pl
from jax.experimental.pallas import tpu as pltpu
from jax.sharding import PartitionSpec as P

DH = 128
SCALE = DH ** (-0.5)
SPATIAL, TEMPORAL = 1, 0
MASKED = -1e30
SCALE_LOG2 = SCALE * math.log2(math.e)
F32 = jnp.float32
BF16 = jnp.bfloat16
MIB = 1024 * 1024


def head_at(kind_ref, first_ref, heads, kind, slot):
    found, seen = jnp.int32(0), jnp.int32(0)
    for head in range(heads):
        hit = kind_ref[first_ref[0] + head] == kind
        found = jnp.where(jnp.logical_and(hit, seen == slot), jnp.int32(head), found)
        seen = seen + hit.astype(jnp.int32)
    return found


def dot_nt(a, b):
    return lax.dot_general(a, b, (((1,), (1,)), ((), ())), preferred_element_type=F32)


def dot_nn(a, b):
    return lax.dot_general(a, b, (((1,), (0,)), ((), ())), preferred_element_type=F32)


def dot_tn(a, b):
    return lax.dot_general(a, b, (((0,), (0,)), ((), ())), preferred_element_type=F32)


def params(mib=32, grid=True):
    return pltpu.CompilerParams(
        dimension_semantics=("arbitrary",) if grid else None, vmem_limit_bytes=mib * MIB
    )


def cost(flops, moved):
    return pl.CostEstimate(flops=int(flops), bytes_accessed=int(moved), transcendentals=0)


def column_spec(count, heads, kind):
    return pl.BlockSpec((count, DH), lambda i, *refs: (0, head_at(*refs[:2], heads, kind, i)))


def head_columns(kind_ref, first_ref, heads, kind, slot):
    return pl.ds(pl.multiple_of(head_at(kind_ref, first_ref, heads, kind, slot) * DH, DH), DH)


def staged_copies(triples, in_sems, out_sems):
    loads = [pltpu.make_async_copy(x, y, in_sems.at[i]) for i, (x, y, _) in enumerate(triples)]
    stores = [pltpu.make_async_copy(y, z, out_sems.at[i]) for i, (_, y, z) in enumerate(triples)]
    for load in loads:
        load.start()
    for load, store in zip(loads, stores):
        load.wait()
        store.start()
    for store in stores:
        store.wait()


def whole_params():
    return pltpu.CompilerParams(vmem_limit_bytes=62 * MIB)


def pack_spatial(kinds, first, arrays, slots, heads, after):
    frames, rows, _ = arrays[0].shape
    count = len(arrays)
    total = slots * count

    def kernel(kind_ref, first_ref, *refs):
        ins, outs = refs[:count], refs[-3 - count // 2 : -3]
        stage, in_sems, out_sems = refs[-3:]
        triples = []
        for slot in range(slots):
            cols = head_columns(kind_ref, first_ref, heads, SPATIAL, slot)
            for place, ref in enumerate(ins):
                target = outs[place // 2].at[slot, place % 2]
                triples.append((ref.at[:, :, cols], stage.at[slot, place], target))
        staged_copies(triples, in_sems, out_sems)

    return pl.pallas_call(
        kernel,
        out_shape=[jax.ShapeDtypeStruct((slots, 2, frames, rows, DH), BF16)] * (count // 2),
        in_specs=[pl.BlockSpec(memory_space=pltpu.SMEM)] * 2
        + [pl.BlockSpec(memory_space=pl.ANY)] * (count + len(after)),
        out_specs=[pl.BlockSpec(memory_space=pl.ANY)] * (count // 2),
        scratch_shapes=[
            pltpu.VMEM((slots, count, frames, rows, DH), BF16),
            pltpu.SemaphoreType.DMA((total,)),
            pltpu.SemaphoreType.DMA((total,)),
        ],
        compiler_params=whole_params(),
        cost_estimate=cost(0, 4 * total * frames * rows * DH),
        name="pack_spatial",
    )(kinds, first, *arrays, *after)


def pack_temporal(kinds, first, arrays, slots, heads):
    frames, rows, _ = arrays[0].shape
    total = 4 * slots

    def kernel(kind_ref, first_ref, *refs):
        ins, (out, stage, in_sems, out_sems) = refs[:4], refs[4:]
        triples = []
        for slot in range(slots):
            cols = head_columns(kind_ref, first_ref, heads, TEMPORAL, slot)
            for place, ref in enumerate(ins):
                triples.append(
                    (ref.at[:, :, cols], stage.at[slot, place], out.at[:, place, slot])
                )
        staged_copies(triples, in_sems, out_sems)

    return pl.pallas_call(
        kernel,
        out_shape=jax.ShapeDtypeStruct((frames, 4, slots, rows, DH), BF16),
        in_specs=[pl.BlockSpec(memory_space=pltpu.SMEM)] * 2
        + [pl.BlockSpec(memory_space=pl.ANY)] * 4,
        out_specs=pl.BlockSpec(memory_space=pl.ANY),
        scratch_shapes=[
            pltpu.VMEM((slots, 4, frames, rows, DH), BF16),
            pltpu.SemaphoreType.DMA((total,)),
            pltpu.SemaphoreType.DMA((total,)),
        ],
        compiler_params=whole_params(),
        cost_estimate=cost(0, 4 * total * frames * rows * DH),
        name="pack_temporal",
    )(kinds, first, *arrays)


def temporal(kinds, first, bands, rows_in, heads):
    frames, _, slots, rows, _ = rows_in.shape
    group = 16
    size = frames * group

    def kernel(kind_ref, first_ref, band_ref, rows_ref, result_ref, held, made, in_sems, out_sems):
        def load(slot):
            return pltpu.make_async_copy(rows_ref.at[:, :, slot], held.at[slot], in_sems.at[slot])

        def store(slot):
            return pltpu.make_async_copy(
                made.at[slot], result_ref.at[:, :, slot], out_sems.at[slot]
            )

        for slot in range(slots):
            load(slot).start()

        @pl.loop(0, slots)
        def _(slot):
            load(slot).wait()
            one_head(kind_ref, first_ref, band_ref, slot, held.at[slot], made.at[slot])
            store(slot).start()

        for slot in range(slots):
            store(slot).wait()

    def one_head(kind_ref, first_ref, band_ref, slot, in_ref, out_ref):
        band = band_ref[first_ref[0] + head_at(kind_ref, first_ref, heads, TEMPORAL, slot)]
        row = lax.broadcasted_iota(jnp.int32, (size, size), 0)
        col = lax.broadcasted_iota(jnp.int32, (size, size), 1)
        same = lax.rem(row, group) == lax.rem(col, group)
        near = jnp.abs(lax.div(row, group) - lax.div(col, group)) <= band
        allowed = jnp.logical_and(same, near)
        parts = [slice(start, start + group) for start in range(0, rows, group)]
        qs, ks, vs, gs = (
            [in_ref[:, place, part].reshape(size, DH) for part in parts] for place in range(4)
        )
        scores = [jnp.where(allowed, dot_nt(k, q), MASKED) for q, k in zip(qs, ks)]
        dprobs = [dot_nt(v, g) for g, v in zip(gs, vs)]
        raised = [
            jnp.exp2((x - jnp.max(x, axis=0, keepdims=True)) * SCALE_LOG2) for x in scores
        ]
        weights = [x * (1.0 / jnp.sum(x, axis=0, keepdims=True)) for x in raised]
        probs = [x.astype(BF16) for x in weights]
        deltas = [jnp.sum(w * dp, axis=0, keepdims=True) for w, dp in zip(weights, dprobs)]
        dscores = [
            (w * (dp - delta) * SCALE).astype(BF16)
            for w, dp, delta in zip(weights, dprobs, deltas)
        ]
        results = (
            [dot_tn(x, v).astype(BF16) for x, v in zip(probs, vs)],
            [dot_tn(x, k).astype(BF16) for x, k in zip(dscores, ks)],
            [dot_nn(x, q).astype(BF16) for x, q in zip(dscores, qs)],
            [dot_nn(x, g).astype(BF16) for x, g in zip(probs, gs)],
        )
        for place, result in enumerate(results):
            for part, value in zip(parts, result):
                out_ref[:, place, part] = value.reshape(frames, group, DH)

    block = (slots, frames, 4, rows, DH)
    return pl.pallas_call(
        kernel,
        out_shape=jax.ShapeDtypeStruct(rows_in.shape, BF16),
        in_specs=[pl.BlockSpec(memory_space=pltpu.SMEM)] * 3
        + [pl.BlockSpec(memory_space=pl.ANY)],
        out_specs=pl.BlockSpec(memory_space=pl.ANY),
        scratch_shapes=[
            pltpu.VMEM(block, BF16),
            pltpu.VMEM(block, BF16),
            pltpu.SemaphoreType.DMA((slots,)),
            pltpu.SemaphoreType.DMA((slots,)),
        ],
        compiler_params=whole_params(),
        cost_estimate=cost(1e10, 4 * rows_in.size),
        name="temporal",
    )(kinds, first, bands, rows_in)


def unpack(kinds, first, rows_in, filled, heads):
    frames, _, slots, rows, _ = rows_in.shape
    count = frames * rows
    held = len(filled)

    def kernel(kind_ref, first_ref, in_ref, *refs):
        for place, ref in enumerate(refs[held:]):
            ref[...] = in_ref[:, place, 0].reshape(count, DH)

    block = pl.BlockSpec((frames, 4, 1, rows, DH), lambda i, *refs: (0, 0, i, 0, 0))
    return pl.pallas_call(
        kernel,
        out_shape=[jax.ShapeDtypeStruct((count, heads * DH), BF16)] * 4,
        grid_spec=pltpu.PrefetchScalarGridSpec(
            num_scalar_prefetch=2,
            grid=(slots,),
            in_specs=[block] + [pl.BlockSpec(memory_space=pl.ANY)] * held,
            out_specs=[column_spec(count, heads, TEMPORAL)] * 4,
        ),
        input_output_aliases={3 + place: place for place in range(held)},
        compiler_params=params(),
        cost_estimate=cost(0, 4 * rows_in.size),
        name="unpack",
    )(kinds, first, rows_in, *filled)


def spatial(kinds, first, frame, arrays, prior, heads):
    count = arrays[0].shape[0]
    slots = prior.shape[0]
    chunk = min(count, 128)

    def kernel(
        kind_ref, first_ref, frame_ref, q_ref, k_ref, v_ref, g_ref, prior_ref,
        out_ref, qgrad_ref, own_ref, stats_ref,
    ):
        has_prior = frame_ref[0] > 0
        k, v = k_ref[...], v_ref[...]
        k_prior, v_prior = prior_ref[0, 0], prior_ref[0, 1]
        own_ref[...] = jnp.zeros_like(own_ref)

        @pl.loop(0, count // chunk)
        def _(step):
            part = pl.ds(pl.multiple_of(step * chunk, chunk), chunk)
            q, g = q_ref[part], g_ref[part]
            own = dot_nt(k, q)
            before = jnp.where(has_prior, dot_nt(k_prior, q), MASKED)
            top = jnp.maximum(
                jnp.max(own, axis=0, keepdims=True), jnp.max(before, axis=0, keepdims=True)
            )
            own, before = (jnp.exp2((x - top) * SCALE_LOG2) for x in (own, before))
            total = jnp.sum(own, axis=0, keepdims=True) + jnp.sum(before, axis=0, keepdims=True)
            inverse = 1.0 / total
            own, before = own * inverse, before * inverse
            own_dp, before_dp = dot_nt(v, g), dot_nt(v_prior, g)
            delta = jnp.sum(own * own_dp, axis=0, keepdims=True) + jnp.sum(
                before * before_dp, axis=0, keepdims=True
            )
            own_prob, before_prob = own.astype(BF16), before.astype(BF16)
            own_ds = (own * (own_dp - delta) * SCALE).astype(BF16)
            before_ds = (before * (before_dp - delta) * SCALE).astype(BF16)
            out_ref[part] = (dot_tn(own_prob, v) + dot_tn(before_prob, v_prior)).astype(BF16)
            qgrad_ref[part] = (dot_tn(own_ds, k) + dot_tn(before_ds, k_prior)).astype(BF16)
            own_ref[0, 0] += dot_nn(own_ds, q)
            own_ref[0, 1] += dot_nn(own_prob, g)
            stats_ref[0, 0:1, part] = top * SCALE + jnp.log(total)
            stats_ref[0, 1:2, part] = delta

    columns = column_spec(count, heads, SPATIAL)
    pair = pl.BlockSpec((1, 2, count, DH), lambda i, *refs: (i, 0, 0, 0))
    whole = jax.ShapeDtypeStruct((count, heads * DH), BF16)
    return pl.pallas_call(
        kernel,
        out_shape=[
            whole,
            whole,
            jax.ShapeDtypeStruct(prior.shape, F32),
            jax.ShapeDtypeStruct((slots, 2, count), F32),
        ],
        grid_spec=pltpu.PrefetchScalarGridSpec(
            num_scalar_prefetch=3,
            grid=(slots,),
            in_specs=[columns] * 4 + [pair],
            out_specs=[
                columns, columns, pair, pl.BlockSpec((1, 2, count), lambda i, *refs: (i, 0, 0))
            ],
        ),
        compiler_params=params(60),
        cost_estimate=cost(2e11, 16 * slots * count * DH),
        name="spatial",
    )(kinds, first, frame, *arrays, prior)


def spatial_next(kinds, first, k, v, following, stats, own, heads):
    slots, _, count, _ = own.shape
    chunk = min(count, 128)

    def kernel(
        kind_ref, first_ref, k_ref, v_ref, next_ref, stats_ref, own_ref, kgrad_ref, vgrad_ref
    ):
        q, g = next_ref[0, 0], next_ref[0, 1]
        lse, delta = stats_ref[0, 0:1], stats_ref[0, 1:2]

        @pl.loop(0, count // chunk)
        def _(step):
            part = pl.ds(pl.multiple_of(step * chunk, chunk), chunk)
            weight = jnp.exp(dot_nt(k_ref[part], q) * SCALE - lse)
            dscore = (weight * (dot_nt(v_ref[part], g) - delta) * SCALE).astype(BF16)
            kgrad_ref[part] = (own_ref[0, 0, part] + dot_nn(dscore, q)).astype(BF16)
            vgrad_ref[part] = (own_ref[0, 1, part] + dot_nn(weight.astype(BF16), g)).astype(BF16)

    columns = column_spec(count, heads, SPATIAL)
    pair = pl.BlockSpec((1, 2, count, DH), lambda i, *refs: (i, 0, 0, 0))
    return pl.pallas_call(
        kernel,
        out_shape=[jax.ShapeDtypeStruct((count, heads * DH), BF16)] * 2,
        grid_spec=pltpu.PrefetchScalarGridSpec(
            num_scalar_prefetch=2,
            grid=(slots,),
            in_specs=[columns, columns, pair]
            + [pl.BlockSpec((1, 2, count), lambda i, *refs: (i, 0, 0)), pair],
            out_specs=[columns] * 2,
        ),
        compiler_params=params(),
        cost_estimate=cost(8 * slots * count * count * DH, 20 * slots * count * DH),
        name="spatial_next",
    )(kinds, first, k, v, following, stats, own)


def passed_along(array, axis, by):
    length = lax.axis_size(axis)
    pairs = [(i, i + by) for i in range(length) if 0 <= i + by < length]
    return lax.ppermute(array, axis, pairs)


def behind(arrays, *others):
    return lax.optimization_barrier((tuple(arrays), others))[0]


def branch(slots, heads, kinds, bands, first, frame, q, k, v, g):
    frames, rows, width = q.shape
    count = frames * rows
    others = heads - slots
    exchange = functools.partial(
        lax.all_to_all, axis_name="ctx", split_axis=0, concat_axis=0, tiled=True
    )
    packed, filled = [], ()
    if slots > 0:
        packed = [pack_temporal(kinds, first, (q, k, v, g), slots, heads)]
        framed = exchange(*packed)
        results = temporal(kinds, first, bands, framed, heads)
        returned = exchange(results)
    if others > 0:
        ahead, back = pack_spatial(kinds, first, (k, v, q, g), others, heads, packed)
        arrived = [passed_along(ahead, "ctx", 1), passed_along(back, "ctx", -1)]
        if slots > 0:
            arrived = behind(arrived, results)
        prior, following = (x.reshape(others, 2, count, DH) for x in arrived)
        flat = [x.reshape(count, width) for x in (q, k, v, g)]
        attended, qgrad, own, stats = spatial(kinds, first, frame, flat, prior, heads)
        stats = passed_along(stats, "ctx", -1)
        grads = spatial_next(kinds, first, flat[1], flat[2], following, stats, own, heads)
        filled = (attended, qgrad, *grads)
    if slots > 0:
        filled = unpack(kinds, first, returned, filled, heads)
    return tuple(filled)


def body(queries, key_rows, value_rows, out_grad, head_kind, frame_band):
    frames = lax.axis_size("ctx")
    count = queries.shape[1]
    heads = queries.shape[2] // DH
    first = lax.axis_index("head").astype(jnp.int32) * heads
    frame = lax.axis_index("ctx").astype(jnp.int32)
    kinds = lax.dynamic_slice_in_dim(head_kind, first, heads)
    slots = jnp.sum((kinds == TEMPORAL).astype(jnp.int32))
    arrays = [
        x.reshape(frames, count // frames, heads * DH)
        for x in (queries, key_rows, value_rows, out_grad)
    ]
    outs = lax.switch(
        slots,
        [functools.partial(branch, n, heads) for n in range(heads + 1)],
        head_kind, frame_band, first.reshape(1), frame.reshape(1), *arrays,
    )
    return tuple(out.reshape(queries.shape) for out in outs)


def solution(mesh):
    rows = P("ctx", None, "head")
    return jax.shard_map(
        body,
        mesh=mesh,
        in_specs=(rows, rows, rows, rows, P(), P()),
        out_specs=(rows, rows, rows, rows),
        check_vma=False,
    )
```

```python
import functools
import math

import jax
import jax.numpy as jnp
from jax import lax
from jax.experimental import pallas as pl
from jax.experimental.pallas import tpu as pltpu
from jax.sharding import PartitionSpec as P

DH = 128
SCALE = DH ** (-0.5)
SPATIAL, TEMPORAL = 1, 0
MASKED = -1e30
SCALE_LOG2 = SCALE * math.log2(math.e)
F32 = jnp.float32
BF16 = jnp.bfloat16
MIB = 1024 * 1024


def head_at(kind_ref, first_ref, heads, kind, slot):
    found, seen = jnp.int32(0), jnp.int32(0)
    for head in range(heads):
        hit = kind_ref[first_ref[0] + head] == kind
        found = jnp.where(jnp.logical_and(hit, seen == slot), jnp.int32(head), found)
        seen = seen + hit.astype(jnp.int32)
    return found


def dot_nt(a, b):
    return lax.dot_general(a, b, (((1,), (1,)), ((), ())), preferred_element_type=F32)


def dot_nn(a, b):
    return lax.dot_general(a, b, (((1,), (0,)), ((), ())), preferred_element_type=F32)


def dot_tn(a, b):
    return lax.dot_general(a, b, (((0,), (0,)), ((), ())), preferred_element_type=F32)


def params(mib=32):
    return pltpu.CompilerParams(
        dimension_semantics=("arbitrary",), vmem_limit_bytes=mib * MIB
    )


def cost(flops, moved):
    return pl.CostEstimate(flops=int(flops), bytes_accessed=int(moved), transcendentals=0)


def column_spec(count, heads, kind):
    return pl.BlockSpec((count, DH), lambda i, *refs: (0, head_at(*refs[:2], heads, kind, i)))


def head_columns(kind_ref, first_ref, heads, kind, slot):
    return pl.ds(pl.multiple_of(head_at(kind_ref, first_ref, heads, kind, slot) * DH, DH), DH)


def staged_copies(triples, in_sems, out_sems):
    loads = [pltpu.make_async_copy(x, y, in_sems.at[i]) for i, (x, y, _) in enumerate(triples)]
    stores = [pltpu.make_async_copy(y, z, out_sems.at[i]) for i, (_, y, z) in enumerate(triples)]
    for load in loads:
        load.start()
    for load, store in zip(loads, stores):
        load.wait()
        store.start()
    for store in stores:
        store.wait()


def whole_params():
    return pltpu.CompilerParams(vmem_limit_bytes=62 * MIB)


def pack_spatial(kinds, first, arrays, slots, heads, after):
    frames, rows, _ = arrays[0].shape
    count = len(arrays)
    total = slots * count

    def kernel(kind_ref, first_ref, *refs):
        ins, outs = refs[:count], refs[-3 - count // 2 : -3]
        stage, in_sems, out_sems = refs[-3:]
        triples = []
        for slot in range(slots):
            cols = head_columns(kind_ref, first_ref, heads, SPATIAL, slot)
            for place, ref in enumerate(ins):
                target = outs[place // 2].at[slot, place % 2]
                triples.append((ref.at[:, :, cols], stage.at[slot, place], target))
        staged_copies(triples, in_sems, out_sems)

    return pl.pallas_call(
        kernel,
        out_shape=[jax.ShapeDtypeStruct((slots, 2, frames, rows, DH), BF16)] * (count // 2),
        in_specs=[pl.BlockSpec(memory_space=pltpu.SMEM)] * 2
        + [pl.BlockSpec(memory_space=pl.ANY)] * (count + len(after)),
        out_specs=[pl.BlockSpec(memory_space=pl.ANY)] * (count // 2),
        scratch_shapes=[
            pltpu.VMEM((slots, count, frames, rows, DH), BF16),
            pltpu.SemaphoreType.DMA((total,)),
            pltpu.SemaphoreType.DMA((total,)),
        ],
        compiler_params=whole_params(),
        cost_estimate=cost(0, 4 * total * frames * rows * DH),
        name="pack_spatial",
    )(kinds, first, *arrays, *after)


def pack_temporal(kinds, first, arrays, slots, heads):
    frames, rows, _ = arrays[0].shape
    total = 4 * slots

    def kernel(kind_ref, first_ref, *refs):
        ins, (out, stage, in_sems, out_sems) = refs[:4], refs[4:]
        triples = []
        for slot in range(slots):
            cols = head_columns(kind_ref, first_ref, heads, TEMPORAL, slot)
            for place, ref in enumerate(ins):
                triples.append(
                    (ref.at[:, :, cols], stage.at[slot, place], out.at[:, place, slot])
                )
        staged_copies(triples, in_sems, out_sems)

    return pl.pallas_call(
        kernel,
        out_shape=jax.ShapeDtypeStruct((frames, 4, slots, rows, DH), BF16),
        in_specs=[pl.BlockSpec(memory_space=pltpu.SMEM)] * 2
        + [pl.BlockSpec(memory_space=pl.ANY)] * 4,
        out_specs=pl.BlockSpec(memory_space=pl.ANY),
        scratch_shapes=[
            pltpu.VMEM((slots, 4, frames, rows, DH), BF16),
            pltpu.SemaphoreType.DMA((total,)),
            pltpu.SemaphoreType.DMA((total,)),
        ],
        compiler_params=whole_params(),
        cost_estimate=cost(0, 4 * total * frames * rows * DH),
        name="pack_temporal",
    )(kinds, first, *arrays)


def temporal(kinds, first, bands, rows_in, heads):
    frames, _, slots, rows, _ = rows_in.shape
    group = 16
    size = frames * group

    def kernel(kind_ref, first_ref, band_ref, rows_ref, result_ref, held, made, in_sems, out_sems):
        def load(slot):
            return pltpu.make_async_copy(rows_ref.at[:, :, slot], held.at[slot], in_sems.at[slot])

        def store(slot):
            return pltpu.make_async_copy(
                made.at[slot], result_ref.at[:, :, slot], out_sems.at[slot]
            )

        for slot in range(slots):
            load(slot).start()

        @pl.loop(0, slots)
        def _(slot):
            load(slot).wait()
            one_head(kind_ref, first_ref, band_ref, slot, held.at[slot], made.at[slot])
            store(slot).start()

        for slot in range(slots):
            store(slot).wait()

    def one_head(kind_ref, first_ref, band_ref, slot, in_ref, out_ref):
        band = band_ref[first_ref[0] + head_at(kind_ref, first_ref, heads, TEMPORAL, slot)]
        row = lax.broadcasted_iota(jnp.int32, (size, size), 0)
        col = lax.broadcasted_iota(jnp.int32, (size, size), 1)
        same = lax.rem(row, group) == lax.rem(col, group)
        near = jnp.abs(lax.div(row, group) - lax.div(col, group)) <= band
        allowed = jnp.logical_and(same, near)
        parts = [slice(start, start + group) for start in range(0, rows, group)]
        qs, ks, vs, gs = (
            [in_ref[:, place, part].reshape(size, DH) for part in parts] for place in range(4)
        )
        scores = [jnp.where(allowed, dot_nt(k, q), MASKED) for q, k in zip(qs, ks)]
        dprobs = [dot_nt(v, g) for g, v in zip(gs, vs)]
        raised = [
            jnp.exp2((x - jnp.max(x, axis=0, keepdims=True)) * SCALE_LOG2) for x in scores
        ]
        weights = [x * (1.0 / jnp.sum(x, axis=0, keepdims=True)) for x in raised]
        probs = [x.astype(BF16) for x in weights]
        deltas = [jnp.sum(w * dp, axis=0, keepdims=True) for w, dp in zip(weights, dprobs)]
        dscores = [
            (w * (dp - delta) * SCALE).astype(BF16)
            for w, dp, delta in zip(weights, dprobs, deltas)
        ]
        results = (
            [dot_tn(x, v).astype(BF16) for x, v in zip(probs, vs)],
            [dot_tn(x, k).astype(BF16) for x, k in zip(dscores, ks)],
            [dot_nn(x, q).astype(BF16) for x, q in zip(dscores, qs)],
            [dot_nn(x, g).astype(BF16) for x, g in zip(probs, gs)],
        )
        for place, result in enumerate(results):
            for part, value in zip(parts, result):
                out_ref[:, place, part] = value.reshape(frames, group, DH)

    block = (slots, frames, 4, rows, DH)
    return pl.pallas_call(
        kernel,
        out_shape=jax.ShapeDtypeStruct(rows_in.shape, BF16),
        in_specs=[pl.BlockSpec(memory_space=pltpu.SMEM)] * 3
        + [pl.BlockSpec(memory_space=pl.ANY)],
        out_specs=pl.BlockSpec(memory_space=pl.ANY),
        scratch_shapes=[
            pltpu.VMEM(block, BF16),
            pltpu.VMEM(block, BF16),
            pltpu.SemaphoreType.DMA((slots,)),
            pltpu.SemaphoreType.DMA((slots,)),
        ],
        compiler_params=whole_params(),
        cost_estimate=cost(1e10, 4 * rows_in.size),
        name="temporal",
    )(kinds, first, bands, rows_in)


def spatial(kinds, first, frame, arrays, prior, heads):
    count = arrays[0].shape[0]
    slots = prior.shape[0]
    chunk = min(count, 128)

    def kernel(
        kind_ref, first_ref, frame_ref, q_ref, k_ref, v_ref, g_ref, prior_ref,
        out_ref, qgrad_ref, own_ref, stats_ref,
    ):
        has_prior = frame_ref[0] > 0
        k, v = k_ref[...], v_ref[...]
        k_prior, v_prior = prior_ref[0, 0], prior_ref[0, 1]
        own_ref[...] = jnp.zeros_like(own_ref)

        @pl.loop(0, count // chunk)
        def _(step):
            part = pl.ds(pl.multiple_of(step * chunk, chunk), chunk)
            q, g = q_ref[part], g_ref[part]
            own = dot_nt(k, q)
            before = jnp.where(has_prior, dot_nt(k_prior, q), MASKED)
            top = jnp.maximum(
                jnp.max(own, axis=0, keepdims=True), jnp.max(before, axis=0, keepdims=True)
            )
            own, before = (jnp.exp2((x - top) * SCALE_LOG2) for x in (own, before))
            total = jnp.sum(own, axis=0, keepdims=True) + jnp.sum(before, axis=0, keepdims=True)
            inverse = 1.0 / total
            own, before = own * inverse, before * inverse
            own_dp, before_dp = dot_nt(v, g), dot_nt(v_prior, g)
            delta = jnp.sum(own * own_dp, axis=0, keepdims=True) + jnp.sum(
                before * before_dp, axis=0, keepdims=True
            )
            own_prob, before_prob = own.astype(BF16), before.astype(BF16)
            own_ds = (own * (own_dp - delta) * SCALE).astype(BF16)
            before_ds = (before * (before_dp - delta) * SCALE).astype(BF16)
            out_ref[part] = (dot_tn(own_prob, v) + dot_tn(before_prob, v_prior)).astype(BF16)
            qgrad_ref[part] = (dot_tn(own_ds, k) + dot_tn(before_ds, k_prior)).astype(BF16)
            own_ref[0, 0] += dot_nn(own_ds, q)
            own_ref[0, 1] += dot_nn(own_prob, g)
            stats_ref[0, 0:1, part] = top * SCALE + jnp.log(total)
            stats_ref[0, 1:2, part] = delta

    columns = column_spec(count, heads, SPATIAL)
    pair = pl.BlockSpec((1, 2, count, DH), lambda i, *refs: (i, 0, 0, 0))
    whole = jax.ShapeDtypeStruct((count, heads * DH), BF16)
    return pl.pallas_call(
        kernel,
        out_shape=[
            whole,
            whole,
            jax.ShapeDtypeStruct(prior.shape, F32),
            jax.ShapeDtypeStruct((slots, 2, count), F32),
        ],
        grid_spec=pltpu.PrefetchScalarGridSpec(
            num_scalar_prefetch=3,
            grid=(slots,),
            in_specs=[columns] * 4 + [pair],
            out_specs=[
                columns, columns, pair, pl.BlockSpec((1, 2, count), lambda i, *refs: (i, 0, 0))
            ],
        ),
        compiler_params=params(60),
        cost_estimate=cost(2e11, 16 * slots * count * DH),
        name="spatial",
    )(kinds, first, frame, *arrays, prior)


def finish(kinds, first, rows_in, filled, k, v, following, stats, own, heads):
    count = k.shape[0]
    slots = 0 if rows_in is None else rows_in.shape[2]
    others = heads - slots
    chunk = min(count, 256)
    ins, scratch = [], []
    if slots:
        frames, _, _, rows, _ = rows_in.shape
        ins += [rows_in]
        scratch += [pltpu.VMEM((slots, 4, frames, rows, DH), BF16)]
        scratch += [pltpu.SemaphoreType.DMA((4 * slots,))] * 2
    if others:
        ins += [*filled, k, v, following, stats, own]
        scratch += [
            pltpu.VMEM((others, 2, count, DH), BF16),
            pltpu.VMEM((others, 2, count, DH), BF16),
            pltpu.VMEM((others, 2, count), F32),
            pltpu.VMEM((others, 2, count, DH), F32),
            pltpu.VMEM((others, 2, count, DH), BF16),
            pltpu.SemaphoreType.DMA((others, 5)),
            pltpu.SemaphoreType.DMA((others, 2)),
        ]

    def kernel(kind_ref, first_ref, *refs):
        in_refs, out_refs = refs[: len(ins)], refs[len(ins) : len(ins) + 4]
        temps = refs[len(ins) + 4 :]
        loads, stores = [], []
        if slots:
            stage, in_sems, out_sems = temps[:3]
            for slot in range(slots):
                cols = head_columns(kind_ref, first_ref, heads, TEMPORAL, slot)
                for place, out in enumerate(out_refs):
                    at, held = 4 * slot + place, stage.at[slot, place]
                    source = in_refs[0].at[:, place, slot]
                    target = out.at[:, cols]
                    loads.append(pltpu.make_async_copy(source, held, in_sems.at[at]))
                    stores.append(
                        pltpu.make_async_copy(held.reshape(count, DH), target, out_sems.at[at])
                    )
        if others:
            k_in, v_in, next_in, stats_in, own_in = in_refs[-5:]
            kv_ref, next_ref, stats_ref, own_ref, made_ref, sems, made_sems = temps[-7:]

            def spatial_loads(slot):
                cols = head_columns(kind_ref, first_ref, heads, SPATIAL, slot)
                pairs = [
                    (k_in.at[:, cols], kv_ref.at[slot, 0]),
                    (v_in.at[:, cols], kv_ref.at[slot, 1]),
                    (next_in.at[slot], next_ref.at[slot]),
                    (stats_in.at[slot], stats_ref.at[slot]),
                    (own_in.at[slot], own_ref.at[slot]),
                ]
                return [
                    pltpu.make_async_copy(*pair, sems.at[slot, i]) for i, pair in enumerate(pairs)
                ]

            def spatial_stores(slot):
                cols = head_columns(kind_ref, first_ref, heads, SPATIAL, slot)
                return [
                    pltpu.make_async_copy(
                        made_ref.at[slot, i], out_refs[2 + i].at[:, cols], made_sems.at[slot, i]
                    )
                    for i in range(2)
                ]

            for slot in range(others):
                for copy in spatial_loads(slot):
                    copy.start()
        for copy in loads:
            copy.start()
        for load, store in zip(loads, stores):
            load.wait()
            store.start()
        if others:

            @pl.loop(0, others)
            def _(slot):
                for copy in spatial_loads(slot):
                    copy.wait()
                q, g = next_ref[slot, 0], next_ref[slot, 1]
                lse, delta = stats_ref[slot, 0:1] * math.log2(math.e), stats_ref[slot, 1:2]
                for start in range(0, count, chunk):
                    part = slice(start, start + chunk)
                    weight = jnp.exp2(dot_nt(kv_ref[slot, 0, part], q) * SCALE_LOG2 - lse)
                    slope = (weight * (dot_nt(kv_ref[slot, 1, part], g) - delta)).astype(BF16)
                    made_ref[slot, 0, part] = (
                        own_ref[slot, 0, part] + dot_nn(slope, q) * SCALE
                    ).astype(BF16)
                    made_ref[slot, 1, part] = (
                        own_ref[slot, 1, part] + dot_nn(weight.astype(BF16), g)
                    ).astype(BF16)
                for copy in spatial_stores(slot):
                    copy.start()

            for slot in range(others):
                for copy in spatial_stores(slot):
                    copy.wait()
        for copy in stores:
            copy.wait()

    place = 2 + (1 if slots else 0)
    return pl.pallas_call(
        kernel,
        out_shape=[jax.ShapeDtypeStruct((count, heads * DH), BF16)] * 4,
        in_specs=[pl.BlockSpec(memory_space=pltpu.SMEM)] * 2
        + [pl.BlockSpec(memory_space=pl.ANY)] * len(ins),
        out_specs=[pl.BlockSpec(memory_space=pl.ANY)] * 4,
        scratch_shapes=scratch,
        input_output_aliases={place: 0, place + 1: 1} if others else {},
        compiler_params=whole_params(),
        cost_estimate=cost(8 * others * count * count * DH, 16 * heads * count * DH),
        name="finish",
    )(kinds, first, *ins)


def passed_along(array, axis, by):
    length = lax.axis_size(axis)
    pairs = [(i, i + by) for i in range(length) if 0 <= i + by < length]
    return lax.ppermute(array, axis, pairs)


def behind(arrays, *others):
    return lax.optimization_barrier((tuple(arrays), others))[0]


def branch(slots, heads, kinds, bands, first, frame, q, k, v, g):
    frames, rows, width = q.shape
    count = frames * rows
    others = heads - slots
    exchange = functools.partial(
        lax.all_to_all, axis_name="ctx", split_axis=0, concat_axis=0, tiled=True
    )
    flat = [x.reshape(count, width) for x in (q, k, v, g)]
    packed = []
    returned = filled = following = stats = own = None
    if slots > 0:
        packed = [pack_temporal(kinds, first, (q, k, v, g), slots, heads)]
        framed = exchange(*packed)
        results = temporal(kinds, first, bands, framed, heads)
        returned = exchange(results)
    if others > 0:
        ahead, back = pack_spatial(kinds, first, (k, v, q, g), others, heads, packed)
        arrived = [passed_along(ahead, "ctx", 1), passed_along(back, "ctx", -1)]
        if slots > 0:
            arrived = behind(arrived, results)
        prior, following = (x.reshape(others, 2, count, DH) for x in arrived)
        attended, qgrad, own, stats = spatial(kinds, first, frame, flat, prior, heads)
        stats = passed_along(stats, "ctx", -1)
        filled = (attended, qgrad)
    return finish(kinds, first, returned, filled, *flat[1:3], following, stats, own, heads)


def body(queries, key_rows, value_rows, out_grad, head_kind, frame_band):
    frames = lax.axis_size("ctx")
    count = queries.shape[1]
    heads = queries.shape[2] // DH
    first = lax.axis_index("head").astype(jnp.int32) * heads
    frame = lax.axis_index("ctx").astype(jnp.int32)
    kinds = lax.dynamic_slice_in_dim(head_kind, first, heads)
    slots = jnp.sum((kinds == TEMPORAL).astype(jnp.int32))
    arrays = [
        x.reshape(frames, count // frames, heads * DH)
        for x in (queries, key_rows, value_rows, out_grad)
    ]
    outs = lax.switch(
        slots,
        [functools.partial(branch, n, heads) for n in range(heads + 1)],
        head_kind, frame_band, first.reshape(1), frame.reshape(1), *arrays,
    )
    return tuple(out.reshape(queries.shape) for out in outs)


def solution(mesh):
    rows = P("ctx", None, "head")
    return jax.shard_map(
        body,
        mesh=mesh,
        in_specs=(rows, rows, rows, rows, P(), P()),
        out_specs=(rows, rows, rows, rows),
        check_vma=False,
    )
```

```python
import functools
import math

import jax
import jax.numpy as jnp
from jax import lax
from jax.experimental import pallas as pl
from jax.experimental.pallas import tpu as pltpu
from jax.sharding import PartitionSpec as P

DH = 128
SCALE = DH ** (-0.5)
SPATIAL, TEMPORAL = 1, 0
MASKED = -1e30
SCALE_LOG2 = SCALE * math.log2(math.e)
F32 = jnp.float32
BF16 = jnp.bfloat16
MIB = 1024 * 1024


def head_at(kind_ref, first_ref, heads, kind, slot):
    found, seen = jnp.int32(0), jnp.int32(0)
    for head in range(heads):
        hit = kind_ref[first_ref[0] + head] == kind
        found = jnp.where(jnp.logical_and(hit, seen == slot), jnp.int32(head), found)
        seen = seen + hit.astype(jnp.int32)
    return found


def dot_nt(a, b):
    return lax.dot_general(a, b, (((1,), (1,)), ((), ())), preferred_element_type=F32)


def dot_nn(a, b):
    return lax.dot_general(a, b, (((1,), (0,)), ((), ())), preferred_element_type=F32)


def dot_tn(a, b):
    return lax.dot_general(a, b, (((0,), (0,)), ((), ())), preferred_element_type=F32)


def params(mib=32):
    return pltpu.CompilerParams(
        dimension_semantics=("arbitrary",), vmem_limit_bytes=mib * MIB
    )


def cost(flops, moved):
    return pl.CostEstimate(flops=int(flops), bytes_accessed=int(moved), transcendentals=0)


def column_spec(count, heads, kind):
    return pl.BlockSpec((count, DH), lambda i, *refs: (0, head_at(*refs[:2], heads, kind, i)))


def head_columns(kind_ref, first_ref, heads, kind, slot):
    return pl.ds(pl.multiple_of(head_at(kind_ref, first_ref, heads, kind, slot) * DH, DH), DH)


def staged_copies(triples, in_sems, out_sems):
    loads = [pltpu.make_async_copy(x, y, in_sems.at[i]) for i, (x, y, _) in enumerate(triples)]
    stores = [pltpu.make_async_copy(y, z, out_sems.at[i]) for i, (_, y, z) in enumerate(triples)]
    for load in loads:
        load.start()
    for load, store in zip(loads, stores):
        load.wait()
        store.start()
    for store in stores:
        store.wait()


def whole_params():
    return pltpu.CompilerParams(vmem_limit_bytes=62 * MIB)


def pack_spatial(kinds, first, arrays, slots, heads, after):
    frames, rows, _ = arrays[0].shape
    count = len(arrays)
    total = slots * count

    def kernel(kind_ref, first_ref, *refs):
        ins, outs = refs[:count], refs[-3 - count // 2 : -3]
        stage, in_sems, out_sems = refs[-3:]
        triples = []
        for slot in range(slots):
            cols = head_columns(kind_ref, first_ref, heads, SPATIAL, slot)
            for place, ref in enumerate(ins):
                target = outs[place // 2].at[slot, place % 2]
                triples.append((ref.at[:, :, cols], stage.at[slot, place], target))
        staged_copies(triples, in_sems, out_sems)

    return pl.pallas_call(
        kernel,
        out_shape=[jax.ShapeDtypeStruct((slots, 2, frames, rows, DH), BF16)] * (count // 2),
        in_specs=[pl.BlockSpec(memory_space=pltpu.SMEM)] * 2
        + [pl.BlockSpec(memory_space=pl.ANY)] * (count + len(after)),
        out_specs=[pl.BlockSpec(memory_space=pl.ANY)] * (count // 2),
        scratch_shapes=[
            pltpu.VMEM((slots, count, frames, rows, DH), BF16),
            pltpu.SemaphoreType.DMA((total,)),
            pltpu.SemaphoreType.DMA((total,)),
        ],
        compiler_params=whole_params(),
        cost_estimate=cost(0, 4 * total * frames * rows * DH),
        name="pack_spatial",
    )(kinds, first, *arrays, *after)


def pack_temporal(kinds, first, arrays, slots, heads):
    frames, rows, _ = arrays[0].shape
    total = 4 * slots

    def kernel(kind_ref, first_ref, *refs):
        ins, (out, stage, in_sems, out_sems) = refs[:4], refs[4:]
        triples = []
        for slot in range(slots):
            cols = head_columns(kind_ref, first_ref, heads, TEMPORAL, slot)
            for place, ref in enumerate(ins):
                triples.append(
                    (ref.at[:, :, cols], stage.at[slot, place], out.at[:, place, slot])
                )
        staged_copies(triples, in_sems, out_sems)

    return pl.pallas_call(
        kernel,
        out_shape=jax.ShapeDtypeStruct((frames, 4, slots, rows, DH), BF16),
        in_specs=[pl.BlockSpec(memory_space=pltpu.SMEM)] * 2
        + [pl.BlockSpec(memory_space=pl.ANY)] * 4,
        out_specs=pl.BlockSpec(memory_space=pl.ANY),
        scratch_shapes=[
            pltpu.VMEM((slots, 4, frames, rows, DH), BF16),
            pltpu.SemaphoreType.DMA((total,)),
            pltpu.SemaphoreType.DMA((total,)),
        ],
        compiler_params=whole_params(),
        cost_estimate=cost(0, 4 * total * frames * rows * DH),
        name="pack_temporal",
    )(kinds, first, *arrays)


def temporal(kinds, first, bands, rows_in, heads):
    frames, _, slots, rows, _ = rows_in.shape
    group = 16
    size = frames * group

    def frame_at(place):
        return lax.rem(place, 2) * (frames // 2) + lax.div(place, 2)

    def kernel(kind_ref, first_ref, band_ref, rows_ref, result_ref, held, made, in_sems, out_sems):
        def load(slot):
            return pltpu.make_async_copy(rows_ref.at[:, :, slot], held.at[slot], in_sems.at[slot])

        def store(slot):
            return pltpu.make_async_copy(
                made.at[slot], result_ref.at[:, :, slot], out_sems.at[slot]
            )

        for slot in range(slots):
            load(slot).start()

        @pl.loop(0, slots)
        def _(slot):
            load(slot).wait()
            one_head(kind_ref, first_ref, band_ref, slot, held.at[slot], made.at[slot])
            store(slot).start()

        for slot in range(slots):
            store(slot).wait()

    def one_head(kind_ref, first_ref, band_ref, slot, in_ref, out_ref):
        band = band_ref[first_ref[0] + head_at(kind_ref, first_ref, heads, TEMPORAL, slot)]
        row = lax.broadcasted_iota(jnp.int32, (size, size), 0)
        col = lax.broadcasted_iota(jnp.int32, (size, size), 1)
        same = lax.rem(row, group) == lax.rem(col, group)
        near = jnp.abs(frame_at(lax.div(row, group)) - frame_at(lax.div(col, group))) <= band
        allowed = jnp.logical_and(same, near)
        parts = [slice(start, start + group) for start in range(0, rows, group)]
        qs, ks, vs, gs = (
            [in_ref[:, place, part].reshape(size, DH) for part in parts] for place in range(4)
        )
        scores = [jnp.where(allowed, dot_nt(k, q), MASKED) for q, k in zip(qs, ks)]
        dprobs = [dot_nt(v, g) for g, v in zip(gs, vs)]
        raised = [
            jnp.exp2((x - jnp.max(x, axis=0, keepdims=True)) * SCALE_LOG2) for x in scores
        ]
        weights = [x * (1.0 / jnp.sum(x, axis=0, keepdims=True)) for x in raised]
        probs = [x.astype(BF16) for x in weights]
        deltas = [jnp.sum(w * dp, axis=0, keepdims=True) for w, dp in zip(weights, dprobs)]
        dscores = [
            (w * (dp - delta) * SCALE).astype(BF16)
            for w, dp, delta in zip(weights, dprobs, deltas)
        ]
        results = (
            [dot_tn(x, v).astype(BF16) for x, v in zip(probs, vs)],
            [dot_tn(x, k).astype(BF16) for x, k in zip(dscores, ks)],
            [dot_nn(x, q).astype(BF16) for x, q in zip(dscores, qs)],
            [dot_nn(x, g).astype(BF16) for x, g in zip(probs, gs)],
        )
        for place, result in enumerate(results):
            for part, value in zip(parts, result):
                out_ref[:, place, part] = value.reshape(frames, group, DH)

    block = (slots, frames, 4, rows, DH)
    return pl.pallas_call(
        kernel,
        out_shape=jax.ShapeDtypeStruct(rows_in.shape, BF16),
        in_specs=[pl.BlockSpec(memory_space=pltpu.SMEM)] * 3
        + [pl.BlockSpec(memory_space=pl.ANY)],
        out_specs=pl.BlockSpec(memory_space=pl.ANY),
        scratch_shapes=[
            pltpu.VMEM(block, BF16),
            pltpu.VMEM(block, BF16),
            pltpu.SemaphoreType.DMA((slots,)),
            pltpu.SemaphoreType.DMA((slots,)),
        ],
        compiler_params=whole_params(),
        cost_estimate=cost(1e10, 4 * rows_in.size),
        name="temporal",
    )(kinds, first, bands, rows_in)


def spatial(kinds, first, frame, arrays, prior, heads):
    count = arrays[0].shape[0]
    slots = prior.shape[0]
    chunk = min(count, 128)

    def kernel(
        kind_ref, first_ref, frame_ref, q_ref, k_ref, v_ref, g_ref, prior_ref,
        out_ref, qgrad_ref, own_ref, stats_ref,
    ):
        has_prior = frame_ref[0] > 0
        k, v = k_ref[...], v_ref[...]
        k_prior, v_prior = prior_ref[0, 0], prior_ref[0, 1]
        own_ref[...] = jnp.zeros_like(own_ref)

        @pl.loop(0, count // chunk)
        def _(step):
            part = pl.ds(pl.multiple_of(step * chunk, chunk), chunk)
            q, g = q_ref[part], g_ref[part]
            own = dot_nt(k, q)
            before = jnp.where(has_prior, dot_nt(k_prior, q), MASKED)
            top = jnp.maximum(
                jnp.max(own, axis=0, keepdims=True), jnp.max(before, axis=0, keepdims=True)
            )
            own, before = (jnp.exp2((x - top) * SCALE_LOG2) for x in (own, before))
            total = jnp.sum(own, axis=0, keepdims=True) + jnp.sum(before, axis=0, keepdims=True)
            inverse = 1.0 / total
            own, before = own * inverse, before * inverse
            own_dp, before_dp = dot_nt(v, g), dot_nt(v_prior, g)
            delta = jnp.sum(own * own_dp, axis=0, keepdims=True) + jnp.sum(
                before * before_dp, axis=0, keepdims=True
            )
            own_prob, before_prob = own.astype(BF16), before.astype(BF16)
            own_ds = (own * (own_dp - delta) * SCALE).astype(BF16)
            before_ds = (before * (before_dp - delta) * SCALE).astype(BF16)
            out_ref[part] = (dot_tn(own_prob, v) + dot_tn(before_prob, v_prior)).astype(BF16)
            qgrad_ref[part] = (dot_tn(own_ds, k) + dot_tn(before_ds, k_prior)).astype(BF16)
            own_ref[0, 0] += dot_nn(own_ds, q)
            own_ref[0, 1] += dot_nn(own_prob, g)
            stats_ref[0, 0:1, part] = top * SCALE + jnp.log(total)
            stats_ref[0, 1:2, part] = delta

    columns = column_spec(count, heads, SPATIAL)
    pair = pl.BlockSpec((1, 2, count, DH), lambda i, *refs: (i, 0, 0, 0))
    whole = jax.ShapeDtypeStruct((count, heads * DH), BF16)
    return pl.pallas_call(
        kernel,
        out_shape=[
            whole,
            whole,
            jax.ShapeDtypeStruct(prior.shape, F32),
            jax.ShapeDtypeStruct((slots, 2, count), F32),
        ],
        grid_spec=pltpu.PrefetchScalarGridSpec(
            num_scalar_prefetch=3,
            grid=(slots,),
            in_specs=[columns] * 4 + [pair],
            out_specs=[
                columns, columns, pair, pl.BlockSpec((1, 2, count), lambda i, *refs: (i, 0, 0))
            ],
        ),
        compiler_params=params(60),
        cost_estimate=cost(2e11, 16 * slots * count * DH),
        name="spatial",
    )(kinds, first, frame, *arrays, prior)


def finish(kinds, first, rows_in, filled, k, v, following, stats, own, heads):
    count = k.shape[0]
    slots = 0 if rows_in is None else rows_in.shape[2]
    others = heads - slots
    chunk = min(count, 256)
    ins, scratch = [], []
    if slots:
        frames, _, _, rows, _ = rows_in.shape
        ins += [rows_in]
        scratch += [pltpu.VMEM((slots, 4, frames, rows, DH), BF16)]
        scratch += [pltpu.SemaphoreType.DMA((4 * slots,))] * 2
    if others:
        ins += [*filled, k, v, following, stats, own]
        scratch += [
            pltpu.VMEM((others, 2, count, DH), BF16),
            pltpu.VMEM((others, 2, count, DH), BF16),
            pltpu.VMEM((others, 2, count), F32),
            pltpu.VMEM((others, 2, count, DH), F32),
            pltpu.VMEM((others, 2, count, DH), BF16),
            pltpu.SemaphoreType.DMA((others, 5)),
            pltpu.SemaphoreType.DMA((others, 2)),
        ]

    def kernel(kind_ref, first_ref, *refs):
        in_refs, out_refs = refs[: len(ins)], refs[len(ins) : len(ins) + 4]
        temps = refs[len(ins) + 4 :]
        loads, stores = [], []
        if slots:
            stage, in_sems, out_sems = temps[:3]
            for slot in range(slots):
                cols = head_columns(kind_ref, first_ref, heads, TEMPORAL, slot)
                for place, out in enumerate(out_refs):
                    at, held = 4 * slot + place, stage.at[slot, place]
                    source = in_refs[0].at[:, place, slot]
                    target = out.at[:, cols]
                    loads.append(pltpu.make_async_copy(source, held, in_sems.at[at]))
                    stores.append(
                        pltpu.make_async_copy(held.reshape(count, DH), target, out_sems.at[at])
                    )
        if others:
            k_in, v_in, next_in, stats_in, own_in = in_refs[-5:]
            kv_ref, next_ref, stats_ref, own_ref, made_ref, sems, made_sems = temps[-7:]

            def spatial_loads(slot):
                cols = head_columns(kind_ref, first_ref, heads, SPATIAL, slot)
                pairs = [
                    (k_in.at[:, cols], kv_ref.at[slot, 0]),
                    (v_in.at[:, cols], kv_ref.at[slot, 1]),
                    (next_in.at[slot], next_ref.at[slot]),
                    (stats_in.at[slot], stats_ref.at[slot]),
                    (own_in.at[slot], own_ref.at[slot]),
                ]
                return [
                    pltpu.make_async_copy(*pair, sems.at[slot, i]) for i, pair in enumerate(pairs)
                ]

            def spatial_stores(slot):
                cols = head_columns(kind_ref, first_ref, heads, SPATIAL, slot)
                return [
                    pltpu.make_async_copy(
                        made_ref.at[slot, i], out_refs[2 + i].at[:, cols], made_sems.at[slot, i]
                    )
                    for i in range(2)
                ]

            for slot in range(others):
                for copy in spatial_loads(slot):
                    copy.start()
        for copy in loads:
            copy.start()
        for load, store in zip(loads, stores):
            load.wait()
            store.start()
        if others:

            @pl.loop(0, others)
            def _(slot):
                for copy in spatial_loads(slot):
                    copy.wait()
                q, g = next_ref[slot, 0], next_ref[slot, 1]
                lse, delta = stats_ref[slot, 0:1] * math.log2(math.e), stats_ref[slot, 1:2]
                for start in range(0, count, chunk):
                    part = slice(start, start + chunk)
                    weight = jnp.exp2(dot_nt(kv_ref[slot, 0, part], q) * SCALE_LOG2 - lse)
                    slope = (weight * (dot_nt(kv_ref[slot, 1, part], g) - delta)).astype(BF16)
                    made_ref[slot, 0, part] = (
                        own_ref[slot, 0, part] + dot_nn(slope, q) * SCALE
                    ).astype(BF16)
                    made_ref[slot, 1, part] = (
                        own_ref[slot, 1, part] + dot_nn(weight.astype(BF16), g)
                    ).astype(BF16)
                for copy in spatial_stores(slot):
                    copy.start()

            for slot in range(others):
                for copy in spatial_stores(slot):
                    copy.wait()
        for copy in stores:
            copy.wait()

    place = 2 + (1 if slots else 0)
    return pl.pallas_call(
        kernel,
        out_shape=[jax.ShapeDtypeStruct((count, heads * DH), BF16)] * 4,
        in_specs=[pl.BlockSpec(memory_space=pltpu.SMEM)] * 2
        + [pl.BlockSpec(memory_space=pl.ANY)] * len(ins),
        out_specs=[pl.BlockSpec(memory_space=pl.ANY)] * 4,
        scratch_shapes=scratch,
        input_output_aliases={place: 0, place + 1: 1} if others else {},
        compiler_params=whole_params(),
        cost_estimate=cost(8 * others * count * count * DH, 16 * heads * count * DH),
        name="finish",
    )(kinds, first, *ins)


def passed_along(array, axis, by):
    length = lax.axis_size(axis)
    pairs = [(i, i + by) for i in range(length) if 0 <= i + by < length]
    return lax.ppermute(array, axis, pairs)


def behind(arrays, *others):
    return lax.optimization_barrier((tuple(arrays), others))[0]


def exchange_order(frames):
    return [half * (frames // 2) + place for place in range(frames // 2) for half in (0, 1)]


def branch(slots, heads, kinds, bands, first, frame, q, k, v, g):
    frames, rows, width = q.shape
    count = frames * rows
    others = heads - slots
    exchange = functools.partial(
        lax.all_to_all, axis_name="ctx", split_axis=0, concat_axis=0, tiled=True,
        axis_index_groups=[exchange_order(frames)],
    )
    flat = [x.reshape(count, width) for x in (q, k, v, g)]
    packed = []
    returned = filled = following = stats = own = None
    if slots > 0:
        packed = [pack_temporal(kinds, first, (q, k, v, g), slots, heads)]
        framed = exchange(*packed)
        results = temporal(kinds, first, bands, framed, heads)
        returned = exchange(results)
    if others > 0:
        ahead, back = pack_spatial(kinds, first, (k, v, q, g), others, heads, packed)
        arrived = [passed_along(ahead, "ctx", 1), passed_along(back, "ctx", -1)]
        if slots > 0:
            arrived = behind(arrived, results)
        prior, following = (x.reshape(others, 2, count, DH) for x in arrived)
        attended, qgrad, own, stats = spatial(kinds, first, frame, flat, prior, heads)
        stats = passed_along(stats, "ctx", -1)
        filled = (attended, qgrad)
    return finish(kinds, first, returned, filled, *flat[1:3], following, stats, own, heads)


def body(queries, key_rows, value_rows, out_grad, head_kind, frame_band):
    frames = lax.axis_size("ctx")
    count = queries.shape[1]
    heads = queries.shape[2] // DH
    first = lax.axis_index("head").astype(jnp.int32) * heads
    frame = lax.axis_index("ctx").astype(jnp.int32)
    kinds = lax.dynamic_slice_in_dim(head_kind, first, heads)
    slots = jnp.sum((kinds == TEMPORAL).astype(jnp.int32))
    arrays = [
        x.reshape(frames, count // frames, heads * DH)
        for x in (queries, key_rows, value_rows, out_grad)
    ]
    outs = lax.switch(
        slots,
        [functools.partial(branch, n, heads) for n in range(heads + 1)],
        head_kind, frame_band, first.reshape(1), frame.reshape(1), *arrays,
    )
    return tuple(out.reshape(queries.shape) for out in outs)


def solution(mesh):
    rows = P("ctx", None, "head")
    return jax.shard_map(
        body,
        mesh=mesh,
        in_specs=(rows, rows, rows, rows, P(), P()),
        out_specs=(rows, rows, rows, rows),
        check_vma=False,
    )
```

```python
import functools
import math

import jax
import jax.numpy as jnp
from jax import lax
from jax.experimental import pallas as pl
from jax.experimental.pallas import tpu as pltpu
from jax.sharding import PartitionSpec as P

DH = 128
SCALE = DH ** (-0.5)
SPATIAL, TEMPORAL = 1, 0
MASKED = -1e30
SCALE_LOG2 = SCALE * math.log2(math.e)
F32 = jnp.float32
BF16 = jnp.bfloat16
MIB = 1024 * 1024


def head_at(kind_ref, first_ref, heads, kind, slot):
    found, seen = jnp.int32(0), jnp.int32(0)
    for head in range(heads):
        hit = kind_ref[first_ref[0] + head] == kind
        found = jnp.where(jnp.logical_and(hit, seen == slot), jnp.int32(head), found)
        seen = seen + hit.astype(jnp.int32)
    return found


def dot_nt(a, b):
    return lax.dot_general(a, b, (((1,), (1,)), ((), ())), preferred_element_type=F32)


def dot_nn(a, b):
    return lax.dot_general(a, b, (((1,), (0,)), ((), ())), preferred_element_type=F32)


def dot_tn(a, b):
    return lax.dot_general(a, b, (((0,), (0,)), ((), ())), preferred_element_type=F32)


def params(mib=32):
    return pltpu.CompilerParams(
        dimension_semantics=("arbitrary",), vmem_limit_bytes=mib * MIB
    )


def cost(flops, moved):
    return pl.CostEstimate(flops=int(flops), bytes_accessed=int(moved), transcendentals=0)


def column_spec(count, heads, kind):
    return pl.BlockSpec((count, DH), lambda i, *refs: (0, head_at(*refs[:2], heads, kind, i)))


def head_columns(kind_ref, first_ref, heads, kind, slot):
    return pl.ds(pl.multiple_of(head_at(kind_ref, first_ref, heads, kind, slot) * DH, DH), DH)


def staged_copies(triples, in_sems, out_sems):
    loads = [pltpu.make_async_copy(x, y, in_sems.at[i]) for i, (x, y, _) in enumerate(triples)]
    stores = [pltpu.make_async_copy(y, z, out_sems.at[i]) for i, (_, y, z) in enumerate(triples)]
    for load in loads:
        load.start()
    for load, store in zip(loads, stores):
        load.wait()
        store.start()
    for store in stores:
        store.wait()


def whole_params():
    return pltpu.CompilerParams(vmem_limit_bytes=62 * MIB)


def pack_spatial(kinds, first, arrays, slots, heads, after):
    frames, rows, _ = arrays[0].shape
    count = len(arrays)
    total = slots * count

    def kernel(kind_ref, first_ref, *refs):
        ins, outs = refs[:count], refs[-3 - count // 2 : -3]
        stage, in_sems, out_sems = refs[-3:]
        triples = []
        for slot in range(slots):
            cols = head_columns(kind_ref, first_ref, heads, SPATIAL, slot)
            for place, ref in enumerate(ins):
                target = outs[place // 2].at[slot, place % 2]
                triples.append((ref.at[:, :, cols], stage.at[slot, place], target))
        staged_copies(triples, in_sems, out_sems)

    return pl.pallas_call(
        kernel,
        out_shape=[jax.ShapeDtypeStruct((slots, 2, frames, rows, DH), BF16)] * (count // 2),
        in_specs=[pl.BlockSpec(memory_space=pltpu.SMEM)] * 2
        + [pl.BlockSpec(memory_space=pl.ANY)] * (count + len(after)),
        out_specs=[pl.BlockSpec(memory_space=pl.ANY)] * (count // 2),
        scratch_shapes=[
            pltpu.VMEM((slots, count, frames, rows, DH), BF16),
            pltpu.SemaphoreType.DMA((total,)),
            pltpu.SemaphoreType.DMA((total,)),
        ],
        compiler_params=whole_params(),
        cost_estimate=cost(0, 4 * total * frames * rows * DH),
        name="pack_spatial",
    )(kinds, first, *arrays, *after)


def pack_temporal(kinds, first, frame, arrays, slots, heads):
    frames, rows, _ = arrays[0].shape

    def kernel(kind_ref, first_ref, frame_ref, *refs):
        ins, outs, (stage, in_sems, out_sems) = refs[:4], refs[4:-3], refs[-3:]
        loads = []
        for slot in range(slots):
            cols = head_columns(kind_ref, first_ref, heads, TEMPORAL, slot)
            for place, ref in enumerate(ins):
                sem = in_sems.at[4 * slot + place]
                loads.append(
                    pltpu.make_async_copy(ref.at[:, :, cols], stage.at[:, place, slot], sem)
                )
        stores = [
            pltpu.make_async_copy(
                stage.at[lax.rem(frame_ref[0] + ahead, frames)], out, out_sems.at[ahead]
            )
            for ahead, out in enumerate(outs)
        ]
        for group in (loads, stores):
            for copy in group:
                copy.start()
            for copy in group:
                copy.wait()

    return pl.pallas_call(
        kernel,
        out_shape=[jax.ShapeDtypeStruct((4, slots, rows, DH), BF16)] * frames,
        in_specs=[pl.BlockSpec(memory_space=pltpu.SMEM)] * 3
        + [pl.BlockSpec(memory_space=pl.ANY)] * 4,
        out_specs=[pl.BlockSpec(memory_space=pl.ANY)] * frames,
        scratch_shapes=[
            pltpu.VMEM((frames, 4, slots, rows, DH), BF16),
            pltpu.SemaphoreType.DMA((4 * slots,)),
            pltpu.SemaphoreType.DMA((frames,)),
        ],
        compiler_params=whole_params(),
        cost_estimate=cost(0, 16 * slots * frames * rows * DH),
        name="pack_temporal",
    )(kinds, first, frame, *arrays)


def temporal(kinds, first, frame, bands, rows_in, heads):
    frames = len(rows_in)
    _, slots, rows, _ = rows_in[0].shape
    group = 16
    size = frames * group

    def kernel(kind_ref, first_ref, frame_ref, band_ref, *refs):
        ins, outs, (held, made, in_sems, out_sems) = refs[:frames], refs[frames:-4], refs[-4:]

        def store(slot):
            return [
                pltpu.make_async_copy(
                    made.at[place, :, slot], out.at[:, slot], out_sems.at[slot, place]
                )
                for place, out in enumerate(outs)
            ]

        loads = [
            pltpu.make_async_copy(ref, held.at[place], in_sems.at[place])
            for place, ref in enumerate(ins)
        ]
        for copy in loads:
            copy.start()
        for copy in loads:
            copy.wait()

        @pl.loop(0, slots)
        def _(slot):
            one_head(
                kind_ref, first_ref, frame_ref, band_ref, slot,
                held.at[:, :, slot], made.at[:, :, slot],
            )
            for copy in store(slot):
                copy.start()

        for slot in range(slots):
            for copy in store(slot):
                copy.wait()

    def one_head(kind_ref, first_ref, frame_ref, band_ref, slot, in_ref, out_ref):
        band = band_ref[first_ref[0] + head_at(kind_ref, first_ref, heads, TEMPORAL, slot)]
        row = lax.broadcasted_iota(jnp.int32, (size, size), 0)
        col = lax.broadcasted_iota(jnp.int32, (size, size), 1)
        same = lax.rem(row, group) == lax.rem(col, group)
        frame_at = lambda place: lax.rem(frame_ref[0] + frames - place, frames)
        distance = jnp.abs(frame_at(lax.div(row, group)) - frame_at(lax.div(col, group)))
        near = distance <= band
        allowed = jnp.logical_and(same, near)
        parts = [slice(start, start + group) for start in range(0, rows, group)]
        qs, ks, vs, gs = (
            [in_ref[:, place, part].reshape(size, DH) for part in parts] for place in range(4)
        )
        scores = [jnp.where(allowed, dot_nt(k, q), MASKED) for q, k in zip(qs, ks)]
        dprobs = [dot_nt(v, g) for g, v in zip(gs, vs)]
        raised = [
            jnp.exp2((x - jnp.max(x, axis=0, keepdims=True)) * SCALE_LOG2) for x in scores
        ]
        weights = [x * (1.0 / jnp.sum(x, axis=0, keepdims=True)) for x in raised]
        probs = [x.astype(BF16) for x in weights]
        deltas = [jnp.sum(w * dp, axis=0, keepdims=True) for w, dp in zip(weights, dprobs)]
        dscores = [
            (w * (dp - delta) * SCALE).astype(BF16)
            for w, dp, delta in zip(weights, dprobs, deltas)
        ]
        results = (
            [dot_tn(x, v).astype(BF16) for x, v in zip(probs, vs)],
            [dot_tn(x, k).astype(BF16) for x, k in zip(dscores, ks)],
            [dot_nn(x, q).astype(BF16) for x, q in zip(dscores, qs)],
            [dot_nn(x, g).astype(BF16) for x, g in zip(probs, gs)],
        )
        for place, result in enumerate(results):
            for part, value in zip(parts, result):
                out_ref[:, place, part] = value.reshape(frames, group, DH)

    block = (frames, 4, slots, rows, DH)
    return pl.pallas_call(
        kernel,
        out_shape=[jax.ShapeDtypeStruct(rows_in[0].shape, BF16)] * frames,
        in_specs=[pl.BlockSpec(memory_space=pltpu.SMEM)] * 4
        + [pl.BlockSpec(memory_space=pl.ANY)] * frames,
        out_specs=[pl.BlockSpec(memory_space=pl.ANY)] * frames,
        scratch_shapes=[
            pltpu.VMEM(block, BF16),
            pltpu.VMEM(block, BF16),
            pltpu.SemaphoreType.DMA((frames,)),
            pltpu.SemaphoreType.DMA((slots, frames)),
        ],
        compiler_params=whole_params(),
        cost_estimate=cost(1e10, 4 * frames * rows_in[0].size),
        name="temporal",
    )(kinds, first, frame, bands, *rows_in)


def spatial(kinds, first, frame, arrays, prior, heads):
    count = arrays[0].shape[0]
    slots = prior.shape[0]
    chunk = min(count, 128)

    def kernel(
        kind_ref, first_ref, frame_ref, q_ref, k_ref, v_ref, g_ref, prior_ref,
        out_ref, qgrad_ref, own_ref, stats_ref,
    ):
        has_prior = frame_ref[0] > 0
        k, v = k_ref[...], v_ref[...]
        k_prior, v_prior = prior_ref[0, 0], prior_ref[0, 1]
        own_ref[...] = jnp.zeros_like(own_ref)

        @pl.loop(0, count // chunk)
        def _(step):
            part = pl.ds(pl.multiple_of(step * chunk, chunk), chunk)
            q, g = q_ref[part], g_ref[part]
            own = dot_nt(k, q)
            before = jnp.where(has_prior, dot_nt(k_prior, q), MASKED)
            top = jnp.maximum(
                jnp.max(own, axis=0, keepdims=True), jnp.max(before, axis=0, keepdims=True)
            )
            own, before = (jnp.exp2((x - top) * SCALE_LOG2) for x in (own, before))
            total = jnp.sum(own, axis=0, keepdims=True) + jnp.sum(before, axis=0, keepdims=True)
            inverse = 1.0 / total
            own, before = own * inverse, before * inverse
            own_dp, before_dp = dot_nt(v, g), dot_nt(v_prior, g)
            delta = jnp.sum(own * own_dp, axis=0, keepdims=True) + jnp.sum(
                before * before_dp, axis=0, keepdims=True
            )
            own_prob, before_prob = own.astype(BF16), before.astype(BF16)
            own_ds = (own * (own_dp - delta) * SCALE).astype(BF16)
            before_ds = (before * (before_dp - delta) * SCALE).astype(BF16)
            out_ref[part] = (dot_tn(own_prob, v) + dot_tn(before_prob, v_prior)).astype(BF16)
            qgrad_ref[part] = (dot_tn(own_ds, k) + dot_tn(before_ds, k_prior)).astype(BF16)
            own_ref[0, 0] += dot_nn(own_ds, q)
            own_ref[0, 1] += dot_nn(own_prob, g)
            stats_ref[0, 0:1, part] = top * SCALE + jnp.log(total)
            stats_ref[0, 1:2, part] = delta

    columns = column_spec(count, heads, SPATIAL)
    pair = pl.BlockSpec((1, 2, count, DH), lambda i, *refs: (i, 0, 0, 0))
    whole = jax.ShapeDtypeStruct((count, heads * DH), BF16)
    return pl.pallas_call(
        kernel,
        out_shape=[
            whole,
            whole,
            jax.ShapeDtypeStruct(prior.shape, F32),
            jax.ShapeDtypeStruct((slots, 2, count), F32),
        ],
        grid_spec=pltpu.PrefetchScalarGridSpec(
            num_scalar_prefetch=3,
            grid=(slots,),
            in_specs=[columns] * 4 + [pair],
            out_specs=[
                columns, columns, pair, pl.BlockSpec((1, 2, count), lambda i, *refs: (i, 0, 0))
            ],
        ),
        compiler_params=params(60),
        cost_estimate=cost(2e11, 16 * slots * count * DH),
        name="spatial",
    )(kinds, first, frame, *arrays, prior)


def finish(kinds, first, frame, rows_in, filled, k, v, following, stats, own, heads):
    count = k.shape[0]
    frames = len(rows_in)
    slots = rows_in[0].shape[1] if frames else 0
    others = heads - slots
    chunk = min(count, 256)
    ins, scratch = [], []
    if slots:
        rows = rows_in[0].shape[2]
        ins += [*rows_in]
        scratch += [pltpu.VMEM((4, slots, frames, rows, DH), BF16)]
        scratch += [pltpu.SemaphoreType.DMA((frames,)), pltpu.SemaphoreType.DMA((4 * slots,))]
    if others:
        ins += [*filled, k, v, following, stats, own]
        scratch += [
            pltpu.VMEM((others, 2, count, DH), BF16),
            pltpu.VMEM((others, 2, count, DH), BF16),
            pltpu.VMEM((others, 2, count), F32),
            pltpu.VMEM((others, 2, count, DH), F32),
            pltpu.VMEM((others, 2, count, DH), BF16),
            pltpu.SemaphoreType.DMA((others, 5)),
            pltpu.SemaphoreType.DMA((others, 2)),
        ]

    def kernel(kind_ref, first_ref, frame_ref, *refs):
        in_refs, out_refs = refs[: len(ins)], refs[len(ins) : len(ins) + 4]
        temps = refs[len(ins) + 4 :]
        loads, stores = [], []
        if slots:
            stage, in_sems, out_sems = temps[:3]
            for ahead in range(frames):
                held = stage.at[:, :, lax.rem(frame_ref[0] + ahead, frames)]
                loads.append(pltpu.make_async_copy(in_refs[ahead], held, in_sems.at[ahead]))
            for slot in range(slots):
                cols = head_columns(kind_ref, first_ref, heads, TEMPORAL, slot)
                for place, out in enumerate(out_refs):
                    source = stage.at[place, slot].reshape(count, DH)
                    sem = out_sems.at[4 * slot + place]
                    stores.append(pltpu.make_async_copy(source, out.at[:, cols], sem))
        if others:
            k_in, v_in, next_in, stats_in, own_in = in_refs[-5:]
            kv_ref, next_ref, stats_ref, own_ref, made_ref, sems, made_sems = temps[-7:]

            def spatial_loads(slot):
                cols = head_columns(kind_ref, first_ref, heads, SPATIAL, slot)
                pairs = [
                    (k_in.at[:, cols], kv_ref.at[slot, 0]),
                    (v_in.at[:, cols], kv_ref.at[slot, 1]),
                    (next_in.at[slot], next_ref.at[slot]),
                    (stats_in.at[slot], stats_ref.at[slot]),
                    (own_in.at[slot], own_ref.at[slot]),
                ]
                return [
                    pltpu.make_async_copy(*pair, sems.at[slot, i]) for i, pair in enumerate(pairs)
                ]

            def spatial_stores(slot):
                cols = head_columns(kind_ref, first_ref, heads, SPATIAL, slot)
                return [
                    pltpu.make_async_copy(
                        made_ref.at[slot, i], out_refs[2 + i].at[:, cols], made_sems.at[slot, i]
                    )
                    for i in range(2)
                ]

            for slot in range(others):
                for copy in spatial_loads(slot):
                    copy.start()
        for copy in loads:
            copy.start()
        for copy in loads:
            copy.wait()
        for copy in stores:
            copy.start()
        if others:

            @pl.loop(0, others)
            def _(slot):
                for copy in spatial_loads(slot):
                    copy.wait()
                q, g = next_ref[slot, 0], next_ref[slot, 1]
                lse, delta = stats_ref[slot, 0:1] * math.log2(math.e), stats_ref[slot, 1:2]
                for start in range(0, count, chunk):
                    part = slice(start, start + chunk)
                    weight = jnp.exp2(dot_nt(kv_ref[slot, 0, part], q) * SCALE_LOG2 - lse)
                    slope = (weight * (dot_nt(kv_ref[slot, 1, part], g) - delta)).astype(BF16)
                    made_ref[slot, 0, part] = (
                        own_ref[slot, 0, part] + dot_nn(slope, q) * SCALE
                    ).astype(BF16)
                    made_ref[slot, 1, part] = (
                        own_ref[slot, 1, part] + dot_nn(weight.astype(BF16), g)
                    ).astype(BF16)
                for copy in spatial_stores(slot):
                    copy.start()

            for slot in range(others):
                for copy in spatial_stores(slot):
                    copy.wait()
        for copy in stores:
            copy.wait()

    place = 3 + frames
    return pl.pallas_call(
        kernel,
        out_shape=[jax.ShapeDtypeStruct((count, heads * DH), BF16)] * 4,
        in_specs=[pl.BlockSpec(memory_space=pltpu.SMEM)] * 3
        + [pl.BlockSpec(memory_space=pl.ANY)] * len(ins),
        out_specs=[pl.BlockSpec(memory_space=pl.ANY)] * 4,
        scratch_shapes=scratch,
        input_output_aliases={place: 0, place + 1: 1} if others else {},
        compiler_params=whole_params(),
        cost_estimate=cost(8 * others * count * count * DH, 16 * heads * count * DH),
        name="finish",
    )(kinds, first, frame, *ins)


def passed_along(array, axis, by):
    length = lax.axis_size(axis)
    pairs = [(i, i + by) for i in range(length) if 0 <= i + by < length]
    return lax.ppermute(array, axis, pairs)


def behind(arrays, *others):
    return lax.optimization_barrier((tuple(arrays), others))[0]


def passed_round(array, axis, by):
    length = lax.axis_size(axis)
    return lax.ppermute(array, axis, [(i, (i + by) % length) for i in range(length)])


def exchange(parts, way):
    frames = len(parts)
    moved = list(parts)
    for by in sorted(range(1, frames), key=lambda i: abs(2 * i - frames)):
        moved[by] = passed_round(parts[by], "ctx", way * by)
    return moved


def branch(slots, heads, kinds, bands, first, frame, q, k, v, g):
    frames, rows, width = q.shape
    count = frames * rows
    others = heads - slots
    flat = [x.reshape(count, width) for x in (q, k, v, g)]
    packed, returned = [], []
    filled = following = stats = own = None
    if slots > 0:
        packed = pack_temporal(kinds, first, frame, (q, k, v, g), slots, heads)
        results = temporal(kinds, first, frame, bands, exchange(packed, 1), heads)
        returned = exchange(results, -1)
    if others > 0:
        ahead, back = pack_spatial(kinds, first, (k, v, q, g), others, heads, packed[:1])
        arrived = [passed_along(ahead, "ctx", 1), passed_along(back, "ctx", -1)]
        if slots > 0:
            arrived = behind(arrived, results[0])
        prior, following = (x.reshape(others, 2, count, DH) for x in arrived)
        attended, qgrad, own, stats = spatial(kinds, first, frame, flat, prior, heads)
        stats = passed_along(stats, "ctx", -1)
        filled = (attended, qgrad)
    return finish(kinds, first, frame, returned, filled, *flat[1:3], following, stats, own, heads)


def body(queries, key_rows, value_rows, out_grad, head_kind, frame_band):
    frames = lax.axis_size("ctx")
    count = queries.shape[1]
    heads = queries.shape[2] // DH
    first = lax.axis_index("head").astype(jnp.int32) * heads
    frame = lax.axis_index("ctx").astype(jnp.int32)
    kinds = lax.dynamic_slice_in_dim(head_kind, first, heads)
    slots = jnp.sum((kinds == TEMPORAL).astype(jnp.int32))
    arrays = [
        x.reshape(frames, count // frames, heads * DH)
        for x in (queries, key_rows, value_rows, out_grad)
    ]
    outs = lax.switch(
        slots,
        [functools.partial(branch, n, heads) for n in range(heads + 1)],
        head_kind, frame_band, first.reshape(1), frame.reshape(1), *arrays,
    )
    return tuple(out.reshape(queries.shape) for out in outs)


def solution(mesh):
    rows = P("ctx", None, "head")
    return jax.shard_map(
        body,
        mesh=mesh,
        in_specs=(rows, rows, rows, rows, P(), P()),
        out_specs=(rows, rows, rows, rows),
        check_vma=False,
    )
```

```python
import functools
import math

import jax
import jax.numpy as jnp
from jax import lax
from jax.experimental import pallas as pl
from jax.experimental.pallas import tpu as pltpu
from jax.sharding import PartitionSpec as P

DH = 128
SCALE = DH ** (-0.5)
SPATIAL, TEMPORAL = 1, 0
MASKED = -1e30
SCALE_LOG2 = SCALE * math.log2(math.e)
F32 = jnp.float32
BF16 = jnp.bfloat16
MIB = 1024 * 1024


def head_at(kind_ref, first_ref, heads, kind, slot):
    found, seen = jnp.int32(0), jnp.int32(0)
    for head in range(heads):
        hit = kind_ref[first_ref[0] + head] == kind
        found = jnp.where(jnp.logical_and(hit, seen == slot), jnp.int32(head), found)
        seen = seen + hit.astype(jnp.int32)
    return found


def dot_nt(a, b):
    return lax.dot_general(a, b, (((1,), (1,)), ((), ())), preferred_element_type=F32)


def dot_nn(a, b):
    return lax.dot_general(a, b, (((1,), (0,)), ((), ())), preferred_element_type=F32)


def dot_tn(a, b):
    return lax.dot_general(a, b, (((0,), (0,)), ((), ())), preferred_element_type=F32)


def params(mib=32):
    return pltpu.CompilerParams(
        dimension_semantics=("arbitrary",), vmem_limit_bytes=mib * MIB
    )


def cost(flops, moved):
    return pl.CostEstimate(flops=int(flops), bytes_accessed=int(moved), transcendentals=0)


def column_spec(count, heads, kind):
    return pl.BlockSpec((count, DH), lambda i, *refs: (0, head_at(*refs[:2], heads, kind, i)))


def head_columns(kind_ref, first_ref, heads, kind, slot):
    return pl.ds(pl.multiple_of(head_at(kind_ref, first_ref, heads, kind, slot) * DH, DH), DH)


def staged_copies(triples, in_sems, out_sems):
    loads = [pltpu.make_async_copy(x, y, in_sems.at[i]) for i, (x, y, _) in enumerate(triples)]
    stores = [pltpu.make_async_copy(y, z, out_sems.at[i]) for i, (_, y, z) in enumerate(triples)]
    for load in loads:
        load.start()
    for load, store in zip(loads, stores):
        load.wait()
        store.start()
    for store in stores:
        store.wait()


def whole_params():
    return pltpu.CompilerParams(vmem_limit_bytes=62 * MIB)


def pack_spatial(kinds, first, arrays, slots, heads, after):
    frames, rows, _ = arrays[0].shape
    count = len(arrays)
    total = slots * count

    def kernel(kind_ref, first_ref, *refs):
        ins, outs = refs[:count], refs[-3 - count // 2 : -3]
        stage, in_sems, out_sems = refs[-3:]
        triples = []
        for slot in range(slots):
            cols = head_columns(kind_ref, first_ref, heads, SPATIAL, slot)
            for place, ref in enumerate(ins):
                target = outs[place // 2].at[slot, place % 2]
                triples.append((ref.at[:, :, cols], stage.at[slot, place], target))
        staged_copies(triples, in_sems, out_sems)

    return pl.pallas_call(
        kernel,
        out_shape=[jax.ShapeDtypeStruct((slots, 2, frames, rows, DH), BF16)] * (count // 2),
        in_specs=[pl.BlockSpec(memory_space=pltpu.SMEM)] * 2
        + [pl.BlockSpec(memory_space=pl.ANY)] * (count + len(after)),
        out_specs=[pl.BlockSpec(memory_space=pl.ANY)] * (count // 2),
        scratch_shapes=[
            pltpu.VMEM((slots, count, frames, rows, DH), BF16),
            pltpu.SemaphoreType.DMA((total,)),
            pltpu.SemaphoreType.DMA((total,)),
        ],
        compiler_params=whole_params(),
        cost_estimate=cost(0, 4 * total * frames * rows * DH),
        name="pack_spatial",
    )(kinds, first, *arrays, *after)


def pack_temporal(kinds, first, frame, arrays, slots, heads, after):
    frames, rows, _ = arrays[0].shape

    def kernel(kind_ref, first_ref, frame_ref, *refs):
        ins, outs, (stage, in_sems, out_sems) = refs[:4], refs[-3 - frames : -3], refs[-3:]
        loads = []
        for slot in range(slots):
            cols = head_columns(kind_ref, first_ref, heads, TEMPORAL, slot)
            for place, ref in enumerate(ins):
                sem = in_sems.at[4 * slot + place]
                loads.append(
                    pltpu.make_async_copy(ref.at[:, :, cols], stage.at[:, place, slot], sem)
                )
        stores = [
            pltpu.make_async_copy(
                stage.at[lax.rem(frame_ref[0] + ahead, frames)], out, out_sems.at[ahead]
            )
            for ahead, out in enumerate(outs)
        ]
        for group in (loads, stores):
            for copy in group:
                copy.start()
            for copy in group:
                copy.wait()

    return pl.pallas_call(
        kernel,
        out_shape=[jax.ShapeDtypeStruct((4, slots, rows, DH), BF16)] * frames,
        in_specs=[pl.BlockSpec(memory_space=pltpu.SMEM)] * 3
        + [pl.BlockSpec(memory_space=pl.ANY)] * (4 + len(after)),
        out_specs=[pl.BlockSpec(memory_space=pl.ANY)] * frames,
        scratch_shapes=[
            pltpu.VMEM((frames, 4, slots, rows, DH), BF16),
            pltpu.SemaphoreType.DMA((4 * slots,)),
            pltpu.SemaphoreType.DMA((frames,)),
        ],
        compiler_params=whole_params(),
        cost_estimate=cost(0, 16 * slots * frames * rows * DH),
        name="pack_temporal",
    )(kinds, first, frame, *arrays, *after)


def temporal(kinds, first, frame, bands, rows_in, heads):
    frames = len(rows_in)
    _, slots, rows, _ = rows_in[0].shape
    group = 16
    size = frames * group

    def kernel(kind_ref, first_ref, frame_ref, band_ref, *refs):
        ins, outs, (held, made, in_sems, out_sems) = refs[:frames], refs[frames:-4], refs[-4:]

        def store(slot):
            return [
                pltpu.make_async_copy(
                    made.at[place, :, slot], out.at[:, slot], out_sems.at[slot, place]
                )
                for place, out in enumerate(outs)
            ]

        loads = [
            pltpu.make_async_copy(ref, held.at[place], in_sems.at[place])
            for place, ref in enumerate(ins)
        ]
        for copy in loads:
            copy.start()
        for copy in loads:
            copy.wait()

        @pl.loop(0, slots)
        def _(slot):
            one_head(
                kind_ref, first_ref, frame_ref, band_ref, slot,
                held.at[:, :, slot], made.at[:, :, slot],
            )
            for copy in store(slot):
                copy.start()

        for slot in range(slots):
            for copy in store(slot):
                copy.wait()

    def one_head(kind_ref, first_ref, frame_ref, band_ref, slot, in_ref, out_ref):
        band = band_ref[first_ref[0] + head_at(kind_ref, first_ref, heads, TEMPORAL, slot)]
        row = lax.broadcasted_iota(jnp.int32, (size, size), 0)
        col = lax.broadcasted_iota(jnp.int32, (size, size), 1)
        same = lax.rem(row, group) == lax.rem(col, group)
        frame_at = lambda place: lax.rem(frame_ref[0] + frames - place, frames)
        distance = jnp.abs(frame_at(lax.div(row, group)) - frame_at(lax.div(col, group)))
        near = distance <= band
        allowed = jnp.logical_and(same, near)
        parts = [slice(start, start + group) for start in range(0, rows, group)]
        qs, ks, vs, gs = (
            [in_ref[:, place, part].reshape(size, DH) for part in parts] for place in range(4)
        )
        scores = [jnp.where(allowed, dot_nt(k, q), MASKED) for q, k in zip(qs, ks)]
        dprobs = [dot_nt(v, g) for g, v in zip(gs, vs)]
        raised = [
            jnp.exp2((x - jnp.max(x, axis=0, keepdims=True)) * SCALE_LOG2) for x in scores
        ]
        weights = [x * (1.0 / jnp.sum(x, axis=0, keepdims=True)) for x in raised]
        probs = [x.astype(BF16) for x in weights]
        deltas = [jnp.sum(w * dp, axis=0, keepdims=True) for w, dp in zip(weights, dprobs)]
        dscores = [
            (w * (dp - delta) * SCALE).astype(BF16)
            for w, dp, delta in zip(weights, dprobs, deltas)
        ]
        results = (
            [dot_tn(x, v).astype(BF16) for x, v in zip(probs, vs)],
            [dot_tn(x, k).astype(BF16) for x, k in zip(dscores, ks)],
            [dot_nn(x, q).astype(BF16) for x, q in zip(dscores, qs)],
            [dot_nn(x, g).astype(BF16) for x, g in zip(probs, gs)],
        )
        for place, result in enumerate(results):
            for part, value in zip(parts, result):
                out_ref[:, place, part] = value.reshape(frames, group, DH)

    block = (frames, 4, slots, rows, DH)
    return pl.pallas_call(
        kernel,
        out_shape=[jax.ShapeDtypeStruct(rows_in[0].shape, BF16)] * frames,
        in_specs=[pl.BlockSpec(memory_space=pltpu.SMEM)] * 4
        + [pl.BlockSpec(memory_space=pl.ANY)] * frames,
        out_specs=[pl.BlockSpec(memory_space=pl.ANY)] * frames,
        scratch_shapes=[
            pltpu.VMEM(block, BF16),
            pltpu.VMEM(block, BF16),
            pltpu.SemaphoreType.DMA((frames,)),
            pltpu.SemaphoreType.DMA((slots, frames)),
        ],
        compiler_params=whole_params(),
        cost_estimate=cost(1e10, 4 * frames * rows_in[0].size),
        name="temporal",
    )(kinds, first, frame, bands, *rows_in)


def spatial(kinds, first, frame, arrays, prior, heads):
    count = arrays[0].shape[0]
    slots = prior.shape[0]
    chunk = min(count, 128)

    def kernel(
        kind_ref, first_ref, frame_ref, q_ref, k_ref, v_ref, g_ref, prior_ref,
        out_ref, qgrad_ref, own_ref, stats_ref,
    ):
        has_prior = frame_ref[0] > 0
        k, v = k_ref[...], v_ref[...]
        k_prior, v_prior = prior_ref[0, 0], prior_ref[0, 1]
        own_ref[...] = jnp.zeros_like(own_ref)

        @pl.loop(0, count // chunk)
        def _(step):
            part = pl.ds(pl.multiple_of(step * chunk, chunk), chunk)
            q, g = q_ref[part], g_ref[part]
            own = dot_nt(k, q)
            before = jnp.where(has_prior, dot_nt(k_prior, q), MASKED)
            top = jnp.maximum(
                jnp.max(own, axis=0, keepdims=True), jnp.max(before, axis=0, keepdims=True)
            )
            own, before = (jnp.exp2((x - top) * SCALE_LOG2) for x in (own, before))
            total = jnp.sum(own, axis=0, keepdims=True) + jnp.sum(before, axis=0, keepdims=True)
            inverse = 1.0 / total
            own, before = own * inverse, before * inverse
            own_dp, before_dp = dot_nt(v, g), dot_nt(v_prior, g)
            delta = jnp.sum(own * own_dp, axis=0, keepdims=True) + jnp.sum(
                before * before_dp, axis=0, keepdims=True
            )
            own_prob, before_prob = own.astype(BF16), before.astype(BF16)
            own_ds = (own * (own_dp - delta) * SCALE).astype(BF16)
            before_ds = (before * (before_dp - delta) * SCALE).astype(BF16)
            out_ref[part] = (dot_tn(own_prob, v) + dot_tn(before_prob, v_prior)).astype(BF16)
            qgrad_ref[part] = (dot_tn(own_ds, k) + dot_tn(before_ds, k_prior)).astype(BF16)
            own_ref[0, 0] += dot_nn(own_ds, q)
            own_ref[0, 1] += dot_nn(own_prob, g)
            stats_ref[0, 0:1, part] = top * SCALE + jnp.log(total)
            stats_ref[0, 1:2, part] = delta

    columns = column_spec(count, heads, SPATIAL)
    pair = pl.BlockSpec((1, 2, count, DH), lambda i, *refs: (i, 0, 0, 0))
    whole = jax.ShapeDtypeStruct((count, heads * DH), BF16)
    return pl.pallas_call(
        kernel,
        out_shape=[
            whole,
            whole,
            jax.ShapeDtypeStruct(prior.shape, F32),
            jax.ShapeDtypeStruct((slots, 2, count), F32),
        ],
        grid_spec=pltpu.PrefetchScalarGridSpec(
            num_scalar_prefetch=3,
            grid=(slots,),
            in_specs=[columns] * 4 + [pair],
            out_specs=[
                columns, columns, pair, pl.BlockSpec((1, 2, count), lambda i, *refs: (i, 0, 0))
            ],
        ),
        compiler_params=params(60),
        cost_estimate=cost(2e11, 16 * slots * count * DH),
        name="spatial",
    )(kinds, first, frame, *arrays, prior)


def finish(kinds, first, frame, rows_in, filled, k, v, following, stats, own, heads):
    count = k.shape[0]
    frames = len(rows_in)
    slots = rows_in[0].shape[1] if frames else 0
    others = heads - slots
    chunk = min(count, 256)
    ins, scratch = [], []
    if slots:
        rows = rows_in[0].shape[2]
        ins += [*rows_in]
        scratch += [pltpu.VMEM((4, slots, frames, rows, DH), BF16)]
        scratch += [pltpu.SemaphoreType.DMA((frames,)), pltpu.SemaphoreType.DMA((4 * slots,))]
    if others:
        ins += [*filled, k, v, following, stats, own]
        scratch += [
            pltpu.VMEM((others, 2, count, DH), BF16),
            pltpu.VMEM((others, 2, count, DH), BF16),
            pltpu.VMEM((others, 2, count), F32),
            pltpu.VMEM((others, 2, count, DH), F32),
            pltpu.VMEM((others, 2, count, DH), BF16),
            pltpu.SemaphoreType.DMA((others, 5)),
            pltpu.SemaphoreType.DMA((others, 2)),
        ]

    def kernel(kind_ref, first_ref, frame_ref, *refs):
        in_refs, out_refs = refs[: len(ins)], refs[len(ins) : len(ins) + 4]
        temps = refs[len(ins) + 4 :]
        loads, stores = [], []
        if slots:
            stage, in_sems, out_sems = temps[:3]
            for ahead in range(frames):
                held = stage.at[:, :, lax.rem(frame_ref[0] + ahead, frames)]
                loads.append(pltpu.make_async_copy(in_refs[ahead], held, in_sems.at[ahead]))
            for slot in range(slots):
                cols = head_columns(kind_ref, first_ref, heads, TEMPORAL, slot)
                for place, out in enumerate(out_refs):
                    source = stage.at[place, slot].reshape(count, DH)
                    sem = out_sems.at[4 * slot + place]
                    stores.append(pltpu.make_async_copy(source, out.at[:, cols], sem))
        if others:
            k_in, v_in, next_in, stats_in, own_in = in_refs[-5:]
            kv_ref, next_ref, stats_ref, own_ref, made_ref, sems, made_sems = temps[-7:]

            def spatial_loads(slot):
                cols = head_columns(kind_ref, first_ref, heads, SPATIAL, slot)
                pairs = [
                    (k_in.at[:, cols], kv_ref.at[slot, 0]),
                    (v_in.at[:, cols], kv_ref.at[slot, 1]),
                    (next_in.at[slot], next_ref.at[slot]),
                    (stats_in.at[slot], stats_ref.at[slot]),
                    (own_in.at[slot], own_ref.at[slot]),
                ]
                return [
                    pltpu.make_async_copy(*pair, sems.at[slot, i]) for i, pair in enumerate(pairs)
                ]

            def spatial_stores(slot):
                cols = head_columns(kind_ref, first_ref, heads, SPATIAL, slot)
                return [
                    pltpu.make_async_copy(
                        made_ref.at[slot, i], out_refs[2 + i].at[:, cols], made_sems.at[slot, i]
                    )
                    for i in range(2)
                ]

            for slot in range(others):
                for copy in spatial_loads(slot):
                    copy.start()
        for copy in loads:
            copy.start()
        for copy in loads:
            copy.wait()
        for copy in stores:
            copy.start()
        if others:

            @pl.loop(0, others)
            def _(slot):
                for copy in spatial_loads(slot):
                    copy.wait()
                q, g = next_ref[slot, 0], next_ref[slot, 1]
                lse, delta = stats_ref[slot, 0:1] * math.log2(math.e), stats_ref[slot, 1:2]
                for start in range(0, count, chunk):
                    part = slice(start, start + chunk)
                    weight = jnp.exp2(dot_nt(kv_ref[slot, 0, part], q) * SCALE_LOG2 - lse)
                    slope = (weight * (dot_nt(kv_ref[slot, 1, part], g) - delta)).astype(BF16)
                    made_ref[slot, 0, part] = (
                        own_ref[slot, 0, part] + dot_nn(slope, q) * SCALE
                    ).astype(BF16)
                    made_ref[slot, 1, part] = (
                        own_ref[slot, 1, part] + dot_nn(weight.astype(BF16), g)
                    ).astype(BF16)
                for copy in spatial_stores(slot):
                    copy.start()

            for slot in range(others):
                for copy in spatial_stores(slot):
                    copy.wait()
        for copy in stores:
            copy.wait()

    place = 3 + frames
    return pl.pallas_call(
        kernel,
        out_shape=[jax.ShapeDtypeStruct((count, heads * DH), BF16)] * 4,
        in_specs=[pl.BlockSpec(memory_space=pltpu.SMEM)] * 3
        + [pl.BlockSpec(memory_space=pl.ANY)] * len(ins),
        out_specs=[pl.BlockSpec(memory_space=pl.ANY)] * 4,
        scratch_shapes=scratch,
        input_output_aliases={place: 0, place + 1: 1} if others else {},
        compiler_params=whole_params(),
        cost_estimate=cost(8 * others * count * count * DH, 16 * heads * count * DH),
        name="finish",
    )(kinds, first, frame, *ins)


def passed_along(array, axis, by):
    length = lax.axis_size(axis)
    pairs = [(i, i + by) for i in range(length) if 0 <= i + by < length]
    return lax.ppermute(array, axis, pairs)


def behind(arrays, *others):
    return lax.optimization_barrier((tuple(arrays), others))[0]


def passed_round(array, axis, by):
    length = lax.axis_size(axis)
    return lax.ppermute(array, axis, [(i, (i + by) % length) for i in range(length)])


def exchange(parts, way):
    frames = len(parts)
    moved = list(parts)
    for by in sorted(range(1, frames), key=lambda i: abs(2 * i - frames)):
        moved[by] = passed_round(parts[by], "ctx", way * by)
    return moved


def branch(slots, heads, kinds, bands, first, frame, q, k, v, g):
    frames, rows, width = q.shape
    count = frames * rows
    others = heads - slots
    flat = [x.reshape(count, width) for x in (q, k, v, g)]
    sent, returned = [], []
    filled = following = stats = own = None
    if others > 0:
        sent = pack_spatial(kinds, first, (k, v, q, g), others, heads, [])
        arrived = [passed_along(sent[0], "ctx", 1), passed_along(sent[1], "ctx", -1)]
        prior, following = (x.reshape(others, 2, count, DH) for x in arrived)
        attended, qgrad, own, stats = spatial(kinds, first, frame, flat, prior, heads)
        stats = passed_along(stats, "ctx", -1)
        filled = (attended, qgrad)
    if slots > 0:
        packed = pack_temporal(kinds, first, frame, (q, k, v, g), slots, heads, sent[:1])
        rows_in = exchange(packed, 1)
        if others > 0:
            rows_in = behind(rows_in, own)
        results = temporal(kinds, first, frame, bands, rows_in, heads)
        returned = exchange(results, -1)
    return finish(kinds, first, frame, returned, filled, *flat[1:3], following, stats, own, heads)


def body(queries, key_rows, value_rows, out_grad, head_kind, frame_band):
    frames = lax.axis_size("ctx")
    count = queries.shape[1]
    heads = queries.shape[2] // DH
    first = lax.axis_index("head").astype(jnp.int32) * heads
    frame = lax.axis_index("ctx").astype(jnp.int32)
    kinds = lax.dynamic_slice_in_dim(head_kind, first, heads)
    slots = jnp.sum((kinds == TEMPORAL).astype(jnp.int32))
    arrays = [
        x.reshape(frames, count // frames, heads * DH)
        for x in (queries, key_rows, value_rows, out_grad)
    ]
    outs = lax.switch(
        slots,
        [functools.partial(branch, n, heads) for n in range(heads + 1)],
        head_kind, frame_band, first.reshape(1), frame.reshape(1), *arrays,
    )
    return tuple(out.reshape(queries.shape) for out in outs)


def solution(mesh):
    rows = P("ctx", None, "head")
    return jax.shard_map(
        body,
        mesh=mesh,
        in_specs=(rows, rows, rows, rows, P(), P()),
        out_specs=(rows, rows, rows, rows),
        check_vma=False,
    )
```

```python
import functools
import math

import jax
import jax.numpy as jnp
from jax import lax
from jax.experimental import pallas as pl
from jax.experimental.pallas import tpu as pltpu
from jax.sharding import PartitionSpec as P

DH = 128
SCALE = DH ** (-0.5)
SPATIAL, TEMPORAL = 1, 0
MASKED = -1e30
SCALE_LOG2 = SCALE * math.log2(math.e)
F32 = jnp.float32
BF16 = jnp.bfloat16
MIB = 1024 * 1024


def head_at(kind_ref, first_ref, heads, kind, slot):
    found, seen = jnp.int32(0), jnp.int32(0)
    for head in range(heads):
        hit = kind_ref[first_ref[0] + head] == kind
        found = jnp.where(jnp.logical_and(hit, seen == slot), jnp.int32(head), found)
        seen = seen + hit.astype(jnp.int32)
    return found


def dot_nt(a, b):
    return lax.dot_general(a, b, (((1,), (1,)), ((), ())), preferred_element_type=F32)


def dot_nn(a, b):
    return lax.dot_general(a, b, (((1,), (0,)), ((), ())), preferred_element_type=F32)


def dot_tn(a, b):
    return lax.dot_general(a, b, (((0,), (0,)), ((), ())), preferred_element_type=F32)


def params(mib=32):
    return pltpu.CompilerParams(
        dimension_semantics=("arbitrary",), vmem_limit_bytes=mib * MIB
    )


def cost(flops, moved):
    return pl.CostEstimate(flops=int(flops), bytes_accessed=int(moved), transcendentals=0)


def column_spec(count, heads, kind):
    return pl.BlockSpec((count, DH), lambda i, *refs: (0, head_at(*refs[:2], heads, kind, i)))


def head_columns(kind_ref, first_ref, heads, kind, slot):
    return pl.ds(pl.multiple_of(head_at(kind_ref, first_ref, heads, kind, slot) * DH, DH), DH)


def staged_copies(triples, in_sems, out_sems):
    loads = [pltpu.make_async_copy(x, y, in_sems.at[i]) for i, (x, y, _) in enumerate(triples)]
    stores = [pltpu.make_async_copy(y, z, out_sems.at[i]) for i, (_, y, z) in enumerate(triples)]
    for load in loads:
        load.start()
    for load, store in zip(loads, stores):
        load.wait()
        store.start()
    for store in stores:
        store.wait()


def whole_params():
    return pltpu.CompilerParams(vmem_limit_bytes=62 * MIB)


def pack_spatial(kinds, first, arrays, slots, heads, after):
    frames, rows, _ = arrays[0].shape
    count = len(arrays)
    total = slots * count

    def kernel(kind_ref, first_ref, *refs):
        ins, outs = refs[:count], refs[-3 - count : -3]
        stage, in_sems, out_sems = refs[-3:]
        triples = []
        for slot in range(slots):
            cols = head_columns(kind_ref, first_ref, heads, SPATIAL, slot)
            for place, ref in enumerate(ins):
                target = outs[place].at[slot]
                triples.append((ref.at[:, :, cols], stage.at[slot, place], target))
        staged_copies(triples, in_sems, out_sems)

    return pl.pallas_call(
        kernel,
        out_shape=[jax.ShapeDtypeStruct((slots, frames, rows, DH), BF16)] * count,
        in_specs=[pl.BlockSpec(memory_space=pltpu.SMEM)] * 2
        + [pl.BlockSpec(memory_space=pl.ANY)] * (count + len(after)),
        out_specs=[pl.BlockSpec(memory_space=pl.ANY)] * count,
        scratch_shapes=[
            pltpu.VMEM((slots, count, frames, rows, DH), BF16),
            pltpu.SemaphoreType.DMA((total,)),
            pltpu.SemaphoreType.DMA((total,)),
        ],
        compiler_params=whole_params(),
        cost_estimate=cost(0, 4 * total * frames * rows * DH),
        name="pack_spatial",
    )(kinds, first, *arrays, *after)


def pack_temporal(kinds, first, arrays, slots, heads):
    frames, rows, _ = arrays[0].shape
    total = 4 * slots

    def kernel(kind_ref, first_ref, *refs):
        ins, (out, stage, in_sems, out_sems) = refs[:4], refs[4:]
        triples = []
        for slot in range(slots):
            cols = head_columns(kind_ref, first_ref, heads, TEMPORAL, slot)
            for place, ref in enumerate(ins):
                triples.append(
                    (ref.at[:, :, cols], stage.at[slot, place], out.at[:, place, slot])
                )
        staged_copies(triples, in_sems, out_sems)

    return pl.pallas_call(
        kernel,
        out_shape=jax.ShapeDtypeStruct((frames, 4, slots, rows, DH), BF16),
        in_specs=[pl.BlockSpec(memory_space=pltpu.SMEM)] * 2
        + [pl.BlockSpec(memory_space=pl.ANY)] * 4,
        out_specs=pl.BlockSpec(memory_space=pl.ANY),
        scratch_shapes=[
            pltpu.VMEM((slots, 4, frames, rows, DH), BF16),
            pltpu.SemaphoreType.DMA((total,)),
            pltpu.SemaphoreType.DMA((total,)),
        ],
        compiler_params=whole_params(),
        cost_estimate=cost(0, 4 * total * frames * rows * DH),
        name="pack_temporal",
    )(kinds, first, *arrays)


def temporal(kinds, first, bands, rows_in, heads):
    frames, _, slots, rows, _ = rows_in.shape
    group = 16
    size = frames * group

    def kernel(kind_ref, first_ref, band_ref, rows_ref, result_ref, held, made, in_sems, out_sems):
        def load(slot):
            return pltpu.make_async_copy(rows_ref.at[:, :, slot], held.at[slot], in_sems.at[slot])

        def store(slot):
            return pltpu.make_async_copy(
                made.at[slot], result_ref.at[:, :, slot], out_sems.at[slot]
            )

        for slot in range(slots):
            load(slot).start()

        @pl.loop(0, slots)
        def _(slot):
            load(slot).wait()
            one_head(kind_ref, first_ref, band_ref, slot, held.at[slot], made.at[slot])
            store(slot).start()

        for slot in range(slots):
            store(slot).wait()

    def one_head(kind_ref, first_ref, band_ref, slot, in_ref, out_ref):
        band = band_ref[first_ref[0] + head_at(kind_ref, first_ref, heads, TEMPORAL, slot)]
        row = lax.broadcasted_iota(jnp.int32, (size, size), 0)
        col = lax.broadcasted_iota(jnp.int32, (size, size), 1)
        same = lax.rem(row, group) == lax.rem(col, group)
        near = jnp.abs(lax.div(row, group) - lax.div(col, group)) <= band
        allowed = jnp.logical_and(same, near)
        parts = [slice(start, start + group) for start in range(0, rows, group)]
        qs, ks, vs, gs = (
            [in_ref[:, place, part].reshape(size, DH) for part in parts] for place in range(4)
        )
        scores = [jnp.where(allowed, dot_nt(k, q), MASKED) for q, k in zip(qs, ks)]
        dprobs = [dot_nt(v, g) for g, v in zip(gs, vs)]
        raised = [
            jnp.exp2((x - jnp.max(x, axis=0, keepdims=True)) * SCALE_LOG2) for x in scores
        ]
        weights = [x * (1.0 / jnp.sum(x, axis=0, keepdims=True)) for x in raised]
        probs = [x.astype(BF16) for x in weights]
        deltas = [jnp.sum(w * dp, axis=0, keepdims=True) for w, dp in zip(weights, dprobs)]
        dscores = [
            (w * (dp - delta) * SCALE).astype(BF16)
            for w, dp, delta in zip(weights, dprobs, deltas)
        ]
        results = (
            [dot_tn(x, v).astype(BF16) for x, v in zip(probs, vs)],
            [dot_tn(x, k).astype(BF16) for x, k in zip(dscores, ks)],
            [dot_nn(x, q).astype(BF16) for x, q in zip(dscores, qs)],
            [dot_nn(x, g).astype(BF16) for x, g in zip(probs, gs)],
        )
        for place, result in enumerate(results):
            for part, value in zip(parts, result):
                out_ref[:, place, part] = value.reshape(frames, group, DH)

    block = (slots, frames, 4, rows, DH)
    return pl.pallas_call(
        kernel,
        out_shape=jax.ShapeDtypeStruct(rows_in.shape, BF16),
        in_specs=[pl.BlockSpec(memory_space=pltpu.SMEM)] * 3
        + [pl.BlockSpec(memory_space=pl.ANY)],
        out_specs=pl.BlockSpec(memory_space=pl.ANY),
        scratch_shapes=[
            pltpu.VMEM(block, BF16),
            pltpu.VMEM(block, BF16),
            pltpu.SemaphoreType.DMA((slots,)),
            pltpu.SemaphoreType.DMA((slots,)),
        ],
        compiler_params=whole_params(),
        cost_estimate=cost(1e10, 4 * rows_in.size),
        name="temporal",
    )(kinds, first, bands, rows_in)


def spatial(kinds, first, frame, arrays, prior, heads):
    count = arrays[0].shape[0]
    slots = prior.shape[0]
    chunk = min(count, 128)

    def kernel(
        kind_ref, first_ref, frame_ref, q_ref, k_ref, v_ref, g_ref, prior_ref,
        out_ref, qgrad_ref, own_ref, stats_ref,
    ):
        has_prior = frame_ref[0] > 0
        k, v = k_ref[...], v_ref[...]
        k_prior, v_prior = prior_ref[0, 0], prior_ref[0, 1]
        own_ref[...] = jnp.zeros_like(own_ref)

        @pl.loop(0, count // chunk)
        def _(step):
            part = pl.ds(pl.multiple_of(step * chunk, chunk), chunk)
            q, g = q_ref[part], g_ref[part]
            own = dot_nt(k, q)
            before = jnp.where(has_prior, dot_nt(k_prior, q), MASKED)
            top = jnp.maximum(
                jnp.max(own, axis=0, keepdims=True), jnp.max(before, axis=0, keepdims=True)
            )
            own, before = (jnp.exp2((x - top) * SCALE_LOG2) for x in (own, before))
            total = jnp.sum(own, axis=0, keepdims=True) + jnp.sum(before, axis=0, keepdims=True)
            inverse = 1.0 / total
            own, before = own * inverse, before * inverse
            own_dp, before_dp = dot_nt(v, g), dot_nt(v_prior, g)
            delta = jnp.sum(own * own_dp, axis=0, keepdims=True) + jnp.sum(
                before * before_dp, axis=0, keepdims=True
            )
            own_prob, before_prob = own.astype(BF16), before.astype(BF16)
            own_ds = (own * (own_dp - delta) * SCALE).astype(BF16)
            before_ds = (before * (before_dp - delta) * SCALE).astype(BF16)
            out_ref[part] = (dot_tn(own_prob, v) + dot_tn(before_prob, v_prior)).astype(BF16)
            qgrad_ref[part] = (dot_tn(own_ds, k) + dot_tn(before_ds, k_prior)).astype(BF16)
            own_ref[0, 0] += dot_nn(own_ds, q)
            own_ref[0, 1] += dot_nn(own_prob, g)
            stats_ref[0, 0:1, part] = top * SCALE + jnp.log(total)
            stats_ref[0, 1:2, part] = delta

    columns = column_spec(count, heads, SPATIAL)
    pair = pl.BlockSpec((1, 2, count, DH), lambda i, *refs: (i, 0, 0, 0))
    whole = jax.ShapeDtypeStruct((count, heads * DH), BF16)
    return pl.pallas_call(
        kernel,
        out_shape=[
            whole,
            whole,
            jax.ShapeDtypeStruct(prior.shape, F32),
            jax.ShapeDtypeStruct((slots, 2, count), F32),
        ],
        grid_spec=pltpu.PrefetchScalarGridSpec(
            num_scalar_prefetch=3,
            grid=(slots,),
            in_specs=[columns] * 4 + [pair],
            out_specs=[
                columns, columns, pair, pl.BlockSpec((1, 2, count), lambda i, *refs: (i, 0, 0))
            ],
        ),
        compiler_params=params(24),
        cost_estimate=cost(2e11, 16 * slots * count * DH),
        name="spatial",
    )(kinds, first, frame, *arrays, prior)


def finish(kinds, first, rows_in, filled, k, v, following, stats, own, heads):
    count = k.shape[0]
    slots = 0 if rows_in is None else rows_in.shape[2]
    others = heads - slots
    chunk = min(count, 256)
    ins, scratch = [], []
    if slots:
        frames, _, _, rows, _ = rows_in.shape
        ins += [rows_in]
        scratch += [pltpu.VMEM((slots, 4, frames, rows, DH), BF16)]
        scratch += [pltpu.SemaphoreType.DMA((4 * slots,))] * 2
    if others:
        ins += [*filled, k, v, following, stats, own]
        scratch += [
            pltpu.VMEM((others, 2, count, DH), BF16),
            pltpu.VMEM((others, 2, count, DH), BF16),
            pltpu.VMEM((others, 2, count), F32),
            pltpu.VMEM((others, 2, count, DH), F32),
            pltpu.VMEM((others, 2, count, DH), BF16),
            pltpu.SemaphoreType.DMA((others, 5)),
            pltpu.SemaphoreType.DMA((others, 2)),
        ]

    def kernel(kind_ref, first_ref, *refs):
        in_refs, out_refs = refs[: len(ins)], refs[len(ins) : len(ins) + 4]
        temps = refs[len(ins) + 4 :]
        loads, stores = [], []
        if slots:
            stage, in_sems, out_sems = temps[:3]
            for slot in range(slots):
                cols = head_columns(kind_ref, first_ref, heads, TEMPORAL, slot)
                for place, out in enumerate(out_refs):
                    at, held = 4 * slot + place, stage.at[slot, place]
                    source = in_refs[0].at[:, place, slot]
                    target = out.at[:, cols]
                    loads.append(pltpu.make_async_copy(source, held, in_sems.at[at]))
                    stores.append(
                        pltpu.make_async_copy(held.reshape(count, DH), target, out_sems.at[at])
                    )
        if others:
            k_in, v_in, next_in, stats_in, own_in = in_refs[-5:]
            kv_ref, next_ref, stats_ref, own_ref, made_ref, sems, made_sems = temps[-7:]

            def spatial_loads(slot):
                cols = head_columns(kind_ref, first_ref, heads, SPATIAL, slot)
                pairs = [
                    (k_in.at[:, cols], kv_ref.at[slot, 0]),
                    (v_in.at[:, cols], kv_ref.at[slot, 1]),
                    (next_in.at[slot], next_ref.at[slot]),
                    (stats_in.at[slot], stats_ref.at[slot]),
                    (own_in.at[slot], own_ref.at[slot]),
                ]
                return [
                    pltpu.make_async_copy(*pair, sems.at[slot, i]) for i, pair in enumerate(pairs)
                ]

            def spatial_stores(slot):
                cols = head_columns(kind_ref, first_ref, heads, SPATIAL, slot)
                return [
                    pltpu.make_async_copy(
                        made_ref.at[slot, i], out_refs[2 + i].at[:, cols], made_sems.at[slot, i]
                    )
                    for i in range(2)
                ]

            for slot in range(others):
                for copy in spatial_loads(slot):
                    copy.start()
        for copy in loads:
            copy.start()
        for load, store in zip(loads, stores):
            load.wait()
            store.start()
        if others:

            @pl.loop(0, others)
            def _(slot):
                for copy in spatial_loads(slot):
                    copy.wait()
                q, g = next_ref[slot, 0], next_ref[slot, 1]
                lse, delta = stats_ref[slot, 0:1] * math.log2(math.e), stats_ref[slot, 1:2]
                for start in range(0, count, chunk):
                    part = slice(start, start + chunk)
                    weight = jnp.exp2(dot_nt(kv_ref[slot, 0, part], q) * SCALE_LOG2 - lse)
                    slope = (weight * (dot_nt(kv_ref[slot, 1, part], g) - delta)).astype(BF16)
                    made_ref[slot, 0, part] = (
                        own_ref[slot, 0, part] + dot_nn(slope, q) * SCALE
                    ).astype(BF16)
                    made_ref[slot, 1, part] = (
                        own_ref[slot, 1, part] + dot_nn(weight.astype(BF16), g)
                    ).astype(BF16)
                for copy in spatial_stores(slot):
                    copy.start()

            for slot in range(others):
                for copy in spatial_stores(slot):
                    copy.wait()
        for copy in stores:
            copy.wait()

    place = 2 + (1 if slots else 0)
    return pl.pallas_call(
        kernel,
        out_shape=[jax.ShapeDtypeStruct((count, heads * DH), BF16)] * 4,
        in_specs=[pl.BlockSpec(memory_space=pltpu.SMEM)] * 2
        + [pl.BlockSpec(memory_space=pl.ANY)] * len(ins),
        out_specs=[pl.BlockSpec(memory_space=pl.ANY)] * 4,
        scratch_shapes=scratch,
        input_output_aliases={place: 0, place + 1: 1} if others else {},
        compiler_params=pltpu.CompilerParams(vmem_limit_bytes=24 * MIB),
        cost_estimate=cost(8 * others * count * count * DH, 16 * heads * count * DH),
        name="finish",
    )(kinds, first, *ins)


def passed_along(array, axis, by):
    length = lax.axis_size(axis)
    pairs = [(i, i + by) for i in range(length) if 0 <= i + by < length]
    return lax.ppermute(array, axis, pairs)


def behind(arrays, *others):
    return lax.optimization_barrier((tuple(arrays), others))[0]


def swapped(array, axis):
    return lax.ppermute(array, axis, [(i, i ^ 1) for i in range(lax.axis_size(axis))])


def crossed(array, axis, by):
    length = lax.axis_size(axis)
    pairs = [(i, i + by * (-1) ** i) for i in range(length)]
    return lax.ppermute(array, axis, [pair for pair in pairs if 0 <= pair[1] < length])


def neighbour_rows(sent, frame, results):
    k, v, q, g = sent
    even = lax.rem(frame[0], 2) == 0
    near = swapped(jnp.where(even, jnp.stack((k, v, q), 1), jnp.stack((q, g, k), 1)), "ctx")
    second = swapped(crossed(jnp.where(even, g, v), "ctx", -2), "ctx")
    first = crossed(near[:, 2], "ctx", 2)
    if results is not None:
        near, first, second = behind((near, first, second), results)
    far, pair = jnp.stack((first, second), 1), near[:, :2]
    return jnp.where(even, far, pair), jnp.where(even, pair, far)


def branch(slots, heads, kinds, bands, first, frame, q, k, v, g):
    frames, rows, width = q.shape
    count = frames * rows
    others = heads - slots
    exchange = functools.partial(
        lax.all_to_all, axis_name="ctx", split_axis=0, concat_axis=0, tiled=True
    )
    flat = [x.reshape(count, width) for x in (q, k, v, g)]
    packed = []
    results = returned = filled = following = stats = own = None
    if slots > 0:
        packed = [pack_temporal(kinds, first, (q, k, v, g), slots, heads)]
        framed = exchange(*packed)
        results = temporal(kinds, first, bands, framed, heads)
        returned = exchange(results)
    if others > 0:
        sent = pack_spatial(kinds, first, (k, v, q, g), others, heads, packed)
        arrived = neighbour_rows(sent, frame, results)
        prior, following = (x.reshape(others, 2, count, DH) for x in arrived)
        attended, qgrad, own, stats = spatial(kinds, first, frame, flat, prior, heads)
        stats = passed_along(stats, "ctx", -1)
        filled = (attended, qgrad)
    return finish(kinds, first, returned, filled, *flat[1:3], following, stats, own, heads)


def body(queries, key_rows, value_rows, out_grad, head_kind, frame_band):
    frames = lax.axis_size("ctx")
    count = queries.shape[1]
    heads = queries.shape[2] // DH
    first = lax.axis_index("head").astype(jnp.int32) * heads
    frame = lax.axis_index("ctx").astype(jnp.int32)
    kinds = lax.dynamic_slice_in_dim(head_kind, first, heads)
    slots = jnp.sum((kinds == TEMPORAL).astype(jnp.int32))
    arrays = [
        x.reshape(frames, count // frames, heads * DH)
        for x in (queries, key_rows, value_rows, out_grad)
    ]
    outs = lax.switch(
        slots,
        [functools.partial(branch, n, heads) for n in range(heads + 1)],
        head_kind, frame_band, first.reshape(1), frame.reshape(1), *arrays,
    )
    return tuple(out.reshape(queries.shape) for out in outs)


def solution(mesh):
    rows = P("ctx", None, "head")
    return jax.shard_map(
        body,
        mesh=mesh,
        in_specs=(rows, rows, rows, rows, P(), P()),
        out_specs=(rows, rows, rows, rows),
        check_vma=False,
    )
```

```python
import functools
import math

import jax
import jax.numpy as jnp
from jax import lax
from jax.experimental import pallas as pl
from jax.experimental.pallas import tpu as pltpu
from jax.sharding import PartitionSpec as P

DH = 128
SCALE = DH ** (-0.5)
SPATIAL, TEMPORAL = 1, 0
MASKED = -1e30
SCALE_LOG2 = SCALE * math.log2(math.e)
F32 = jnp.float32
BF16 = jnp.bfloat16
MIB = 1024 * 1024


def head_at(kind_ref, first_ref, heads, kind, slot):
    found, seen = jnp.int32(0), jnp.int32(0)
    for head in range(heads):
        hit = kind_ref[first_ref[0] + head] == kind
        found = jnp.where(jnp.logical_and(hit, seen == slot), jnp.int32(head), found)
        seen = seen + hit.astype(jnp.int32)
    return found


def dot_nt(a, b):
    return lax.dot_general(a, b, (((1,), (1,)), ((), ())), preferred_element_type=F32)


def dot_nn(a, b):
    return lax.dot_general(a, b, (((1,), (0,)), ((), ())), preferred_element_type=F32)


def dot_tn(a, b):
    return lax.dot_general(a, b, (((0,), (0,)), ((), ())), preferred_element_type=F32)


def params(mib=32):
    return pltpu.CompilerParams(
        dimension_semantics=("arbitrary",), vmem_limit_bytes=mib * MIB
    )


def cost(flops, moved):
    return pl.CostEstimate(flops=int(flops), bytes_accessed=int(moved), transcendentals=0)


def column_spec(count, heads, kind):
    return pl.BlockSpec((count, DH), lambda i, *refs: (0, head_at(*refs[:2], heads, kind, i)))


def head_columns(kind_ref, first_ref, heads, kind, slot):
    return pl.ds(pl.multiple_of(head_at(kind_ref, first_ref, heads, kind, slot) * DH, DH), DH)


def staged_copies(triples, in_sems, out_sems):
    loads = [pltpu.make_async_copy(x, y, in_sems.at[i]) for i, (x, y, _) in enumerate(triples)]
    stores = [pltpu.make_async_copy(y, z, out_sems.at[i]) for i, (_, y, z) in enumerate(triples)]
    for load in loads:
        load.start()
    for load, store in zip(loads, stores):
        load.wait()
        store.start()
    for store in stores:
        store.wait()


def whole_params():
    return pltpu.CompilerParams(vmem_limit_bytes=62 * MIB)


def pack_spatial(kinds, first, arrays, slots, heads, after):
    frames, rows, _ = arrays[0].shape
    count = len(arrays)
    total = slots * count

    def kernel(kind_ref, first_ref, *refs):
        ins, outs = refs[:count], refs[-3 - count // 2 : -3]
        stage, in_sems, out_sems = refs[-3:]
        triples = []
        for slot in range(slots):
            cols = head_columns(kind_ref, first_ref, heads, SPATIAL, slot)
            for place, ref in enumerate(ins):
                target = outs[place // 2].at[slot, place % 2]
                triples.append((ref.at[:, :, cols], stage.at[slot, place], target))
        staged_copies(triples, in_sems, out_sems)

    return pl.pallas_call(
        kernel,
        out_shape=[jax.ShapeDtypeStruct((slots, 2, frames, rows, DH), BF16)] * (count // 2),
        in_specs=[pl.BlockSpec(memory_space=pltpu.SMEM)] * 2
        + [pl.BlockSpec(memory_space=pl.ANY)] * (count + len(after)),
        out_specs=[pl.BlockSpec(memory_space=pl.ANY)] * (count // 2),
        scratch_shapes=[
            pltpu.VMEM((slots, count, frames, rows, DH), BF16),
            pltpu.SemaphoreType.DMA((total,)),
            pltpu.SemaphoreType.DMA((total,)),
        ],
        compiler_params=whole_params(),
        cost_estimate=cost(0, 4 * total * frames * rows * DH),
        name="pack_spatial",
    )(kinds, first, *arrays, *after)


def pack_temporal(kinds, first, arrays, slots, heads):
    frames, rows, _ = arrays[0].shape
    total = 4 * slots

    def kernel(kind_ref, first_ref, *refs):
        ins, (out, stage, in_sems, out_sems) = refs[:4], refs[4:]
        triples = []
        for slot in range(slots):
            cols = head_columns(kind_ref, first_ref, heads, TEMPORAL, slot)
            for place, ref in enumerate(ins):
                triples.append(
                    (ref.at[:, :, cols], stage.at[slot, place], out.at[:, place, slot])
                )
        staged_copies(triples, in_sems, out_sems)

    return pl.pallas_call(
        kernel,
        out_shape=jax.ShapeDtypeStruct((frames, 4, slots, rows, DH), BF16),
        in_specs=[pl.BlockSpec(memory_space=pltpu.SMEM)] * 2
        + [pl.BlockSpec(memory_space=pl.ANY)] * 4,
        out_specs=pl.BlockSpec(memory_space=pl.ANY),
        scratch_shapes=[
            pltpu.VMEM((slots, 4, frames, rows, DH), BF16),
            pltpu.SemaphoreType.DMA((total,)),
            pltpu.SemaphoreType.DMA((total,)),
        ],
        compiler_params=whole_params(),
        cost_estimate=cost(0, 4 * total * frames * rows * DH),
        name="pack_temporal",
    )(kinds, first, *arrays)


def temporal(kinds, first, bands, rows_in, heads):
    frames, _, slots, rows, _ = rows_in.shape
    group = 16
    size = frames * group

    def kernel(kind_ref, first_ref, band_ref, rows_ref, result_ref, held, made, in_sems, out_sems):
        def load(slot):
            return pltpu.make_async_copy(rows_ref.at[:, :, slot], held.at[slot], in_sems.at[slot])

        def store(slot):
            return pltpu.make_async_copy(
                made.at[slot], result_ref.at[:, :, slot], out_sems.at[slot]
            )

        for slot in range(slots):
            load(slot).start()

        @pl.loop(0, slots)
        def _(slot):
            load(slot).wait()
            one_head(kind_ref, first_ref, band_ref, slot, held.at[slot], made.at[slot])
            store(slot).start()

        for slot in range(slots):
            store(slot).wait()

    def one_head(kind_ref, first_ref, band_ref, slot, in_ref, out_ref):
        band = band_ref[first_ref[0] + head_at(kind_ref, first_ref, heads, TEMPORAL, slot)]
        row = lax.broadcasted_iota(jnp.int32, (size, size), 0)
        col = lax.broadcasted_iota(jnp.int32, (size, size), 1)
        same = lax.rem(row, group) == lax.rem(col, group)
        near = jnp.abs(lax.div(row, group) - lax.div(col, group)) <= band
        allowed = jnp.logical_and(same, near)
        parts = [slice(start, start + group) for start in range(0, rows, group)]
        qs, ks, vs, gs = (
            [in_ref[:, place, part].reshape(size, DH) for part in parts] for place in range(4)
        )
        scores = [jnp.where(allowed, dot_nt(k, q), MASKED) for q, k in zip(qs, ks)]
        dprobs = [dot_nt(v, g) for g, v in zip(gs, vs)]
        raised = [
            jnp.exp2((x - jnp.max(x, axis=0, keepdims=True)) * SCALE_LOG2) for x in scores
        ]
        weights = [x * (1.0 / jnp.sum(x, axis=0, keepdims=True)) for x in raised]
        probs = [x.astype(BF16) for x in weights]
        deltas = [jnp.sum(w * dp, axis=0, keepdims=True) for w, dp in zip(weights, dprobs)]
        dscores = [
            (w * (dp - delta) * SCALE).astype(BF16)
            for w, dp, delta in zip(weights, dprobs, deltas)
        ]
        results = (
            [dot_tn(x, v).astype(BF16) for x, v in zip(probs, vs)],
            [dot_tn(x, k).astype(BF16) for x, k in zip(dscores, ks)],
            [dot_nn(x, q).astype(BF16) for x, q in zip(dscores, qs)],
            [dot_nn(x, g).astype(BF16) for x, g in zip(probs, gs)],
        )
        for place, result in enumerate(results):
            for part, value in zip(parts, result):
                out_ref[:, place, part] = value.reshape(frames, group, DH)

    block = (slots, frames, 4, rows, DH)
    return pl.pallas_call(
        kernel,
        out_shape=jax.ShapeDtypeStruct(rows_in.shape, BF16),
        in_specs=[pl.BlockSpec(memory_space=pltpu.SMEM)] * 3
        + [pl.BlockSpec(memory_space=pl.ANY)],
        out_specs=pl.BlockSpec(memory_space=pl.ANY),
        scratch_shapes=[
            pltpu.VMEM(block, BF16),
            pltpu.VMEM(block, BF16),
            pltpu.SemaphoreType.DMA((slots,)),
            pltpu.SemaphoreType.DMA((slots,)),
        ],
        compiler_params=whole_params(),
        cost_estimate=cost(1e10, 4 * rows_in.size),
        name="temporal",
    )(kinds, first, bands, rows_in)


def spatial(kinds, first, frame, arrays, prior, heads):
    count = arrays[0].shape[0]
    slots = prior.shape[0]
    chunk = min(count, 128)

    def kernel(
        kind_ref, first_ref, frame_ref, q_ref, k_ref, v_ref, g_ref, prior_ref,
        out_ref, qgrad_ref, own_ref, stats_ref,
    ):
        has_prior = frame_ref[0] > 0
        k, v = k_ref[...], v_ref[...]
        k_prior, v_prior = prior_ref[0, 0], prior_ref[0, 1]
        own_ref[...] = jnp.zeros_like(own_ref)

        @pl.loop(0, count // chunk)
        def _(step):
            part = pl.ds(pl.multiple_of(step * chunk, chunk), chunk)
            q, g = q_ref[part], g_ref[part]
            own = dot_nt(k, q)
            before = jnp.where(has_prior, dot_nt(k_prior, q), MASKED)
            top = jnp.maximum(
                jnp.max(own, axis=0, keepdims=True), jnp.max(before, axis=0, keepdims=True)
            )
            own, before = (jnp.exp2((x - top) * SCALE_LOG2) for x in (own, before))
            total = jnp.sum(own, axis=0, keepdims=True) + jnp.sum(before, axis=0, keepdims=True)
            inverse = 1.0 / total
            own, before = own * inverse, before * inverse
            own_dp, before_dp = dot_nt(v, g), dot_nt(v_prior, g)
            delta = jnp.sum(own * own_dp, axis=0, keepdims=True) + jnp.sum(
                before * before_dp, axis=0, keepdims=True
            )
            own_prob, before_prob = own.astype(BF16), before.astype(BF16)
            own_ds = (own * (own_dp - delta) * SCALE).astype(BF16)
            before_ds = (before * (before_dp - delta) * SCALE).astype(BF16)
            out_ref[part] = (dot_tn(own_prob, v) + dot_tn(before_prob, v_prior)).astype(BF16)
            qgrad_ref[part] = (dot_tn(own_ds, k) + dot_tn(before_ds, k_prior)).astype(BF16)
            own_ref[0, 0] += dot_nn(own_ds, q)
            own_ref[0, 1] += dot_nn(own_prob, g)
            stats_ref[0, 0:1, part] = top * SCALE + jnp.log(total)
            stats_ref[0, 1:2, part] = delta

    columns = column_spec(count, heads, SPATIAL)
    pair = pl.BlockSpec((1, 2, count, DH), lambda i, *refs: (i, 0, 0, 0))
    whole = jax.ShapeDtypeStruct((count, heads * DH), BF16)
    return pl.pallas_call(
        kernel,
        out_shape=[
            whole,
            whole,
            jax.ShapeDtypeStruct(prior.shape, F32),
            jax.ShapeDtypeStruct((slots, 2, count), F32),
        ],
        grid_spec=pltpu.PrefetchScalarGridSpec(
            num_scalar_prefetch=3,
            grid=(slots,),
            in_specs=[columns] * 4 + [pair],
            out_specs=[
                columns, columns, pair, pl.BlockSpec((1, 2, count), lambda i, *refs: (i, 0, 0))
            ],
        ),
        compiler_params=params(24),
        cost_estimate=cost(2e11, 16 * slots * count * DH),
        name="spatial",
    )(kinds, first, frame, *arrays, prior)


def spatial_next(kinds, first, k, v, following, stats, own, heads):
    slots, _, count, _ = own.shape
    chunk = min(count, 256)

    def kernel(
        kind_ref, first_ref, k_in, v_in, next_in, stats_in, own_in, k_out, v_out,
        kv_ref, next_ref, stats_ref, own_ref, made_ref, in_sems, out_sems,
    ):
        def loads(slot):
            cols = head_columns(kind_ref, first_ref, heads, SPATIAL, slot)
            pairs = [
                (k_in.at[:, cols], kv_ref.at[slot, 0]),
                (v_in.at[:, cols], kv_ref.at[slot, 1]),
                (next_in.at[slot], next_ref.at[slot]),
                (stats_in.at[slot], stats_ref.at[slot]),
                (own_in.at[slot], own_ref.at[slot]),
            ]
            return [
                pltpu.make_async_copy(*pair, in_sems.at[slot, i]) for i, pair in enumerate(pairs)
            ]

        def stores(slot):
            cols = head_columns(kind_ref, first_ref, heads, SPATIAL, slot)
            return [
                pltpu.make_async_copy(made_ref.at[slot, i], out.at[:, cols], out_sems.at[slot, i])
                for i, out in enumerate((k_out, v_out))
            ]

        for slot in range(slots):
            for copy in loads(slot):
                copy.start()

        @pl.loop(0, slots)
        def _(slot):
            for copy in loads(slot):
                copy.wait()
            q, g = next_ref[slot, 0], next_ref[slot, 1]
            lse, delta = stats_ref[slot, 0:1] * math.log2(math.e), stats_ref[slot, 1:2]
            for start in range(0, count, chunk):
                part = slice(start, start + chunk)
                weight = jnp.exp2(dot_nt(kv_ref[slot, 0, part], q) * SCALE_LOG2 - lse)
                slope = (weight * (dot_nt(kv_ref[slot, 1, part], g) - delta)).astype(BF16)
                made_ref[slot, 0, part] = (
                    own_ref[slot, 0, part] + dot_nn(slope, q) * SCALE
                ).astype(BF16)
                made_ref[slot, 1, part] = (
                    own_ref[slot, 1, part] + dot_nn(weight.astype(BF16), g)
                ).astype(BF16)
            for copy in stores(slot):
                copy.start()

        for slot in range(slots):
            for copy in stores(slot):
                copy.wait()

    return pl.pallas_call(
        kernel,
        out_shape=[jax.ShapeDtypeStruct(k.shape, BF16)] * 2,
        in_specs=[pl.BlockSpec(memory_space=pltpu.SMEM)] * 2
        + [pl.BlockSpec(memory_space=pl.ANY)] * 5,
        out_specs=[pl.BlockSpec(memory_space=pl.ANY)] * 2,
        scratch_shapes=[
            pltpu.VMEM((slots, 2, count, DH), BF16),
            pltpu.VMEM((slots, 2, count, DH), BF16),
            pltpu.VMEM((slots, 2, count), F32),
            pltpu.VMEM((slots, 2, count, DH), F32),
            pltpu.VMEM((slots, 2, count, DH), BF16),
            pltpu.SemaphoreType.DMA((slots, 5)),
            pltpu.SemaphoreType.DMA((slots, 2)),
        ],
        compiler_params=pltpu.CompilerParams(vmem_limit_bytes=24 * MIB),
        cost_estimate=cost(8 * slots * count * count * DH, 20 * slots * count * DH),
        name="spatial_next",
    )(kinds, first, k, v, following, stats, own)


def unpack(kinds, first, rows_in, filled, heads):
    frames, _, slots, rows, _ = rows_in.shape
    count = frames * rows
    total = 4 * slots

    def kernel(kind_ref, first_ref, in_ref, *refs):
        outs, (stage, in_sems, out_sems) = refs[-7:-3], refs[-3:]
        triples = []
        for slot in range(slots):
            cols = head_columns(kind_ref, first_ref, heads, TEMPORAL, slot)
            for place, out in enumerate(outs):
                held = stage.at[slot, place]
                triples.append((in_ref.at[:, place, slot], held, out.at[:, :, cols]))
        staged_copies(triples, in_sems, out_sems)

    shape = (frames, rows, heads * DH)
    filled = [x.reshape(shape) for x in filled]
    outs = pl.pallas_call(
        kernel,
        out_shape=[jax.ShapeDtypeStruct(shape, BF16)] * 4,
        in_specs=[pl.BlockSpec(memory_space=pltpu.SMEM)] * 2
        + [pl.BlockSpec(memory_space=pl.ANY)] * (1 + len(filled)),
        out_specs=[pl.BlockSpec(memory_space=pl.ANY)] * 4,
        scratch_shapes=[
            pltpu.VMEM((slots, 4, frames, rows, DH), BF16),
            pltpu.SemaphoreType.DMA((total,)),
            pltpu.SemaphoreType.DMA((total,)),
        ],
        input_output_aliases={3 + place: place for place in range(len(filled))},
        compiler_params=pltpu.CompilerParams(vmem_limit_bytes=24 * MIB),
        cost_estimate=cost(0, 4 * rows_in.size),
        name="unpack",
    )(kinds, first, rows_in, *filled)
    return [x.reshape(count, heads * DH) for x in outs]


def passed_along(array, axis, by):
    length = lax.axis_size(axis)
    pairs = [(i, i + by) for i in range(length) if 0 <= i + by < length]
    return lax.ppermute(array, axis, pairs)


def behind(arrays, *others):
    return lax.optimization_barrier((tuple(arrays), others))[0]


def branch(slots, heads, kinds, bands, first, frame, q, k, v, g):
    frames, rows, width = q.shape
    count = frames * rows
    others = heads - slots
    exchange = functools.partial(
        lax.all_to_all, axis_name="ctx", split_axis=0, concat_axis=0, tiled=True
    )
    flat = [x.reshape(count, width) for x in (q, k, v, g)]
    packed = []
    filled = ()
    if slots > 0:
        packed = [pack_temporal(kinds, first, (q, k, v, g), slots, heads)]
        framed = exchange(*packed)
        results = temporal(kinds, first, bands, framed, heads)
        returned = exchange(results)
    if others > 0:
        ahead, back = pack_spatial(kinds, first, (k, v, q, g), others, heads, packed)
        arrived = [passed_along(ahead, "ctx", 1), passed_along(back, "ctx", -1)]
        if slots > 0:
            arrived = behind(arrived, results)
        prior, following = (x.reshape(others, 2, count, DH) for x in arrived)
        attended, qgrad, own, stats = spatial(kinds, first, frame, flat, prior, heads)
        stats = passed_along(stats, "ctx", -1)
        grads = spatial_next(kinds, first, *flat[1:3], following, stats, own, heads)
        filled = (attended, qgrad, *grads)
    if slots > 0:
        filled = unpack(kinds, first, returned, filled, heads)
    return tuple(filled)


def body(queries, key_rows, value_rows, out_grad, head_kind, frame_band):
    frames = lax.axis_size("ctx")
    count = queries.shape[1]
    heads = queries.shape[2] // DH
    first = lax.axis_index("head").astype(jnp.int32) * heads
    frame = lax.axis_index("ctx").astype(jnp.int32)
    kinds = lax.dynamic_slice_in_dim(head_kind, first, heads)
    slots = jnp.sum((kinds == TEMPORAL).astype(jnp.int32))
    arrays = [
        x.reshape(frames, count // frames, heads * DH)
        for x in (queries, key_rows, value_rows, out_grad)
    ]
    outs = lax.switch(
        slots,
        [functools.partial(branch, n, heads) for n in range(heads + 1)],
        head_kind, frame_band, first.reshape(1), frame.reshape(1), *arrays,
    )
    return tuple(out.reshape(queries.shape) for out in outs)


def solution(mesh):
    rows = P("ctx", None, "head")
    return jax.shard_map(
        body,
        mesh=mesh,
        in_specs=(rows, rows, rows, rows, P(), P()),
        out_specs=(rows, rows, rows, rows),
        check_vma=False,
    )
```

```python
import functools
import math

import jax
import jax.numpy as jnp
from jax import lax
from jax.experimental import pallas as pl
from jax.experimental.pallas import tpu as pltpu
from jax.sharding import PartitionSpec as P

DH = 128
SCALE = DH ** (-0.5)
SPATIAL, TEMPORAL = 1, 0
MASKED = -1e30
SCALE_LOG2 = SCALE * math.log2(math.e)
F32 = jnp.float32
BF16 = jnp.bfloat16
MIB = 1024 * 1024


def head_at(kind_ref, first_ref, heads, kind, slot):
    found, seen = jnp.int32(0), jnp.int32(0)
    for head in range(heads):
        hit = kind_ref[first_ref[0] + head] == kind
        found = jnp.where(jnp.logical_and(hit, seen == slot), jnp.int32(head), found)
        seen = seen + hit.astype(jnp.int32)
    return found


def dot_nt(a, b):
    return lax.dot_general(a, b, (((1,), (1,)), ((), ())), preferred_element_type=F32)


def dot_nn(a, b):
    return lax.dot_general(a, b, (((1,), (0,)), ((), ())), preferred_element_type=F32)


def dot_tn(a, b):
    return lax.dot_general(a, b, (((0,), (0,)), ((), ())), preferred_element_type=F32)


def params(mib=32):
    return pltpu.CompilerParams(
        dimension_semantics=("arbitrary",), vmem_limit_bytes=mib * MIB
    )


def cost(flops, moved):
    return pl.CostEstimate(flops=int(flops), bytes_accessed=int(moved), transcendentals=0)


def column_spec(count, heads, kind):
    return pl.BlockSpec((count, DH), lambda i, *refs: (0, head_at(*refs[:2], heads, kind, i)))


def head_columns(kind_ref, first_ref, heads, kind, slot):
    return pl.ds(pl.multiple_of(head_at(kind_ref, first_ref, heads, kind, slot) * DH, DH), DH)


def staged_copies(triples, in_sems, out_sems):
    loads = [pltpu.make_async_copy(x, y, in_sems.at[i]) for i, (x, y, _) in enumerate(triples)]
    stores = [pltpu.make_async_copy(y, z, out_sems.at[i]) for i, (_, y, z) in enumerate(triples)]
    for load in loads:
        load.start()
    for load, store in zip(loads, stores):
        load.wait()
        store.start()
    for store in stores:
        store.wait()


def whole_params():
    return pltpu.CompilerParams(vmem_limit_bytes=62 * MIB)


def pack_spatial(kinds, first, arrays, slots, heads, after):
    frames, rows, _ = arrays[0].shape
    count = len(arrays)
    total = slots * count

    def kernel(kind_ref, first_ref, *refs):
        ins, outs = refs[:count], refs[-3 - count // 2 : -3]
        stage, in_sems, out_sems = refs[-3:]
        triples = []
        for slot in range(slots):
            cols = head_columns(kind_ref, first_ref, heads, SPATIAL, slot)
            for place, ref in enumerate(ins):
                target = outs[place // 2].at[slot, place % 2]
                triples.append((ref.at[:, :, cols], stage.at[slot, place], target))
        staged_copies(triples, in_sems, out_sems)

    return pl.pallas_call(
        kernel,
        out_shape=[jax.ShapeDtypeStruct((slots, 2, frames, rows, DH), BF16)] * (count // 2),
        in_specs=[pl.BlockSpec(memory_space=pltpu.SMEM)] * 2
        + [pl.BlockSpec(memory_space=pl.ANY)] * (count + len(after)),
        out_specs=[pl.BlockSpec(memory_space=pl.ANY)] * (count // 2),
        scratch_shapes=[
            pltpu.VMEM((slots, count, frames, rows, DH), BF16),
            pltpu.SemaphoreType.DMA((total,)),
            pltpu.SemaphoreType.DMA((total,)),
        ],
        compiler_params=whole_params(),
        cost_estimate=cost(0, 4 * total * frames * rows * DH),
        name="pack_spatial",
    )(kinds, first, *arrays, *after)


def pack_temporal(kinds, first, arrays, slots, heads):
    frames, rows, _ = arrays[0].shape
    total = 4 * slots

    def kernel(kind_ref, first_ref, *refs):
        ins, (out, stage, in_sems, out_sems) = refs[:4], refs[4:]
        triples = []
        for slot in range(slots):
            cols = head_columns(kind_ref, first_ref, heads, TEMPORAL, slot)
            for place, ref in enumerate(ins):
                triples.append(
                    (ref.at[:, :, cols], stage.at[slot, place], out.at[:, place, slot])
                )
        staged_copies(triples, in_sems, out_sems)

    return pl.pallas_call(
        kernel,
        out_shape=jax.ShapeDtypeStruct((frames, 4, slots, rows, DH), BF16),
        in_specs=[pl.BlockSpec(memory_space=pltpu.SMEM)] * 2
        + [pl.BlockSpec(memory_space=pl.ANY)] * 4,
        out_specs=pl.BlockSpec(memory_space=pl.ANY),
        scratch_shapes=[
            pltpu.VMEM((slots, 4, frames, rows, DH), BF16),
            pltpu.SemaphoreType.DMA((total,)),
            pltpu.SemaphoreType.DMA((total,)),
        ],
        compiler_params=whole_params(),
        cost_estimate=cost(0, 4 * total * frames * rows * DH),
        name="pack_temporal",
    )(kinds, first, *arrays)


def temporal(kinds, first, bands, rows_in, heads):
    frames, _, slots, rows, _ = rows_in.shape
    group = 16
    size = frames * group

    def kernel(kind_ref, first_ref, band_ref, rows_ref, result_ref, held, made, in_sems, out_sems):
        def load(slot):
            return pltpu.make_async_copy(rows_ref.at[:, :, slot], held.at[slot], in_sems.at[slot])

        def store(slot):
            return pltpu.make_async_copy(
                made.at[slot], result_ref.at[:, :, slot], out_sems.at[slot]
            )

        for slot in range(slots):
            load(slot).start()

        def work(members):
            for slot in members:
                load(slot).wait()
            some_heads(
                kind_ref, first_ref, band_ref,
                [(slot, held.at[slot], made.at[slot]) for slot in members],
            )
            for slot in members:
                store(slot).start()

        if slots > 1:

            @pl.loop(0, slots // 2)
            def _(pair):
                work([2 * pair, 2 * pair + 1])

        if slots % 2:
            work([slots - 1])
        for slot in range(slots):
            store(slot).wait()

    def some_heads(kind_ref, first_ref, band_ref, members):
        row = lax.broadcasted_iota(jnp.int32, (size, size), 0)
        col = lax.broadcasted_iota(jnp.int32, (size, size), 1)
        same = lax.rem(row, group) == lax.rem(col, group)
        distance = jnp.where(same, jnp.abs(lax.div(row, group) - lax.div(col, group)), frames)
        parts = [slice(start, start + group) for start in range(0, rows, group)]
        allowed, qs, ks, vs, gs = [], [], [], [], []
        for slot, in_ref, _ in members:
            head = head_at(kind_ref, first_ref, heads, TEMPORAL, slot)
            band = jnp.minimum(band_ref[first_ref[0] + head], frames - 1)
            allowed += [distance <= band] * len(parts)
            for place, rows_of in enumerate((qs, ks, vs, gs)):
                rows_of += [in_ref[:, place, part].reshape(size, DH) for part in parts]
        scores = [
            jnp.where(ok, dot_nt(k, q), MASKED) for ok, q, k in zip(allowed, qs, ks)
        ]
        dprobs = [dot_nt(v, g) for g, v in zip(gs, vs)]
        raised = [
            jnp.exp2((x - jnp.max(x, axis=0, keepdims=True)) * SCALE_LOG2) for x in scores
        ]
        weights = [x * (1.0 / jnp.sum(x, axis=0, keepdims=True)) for x in raised]
        probs = [x.astype(BF16) for x in weights]
        deltas = [jnp.sum(w * dp, axis=0, keepdims=True) for w, dp in zip(weights, dprobs)]
        dscores = [
            (w * (dp - delta) * SCALE).astype(BF16)
            for w, dp, delta in zip(weights, dprobs, deltas)
        ]
        results = (
            [dot_tn(x, v).astype(BF16) for x, v in zip(probs, vs)],
            [dot_tn(x, k).astype(BF16) for x, k in zip(dscores, ks)],
            [dot_nn(x, q).astype(BF16) for x, q in zip(dscores, qs)],
            [dot_nn(x, g).astype(BF16) for x, g in zip(probs, gs)],
        )
        for place, result in enumerate(results):
            targets = [(out_ref, part) for _, _, out_ref in members for part in parts]
            for (out_ref, part), value in zip(targets, result):
                out_ref[:, place, part] = value.reshape(frames, group, DH)

    block = (slots, frames, 4, rows, DH)
    return pl.pallas_call(
        kernel,
        out_shape=jax.ShapeDtypeStruct(rows_in.shape, BF16),
        in_specs=[pl.BlockSpec(memory_space=pltpu.SMEM)] * 3
        + [pl.BlockSpec(memory_space=pl.ANY)],
        out_specs=pl.BlockSpec(memory_space=pl.ANY),
        scratch_shapes=[
            pltpu.VMEM(block, BF16),
            pltpu.VMEM(block, BF16),
            pltpu.SemaphoreType.DMA((slots,)),
            pltpu.SemaphoreType.DMA((slots,)),
        ],
        compiler_params=whole_params(),
        cost_estimate=cost(1e10, 4 * rows_in.size),
        name="temporal",
    )(kinds, first, bands, rows_in)


def spatial(kinds, first, frame, arrays, prior, heads):
    count = arrays[0].shape[0]
    slots = prior.shape[0]
    chunk = min(count, 128)

    def kernel(
        kind_ref, first_ref, frame_ref, q_ref, k_ref, v_ref, g_ref, prior_ref,
        out_ref, qgrad_ref, own_ref, stats_ref,
    ):
        has_prior = frame_ref[0] > 0
        k, v = k_ref[...], v_ref[...]
        k_prior, v_prior = prior_ref[0, 0], prior_ref[0, 1]
        own_ref[...] = jnp.zeros_like(own_ref)

        @pl.loop(0, count // chunk)
        def _(step):
            part = pl.ds(pl.multiple_of(step * chunk, chunk), chunk)
            q, g = q_ref[part], g_ref[part]
            own = dot_nt(k, q)
            before = jnp.where(has_prior, dot_nt(k_prior, q), MASKED)
            top = jnp.maximum(
                jnp.max(own, axis=0, keepdims=True), jnp.max(before, axis=0, keepdims=True)
            )
            own, before = (jnp.exp2((x - top) * SCALE_LOG2) for x in (own, before))
            total = jnp.sum(own, axis=0, keepdims=True) + jnp.sum(before, axis=0, keepdims=True)
            inverse = 1.0 / total
            own, before = own * inverse, before * inverse
            own_dp, before_dp = dot_nt(v, g), dot_nt(v_prior, g)
            delta = jnp.sum(own * own_dp, axis=0, keepdims=True) + jnp.sum(
                before * before_dp, axis=0, keepdims=True
            )
            own_prob, before_prob = own.astype(BF16), before.astype(BF16)
            own_ds = (own * (own_dp - delta) * SCALE).astype(BF16)
            before_ds = (before * (before_dp - delta) * SCALE).astype(BF16)
            out_ref[part] = (dot_tn(own_prob, v) + dot_tn(before_prob, v_prior)).astype(BF16)
            qgrad_ref[part] = (dot_tn(own_ds, k) + dot_tn(before_ds, k_prior)).astype(BF16)
            own_ref[0, 0] += dot_nn(own_ds, q)
            own_ref[0, 1] += dot_nn(own_prob, g)
            stats_ref[0, 0:1, part] = top * SCALE + jnp.log(total)
            stats_ref[0, 1:2, part] = delta

    columns = column_spec(count, heads, SPATIAL)
    pair = pl.BlockSpec((1, 2, count, DH), lambda i, *refs: (i, 0, 0, 0))
    whole = jax.ShapeDtypeStruct((count, heads * DH), BF16)
    return pl.pallas_call(
        kernel,
        out_shape=[
            whole,
            whole,
            jax.ShapeDtypeStruct(prior.shape, F32),
            jax.ShapeDtypeStruct((slots, 2, count), F32),
        ],
        grid_spec=pltpu.PrefetchScalarGridSpec(
            num_scalar_prefetch=3,
            grid=(slots,),
            in_specs=[columns] * 4 + [pair],
            out_specs=[
                columns, columns, pair, pl.BlockSpec((1, 2, count), lambda i, *refs: (i, 0, 0))
            ],
        ),
        compiler_params=params(24),
        cost_estimate=cost(2e11, 16 * slots * count * DH),
        name="spatial",
    )(kinds, first, frame, *arrays, prior)


def spatial_next(kinds, first, k, v, following, stats, own, heads):
    slots, _, count, _ = own.shape
    chunk = min(count, 256)

    def kernel(
        kind_ref, first_ref, k_in, v_in, next_in, stats_in, own_in, k_out, v_out,
        kv_ref, next_ref, stats_ref, own_ref, made_ref, in_sems, out_sems,
    ):
        def loads(slot):
            cols = head_columns(kind_ref, first_ref, heads, SPATIAL, slot)
            pairs = [
                (k_in.at[:, cols], kv_ref.at[slot, 0]),
                (v_in.at[:, cols], kv_ref.at[slot, 1]),
                (next_in.at[slot], next_ref.at[slot]),
                (stats_in.at[slot], stats_ref.at[slot]),
                (own_in.at[slot], own_ref.at[slot]),
            ]
            return [
                pltpu.make_async_copy(*pair, in_sems.at[slot, i]) for i, pair in enumerate(pairs)
            ]

        def stores(slot):
            cols = head_columns(kind_ref, first_ref, heads, SPATIAL, slot)
            return [
                pltpu.make_async_copy(made_ref.at[slot, i], out.at[:, cols], out_sems.at[slot, i])
                for i, out in enumerate((k_out, v_out))
            ]

        for slot in range(slots):
            for copy in loads(slot):
                copy.start()

        @pl.loop(0, slots)
        def _(slot):
            for copy in loads(slot):
                copy.wait()
            q, g = next_ref[slot, 0], next_ref[slot, 1]
            lse, delta = stats_ref[slot, 0:1] * math.log2(math.e), stats_ref[slot, 1:2]
            for start in range(0, count, chunk):
                part = slice(start, start + chunk)
                weight = jnp.exp2(dot_nt(kv_ref[slot, 0, part], q) * SCALE_LOG2 - lse)
                slope = (weight * (dot_nt(kv_ref[slot, 1, part], g) - delta)).astype(BF16)
                made_ref[slot, 0, part] = (
                    own_ref[slot, 0, part] + dot_nn(slope, q) * SCALE
                ).astype(BF16)
                made_ref[slot, 1, part] = (
                    own_ref[slot, 1, part] + dot_nn(weight.astype(BF16), g)
                ).astype(BF16)
            for copy in stores(slot):
                copy.start()

        for slot in range(slots):
            for copy in stores(slot):
                copy.wait()

    return pl.pallas_call(
        kernel,
        out_shape=[jax.ShapeDtypeStruct(k.shape, BF16)] * 2,
        in_specs=[pl.BlockSpec(memory_space=pltpu.SMEM)] * 2
        + [pl.BlockSpec(memory_space=pl.ANY)] * 5,
        out_specs=[pl.BlockSpec(memory_space=pl.ANY)] * 2,
        scratch_shapes=[
            pltpu.VMEM((slots, 2, count, DH), BF16),
            pltpu.VMEM((slots, 2, count, DH), BF16),
            pltpu.VMEM((slots, 2, count), F32),
            pltpu.VMEM((slots, 2, count, DH), F32),
            pltpu.VMEM((slots, 2, count, DH), BF16),
            pltpu.SemaphoreType.DMA((slots, 5)),
            pltpu.SemaphoreType.DMA((slots, 2)),
        ],
        compiler_params=pltpu.CompilerParams(vmem_limit_bytes=24 * MIB),
        cost_estimate=cost(8 * slots * count * count * DH, 20 * slots * count * DH),
        name="spatial_next",
    )(kinds, first, k, v, following, stats, own)


def unpack(kinds, first, rows_in, filled, heads):
    frames, _, slots, rows, _ = rows_in.shape
    count = frames * rows
    total = 4 * slots

    def kernel(kind_ref, first_ref, in_ref, *refs):
        outs, (stage, in_sems, out_sems) = refs[-7:-3], refs[-3:]
        triples = []
        for slot in range(slots):
            cols = head_columns(kind_ref, first_ref, heads, TEMPORAL, slot)
            for place, out in enumerate(outs):
                held = stage.at[slot, place]
                triples.append((in_ref.at[:, place, slot], held, out.at[:, :, cols]))
        staged_copies(triples, in_sems, out_sems)

    shape = (frames, rows, heads * DH)
    filled = [x.reshape(shape) for x in filled]
    outs = pl.pallas_call(
        kernel,
        out_shape=[jax.ShapeDtypeStruct(shape, BF16)] * 4,
        in_specs=[pl.BlockSpec(memory_space=pltpu.SMEM)] * 2
        + [pl.BlockSpec(memory_space=pl.ANY)] * (1 + len(filled)),
        out_specs=[pl.BlockSpec(memory_space=pl.ANY)] * 4,
        scratch_shapes=[
            pltpu.VMEM((slots, 4, frames, rows, DH), BF16),
            pltpu.SemaphoreType.DMA((total,)),
            pltpu.SemaphoreType.DMA((total,)),
        ],
        input_output_aliases={3 + place: place for place in range(len(filled))},
        compiler_params=pltpu.CompilerParams(vmem_limit_bytes=24 * MIB),
        cost_estimate=cost(0, 4 * rows_in.size),
        name="unpack",
    )(kinds, first, rows_in, *filled)
    return [x.reshape(count, heads * DH) for x in outs]


def passed_along(array, axis, by):
    length = lax.axis_size(axis)
    pairs = [(i, i + by) for i in range(length) if 0 <= i + by < length]
    return lax.ppermute(array, axis, pairs)


def behind(arrays, *others):
    return lax.optimization_barrier((tuple(arrays), others))[0]


def branch(slots, heads, kinds, bands, first, frame, q, k, v, g):
    frames, rows, width = q.shape
    count = frames * rows
    others = heads - slots
    exchange = functools.partial(
        lax.all_to_all, axis_name="ctx", split_axis=0, concat_axis=0, tiled=True
    )
    flat = [x.reshape(count, width) for x in (q, k, v, g)]
    packed = []
    filled = ()
    if slots > 0:
        packed = [pack_temporal(kinds, first, (q, k, v, g), slots, heads)]
        framed = exchange(*packed)
        results = temporal(kinds, first, bands, framed, heads)
        returned = exchange(results)
    if others > 0:
        ahead, back = pack_spatial(kinds, first, (k, v, q, g), others, heads, packed)
        arrived = [passed_along(ahead, "ctx", 1), passed_along(back, "ctx", -1)]
        if slots > 0:
            arrived = behind(arrived, results)
        prior, following = (x.reshape(others, 2, count, DH) for x in arrived)
        attended, qgrad, own, stats = spatial(kinds, first, frame, flat, prior, heads)
        stats = passed_along(stats, "ctx", -1)
        grads = spatial_next(kinds, first, *flat[1:3], following, stats, own, heads)
        filled = (attended, qgrad, *grads)
    if slots > 0:
        filled = unpack(kinds, first, returned, filled, heads)
    return tuple(filled)


def body(queries, key_rows, value_rows, out_grad, head_kind, frame_band):
    frames = lax.axis_size("ctx")
    count = queries.shape[1]
    heads = queries.shape[2] // DH
    first = lax.axis_index("head").astype(jnp.int32) * heads
    frame = lax.axis_index("ctx").astype(jnp.int32)
    offset = jnp.arange(head_kind.shape[0], dtype=jnp.int32) - first
    here = jnp.logical_and(offset >= 0, offset < heads)
    slots = jnp.sum(jnp.logical_and(here, head_kind == TEMPORAL).astype(jnp.int32))
    arrays = [
        x.reshape(frames, count // frames, heads * DH)
        for x in (queries, key_rows, value_rows, out_grad)
    ]
    outs = lax.switch(
        slots,
        [functools.partial(branch, n, heads) for n in range(heads + 1)],
        head_kind, frame_band, first.reshape(1), frame.reshape(1), *arrays,
    )
    return tuple(out.reshape(queries.shape) for out in outs)


def solution(mesh):
    rows = P("ctx", None, "head")
    return jax.shard_map(
        body,
        mesh=mesh,
        in_specs=(rows, rows, rows, rows, P(), P()),
        out_specs=(rows, rows, rows, rows),
        check_vma=False,
    )
```

```python
import functools
import math

import jax
import jax.numpy as jnp
from jax import lax
from jax.experimental import pallas as pl
from jax.experimental.pallas import tpu as pltpu
from jax.sharding import PartitionSpec as P

DH = 128
SCALE = DH ** (-0.5)
SPATIAL, TEMPORAL = 1, 0
MASKED = -1e30
SCALE_LOG2 = SCALE * math.log2(math.e)
F32 = jnp.float32
BF16 = jnp.bfloat16
MIB = 1024 * 1024


def head_at(kind_ref, first_ref, heads, kind, slot):
    found, seen = jnp.int32(0), jnp.int32(0)
    for head in range(heads):
        hit = kind_ref[first_ref[0] + head] == kind
        found = jnp.where(jnp.logical_and(hit, seen == slot), jnp.int32(head), found)
        seen = seen + hit.astype(jnp.int32)
    return found


def dot_nt(a, b):
    return lax.dot_general(a, b, (((1,), (1,)), ((), ())), preferred_element_type=F32)


def dot_nn(a, b):
    return lax.dot_general(a, b, (((1,), (0,)), ((), ())), preferred_element_type=F32)


def dot_tn(a, b):
    return lax.dot_general(a, b, (((0,), (0,)), ((), ())), preferred_element_type=F32)


def params(mib=32):
    return pltpu.CompilerParams(
        dimension_semantics=("arbitrary",), vmem_limit_bytes=mib * MIB
    )


def cost(flops, moved):
    return pl.CostEstimate(flops=int(flops), bytes_accessed=int(moved), transcendentals=0)


def column_spec(count, heads, kind):
    return pl.BlockSpec((count, DH), lambda i, *refs: (0, head_at(*refs[:2], heads, kind, i)))


def head_columns(kind_ref, first_ref, heads, kind, slot):
    return pl.ds(pl.multiple_of(head_at(kind_ref, first_ref, heads, kind, slot) * DH, DH), DH)


def staged_copies(triples, in_sems, out_sems):
    loads = [pltpu.make_async_copy(x, y, in_sems.at[i]) for i, (x, y, _) in enumerate(triples)]
    stores = [pltpu.make_async_copy(y, z, out_sems.at[i]) for i, (_, y, z) in enumerate(triples)]
    for load in loads:
        load.start()
    for load, store in zip(loads, stores):
        load.wait()
        store.start()
    for store in stores:
        store.wait()


def whole_params():
    return pltpu.CompilerParams(vmem_limit_bytes=62 * MIB)


def pack_spatial(kinds, first, arrays, slots, heads, after):
    frames, rows, _ = arrays[0].shape
    count = len(arrays)
    total = slots * count

    def kernel(kind_ref, first_ref, *refs):
        ins, outs = refs[:count], refs[-3 - count // 2 : -3]
        stage, in_sems, out_sems = refs[-3:]
        triples = []
        for slot in range(slots):
            cols = head_columns(kind_ref, first_ref, heads, SPATIAL, slot)
            for place, ref in enumerate(ins):
                target = outs[place // 2].at[slot, place % 2]
                triples.append((ref.at[:, :, cols], stage.at[slot, place], target))
        staged_copies(triples, in_sems, out_sems)

    return pl.pallas_call(
        kernel,
        out_shape=[jax.ShapeDtypeStruct((slots, 2, frames, rows, DH), BF16)] * (count // 2),
        in_specs=[pl.BlockSpec(memory_space=pltpu.SMEM)] * 2
        + [pl.BlockSpec(memory_space=pl.ANY)] * (count + len(after)),
        out_specs=[pl.BlockSpec(memory_space=pl.ANY)] * (count // 2),
        scratch_shapes=[
            pltpu.VMEM((slots, count, frames, rows, DH), BF16),
            pltpu.SemaphoreType.DMA((total,)),
            pltpu.SemaphoreType.DMA((total,)),
        ],
        compiler_params=whole_params(),
        cost_estimate=cost(0, 4 * total * frames * rows * DH),
        name="pack_spatial",
    )(kinds, first, *arrays, *after)


def pack_temporal(kinds, first, arrays, slots, heads):
    frames, rows, _ = arrays[0].shape
    total = 4 * slots

    def kernel(kind_ref, first_ref, *refs):
        ins, (out, stage, in_sems, out_sems) = refs[:4], refs[4:]
        triples = []
        for slot in range(slots):
            cols = head_columns(kind_ref, first_ref, heads, TEMPORAL, slot)
            for place, ref in enumerate(ins):
                triples.append(
                    (ref.at[:, :, cols], stage.at[slot, place], out.at[:, place, slot])
                )
        staged_copies(triples, in_sems, out_sems)

    return pl.pallas_call(
        kernel,
        out_shape=jax.ShapeDtypeStruct((frames, 4, slots, rows, DH), BF16),
        in_specs=[pl.BlockSpec(memory_space=pltpu.SMEM)] * 2
        + [pl.BlockSpec(memory_space=pl.ANY)] * 4,
        out_specs=pl.BlockSpec(memory_space=pl.ANY),
        scratch_shapes=[
            pltpu.VMEM((slots, 4, frames, rows, DH), BF16),
            pltpu.SemaphoreType.DMA((total,)),
            pltpu.SemaphoreType.DMA((total,)),
        ],
        compiler_params=whole_params(),
        cost_estimate=cost(0, 4 * total * frames * rows * DH),
        name="pack_temporal",
    )(kinds, first, *arrays)


def temporal(kinds, first, bands, rows_in, heads):
    frames, _, slots, rows, _ = rows_in.shape
    group = 16
    size = frames * group

    def kernel(kind_ref, first_ref, band_ref, rows_ref, result_ref, held, made, in_sems, out_sems):
        def load(slot):
            return pltpu.make_async_copy(rows_ref.at[:, :, slot], held.at[slot], in_sems.at[slot])

        def store(slot):
            return pltpu.make_async_copy(
                made.at[slot], result_ref.at[:, :, slot], out_sems.at[slot]
            )

        for slot in range(slots):
            load(slot).start()

        def work(members):
            for slot in members:
                load(slot).wait()
            some_heads(
                kind_ref, first_ref, band_ref,
                [(slot, held.at[slot], made.at[slot]) for slot in members],
            )
            for slot in members:
                store(slot).start()

        if slots > 1:

            @pl.loop(0, slots // 2)
            def _(pair):
                work([2 * pair, 2 * pair + 1])

        if slots % 2:
            work([slots - 1])
        for slot in range(slots):
            store(slot).wait()

    def some_heads(kind_ref, first_ref, band_ref, members):
        row = lax.broadcasted_iota(jnp.int32, (size, size), 0)
        col = lax.broadcasted_iota(jnp.int32, (size, size), 1)
        same = lax.rem(row, group) == lax.rem(col, group)
        distance = jnp.where(same, jnp.abs(lax.div(row, group) - lax.div(col, group)), frames)
        parts = [slice(start, start + group) for start in range(0, rows, group)]
        allowed, qs, ks, vs, gs = [], [], [], [], []
        for slot, in_ref, _ in members:
            head = head_at(kind_ref, first_ref, heads, TEMPORAL, slot)
            band = jnp.minimum(band_ref[first_ref[0] + head], frames - 1)
            allowed += [distance <= band] * len(parts)
            for place, rows_of in enumerate((qs, ks, vs, gs)):
                rows_of += [in_ref[:, place, part].reshape(size, DH) for part in parts]
        scores = [
            jnp.where(ok, dot_nt(k, q), MASKED) for ok, q, k in zip(allowed, qs, ks)
        ]
        dprobs = [dot_nt(v, g) for g, v in zip(gs, vs)]
        raised = [
            jnp.exp2((x - jnp.max(x, axis=0, keepdims=True)) * SCALE_LOG2) for x in scores
        ]
        weights = [x * (1.0 / jnp.sum(x, axis=0, keepdims=True)) for x in raised]
        probs = [x.astype(BF16) for x in weights]
        deltas = [jnp.sum(w * dp, axis=0, keepdims=True) for w, dp in zip(weights, dprobs)]
        dscores = [
            (w * (dp - delta) * SCALE).astype(BF16)
            for w, dp, delta in zip(weights, dprobs, deltas)
        ]
        results = (
            [dot_tn(x, v).astype(BF16) for x, v in zip(probs, vs)],
            [dot_tn(x, k).astype(BF16) for x, k in zip(dscores, ks)],
            [dot_nn(x, q).astype(BF16) for x, q in zip(dscores, qs)],
            [dot_nn(x, g).astype(BF16) for x, g in zip(probs, gs)],
        )
        for place, result in enumerate(results):
            targets = [(out_ref, part) for _, _, out_ref in members for part in parts]
            for (out_ref, part), value in zip(targets, result):
                out_ref[:, place, part] = value.reshape(frames, group, DH)

    block = (slots, frames, 4, rows, DH)
    return pl.pallas_call(
        kernel,
        out_shape=jax.ShapeDtypeStruct(rows_in.shape, BF16),
        in_specs=[pl.BlockSpec(memory_space=pltpu.SMEM)] * 3
        + [pl.BlockSpec(memory_space=pl.ANY)],
        out_specs=pl.BlockSpec(memory_space=pl.ANY),
        scratch_shapes=[
            pltpu.VMEM(block, BF16),
            pltpu.VMEM(block, BF16),
            pltpu.SemaphoreType.DMA((slots,)),
            pltpu.SemaphoreType.DMA((slots,)),
        ],
        compiler_params=whole_params(),
        cost_estimate=cost(1e10, 4 * rows_in.size),
        name="temporal",
    )(kinds, first, bands, rows_in)


def spatial(kinds, first, frame, arrays, prior, heads):
    count = arrays[0].shape[0]
    slots = prior.shape[0]
    chunk = min(count, 128)

    def kernel(
        kind_ref, first_ref, frame_ref, q_ref, k_ref, v_ref, g_ref, prior_ref,
        out_ref, qgrad_ref, own_ref, stats_ref,
    ):
        has_prior = frame_ref[0] > 0
        k, v = k_ref[...], v_ref[...]
        k_prior, v_prior = prior_ref[0, 0], prior_ref[0, 1]
        own_ref[...] = jnp.zeros_like(own_ref)

        @pl.loop(0, count // chunk)
        def _(step):
            part = pl.ds(pl.multiple_of(step * chunk, chunk), chunk)
            q, g = q_ref[part], g_ref[part]
            own = dot_nt(k, q)
            before = jnp.where(has_prior, dot_nt(k_prior, q), MASKED)
            top = jnp.maximum(
                jnp.max(own, axis=0, keepdims=True), jnp.max(before, axis=0, keepdims=True)
            )
            own, before = (jnp.exp2((x - top) * SCALE_LOG2) for x in (own, before))
            total = jnp.sum(own, axis=0, keepdims=True) + jnp.sum(before, axis=0, keepdims=True)
            inverse = 1.0 / total
            own, before = own * inverse, before * inverse
            own_dp, before_dp = dot_nt(v, g), dot_nt(v_prior, g)
            delta = jnp.sum(own * own_dp, axis=0, keepdims=True) + jnp.sum(
                before * before_dp, axis=0, keepdims=True
            )
            own_prob, before_prob = own.astype(BF16), before.astype(BF16)
            own_ds = (own * (own_dp - delta) * SCALE).astype(BF16)
            before_ds = (before * (before_dp - delta) * SCALE).astype(BF16)
            out_ref[part] = (dot_tn(own_prob, v) + dot_tn(before_prob, v_prior)).astype(BF16)
            qgrad_ref[part] = (dot_tn(own_ds, k) + dot_tn(before_ds, k_prior)).astype(BF16)
            own_ref[0, 0] += dot_nn(own_ds, q)
            own_ref[0, 1] += dot_nn(own_prob, g)
            stats_ref[0, 0:1, part] = top * SCALE + jnp.log(total)
            stats_ref[0, 1:2, part] = delta

    columns = column_spec(count, heads, SPATIAL)
    pair = pl.BlockSpec((1, 2, count, DH), lambda i, *refs: (i, 0, 0, 0))
    whole = jax.ShapeDtypeStruct((count, heads * DH), BF16)
    return pl.pallas_call(
        kernel,
        out_shape=[
            whole,
            whole,
            jax.ShapeDtypeStruct(prior.shape, F32),
            jax.ShapeDtypeStruct((slots, 2, count), F32),
        ],
        grid_spec=pltpu.PrefetchScalarGridSpec(
            num_scalar_prefetch=3,
            grid=(slots,),
            in_specs=[columns] * 4 + [pair],
            out_specs=[
                columns, columns, pair, pl.BlockSpec((1, 2, count), lambda i, *refs: (i, 0, 0))
            ],
        ),
        compiler_params=params(24),
        cost_estimate=cost(2e11, 16 * slots * count * DH),
        name="spatial",
    )(kinds, first, frame, *arrays, prior)


def spatial_next(kinds, first, k, v, following, stats, own, heads):
    slots, _, count, _ = own.shape
    chunk = min(count, 256)

    def kernel(
        kind_ref, first_ref, k_in, v_in, next_in, stats_in, own_in, k_out, v_out,
        kv_ref, next_ref, stats_ref, own_ref, made_ref, in_sems, out_sems,
    ):
        def loads(slot):
            cols = head_columns(kind_ref, first_ref, heads, SPATIAL, slot)
            pairs = [
                (k_in.at[:, cols], kv_ref.at[slot, 0]),
                (v_in.at[:, cols], kv_ref.at[slot, 1]),
                (next_in.at[slot], next_ref.at[slot]),
                (stats_in.at[slot], stats_ref.at[slot]),
                (own_in.at[slot], own_ref.at[slot]),
            ]
            return [
                pltpu.make_async_copy(*pair, in_sems.at[slot, i]) for i, pair in enumerate(pairs)
            ]

        def stores(slot):
            cols = head_columns(kind_ref, first_ref, heads, SPATIAL, slot)
            return [
                pltpu.make_async_copy(made_ref.at[slot, i], out.at[:, cols], out_sems.at[slot, i])
                for i, out in enumerate((k_out, v_out))
            ]

        for slot in range(slots):
            for copy in loads(slot):
                copy.start()

        @pl.loop(0, slots)
        def _(slot):
            for copy in loads(slot):
                copy.wait()
            q, g = next_ref[slot, 0], next_ref[slot, 1]
            lse, delta = stats_ref[slot, 0:1] * math.log2(math.e), stats_ref[slot, 1:2]
            for start in range(0, count, chunk):
                part = slice(start, start + chunk)
                weight = jnp.exp2(dot_nt(kv_ref[slot, 0, part], q) * SCALE_LOG2 - lse)
                slope = (weight * (dot_nt(kv_ref[slot, 1, part], g) - delta)).astype(BF16)
                made_ref[slot, 0, part] = (
                    own_ref[slot, 0, part] + dot_nn(slope, q) * SCALE
                ).astype(BF16)
                made_ref[slot, 1, part] = (
                    own_ref[slot, 1, part] + dot_nn(weight.astype(BF16), g)
                ).astype(BF16)
            for copy in stores(slot):
                copy.start()

        for slot in range(slots):
            for copy in stores(slot):
                copy.wait()

    return pl.pallas_call(
        kernel,
        out_shape=[jax.ShapeDtypeStruct(k.shape, BF16)] * 2,
        in_specs=[pl.BlockSpec(memory_space=pltpu.SMEM)] * 2
        + [pl.BlockSpec(memory_space=pl.ANY)] * 5,
        out_specs=[pl.BlockSpec(memory_space=pl.ANY)] * 2,
        scratch_shapes=[
            pltpu.VMEM((slots, 2, count, DH), BF16),
            pltpu.VMEM((slots, 2, count, DH), BF16),
            pltpu.VMEM((slots, 2, count), F32),
            pltpu.VMEM((slots, 2, count, DH), F32),
            pltpu.VMEM((slots, 2, count, DH), BF16),
            pltpu.SemaphoreType.DMA((slots, 5)),
            pltpu.SemaphoreType.DMA((slots, 2)),
        ],
        compiler_params=pltpu.CompilerParams(vmem_limit_bytes=24 * MIB),
        cost_estimate=cost(8 * slots * count * count * DH, 20 * slots * count * DH),
        name="spatial_next",
    )(kinds, first, k, v, following, stats, own)


def unpack(kinds, first, rows_in, filled, heads):
    frames, _, slots, rows, _ = rows_in.shape
    count = frames * rows
    total = 4 * slots

    def kernel(kind_ref, first_ref, in_ref, *refs):
        outs, (stage, in_sems, out_sems) = refs[-7:-3], refs[-3:]
        triples = []
        for slot in range(slots):
            cols = head_columns(kind_ref, first_ref, heads, TEMPORAL, slot)
            for place, out in enumerate(outs):
                held = stage.at[slot, place]
                triples.append((in_ref.at[:, place, slot], held, out.at[:, :, cols]))
        staged_copies(triples, in_sems, out_sems)

    shape = (frames, rows, heads * DH)
    filled = [x.reshape(shape) for x in filled]
    outs = pl.pallas_call(
        kernel,
        out_shape=[jax.ShapeDtypeStruct(shape, BF16)] * 4,
        in_specs=[pl.BlockSpec(memory_space=pltpu.SMEM)] * 2
        + [pl.BlockSpec(memory_space=pl.ANY)] * (1 + len(filled)),
        out_specs=[pl.BlockSpec(memory_space=pl.ANY)] * 4,
        scratch_shapes=[
            pltpu.VMEM((slots, 4, frames, rows, DH), BF16),
            pltpu.SemaphoreType.DMA((total,)),
            pltpu.SemaphoreType.DMA((total,)),
        ],
        input_output_aliases={3 + place: place for place in range(len(filled))},
        compiler_params=pltpu.CompilerParams(vmem_limit_bytes=24 * MIB),
        cost_estimate=cost(0, 4 * rows_in.size),
        name="unpack",
    )(kinds, first, rows_in, *filled)
    return [x.reshape(count, heads * DH) for x in outs]


def passed_along(array, axis, by):
    length = lax.axis_size(axis)
    pairs = [(i, i + by) for i in range(length) if 0 <= i + by < length]
    return lax.ppermute(array, axis, pairs)


def behind(arrays, *others):
    return lax.optimization_barrier((tuple(arrays), others))[0]


def neighbour_rows(ahead, back, frame, results):
    length = lax.axis_size("ctx")
    even = lax.rem(frame[0], 2) == 0
    far = [(i, i - 1 if i % 2 == 0 else i + 1) for i in range(length)]
    far = [pair for pair in far if 0 <= pair[1] < length]
    near = [(i, i + 1 if i % 2 == 0 else i - 1) for i in range(length)]
    near = lax.ppermute(jnp.where(even, ahead, back), "ctx", near)
    far = lax.ppermute(jnp.where(even, back, ahead), "ctx", far)
    if results is not None:
        near, far = behind((near, far), results)
    return jnp.where(even, far, near), jnp.where(even, near, far)


def branch(slots, heads, kinds, bands, first, frame, q, k, v, g):
    frames, rows, width = q.shape
    count = frames * rows
    others = heads - slots
    exchange = functools.partial(
        lax.all_to_all, axis_name="ctx", split_axis=0, concat_axis=0, tiled=True
    )
    flat = [x.reshape(count, width) for x in (q, k, v, g)]
    packed = []
    filled, results = (), None
    if slots > 0:
        packed = [pack_temporal(kinds, first, (q, k, v, g), slots, heads)]
        framed = exchange(*packed)
        results = temporal(kinds, first, bands, framed, heads)
        returned = exchange(results)
    if others > 0:
        ahead, back = pack_spatial(kinds, first, (k, v, q, g), others, heads, packed)
        arrived = neighbour_rows(ahead, back, frame, results)
        prior, following = (x.reshape(others, 2, count, DH) for x in arrived)
        attended, qgrad, own, stats = spatial(kinds, first, frame, flat, prior, heads)
        stats = passed_along(stats, "ctx", -1)
        grads = spatial_next(kinds, first, *flat[1:3], following, stats, own, heads)
        filled = (attended, qgrad, *grads)
    if slots > 0:
        filled = unpack(kinds, first, returned, filled, heads)
    return tuple(filled)


def body(queries, key_rows, value_rows, out_grad, head_kind, frame_band):
    frames = lax.axis_size("ctx")
    count = queries.shape[1]
    heads = queries.shape[2] // DH
    first = lax.axis_index("head").astype(jnp.int32) * heads
    frame = lax.axis_index("ctx").astype(jnp.int32)
    offset = jnp.arange(head_kind.shape[0], dtype=jnp.int32) - first
    here = jnp.logical_and(offset >= 0, offset < heads)
    slots = jnp.sum(jnp.logical_and(here, head_kind == TEMPORAL).astype(jnp.int32))
    arrays = [
        x.reshape(frames, count // frames, heads * DH)
        for x in (queries, key_rows, value_rows, out_grad)
    ]
    outs = lax.switch(
        slots,
        [functools.partial(branch, n, heads) for n in range(heads + 1)],
        head_kind, frame_band, first.reshape(1), frame.reshape(1), *arrays,
    )
    return tuple(out.reshape(queries.shape) for out in outs)


def solution(mesh):
    rows = P("ctx", None, "head")
    return jax.shard_map(
        body,
        mesh=mesh,
        in_specs=(rows, rows, rows, rows, P(), P()),
        out_specs=(rows, rows, rows, rows),
        check_vma=False,
    )
```

```python
import functools
import math

import jax
import jax.numpy as jnp
from jax import lax
from jax.experimental import pallas as pl
from jax.experimental.pallas import tpu as pltpu
from jax.sharding import PartitionSpec as P

DH = 128
SCALE = DH ** (-0.5)
SPATIAL, TEMPORAL = 1, 0
MASKED = -1e30
SCALE_LOG2 = SCALE * math.log2(math.e)
F32 = jnp.float32
BF16 = jnp.bfloat16
MIB = 1024 * 1024


def head_at(kind_ref, first_ref, heads, kind, slot):
    found, seen = jnp.int32(0), jnp.int32(0)
    for head in range(heads):
        hit = kind_ref[first_ref[0] + head] == kind
        found = jnp.where(jnp.logical_and(hit, seen == slot), jnp.int32(head), found)
        seen = seen + hit.astype(jnp.int32)
    return found


def dot_nt(a, b):
    return lax.dot_general(a, b, (((1,), (1,)), ((), ())), preferred_element_type=F32)


def dot_nn(a, b):
    return lax.dot_general(a, b, (((1,), (0,)), ((), ())), preferred_element_type=F32)


def dot_tn(a, b):
    return lax.dot_general(a, b, (((0,), (0,)), ((), ())), preferred_element_type=F32)


def params(mib=32):
    return pltpu.CompilerParams(
        dimension_semantics=("arbitrary",), vmem_limit_bytes=mib * MIB
    )


def cost(flops, moved):
    return pl.CostEstimate(flops=int(flops), bytes_accessed=int(moved), transcendentals=0)


def column_spec(count, heads, kind):
    return pl.BlockSpec((count, DH), lambda i, *refs: (0, head_at(*refs[:2], heads, kind, i)))


def head_columns(kind_ref, first_ref, heads, kind, slot):
    return pl.ds(pl.multiple_of(head_at(kind_ref, first_ref, heads, kind, slot) * DH, DH), DH)


def staged_copies(triples, in_sems, out_sems):
    loads = [pltpu.make_async_copy(x, y, in_sems.at[i]) for i, (x, y, _) in enumerate(triples)]
    stores = [pltpu.make_async_copy(y, z, out_sems.at[i]) for i, (_, y, z) in enumerate(triples)]
    for load in loads:
        load.start()
    for load, store in zip(loads, stores):
        load.wait()
        store.start()
    for store in stores:
        store.wait()


def whole_params():
    return pltpu.CompilerParams(vmem_limit_bytes=62 * MIB)


def pack_spatial(kinds, first, arrays, slots, heads, after):
    frames, rows, _ = arrays[0].shape
    count = len(arrays)
    total = slots * count

    def kernel(kind_ref, first_ref, *refs):
        ins, outs = refs[:count], refs[-3 - count // 2 : -3]
        stage, in_sems, out_sems = refs[-3:]
        triples = []
        for slot in range(slots):
            cols = head_columns(kind_ref, first_ref, heads, SPATIAL, slot)
            for place, ref in enumerate(ins):
                target = outs[place // 2].at[slot, place % 2]
                triples.append((ref.at[:, :, cols], stage.at[slot, place], target))
        staged_copies(triples, in_sems, out_sems)

    return pl.pallas_call(
        kernel,
        out_shape=[jax.ShapeDtypeStruct((slots, 2, frames, rows, DH), BF16)] * (count // 2),
        in_specs=[pl.BlockSpec(memory_space=pltpu.SMEM)] * 2
        + [pl.BlockSpec(memory_space=pl.ANY)] * (count + len(after)),
        out_specs=[pl.BlockSpec(memory_space=pl.ANY)] * (count // 2),
        scratch_shapes=[
            pltpu.VMEM((slots, count, frames, rows, DH), BF16),
            pltpu.SemaphoreType.DMA((total,)),
            pltpu.SemaphoreType.DMA((total,)),
        ],
        compiler_params=whole_params(),
        cost_estimate=cost(0, 4 * total * frames * rows * DH),
        name="pack_spatial",
    )(kinds, first, *arrays, *after)


def pack_temporal(kinds, first, arrays, slots, heads):
    frames, rows, _ = arrays[0].shape
    total = 4 * slots

    def kernel(kind_ref, first_ref, *refs):
        ins, (out, stage, in_sems, out_sems) = refs[:4], refs[4:]
        triples = []
        for slot in range(slots):
            cols = head_columns(kind_ref, first_ref, heads, TEMPORAL, slot)
            for place, ref in enumerate(ins):
                triples.append(
                    (ref.at[:, :, cols], stage.at[slot, place], out.at[:, place, slot])
                )
        staged_copies(triples, in_sems, out_sems)

    return pl.pallas_call(
        kernel,
        out_shape=jax.ShapeDtypeStruct((frames, 4, slots, rows, DH), BF16),
        in_specs=[pl.BlockSpec(memory_space=pltpu.SMEM)] * 2
        + [pl.BlockSpec(memory_space=pl.ANY)] * 4,
        out_specs=pl.BlockSpec(memory_space=pl.ANY),
        scratch_shapes=[
            pltpu.VMEM((slots, 4, frames, rows, DH), BF16),
            pltpu.SemaphoreType.DMA((total,)),
            pltpu.SemaphoreType.DMA((total,)),
        ],
        compiler_params=whole_params(),
        cost_estimate=cost(0, 4 * total * frames * rows * DH),
        name="pack_temporal",
    )(kinds, first, *arrays)


def temporal(kinds, first, bands, rows_in, heads):
    frames, _, slots, rows, _ = rows_in.shape
    group = 16
    size = frames * group

    def kernel(kind_ref, first_ref, band_ref, rows_ref, result_ref, held, made, in_sems, out_sems):
        def load(slot):
            return pltpu.make_async_copy(rows_ref.at[:, :, slot], held.at[slot], in_sems.at[slot])

        def store(slot):
            return pltpu.make_async_copy(
                made.at[slot], result_ref.at[:, :, slot], out_sems.at[slot]
            )

        for slot in range(slots):
            load(slot).start()

        def work(members):
            for slot in members:
                load(slot).wait()
            some_heads(
                kind_ref, first_ref, band_ref,
                [(slot, held.at[slot], made.at[slot]) for slot in members],
            )
            for slot in members:
                store(slot).start()

        if slots > 1:

            @pl.loop(0, slots // 2)
            def _(pair):
                work([2 * pair, 2 * pair + 1])

        if slots % 2:
            work([slots - 1])
        for slot in range(slots):
            store(slot).wait()

    def some_heads(kind_ref, first_ref, band_ref, members):
        row = lax.broadcasted_iota(jnp.int32, (size, size), 0)
        col = lax.broadcasted_iota(jnp.int32, (size, size), 1)
        same = lax.rem(row, group) == lax.rem(col, group)
        distance = jnp.where(same, jnp.abs(lax.div(row, group) - lax.div(col, group)), frames)
        parts = [slice(start, start + group) for start in range(0, rows, group)]
        allowed, qs, ks, vs, gs = [], [], [], [], []
        for slot, in_ref, _ in members:
            head = head_at(kind_ref, first_ref, heads, TEMPORAL, slot)
            band = jnp.minimum(band_ref[first_ref[0] + head], frames - 1)
            allowed += [distance <= band] * len(parts)
            for place, rows_of in enumerate((qs, ks, vs, gs)):
                rows_of += [in_ref[:, place, part].reshape(size, DH) for part in parts]
        scores = [
            jnp.where(ok, dot_nt(k, q), MASKED) for ok, q, k in zip(allowed, qs, ks)
        ]
        dprobs = [dot_nt(v, g) for g, v in zip(gs, vs)]
        raised = [
            jnp.exp2((x - jnp.max(x, axis=0, keepdims=True)) * SCALE_LOG2) for x in scores
        ]
        weights = [x * (1.0 / jnp.sum(x, axis=0, keepdims=True)) for x in raised]
        probs = [x.astype(BF16) for x in weights]
        deltas = [jnp.sum(w * dp, axis=0, keepdims=True) for w, dp in zip(weights, dprobs)]
        dscores = [
            (w * (dp - delta) * SCALE).astype(BF16)
            for w, dp, delta in zip(weights, dprobs, deltas)
        ]
        results = (
            [dot_tn(x, v).astype(BF16) for x, v in zip(probs, vs)],
            [dot_tn(x, k).astype(BF16) for x, k in zip(dscores, ks)],
            [dot_nn(x, q).astype(BF16) for x, q in zip(dscores, qs)],
            [dot_nn(x, g).astype(BF16) for x, g in zip(probs, gs)],
        )
        for place, result in enumerate(results):
            targets = [(out_ref, part) for _, _, out_ref in members for part in parts]
            for (out_ref, part), value in zip(targets, result):
                out_ref[:, place, part] = value.reshape(frames, group, DH)

    block = (slots, frames, 4, rows, DH)
    return pl.pallas_call(
        kernel,
        out_shape=jax.ShapeDtypeStruct(rows_in.shape, BF16),
        in_specs=[pl.BlockSpec(memory_space=pltpu.SMEM)] * 3
        + [pl.BlockSpec(memory_space=pl.ANY)],
        out_specs=pl.BlockSpec(memory_space=pl.ANY),
        scratch_shapes=[
            pltpu.VMEM(block, BF16),
            pltpu.VMEM(block, BF16),
            pltpu.SemaphoreType.DMA((slots,)),
            pltpu.SemaphoreType.DMA((slots,)),
        ],
        compiler_params=whole_params(),
        cost_estimate=cost(1e10, 4 * rows_in.size),
        name="temporal",
    )(kinds, first, bands, rows_in)


def spatial(kinds, first, frame, arrays, prior, heads):
    count = arrays[0].shape[0]
    slots = prior.shape[0]
    chunk = min(count, 128)

    def kernel(
        kind_ref, first_ref, frame_ref, q_ref, k_ref, v_ref, g_ref, prior_ref,
        out_ref, qgrad_ref, own_ref, stats_ref,
    ):
        has_prior = frame_ref[0] > 0
        k, v = k_ref[...], v_ref[...]
        k_prior, v_prior = prior_ref[0, 0], prior_ref[0, 1]
        own_ref[...] = jnp.zeros_like(own_ref)

        @pl.loop(0, count // chunk)
        def _(step):
            part = pl.ds(pl.multiple_of(step * chunk, chunk), chunk)
            q, g = q_ref[part], g_ref[part]
            own = dot_nt(k, q)
            before = jnp.where(has_prior, dot_nt(k_prior, q), MASKED)
            top = jnp.maximum(
                jnp.max(own, axis=0, keepdims=True), jnp.max(before, axis=0, keepdims=True)
            )
            own, before = (jnp.exp2((x - top) * SCALE_LOG2) for x in (own, before))
            total = jnp.sum(own, axis=0, keepdims=True) + jnp.sum(before, axis=0, keepdims=True)
            inverse = 1.0 / total
            own, before = own * inverse, before * inverse
            own_dp, before_dp = dot_nt(v, g), dot_nt(v_prior, g)
            delta = jnp.sum(own * own_dp, axis=0, keepdims=True) + jnp.sum(
                before * before_dp, axis=0, keepdims=True
            )
            own_prob, before_prob = own.astype(BF16), before.astype(BF16)
            own_ds = (own * (own_dp - delta) * SCALE).astype(BF16)
            before_ds = (before * (before_dp - delta) * SCALE).astype(BF16)
            out_ref[part] = (dot_tn(own_prob, v) + dot_tn(before_prob, v_prior)).astype(BF16)
            qgrad_ref[part] = (dot_tn(own_ds, k) + dot_tn(before_ds, k_prior)).astype(BF16)
            own_ref[0, 0] += dot_nn(own_ds, q)
            own_ref[0, 1] += dot_nn(own_prob, g)
            stats_ref[0, 0:1, part] = top * SCALE + jnp.log(total)
            stats_ref[0, 1:2, part] = delta

    columns = column_spec(count, heads, SPATIAL)
    pair = pl.BlockSpec((1, 2, count, DH), lambda i, *refs: (i, 0, 0, 0))
    whole = jax.ShapeDtypeStruct((count, heads * DH), BF16)
    return pl.pallas_call(
        kernel,
        out_shape=[
            whole,
            whole,
            jax.ShapeDtypeStruct(prior.shape, F32),
            jax.ShapeDtypeStruct((slots, 2, count), F32),
        ],
        grid_spec=pltpu.PrefetchScalarGridSpec(
            num_scalar_prefetch=3,
            grid=(slots,),
            in_specs=[columns] * 4 + [pair],
            out_specs=[
                columns, columns, pair, pl.BlockSpec((1, 2, count), lambda i, *refs: (i, 0, 0))
            ],
        ),
        compiler_params=params(24),
        cost_estimate=cost(2e11, 16 * slots * count * DH),
        name="spatial",
    )(kinds, first, frame, *arrays, prior)


def spatial_next(kinds, first, k, v, following, stats, own, heads):
    slots, _, count, _ = own.shape
    chunk = min(count, 256)

    def kernel(
        kind_ref, first_ref, k_in, v_in, next_in, stats_in, own_in, k_out, v_out,
        kv_ref, next_ref, stats_ref, own_ref, made_ref, in_sems, out_sems,
    ):
        def loads(slot):
            cols = head_columns(kind_ref, first_ref, heads, SPATIAL, slot)
            pairs = [
                (k_in.at[:, cols], kv_ref.at[slot, 0]),
                (v_in.at[:, cols], kv_ref.at[slot, 1]),
                (next_in.at[slot], next_ref.at[slot]),
                (stats_in.at[slot], stats_ref.at[slot]),
                (own_in.at[slot], own_ref.at[slot]),
            ]
            return [
                pltpu.make_async_copy(*pair, in_sems.at[slot, i]) for i, pair in enumerate(pairs)
            ]

        def stores(slot):
            cols = head_columns(kind_ref, first_ref, heads, SPATIAL, slot)
            return [
                pltpu.make_async_copy(made_ref.at[slot, i], out.at[:, cols], out_sems.at[slot, i])
                for i, out in enumerate((k_out, v_out))
            ]

        for slot in range(slots):
            for copy in loads(slot):
                copy.start()

        @pl.loop(0, slots)
        def _(slot):
            for copy in loads(slot):
                copy.wait()
            q, g = next_ref[slot, 0], next_ref[slot, 1]
            lse, delta = stats_ref[slot, 0:1] * math.log2(math.e), stats_ref[slot, 1:2]
            for start in range(0, count, chunk):
                part = slice(start, start + chunk)
                weight = jnp.exp2(dot_nt(kv_ref[slot, 0, part], q) * SCALE_LOG2 - lse)
                slope = (weight * (dot_nt(kv_ref[slot, 1, part], g) - delta)).astype(BF16)
                made_ref[slot, 0, part] = (
                    own_ref[slot, 0, part] + dot_nn(slope, q) * SCALE
                ).astype(BF16)
                made_ref[slot, 1, part] = (
                    own_ref[slot, 1, part] + dot_nn(weight.astype(BF16), g)
                ).astype(BF16)
            for copy in stores(slot):
                copy.start()

        for slot in range(slots):
            for copy in stores(slot):
                copy.wait()

    return pl.pallas_call(
        kernel,
        out_shape=[jax.ShapeDtypeStruct(k.shape, BF16)] * 2,
        in_specs=[pl.BlockSpec(memory_space=pltpu.SMEM)] * 2
        + [pl.BlockSpec(memory_space=pl.ANY)] * 5,
        out_specs=[pl.BlockSpec(memory_space=pl.ANY)] * 2,
        scratch_shapes=[
            pltpu.VMEM((slots, 2, count, DH), BF16),
            pltpu.VMEM((slots, 2, count, DH), BF16),
            pltpu.VMEM((slots, 2, count), F32),
            pltpu.VMEM((slots, 2, count, DH), F32),
            pltpu.VMEM((slots, 2, count, DH), BF16),
            pltpu.SemaphoreType.DMA((slots, 5)),
            pltpu.SemaphoreType.DMA((slots, 2)),
        ],
        compiler_params=pltpu.CompilerParams(vmem_limit_bytes=24 * MIB),
        cost_estimate=cost(8 * slots * count * count * DH, 20 * slots * count * DH),
        name="spatial_next",
    )(kinds, first, k, v, following, stats, own)


def unpack(kinds, first, rows_in, filled, heads):
    frames, _, slots, rows, _ = rows_in.shape
    count = frames * rows
    total = 4 * slots

    def kernel(kind_ref, first_ref, in_ref, *refs):
        outs, (stage, in_sems, out_sems) = refs[-7:-3], refs[-3:]
        triples = []
        for slot in range(slots):
            cols = head_columns(kind_ref, first_ref, heads, TEMPORAL, slot)
            for place, out in enumerate(outs):
                held = stage.at[slot, place]
                triples.append((in_ref.at[:, place, slot], held, out.at[:, :, cols]))
        staged_copies(triples, in_sems, out_sems)

    shape = (frames, rows, heads * DH)
    filled = [x.reshape(shape) for x in filled]
    outs = pl.pallas_call(
        kernel,
        out_shape=[jax.ShapeDtypeStruct(shape, BF16)] * 4,
        in_specs=[pl.BlockSpec(memory_space=pltpu.SMEM)] * 2
        + [pl.BlockSpec(memory_space=pl.ANY)] * (1 + len(filled)),
        out_specs=[pl.BlockSpec(memory_space=pl.ANY)] * 4,
        scratch_shapes=[
            pltpu.VMEM((slots, 4, frames, rows, DH), BF16),
            pltpu.SemaphoreType.DMA((total,)),
            pltpu.SemaphoreType.DMA((total,)),
        ],
        input_output_aliases={3 + place: place for place in range(len(filled))},
        compiler_params=pltpu.CompilerParams(vmem_limit_bytes=24 * MIB),
        cost_estimate=cost(0, 4 * rows_in.size),
        name="unpack",
    )(kinds, first, rows_in, *filled)
    return [x.reshape(count, heads * DH) for x in outs]


def passed_along(array, axis, by):
    length = lax.axis_size(axis)
    pairs = [(i, i + by) for i in range(length) if 0 <= i + by < length]
    return lax.ppermute(array, axis, pairs)


def behind(arrays, *others):
    return lax.optimization_barrier((tuple(arrays), others))[0]


def neighbour_rows(ahead, back, frame, framed, results):
    length = lax.axis_size("ctx")
    even = lax.rem(frame[0], 2) == 0
    far = [(i, i - 1 if i % 2 == 0 else i + 1) for i in range(length)]
    far = [pair for pair in far if 0 <= pair[1] < length]
    near = [(i, i + 1 if i % 2 == 0 else i - 1) for i in range(length)]
    near = lax.ppermute(jnp.where(even, ahead, back), "ctx", near)
    distant = jnp.where(even, back, ahead)
    if framed is not None:
        (distant,) = behind([distant], framed)
    far = lax.ppermute(distant, "ctx", far)
    if results is not None:
        near, far = behind((near, far), results)
    return jnp.where(even, far, near), jnp.where(even, near, far)


def branch(slots, heads, kinds, bands, first, frame, q, k, v, g):
    frames, rows, width = q.shape
    count = frames * rows
    others = heads - slots
    exchange = functools.partial(
        lax.all_to_all, axis_name="ctx", split_axis=0, concat_axis=0, tiled=True
    )
    flat = [x.reshape(count, width) for x in (q, k, v, g)]
    packed = []
    filled, framed, results = (), None, None
    if slots > 0:
        packed = [pack_temporal(kinds, first, (q, k, v, g), slots, heads)]
        framed = exchange(*packed)
        results = temporal(kinds, first, bands, framed, heads)
        returned = exchange(results)
    if others > 0:
        ahead, back = pack_spatial(kinds, first, (k, v, q, g), others, heads, packed)
        arrived = neighbour_rows(ahead, back, frame, framed, results)
        prior, following = (x.reshape(others, 2, count, DH) for x in arrived)
        attended, qgrad, own, stats = spatial(kinds, first, frame, flat, prior, heads)
        stats = passed_along(stats, "ctx", -1)
        grads = spatial_next(kinds, first, *flat[1:3], following, stats, own, heads)
        filled = (attended, qgrad, *grads)
    if slots > 0:
        filled = unpack(kinds, first, returned, filled, heads)
    return tuple(filled)


def body(queries, key_rows, value_rows, out_grad, head_kind, frame_band):
    frames = lax.axis_size("ctx")
    count = queries.shape[1]
    heads = queries.shape[2] // DH
    first = lax.axis_index("head").astype(jnp.int32) * heads
    frame = lax.axis_index("ctx").astype(jnp.int32)
    offset = jnp.arange(head_kind.shape[0], dtype=jnp.int32) - first
    here = jnp.logical_and(offset >= 0, offset < heads)
    slots = jnp.sum(jnp.logical_and(here, head_kind == TEMPORAL).astype(jnp.int32))
    arrays = [
        x.reshape(frames, count // frames, heads * DH)
        for x in (queries, key_rows, value_rows, out_grad)
    ]
    outs = lax.switch(
        slots,
        [functools.partial(branch, n, heads) for n in range(heads + 1)],
        head_kind, frame_band, first.reshape(1), frame.reshape(1), *arrays,
    )
    return tuple(out.reshape(queries.shape) for out in outs)


def solution(mesh):
    rows = P("ctx", None, "head")
    return jax.shard_map(
        body,
        mesh=mesh,
        in_specs=(rows, rows, rows, rows, P(), P()),
        out_specs=(rows, rows, rows, rows),
        check_vma=False,
    )
```

```python
import functools
import math

import jax
import jax.numpy as jnp
from jax import lax
from jax.experimental import pallas as pl
from jax.experimental.pallas import tpu as pltpu
from jax.sharding import PartitionSpec as P

DH = 128
SCALE = DH ** (-0.5)
SPATIAL, TEMPORAL = 1, 0
MASKED = -1e30
SCALE_LOG2 = SCALE * math.log2(math.e)
F32 = jnp.float32
BF16 = jnp.bfloat16
MIB = 1024 * 1024


def head_at(kind_ref, first_ref, heads, kind, slot):
    found, seen = jnp.int32(0), jnp.int32(0)
    for head in range(heads):
        hit = kind_ref[first_ref[0] + head] == kind
        found = jnp.where(jnp.logical_and(hit, seen == slot), jnp.int32(head), found)
        seen = seen + hit.astype(jnp.int32)
    return found


def dot_nt(a, b):
    return lax.dot_general(a, b, (((1,), (1,)), ((), ())), preferred_element_type=F32)


def dot_nn(a, b):
    return lax.dot_general(a, b, (((1,), (0,)), ((), ())), preferred_element_type=F32)


def dot_tn(a, b):
    return lax.dot_general(a, b, (((0,), (0,)), ((), ())), preferred_element_type=F32)


def params(mib=32):
    return pltpu.CompilerParams(
        dimension_semantics=("arbitrary",), vmem_limit_bytes=mib * MIB
    )


def cost(flops, moved):
    return pl.CostEstimate(flops=int(flops), bytes_accessed=int(moved), transcendentals=0)


def column_spec(count, heads, kind):
    return pl.BlockSpec((count, DH), lambda i, *refs: (0, head_at(*refs[:2], heads, kind, i)))


def head_columns(kind_ref, first_ref, heads, kind, slot):
    return pl.ds(pl.multiple_of(head_at(kind_ref, first_ref, heads, kind, slot) * DH, DH), DH)


def staged_copies(triples, in_sems, out_sems):
    loads = [pltpu.make_async_copy(x, y, in_sems.at[i]) for i, (x, y, _) in enumerate(triples)]
    stores = [pltpu.make_async_copy(y, z, out_sems.at[i]) for i, (_, y, z) in enumerate(triples)]
    for load in loads:
        load.start()
    for load, store in zip(loads, stores):
        load.wait()
        store.start()
    for store in stores:
        store.wait()


def whole_params():
    return pltpu.CompilerParams(vmem_limit_bytes=62 * MIB)


def pack_spatial(kinds, first, arrays, slots, heads, after):
    frames, rows, _ = arrays[0].shape
    count = len(arrays)
    total = slots * count

    def kernel(kind_ref, first_ref, *refs):
        ins, outs = refs[:count], refs[-3 - count // 2 : -3]
        stage, in_sems, out_sems = refs[-3:]
        triples = []
        for slot in range(slots):
            cols = head_columns(kind_ref, first_ref, heads, SPATIAL, slot)
            for place, ref in enumerate(ins):
                target = outs[place // 2].at[slot, place % 2]
                triples.append((ref.at[:, :, cols], stage.at[slot, place], target))
        staged_copies(triples, in_sems, out_sems)

    return pl.pallas_call(
        kernel,
        out_shape=[jax.ShapeDtypeStruct((slots, 2, frames, rows, DH), BF16)] * (count // 2),
        in_specs=[pl.BlockSpec(memory_space=pltpu.SMEM)] * 2
        + [pl.BlockSpec(memory_space=pl.ANY)] * (count + len(after)),
        out_specs=[pl.BlockSpec(memory_space=pl.ANY)] * (count // 2),
        scratch_shapes=[
            pltpu.VMEM((slots, count, frames, rows, DH), BF16),
            pltpu.SemaphoreType.DMA((total,)),
            pltpu.SemaphoreType.DMA((total,)),
        ],
        compiler_params=whole_params(),
        cost_estimate=cost(0, 4 * total * frames * rows * DH),
        name="pack_spatial",
    )(kinds, first, *arrays, *after)


def pack_temporal(kinds, first, arrays, slots, heads):
    frames, rows, _ = arrays[0].shape
    total = 4 * slots

    def kernel(kind_ref, first_ref, *refs):
        ins, (out, stage, in_sems, out_sems) = refs[:4], refs[4:]
        triples = []
        for slot in range(slots):
            cols = head_columns(kind_ref, first_ref, heads, TEMPORAL, slot)
            for place, ref in enumerate(ins):
                triples.append(
                    (ref.at[:, :, cols], stage.at[slot, place], out.at[:, place, slot])
                )
        staged_copies(triples, in_sems, out_sems)

    return pl.pallas_call(
        kernel,
        out_shape=jax.ShapeDtypeStruct((frames, 4, slots, rows, DH), BF16),
        in_specs=[pl.BlockSpec(memory_space=pltpu.SMEM)] * 2
        + [pl.BlockSpec(memory_space=pl.ANY)] * 4,
        out_specs=pl.BlockSpec(memory_space=pl.ANY),
        scratch_shapes=[
            pltpu.VMEM((slots, 4, frames, rows, DH), BF16),
            pltpu.SemaphoreType.DMA((total,)),
            pltpu.SemaphoreType.DMA((total,)),
        ],
        compiler_params=whole_params(),
        cost_estimate=cost(0, 4 * total * frames * rows * DH),
        name="pack_temporal",
    )(kinds, first, *arrays)


def temporal(kinds, first, bands, rows_in, heads):
    frames, _, slots, rows, _ = rows_in.shape
    group = 16
    size = frames * group

    def frame_at(place):
        return lax.rem(place, 2) * (frames // 2) + lax.div(place, 2)

    def kernel(kind_ref, first_ref, band_ref, rows_ref, result_ref, held, made, in_sems, out_sems):
        def load(slot):
            return pltpu.make_async_copy(rows_ref.at[:, :, slot], held.at[slot], in_sems.at[slot])

        def store(slot):
            return pltpu.make_async_copy(
                made.at[slot], result_ref.at[:, :, slot], out_sems.at[slot]
            )

        for slot in range(slots):
            load(slot).start()

        def work(members):
            for slot in members:
                load(slot).wait()
            some_heads(
                kind_ref, first_ref, band_ref,
                [(slot, held.at[slot], made.at[slot]) for slot in members],
            )
            for slot in members:
                store(slot).start()

        if slots > 1:

            @pl.loop(0, slots // 2)
            def _(pair):
                work([2 * pair, 2 * pair + 1])

        if slots % 2:
            work([slots - 1])
        for slot in range(slots):
            store(slot).wait()

    def some_heads(kind_ref, first_ref, band_ref, members):
        row = lax.broadcasted_iota(jnp.int32, (size, size), 0)
        col = lax.broadcasted_iota(jnp.int32, (size, size), 1)
        same = lax.rem(row, group) == lax.rem(col, group)
        apart = jnp.abs(frame_at(lax.div(row, group)) - frame_at(lax.div(col, group)))
        distance = jnp.where(same, apart, frames)
        parts = [slice(start, start + group) for start in range(0, rows, group)]
        allowed, qs, ks, vs, gs = [], [], [], [], []
        for slot, in_ref, _ in members:
            head = head_at(kind_ref, first_ref, heads, TEMPORAL, slot)
            band = jnp.minimum(band_ref[first_ref[0] + head], frames - 1)
            allowed += [distance <= band] * len(parts)
            for place, rows_of in enumerate((qs, ks, vs, gs)):
                rows_of += [in_ref[:, place, part].reshape(size, DH) for part in parts]
        scores = [
            jnp.where(ok, dot_nt(k, q), MASKED) for ok, q, k in zip(allowed, qs, ks)
        ]
        dprobs = [dot_nt(v, g) for g, v in zip(gs, vs)]
        raised = [
            jnp.exp2((x - jnp.max(x, axis=0, keepdims=True)) * SCALE_LOG2) for x in scores
        ]
        weights = [x * (1.0 / jnp.sum(x, axis=0, keepdims=True)) for x in raised]
        probs = [x.astype(BF16) for x in weights]
        deltas = [jnp.sum(w * dp, axis=0, keepdims=True) for w, dp in zip(weights, dprobs)]
        dscores = [
            (w * (dp - delta) * SCALE).astype(BF16)
            for w, dp, delta in zip(weights, dprobs, deltas)
        ]
        results = (
            [dot_tn(x, v).astype(BF16) for x, v in zip(probs, vs)],
            [dot_tn(x, k).astype(BF16) for x, k in zip(dscores, ks)],
            [dot_nn(x, q).astype(BF16) for x, q in zip(dscores, qs)],
            [dot_nn(x, g).astype(BF16) for x, g in zip(probs, gs)],
        )
        for place, result in enumerate(results):
            targets = [(out_ref, part) for _, _, out_ref in members for part in parts]
            for (out_ref, part), value in zip(targets, result):
                out_ref[:, place, part] = value.reshape(frames, group, DH)

    block = (slots, frames, 4, rows, DH)
    return pl.pallas_call(
        kernel,
        out_shape=jax.ShapeDtypeStruct(rows_in.shape, BF16),
        in_specs=[pl.BlockSpec(memory_space=pltpu.SMEM)] * 3
        + [pl.BlockSpec(memory_space=pl.ANY)],
        out_specs=pl.BlockSpec(memory_space=pl.ANY),
        scratch_shapes=[
            pltpu.VMEM(block, BF16),
            pltpu.VMEM(block, BF16),
            pltpu.SemaphoreType.DMA((slots,)),
            pltpu.SemaphoreType.DMA((slots,)),
        ],
        compiler_params=whole_params(),
        cost_estimate=cost(1e10, 4 * rows_in.size),
        name="temporal",
    )(kinds, first, bands, rows_in)


def spatial(kinds, first, frame, arrays, prior, heads):
    count = arrays[0].shape[0]
    slots = prior.shape[0]
    chunk = min(count, 128)

    def kernel(
        kind_ref, first_ref, frame_ref, q_ref, k_ref, v_ref, g_ref, prior_ref,
        out_ref, qgrad_ref, own_ref, stats_ref,
    ):
        has_prior = frame_ref[0] > 0
        k, v = k_ref[...], v_ref[...]
        k_prior, v_prior = prior_ref[0, 0], prior_ref[0, 1]
        own_ref[...] = jnp.zeros_like(own_ref)

        @pl.loop(0, count // chunk)
        def _(step):
            part = pl.ds(pl.multiple_of(step * chunk, chunk), chunk)
            q, g = q_ref[part], g_ref[part]
            own = dot_nt(k, q)
            before = jnp.where(has_prior, dot_nt(k_prior, q), MASKED)
            top = jnp.maximum(
                jnp.max(own, axis=0, keepdims=True), jnp.max(before, axis=0, keepdims=True)
            )
            own, before = (jnp.exp2((x - top) * SCALE_LOG2) for x in (own, before))
            total = jnp.sum(own, axis=0, keepdims=True) + jnp.sum(before, axis=0, keepdims=True)
            inverse = 1.0 / total
            own, before = own * inverse, before * inverse
            own_dp, before_dp = dot_nt(v, g), dot_nt(v_prior, g)
            delta = jnp.sum(own * own_dp, axis=0, keepdims=True) + jnp.sum(
                before * before_dp, axis=0, keepdims=True
            )
            own_prob, before_prob = own.astype(BF16), before.astype(BF16)
            own_ds = (own * (own_dp - delta) * SCALE).astype(BF16)
            before_ds = (before * (before_dp - delta) * SCALE).astype(BF16)
            out_ref[part] = (dot_tn(own_prob, v) + dot_tn(before_prob, v_prior)).astype(BF16)
            qgrad_ref[part] = (dot_tn(own_ds, k) + dot_tn(before_ds, k_prior)).astype(BF16)
            own_ref[0, 0] += dot_nn(own_ds, q)
            own_ref[0, 1] += dot_nn(own_prob, g)
            stats_ref[0, 0:1, part] = top * SCALE + jnp.log(total)
            stats_ref[0, 1:2, part] = delta

    columns = column_spec(count, heads, SPATIAL)
    pair = pl.BlockSpec((1, 2, count, DH), lambda i, *refs: (i, 0, 0, 0))
    whole = jax.ShapeDtypeStruct((count, heads * DH), BF16)
    return pl.pallas_call(
        kernel,
        out_shape=[
            whole,
            whole,
            jax.ShapeDtypeStruct(prior.shape, F32),
            jax.ShapeDtypeStruct((slots, 2, count), F32),
        ],
        grid_spec=pltpu.PrefetchScalarGridSpec(
            num_scalar_prefetch=3,
            grid=(slots,),
            in_specs=[columns] * 4 + [pair],
            out_specs=[
                columns, columns, pair, pl.BlockSpec((1, 2, count), lambda i, *refs: (i, 0, 0))
            ],
        ),
        compiler_params=params(24),
        cost_estimate=cost(2e11, 16 * slots * count * DH),
        name="spatial",
    )(kinds, first, frame, *arrays, prior)


def spatial_next(kinds, first, k, v, following, stats, own, heads):
    slots, _, count, _ = own.shape
    chunk = min(count, 256)

    def kernel(
        kind_ref, first_ref, k_in, v_in, next_in, stats_in, own_in, k_out, v_out,
        kv_ref, next_ref, stats_ref, own_ref, made_ref, in_sems, out_sems,
    ):
        def loads(slot):
            cols = head_columns(kind_ref, first_ref, heads, SPATIAL, slot)
            pairs = [
                (k_in.at[:, cols], kv_ref.at[slot, 0]),
                (v_in.at[:, cols], kv_ref.at[slot, 1]),
                (next_in.at[slot], next_ref.at[slot]),
                (stats_in.at[slot], stats_ref.at[slot]),
                (own_in.at[slot], own_ref.at[slot]),
            ]
            return [
                pltpu.make_async_copy(*pair, in_sems.at[slot, i]) for i, pair in enumerate(pairs)
            ]

        def stores(slot):
            cols = head_columns(kind_ref, first_ref, heads, SPATIAL, slot)
            return [
                pltpu.make_async_copy(made_ref.at[slot, i], out.at[:, cols], out_sems.at[slot, i])
                for i, out in enumerate((k_out, v_out))
            ]

        for slot in range(slots):
            for copy in loads(slot):
                copy.start()

        @pl.loop(0, slots)
        def _(slot):
            for copy in loads(slot):
                copy.wait()
            q, g = next_ref[slot, 0], next_ref[slot, 1]
            lse, delta = stats_ref[slot, 0:1] * math.log2(math.e), stats_ref[slot, 1:2]
            for start in range(0, count, chunk):
                part = slice(start, start + chunk)
                weight = jnp.exp2(dot_nt(kv_ref[slot, 0, part], q) * SCALE_LOG2 - lse)
                slope = (weight * (dot_nt(kv_ref[slot, 1, part], g) - delta)).astype(BF16)
                made_ref[slot, 0, part] = (
                    own_ref[slot, 0, part] + dot_nn(slope, q) * SCALE
                ).astype(BF16)
                made_ref[slot, 1, part] = (
                    own_ref[slot, 1, part] + dot_nn(weight.astype(BF16), g)
                ).astype(BF16)
            for copy in stores(slot):
                copy.start()

        for slot in range(slots):
            for copy in stores(slot):
                copy.wait()

    return pl.pallas_call(
        kernel,
        out_shape=[jax.ShapeDtypeStruct(k.shape, BF16)] * 2,
        in_specs=[pl.BlockSpec(memory_space=pltpu.SMEM)] * 2
        + [pl.BlockSpec(memory_space=pl.ANY)] * 5,
        out_specs=[pl.BlockSpec(memory_space=pl.ANY)] * 2,
        scratch_shapes=[
            pltpu.VMEM((slots, 2, count, DH), BF16),
            pltpu.VMEM((slots, 2, count, DH), BF16),
            pltpu.VMEM((slots, 2, count), F32),
            pltpu.VMEM((slots, 2, count, DH), F32),
            pltpu.VMEM((slots, 2, count, DH), BF16),
            pltpu.SemaphoreType.DMA((slots, 5)),
            pltpu.SemaphoreType.DMA((slots, 2)),
        ],
        compiler_params=pltpu.CompilerParams(vmem_limit_bytes=24 * MIB),
        cost_estimate=cost(8 * slots * count * count * DH, 20 * slots * count * DH),
        name="spatial_next",
    )(kinds, first, k, v, following, stats, own)


def unpack(kinds, first, rows_in, filled, heads):
    frames, _, slots, rows, _ = rows_in.shape
    count = frames * rows
    total = 4 * slots

    def kernel(kind_ref, first_ref, in_ref, *refs):
        outs, (stage, in_sems, out_sems) = refs[-7:-3], refs[-3:]
        triples = []
        for slot in range(slots):
            cols = head_columns(kind_ref, first_ref, heads, TEMPORAL, slot)
            for place, out in enumerate(outs):
                held = stage.at[slot, place]
                triples.append((in_ref.at[:, place, slot], held, out.at[:, :, cols]))
        staged_copies(triples, in_sems, out_sems)

    shape = (frames, rows, heads * DH)
    filled = [x.reshape(shape) for x in filled]
    outs = pl.pallas_call(
        kernel,
        out_shape=[jax.ShapeDtypeStruct(shape, BF16)] * 4,
        in_specs=[pl.BlockSpec(memory_space=pltpu.SMEM)] * 2
        + [pl.BlockSpec(memory_space=pl.ANY)] * (1 + len(filled)),
        out_specs=[pl.BlockSpec(memory_space=pl.ANY)] * 4,
        scratch_shapes=[
            pltpu.VMEM((slots, 4, frames, rows, DH), BF16),
            pltpu.SemaphoreType.DMA((total,)),
            pltpu.SemaphoreType.DMA((total,)),
        ],
        input_output_aliases={3 + place: place for place in range(len(filled))},
        compiler_params=pltpu.CompilerParams(vmem_limit_bytes=24 * MIB),
        cost_estimate=cost(0, 4 * rows_in.size),
        name="unpack",
    )(kinds, first, rows_in, *filled)
    return [x.reshape(count, heads * DH) for x in outs]


def passed_along(array, axis, by):
    length = lax.axis_size(axis)
    pairs = [(i, i + by) for i in range(length) if 0 <= i + by < length]
    return lax.ppermute(array, axis, pairs)


def behind(arrays, *others):
    return lax.optimization_barrier((tuple(arrays), others))[0]


def neighbour_rows(ahead, back, frame, results):
    length = lax.axis_size("ctx")
    even = lax.rem(frame[0], 2) == 0
    far = [(i, i - 1 if i % 2 == 0 else i + 1) for i in range(length)]
    far = [pair for pair in far if 0 <= pair[1] < length]
    near = [(i, i + 1 if i % 2 == 0 else i - 1) for i in range(length)]
    near = lax.ppermute(jnp.where(even, ahead, back), "ctx", near)
    far = lax.ppermute(jnp.where(even, back, ahead), "ctx", far)
    if results is not None:
        near, far = behind((near, far), results)
    return jnp.where(even, far, near), jnp.where(even, near, far)


def exchange_order(frames):
    return [half * (frames // 2) + place for place in range(frames // 2) for half in (0, 1)]


def branch(slots, heads, kinds, bands, first, frame, q, k, v, g):
    frames, rows, width = q.shape
    count = frames * rows
    others = heads - slots
    exchange = functools.partial(
        lax.all_to_all, axis_name="ctx", split_axis=0, concat_axis=0, tiled=True,
        axis_index_groups=[exchange_order(frames)],
    )
    flat = [x.reshape(count, width) for x in (q, k, v, g)]
    packed = []
    filled, results = (), None
    if slots > 0:
        packed = [pack_temporal(kinds, first, (q, k, v, g), slots, heads)]
        framed = exchange(*packed)
        results = temporal(kinds, first, bands, framed, heads)
        returned = exchange(results)
    if others > 0:
        ahead, back = pack_spatial(kinds, first, (k, v, q, g), others, heads, packed)
        arrived = neighbour_rows(ahead, back, frame, results)
        prior, following = (x.reshape(others, 2, count, DH) for x in arrived)
        attended, qgrad, own, stats = spatial(kinds, first, frame, flat, prior, heads)
        stats = passed_along(stats, "ctx", -1)
        grads = spatial_next(kinds, first, *flat[1:3], following, stats, own, heads)
        filled = (attended, qgrad, *grads)
    if slots > 0:
        filled = unpack(kinds, first, returned, filled, heads)
    return tuple(filled)


def body(queries, key_rows, value_rows, out_grad, head_kind, frame_band):
    frames = lax.axis_size("ctx")
    count = queries.shape[1]
    heads = queries.shape[2] // DH
    first = lax.axis_index("head").astype(jnp.int32) * heads
    frame = lax.axis_index("ctx").astype(jnp.int32)
    offset = jnp.arange(head_kind.shape[0], dtype=jnp.int32) - first
    here = jnp.logical_and(offset >= 0, offset < heads)
    slots = jnp.sum(jnp.logical_and(here, head_kind == TEMPORAL).astype(jnp.int32))
    arrays = [
        x.reshape(frames, count // frames, heads * DH)
        for x in (queries, key_rows, value_rows, out_grad)
    ]
    outs = lax.switch(
        slots,
        [functools.partial(branch, n, heads) for n in range(heads + 1)],
        head_kind, frame_band, first.reshape(1), frame.reshape(1), *arrays,
    )
    return tuple(out.reshape(queries.shape) for out in outs)


def solution(mesh):
    rows = P("ctx", None, "head")
    return jax.shard_map(
        body,
        mesh=mesh,
        in_specs=(rows, rows, rows, rows, P(), P()),
        out_specs=(rows, rows, rows, rows),
        check_vma=False,
    )
```

```python
import functools
import math

import jax
import jax.numpy as jnp
from jax import lax
from jax.experimental import pallas as pl
from jax.experimental.pallas import tpu as pltpu
from jax.sharding import PartitionSpec as P

DH = 128
SCALE = DH ** (-0.5)
SPATIAL, TEMPORAL = 1, 0
MASKED = -1e30
SCALE_LOG2 = SCALE * math.log2(math.e)
F32 = jnp.float32
BF16 = jnp.bfloat16
MIB = 1024 * 1024


def head_at(kind_ref, first_ref, heads, kind, slot):
    found, seen = jnp.int32(0), jnp.int32(0)
    for head in range(heads):
        hit = kind_ref[first_ref[0] + head] == kind
        found = jnp.where(jnp.logical_and(hit, seen == slot), jnp.int32(head), found)
        seen = seen + hit.astype(jnp.int32)
    return found


def dot_nt(a, b):
    return lax.dot_general(a, b, (((1,), (1,)), ((), ())), preferred_element_type=F32)


def dot_nn(a, b):
    return lax.dot_general(a, b, (((1,), (0,)), ((), ())), preferred_element_type=F32)


def dot_tn(a, b):
    return lax.dot_general(a, b, (((0,), (0,)), ((), ())), preferred_element_type=F32)


def params(mib=32):
    return pltpu.CompilerParams(
        dimension_semantics=("arbitrary",), vmem_limit_bytes=mib * MIB
    )


def cost(flops, moved):
    return pl.CostEstimate(flops=int(flops), bytes_accessed=int(moved), transcendentals=0)


def column_spec(count, heads, kind):
    return pl.BlockSpec((count, DH), lambda i, *refs: (0, head_at(*refs[:2], heads, kind, i)))


def head_columns(kind_ref, first_ref, heads, kind, slot):
    return pl.ds(pl.multiple_of(head_at(kind_ref, first_ref, heads, kind, slot) * DH, DH), DH)


def staged_copies(triples, in_sems, out_sems):
    loads = [pltpu.make_async_copy(x, y, in_sems.at[i]) for i, (x, y, _) in enumerate(triples)]
    stores = [pltpu.make_async_copy(y, z, out_sems.at[i]) for i, (_, y, z) in enumerate(triples)]
    for load in loads:
        load.start()
    for load, store in zip(loads, stores):
        load.wait()
        store.start()
    for store in stores:
        store.wait()


def whole_params():
    return pltpu.CompilerParams(vmem_limit_bytes=62 * MIB)


def pack_spatial(kinds, first, arrays, slots, heads, after):
    frames, rows, _ = arrays[0].shape
    count = len(arrays)
    total = slots * count

    def kernel(kind_ref, first_ref, *refs):
        ins, outs = refs[:count], refs[-3 - count // 2 : -3]
        stage, in_sems, out_sems = refs[-3:]
        triples = []
        for slot in range(slots):
            cols = head_columns(kind_ref, first_ref, heads, SPATIAL, slot)
            for place, ref in enumerate(ins):
                target = outs[place // 2].at[slot, place % 2]
                triples.append((ref.at[:, :, cols], stage.at[slot, place], target))
        staged_copies(triples, in_sems, out_sems)

    return pl.pallas_call(
        kernel,
        out_shape=[jax.ShapeDtypeStruct((slots, 2, frames, rows, DH), BF16)] * (count // 2),
        in_specs=[pl.BlockSpec(memory_space=pltpu.SMEM)] * 2
        + [pl.BlockSpec(memory_space=pl.ANY)] * (count + len(after)),
        out_specs=[pl.BlockSpec(memory_space=pl.ANY)] * (count // 2),
        scratch_shapes=[
            pltpu.VMEM((slots, count, frames, rows, DH), BF16),
            pltpu.SemaphoreType.DMA((total,)),
            pltpu.SemaphoreType.DMA((total,)),
        ],
        compiler_params=whole_params(),
        cost_estimate=cost(0, 4 * total * frames * rows * DH),
        name="pack_spatial",
    )(kinds, first, *arrays, *after)


def pack_temporal(kinds, first, arrays, slots, heads):
    frames, rows, _ = arrays[0].shape
    total = 4 * slots

    def kernel(kind_ref, first_ref, *refs):
        ins, (out, stage, in_sems, out_sems) = refs[:4], refs[4:]
        triples = []
        for slot in range(slots):
            cols = head_columns(kind_ref, first_ref, heads, TEMPORAL, slot)
            for place, ref in enumerate(ins):
                triples.append(
                    (ref.at[:, :, cols], stage.at[slot, place], out.at[:, place, slot])
                )
        staged_copies(triples, in_sems, out_sems)

    return pl.pallas_call(
        kernel,
        out_shape=jax.ShapeDtypeStruct((frames, 4, slots, rows, DH), BF16),
        in_specs=[pl.BlockSpec(memory_space=pltpu.SMEM)] * 2
        + [pl.BlockSpec(memory_space=pl.ANY)] * 4,
        out_specs=pl.BlockSpec(memory_space=pl.ANY),
        scratch_shapes=[
            pltpu.VMEM((slots, 4, frames, rows, DH), BF16),
            pltpu.SemaphoreType.DMA((total,)),
            pltpu.SemaphoreType.DMA((total,)),
        ],
        compiler_params=whole_params(),
        cost_estimate=cost(0, 4 * total * frames * rows * DH),
        name="pack_temporal",
    )(kinds, first, *arrays)


def temporal(kinds, first, bands, rows_in, heads):
    frames, _, slots, rows, _ = rows_in.shape
    group = 16
    size = frames * group

    def frame_at(place):
        half = frames // 2
        return place + (place == half - 1).astype(jnp.int32) - (place == half).astype(jnp.int32)

    def kernel(kind_ref, first_ref, band_ref, rows_ref, result_ref, held, made, in_sems, out_sems):
        def load(slot):
            return pltpu.make_async_copy(rows_ref.at[:, :, slot], held.at[slot], in_sems.at[slot])

        def store(slot):
            return pltpu.make_async_copy(
                made.at[slot], result_ref.at[:, :, slot], out_sems.at[slot]
            )

        for slot in range(slots):
            load(slot).start()

        def work(members):
            for slot in members:
                load(slot).wait()
            some_heads(
                kind_ref, first_ref, band_ref,
                [(slot, held.at[slot], made.at[slot]) for slot in members],
            )
            for slot in members:
                store(slot).start()

        if slots > 1:

            @pl.loop(0, slots // 2)
            def _(pair):
                work([2 * pair, 2 * pair + 1])

        if slots % 2:
            work([slots - 1])
        for slot in range(slots):
            store(slot).wait()

    def some_heads(kind_ref, first_ref, band_ref, members):
        row = lax.broadcasted_iota(jnp.int32, (size, size), 0)
        col = lax.broadcasted_iota(jnp.int32, (size, size), 1)
        same = lax.rem(row, group) == lax.rem(col, group)
        apart = jnp.abs(frame_at(lax.div(row, group)) - frame_at(lax.div(col, group)))
        distance = jnp.where(same, apart, frames)
        parts = [slice(start, start + group) for start in range(0, rows, group)]
        allowed, qs, ks, vs, gs = [], [], [], [], []
        for slot, in_ref, _ in members:
            head = head_at(kind_ref, first_ref, heads, TEMPORAL, slot)
            band = jnp.minimum(band_ref[first_ref[0] + head], frames - 1)
            allowed += [distance <= band] * len(parts)
            for place, rows_of in enumerate((qs, ks, vs, gs)):
                rows_of += [in_ref[:, place, part].reshape(size, DH) for part in parts]
        scores = [
            jnp.where(ok, dot_nt(k, q), MASKED) for ok, q, k in zip(allowed, qs, ks)
        ]
        dprobs = [dot_nt(v, g) for g, v in zip(gs, vs)]
        raised = [
            jnp.exp2((x - jnp.max(x, axis=0, keepdims=True)) * SCALE_LOG2) for x in scores
        ]
        weights = [x * (1.0 / jnp.sum(x, axis=0, keepdims=True)) for x in raised]
        probs = [x.astype(BF16) for x in weights]
        deltas = [jnp.sum(w * dp, axis=0, keepdims=True) for w, dp in zip(weights, dprobs)]
        dscores = [
            (w * (dp - delta) * SCALE).astype(BF16)
            for w, dp, delta in zip(weights, dprobs, deltas)
        ]
        results = (
            [dot_tn(x, v).astype(BF16) for x, v in zip(probs, vs)],
            [dot_tn(x, k).astype(BF16) for x, k in zip(dscores, ks)],
            [dot_nn(x, q).astype(BF16) for x, q in zip(dscores, qs)],
            [dot_nn(x, g).astype(BF16) for x, g in zip(probs, gs)],
        )
        for place, result in enumerate(results):
            targets = [(out_ref, part) for _, _, out_ref in members for part in parts]
            for (out_ref, part), value in zip(targets, result):
                out_ref[:, place, part] = value.reshape(frames, group, DH)

    block = (slots, frames, 4, rows, DH)
    return pl.pallas_call(
        kernel,
        out_shape=jax.ShapeDtypeStruct(rows_in.shape, BF16),
        in_specs=[pl.BlockSpec(memory_space=pltpu.SMEM)] * 3
        + [pl.BlockSpec(memory_space=pl.ANY)],
        out_specs=pl.BlockSpec(memory_space=pl.ANY),
        scratch_shapes=[
            pltpu.VMEM(block, BF16),
            pltpu.VMEM(block, BF16),
            pltpu.SemaphoreType.DMA((slots,)),
            pltpu.SemaphoreType.DMA((slots,)),
        ],
        compiler_params=whole_params(),
        cost_estimate=cost(1e10, 4 * rows_in.size),
        name="temporal",
    )(kinds, first, bands, rows_in)


def spatial(kinds, first, frame, arrays, prior, heads):
    count = arrays[0].shape[0]
    slots = prior.shape[0]
    chunk = min(count, 128)

    def kernel(
        kind_ref, first_ref, frame_ref, q_ref, k_ref, v_ref, g_ref, prior_ref,
        out_ref, qgrad_ref, own_ref, stats_ref,
    ):
        has_prior = frame_ref[0] > 0
        k, v = k_ref[...], v_ref[...]
        k_prior, v_prior = prior_ref[0, 0], prior_ref[0, 1]
        own_ref[...] = jnp.zeros_like(own_ref)

        @pl.loop(0, count // chunk)
        def _(step):
            part = pl.ds(pl.multiple_of(step * chunk, chunk), chunk)
            q, g = q_ref[part], g_ref[part]
            own = dot_nt(k, q)
            before = jnp.where(has_prior, dot_nt(k_prior, q), MASKED)
            top = jnp.maximum(
                jnp.max(own, axis=0, keepdims=True), jnp.max(before, axis=0, keepdims=True)
            )
            own, before = (jnp.exp2((x - top) * SCALE_LOG2) for x in (own, before))
            total = jnp.sum(own, axis=0, keepdims=True) + jnp.sum(before, axis=0, keepdims=True)
            inverse = 1.0 / total
            own, before = own * inverse, before * inverse
            own_dp, before_dp = dot_nt(v, g), dot_nt(v_prior, g)
            delta = jnp.sum(own * own_dp, axis=0, keepdims=True) + jnp.sum(
                before * before_dp, axis=0, keepdims=True
            )
            own_prob, before_prob = own.astype(BF16), before.astype(BF16)
            own_ds = (own * (own_dp - delta) * SCALE).astype(BF16)
            before_ds = (before * (before_dp - delta) * SCALE).astype(BF16)
            out_ref[part] = (dot_tn(own_prob, v) + dot_tn(before_prob, v_prior)).astype(BF16)
            qgrad_ref[part] = (dot_tn(own_ds, k) + dot_tn(before_ds, k_prior)).astype(BF16)
            own_ref[0, 0] += dot_nn(own_ds, q)
            own_ref[0, 1] += dot_nn(own_prob, g)
            stats_ref[0, 0:1, part] = top * SCALE + jnp.log(total)
            stats_ref[0, 1:2, part] = delta

    columns = column_spec(count, heads, SPATIAL)
    pair = pl.BlockSpec((1, 2, count, DH), lambda i, *refs: (i, 0, 0, 0))
    whole = jax.ShapeDtypeStruct((count, heads * DH), BF16)
    return pl.pallas_call(
        kernel,
        out_shape=[
            whole,
            whole,
            jax.ShapeDtypeStruct(prior.shape, F32),
            jax.ShapeDtypeStruct((slots, 2, count), F32),
        ],
        grid_spec=pltpu.PrefetchScalarGridSpec(
            num_scalar_prefetch=3,
            grid=(slots,),
            in_specs=[columns] * 4 + [pair],
            out_specs=[
                columns, columns, pair, pl.BlockSpec((1, 2, count), lambda i, *refs: (i, 0, 0))
            ],
        ),
        compiler_params=params(24),
        cost_estimate=cost(2e11, 16 * slots * count * DH),
        name="spatial",
    )(kinds, first, frame, *arrays, prior)


def spatial_next(kinds, first, k, v, following, stats, own, heads):
    slots, _, count, _ = own.shape
    chunk = min(count, 256)

    def kernel(
        kind_ref, first_ref, k_in, v_in, next_in, stats_in, own_in, k_out, v_out,
        kv_ref, next_ref, stats_ref, own_ref, made_ref, in_sems, out_sems,
    ):
        def loads(slot):
            cols = head_columns(kind_ref, first_ref, heads, SPATIAL, slot)
            pairs = [
                (k_in.at[:, cols], kv_ref.at[slot, 0]),
                (v_in.at[:, cols], kv_ref.at[slot, 1]),
                (next_in.at[slot], next_ref.at[slot]),
                (stats_in.at[slot], stats_ref.at[slot]),
                (own_in.at[slot], own_ref.at[slot]),
            ]
            return [
                pltpu.make_async_copy(*pair, in_sems.at[slot, i]) for i, pair in enumerate(pairs)
            ]

        def stores(slot):
            cols = head_columns(kind_ref, first_ref, heads, SPATIAL, slot)
            return [
                pltpu.make_async_copy(made_ref.at[slot, i], out.at[:, cols], out_sems.at[slot, i])
                for i, out in enumerate((k_out, v_out))
            ]

        for slot in range(slots):
            for copy in loads(slot):
                copy.start()

        @pl.loop(0, slots)
        def _(slot):
            for copy in loads(slot):
                copy.wait()
            q, g = next_ref[slot, 0], next_ref[slot, 1]
            lse, delta = stats_ref[slot, 0:1] * math.log2(math.e), stats_ref[slot, 1:2]
            for start in range(0, count, chunk):
                part = slice(start, start + chunk)
                weight = jnp.exp2(dot_nt(kv_ref[slot, 0, part], q) * SCALE_LOG2 - lse)
                slope = (weight * (dot_nt(kv_ref[slot, 1, part], g) - delta)).astype(BF16)
                made_ref[slot, 0, part] = (
                    own_ref[slot, 0, part] + dot_nn(slope, q) * SCALE
                ).astype(BF16)
                made_ref[slot, 1, part] = (
                    own_ref[slot, 1, part] + dot_nn(weight.astype(BF16), g)
                ).astype(BF16)
            for copy in stores(slot):
                copy.start()

        for slot in range(slots):
            for copy in stores(slot):
                copy.wait()

    return pl.pallas_call(
        kernel,
        out_shape=[jax.ShapeDtypeStruct(k.shape, BF16)] * 2,
        in_specs=[pl.BlockSpec(memory_space=pltpu.SMEM)] * 2
        + [pl.BlockSpec(memory_space=pl.ANY)] * 5,
        out_specs=[pl.BlockSpec(memory_space=pl.ANY)] * 2,
        scratch_shapes=[
            pltpu.VMEM((slots, 2, count, DH), BF16),
            pltpu.VMEM((slots, 2, count, DH), BF16),
            pltpu.VMEM((slots, 2, count), F32),
            pltpu.VMEM((slots, 2, count, DH), F32),
            pltpu.VMEM((slots, 2, count, DH), BF16),
            pltpu.SemaphoreType.DMA((slots, 5)),
            pltpu.SemaphoreType.DMA((slots, 2)),
        ],
        compiler_params=pltpu.CompilerParams(vmem_limit_bytes=24 * MIB),
        cost_estimate=cost(8 * slots * count * count * DH, 20 * slots * count * DH),
        name="spatial_next",
    )(kinds, first, k, v, following, stats, own)


def unpack(kinds, first, rows_in, filled, heads):
    frames, _, slots, rows, _ = rows_in.shape
    count = frames * rows
    total = 4 * slots

    def kernel(kind_ref, first_ref, in_ref, *refs):
        outs, (stage, in_sems, out_sems) = refs[-7:-3], refs[-3:]
        triples = []
        for slot in range(slots):
            cols = head_columns(kind_ref, first_ref, heads, TEMPORAL, slot)
            for place, out in enumerate(outs):
                held = stage.at[slot, place]
                triples.append((in_ref.at[:, place, slot], held, out.at[:, :, cols]))
        staged_copies(triples, in_sems, out_sems)

    shape = (frames, rows, heads * DH)
    filled = [x.reshape(shape) for x in filled]
    outs = pl.pallas_call(
        kernel,
        out_shape=[jax.ShapeDtypeStruct(shape, BF16)] * 4,
        in_specs=[pl.BlockSpec(memory_space=pltpu.SMEM)] * 2
        + [pl.BlockSpec(memory_space=pl.ANY)] * (1 + len(filled)),
        out_specs=[pl.BlockSpec(memory_space=pl.ANY)] * 4,
        scratch_shapes=[
            pltpu.VMEM((slots, 4, frames, rows, DH), BF16),
            pltpu.SemaphoreType.DMA((total,)),
            pltpu.SemaphoreType.DMA((total,)),
        ],
        input_output_aliases={3 + place: place for place in range(len(filled))},
        compiler_params=pltpu.CompilerParams(vmem_limit_bytes=24 * MIB),
        cost_estimate=cost(0, 4 * rows_in.size),
        name="unpack",
    )(kinds, first, rows_in, *filled)
    return [x.reshape(count, heads * DH) for x in outs]


def passed_along(array, axis, by):
    length = lax.axis_size(axis)
    pairs = [(i, i + by) for i in range(length) if 0 <= i + by < length]
    return lax.ppermute(array, axis, pairs)


def behind(arrays, *others):
    return lax.optimization_barrier((tuple(arrays), others))[0]


def neighbour_rows(ahead, back, frame, results):
    length = lax.axis_size("ctx")
    even = lax.rem(frame[0], 2) == 0
    far = [(i, i - 1 if i % 2 == 0 else i + 1) for i in range(length)]
    far = [pair for pair in far if 0 <= pair[1] < length]
    near = [(i, i + 1 if i % 2 == 0 else i - 1) for i in range(length)]
    near = lax.ppermute(jnp.where(even, ahead, back), "ctx", near)
    far = lax.ppermute(jnp.where(even, back, ahead), "ctx", far)
    if results is not None:
        near, far = behind((near, far), results)
    return jnp.where(even, far, near), jnp.where(even, near, far)


def exchange_order(frames):
    half = frames // 2
    return [*range(half - 1), half, half - 1, *range(half + 1, frames)]


def branch(slots, heads, kinds, bands, first, frame, q, k, v, g):
    frames, rows, width = q.shape
    count = frames * rows
    others = heads - slots
    exchange = functools.partial(
        lax.all_to_all, axis_name="ctx", split_axis=0, concat_axis=0, tiled=True,
        axis_index_groups=[exchange_order(frames)],
    )
    flat = [x.reshape(count, width) for x in (q, k, v, g)]
    packed = []
    filled, results = (), None
    if slots > 0:
        packed = [pack_temporal(kinds, first, (q, k, v, g), slots, heads)]
        framed = exchange(*packed)
        results = temporal(kinds, first, bands, framed, heads)
        returned = exchange(results)
    if others > 0:
        ahead, back = pack_spatial(kinds, first, (k, v, q, g), others, heads, packed)
        arrived = neighbour_rows(ahead, back, frame, results)
        prior, following = (x.reshape(others, 2, count, DH) for x in arrived)
        attended, qgrad, own, stats = spatial(kinds, first, frame, flat, prior, heads)
        stats = passed_along(stats, "ctx", -1)
        grads = spatial_next(kinds, first, *flat[1:3], following, stats, own, heads)
        filled = (attended, qgrad, *grads)
    if slots > 0:
        filled = unpack(kinds, first, returned, filled, heads)
    return tuple(filled)


def body(queries, key_rows, value_rows, out_grad, head_kind, frame_band):
    frames = lax.axis_size("ctx")
    count = queries.shape[1]
    heads = queries.shape[2] // DH
    first = lax.axis_index("head").astype(jnp.int32) * heads
    frame = lax.axis_index("ctx").astype(jnp.int32)
    offset = jnp.arange(head_kind.shape[0], dtype=jnp.int32) - first
    here = jnp.logical_and(offset >= 0, offset < heads)
    slots = jnp.sum(jnp.logical_and(here, head_kind == TEMPORAL).astype(jnp.int32))
    arrays = [
        x.reshape(frames, count // frames, heads * DH)
        for x in (queries, key_rows, value_rows, out_grad)
    ]
    outs = lax.switch(
        slots,
        [functools.partial(branch, n, heads) for n in range(heads + 1)],
        head_kind, frame_band, first.reshape(1), frame.reshape(1), *arrays,
    )
    return tuple(out.reshape(queries.shape) for out in outs)


def solution(mesh):
    rows = P("ctx", None, "head")
    return jax.shard_map(
        body,
        mesh=mesh,
        in_specs=(rows, rows, rows, rows, P(), P()),
        out_specs=(rows, rows, rows, rows),
        check_vma=False,
    )
```

```python
import functools
import math

import jax
import jax.numpy as jnp
from jax import lax
from jax.experimental import pallas as pl
from jax.experimental.pallas import tpu as pltpu
from jax.sharding import PartitionSpec as P

DH = 128
SCALE = DH ** (-0.5)
SPATIAL, TEMPORAL = 1, 0
MASKED = -1e30
SCALE_LOG2 = SCALE * math.log2(math.e)
F32 = jnp.float32
BF16 = jnp.bfloat16
MIB = 1024 * 1024


def head_at(kind_ref, first_ref, heads, kind, slot):
    found, seen = jnp.int32(0), jnp.int32(0)
    for head in range(heads):
        hit = kind_ref[first_ref[0] + head] == kind
        found = jnp.where(jnp.logical_and(hit, seen == slot), jnp.int32(head), found)
        seen = seen + hit.astype(jnp.int32)
    return found


def dot_nt(a, b):
    return lax.dot_general(a, b, (((1,), (1,)), ((), ())), preferred_element_type=F32)


def dot_nn(a, b):
    return lax.dot_general(a, b, (((1,), (0,)), ((), ())), preferred_element_type=F32)


def dot_tn(a, b):
    return lax.dot_general(a, b, (((0,), (0,)), ((), ())), preferred_element_type=F32)


def params(mib=32):
    return pltpu.CompilerParams(
        dimension_semantics=("arbitrary",), vmem_limit_bytes=mib * MIB
    )


def cost(flops, moved):
    return pl.CostEstimate(flops=int(flops), bytes_accessed=int(moved), transcendentals=0)


def column_spec(count, heads, kind):
    return pl.BlockSpec((count, DH), lambda i, *refs: (0, head_at(*refs[:2], heads, kind, i)))


def head_columns(kind_ref, first_ref, heads, kind, slot):
    return pl.ds(pl.multiple_of(head_at(kind_ref, first_ref, heads, kind, slot) * DH, DH), DH)


def staged_copies(triples, in_sems, out_sems):
    loads = [pltpu.make_async_copy(x, y, in_sems.at[i]) for i, (x, y, _) in enumerate(triples)]
    stores = [pltpu.make_async_copy(y, z, out_sems.at[i]) for i, (_, y, z) in enumerate(triples)]
    for load in loads:
        load.start()
    for load, store in zip(loads, stores):
        load.wait()
        store.start()
    for store in stores:
        store.wait()


def whole_params():
    return pltpu.CompilerParams(vmem_limit_bytes=62 * MIB)


def pack_spatial(kinds, first, arrays, slots, heads, after):
    frames, rows, _ = arrays[0].shape
    count = len(arrays)
    total = slots * count

    def kernel(kind_ref, first_ref, *refs):
        ins, outs = refs[:count], refs[-3 - count // 2 : -3]
        stage, in_sems, out_sems = refs[-3:]
        triples = []
        for slot in range(slots):
            cols = head_columns(kind_ref, first_ref, heads, SPATIAL, slot)
            for place, ref in enumerate(ins):
                target = outs[place // 2].at[slot, place % 2]
                triples.append((ref.at[:, :, cols], stage.at[slot, place], target))
        staged_copies(triples, in_sems, out_sems)

    return pl.pallas_call(
        kernel,
        out_shape=[jax.ShapeDtypeStruct((slots, 2, frames, rows, DH), BF16)] * (count // 2),
        in_specs=[pl.BlockSpec(memory_space=pltpu.SMEM)] * 2
        + [pl.BlockSpec(memory_space=pl.ANY)] * (count + len(after)),
        out_specs=[pl.BlockSpec(memory_space=pl.ANY)] * (count // 2),
        scratch_shapes=[
            pltpu.VMEM((slots, count, frames, rows, DH), BF16),
            pltpu.SemaphoreType.DMA((total,)),
            pltpu.SemaphoreType.DMA((total,)),
        ],
        compiler_params=whole_params(),
        cost_estimate=cost(0, 4 * total * frames * rows * DH),
        name="pack_spatial",
    )(kinds, first, *arrays, *after)


def pack_temporal(kinds, first, arrays, slots, heads):
    frames, rows, _ = arrays[0].shape
    total = 4 * slots

    def kernel(kind_ref, first_ref, *refs):
        ins, (out, stage, in_sems, out_sems) = refs[:4], refs[4:]
        triples = []
        for slot in range(slots):
            cols = head_columns(kind_ref, first_ref, heads, TEMPORAL, slot)
            for place, ref in enumerate(ins):
                triples.append(
                    (ref.at[:, :, cols], stage.at[slot, place], out.at[:, place, slot])
                )
        staged_copies(triples, in_sems, out_sems)

    return pl.pallas_call(
        kernel,
        out_shape=jax.ShapeDtypeStruct((frames, 4, slots, rows, DH), BF16),
        in_specs=[pl.BlockSpec(memory_space=pltpu.SMEM)] * 2
        + [pl.BlockSpec(memory_space=pl.ANY)] * 4,
        out_specs=pl.BlockSpec(memory_space=pl.ANY),
        scratch_shapes=[
            pltpu.VMEM((slots, 4, frames, rows, DH), BF16),
            pltpu.SemaphoreType.DMA((total,)),
            pltpu.SemaphoreType.DMA((total,)),
        ],
        compiler_params=whole_params(),
        cost_estimate=cost(0, 4 * total * frames * rows * DH),
        name="pack_temporal",
    )(kinds, first, *arrays)


def temporal(kinds, first, bands, rows_in, heads):
    frames, _, slots, rows, _ = rows_in.shape
    group = 16
    size = frames * group

    def frame_at(place):
        half = frames // 2
        return place + (place == half - 1).astype(jnp.int32) - (place == half).astype(jnp.int32)

    def kernel(kind_ref, first_ref, band_ref, rows_ref, result_ref, held, made, in_sems, out_sems):
        def load(slot):
            return pltpu.make_async_copy(rows_ref.at[:, :, slot], held.at[slot], in_sems.at[slot])

        def store(slot):
            return pltpu.make_async_copy(
                made.at[slot], result_ref.at[:, :, slot], out_sems.at[slot]
            )

        for slot in range(slots):
            load(slot).start()

        def work(members):
            for slot in members:
                load(slot).wait()
            some_heads(
                kind_ref, first_ref, band_ref,
                [(slot, held.at[slot], made.at[slot]) for slot in members],
            )
            for slot in members:
                store(slot).start()

        if slots > 1:

            @pl.loop(0, slots // 2)
            def _(pair):
                work([2 * pair, 2 * pair + 1])

        if slots % 2:
            work([slots - 1])
        for slot in range(slots):
            store(slot).wait()

    def some_heads(kind_ref, first_ref, band_ref, members):
        row = lax.broadcasted_iota(jnp.int32, (size, size), 0)
        col = lax.broadcasted_iota(jnp.int32, (size, size), 1)
        same = lax.rem(row, group) == lax.rem(col, group)
        apart = jnp.abs(frame_at(lax.div(row, group)) - frame_at(lax.div(col, group)))
        distance = jnp.where(same, apart, frames)
        parts = [slice(start, start + group) for start in range(0, rows, group)]
        allowed, qs, ks, vs, gs = [], [], [], [], []
        for slot, in_ref, _ in members:
            head = head_at(kind_ref, first_ref, heads, TEMPORAL, slot)
            band = jnp.minimum(band_ref[first_ref[0] + head], frames - 1)
            allowed += [distance <= band] * len(parts)
            for place, rows_of in enumerate((qs, ks, vs, gs)):
                rows_of += [in_ref[:, place, part].reshape(size, DH) for part in parts]
        scores = [
            jnp.where(ok, dot_nt(k, q), MASKED) for ok, q, k in zip(allowed, qs, ks)
        ]
        dprobs = [dot_nt(v, g) for g, v in zip(gs, vs)]
        raised = [
            jnp.exp2((x - jnp.max(x, axis=0, keepdims=True)) * SCALE_LOG2) for x in scores
        ]
        weights = [x * (1.0 / jnp.sum(x, axis=0, keepdims=True)) for x in raised]
        probs = [x.astype(BF16) for x in weights]
        deltas = [jnp.sum(w * dp, axis=0, keepdims=True) for w, dp in zip(weights, dprobs)]
        dscores = [
            (w * (dp - delta) * SCALE).astype(BF16)
            for w, dp, delta in zip(weights, dprobs, deltas)
        ]
        results = (
            [dot_tn(x, v).astype(BF16) for x, v in zip(probs, vs)],
            [dot_tn(x, k).astype(BF16) for x, k in zip(dscores, ks)],
            [dot_nn(x, q).astype(BF16) for x, q in zip(dscores, qs)],
            [dot_nn(x, g).astype(BF16) for x, g in zip(probs, gs)],
        )
        for place, result in enumerate(results):
            targets = [(out_ref, part) for _, _, out_ref in members for part in parts]
            for (out_ref, part), value in zip(targets, result):
                out_ref[:, place, part] = value.reshape(frames, group, DH)

    block = (slots, frames, 4, rows, DH)
    return pl.pallas_call(
        kernel,
        out_shape=jax.ShapeDtypeStruct(rows_in.shape, BF16),
        in_specs=[pl.BlockSpec(memory_space=pltpu.SMEM)] * 3
        + [pl.BlockSpec(memory_space=pl.ANY)],
        out_specs=pl.BlockSpec(memory_space=pl.ANY),
        scratch_shapes=[
            pltpu.VMEM(block, BF16),
            pltpu.VMEM(block, BF16),
            pltpu.SemaphoreType.DMA((slots,)),
            pltpu.SemaphoreType.DMA((slots,)),
        ],
        compiler_params=whole_params(),
        cost_estimate=cost(1e10, 4 * rows_in.size),
        name="temporal",
    )(kinds, first, bands, rows_in)


def spatial(kinds, first, frame, arrays, prior, heads):
    count = arrays[0].shape[0]
    slots = prior.shape[0]
    chunk = min(count, 128)

    def kernel(
        kind_ref, first_ref, frame_ref, q_ref, k_ref, v_ref, g_ref, prior_ref,
        out_ref, qgrad_ref, own_ref, stats_ref,
    ):
        has_prior = frame_ref[0] > 0
        k, v = k_ref[...], v_ref[...]
        k_prior, v_prior = prior_ref[0, 0], prior_ref[0, 1]
        own_ref[...] = jnp.zeros_like(own_ref)

        @pl.loop(0, count // chunk)
        def _(step):
            part = pl.ds(pl.multiple_of(step * chunk, chunk), chunk)
            q, g = q_ref[part], g_ref[part]
            own = dot_nt(k, q)
            before = jnp.where(has_prior, dot_nt(k_prior, q), MASKED)
            top = jnp.maximum(
                jnp.max(own, axis=0, keepdims=True), jnp.max(before, axis=0, keepdims=True)
            )
            own, before = (jnp.exp2((x - top) * SCALE_LOG2) for x in (own, before))
            total = jnp.sum(own, axis=0, keepdims=True) + jnp.sum(before, axis=0, keepdims=True)
            inverse = 1.0 / total
            own, before = own * inverse, before * inverse
            own_dp, before_dp = dot_nt(v, g), dot_nt(v_prior, g)
            delta = jnp.sum(own * own_dp, axis=0, keepdims=True) + jnp.sum(
                before * before_dp, axis=0, keepdims=True
            )
            own_prob, before_prob = own.astype(BF16), before.astype(BF16)
            own_ds = (own * (own_dp - delta) * SCALE).astype(BF16)
            before_ds = (before * (before_dp - delta) * SCALE).astype(BF16)
            out_ref[part] = (dot_tn(own_prob, v) + dot_tn(before_prob, v_prior)).astype(BF16)
            qgrad_ref[part] = (dot_tn(own_ds, k) + dot_tn(before_ds, k_prior)).astype(BF16)
            own_ref[0, 0] += dot_nn(own_ds, q)
            own_ref[0, 1] += dot_nn(own_prob, g)
            stats_ref[0, 0:1, part] = top * SCALE + jnp.log(total)
            stats_ref[0, 1:2, part] = delta

    columns = column_spec(count, heads, SPATIAL)
    pair = pl.BlockSpec((1, 2, count, DH), lambda i, *refs: (i, 0, 0, 0))
    whole = jax.ShapeDtypeStruct((count, heads * DH), BF16)
    return pl.pallas_call(
        kernel,
        out_shape=[
            whole,
            whole,
            jax.ShapeDtypeStruct(prior.shape, F32),
            jax.ShapeDtypeStruct((slots, 2, count), F32),
        ],
        grid_spec=pltpu.PrefetchScalarGridSpec(
            num_scalar_prefetch=3,
            grid=(slots,),
            in_specs=[columns] * 4 + [pair],
            out_specs=[
                columns, columns, pair, pl.BlockSpec((1, 2, count), lambda i, *refs: (i, 0, 0))
            ],
        ),
        compiler_params=params(24),
        cost_estimate=cost(2e11, 16 * slots * count * DH),
        name="spatial",
    )(kinds, first, frame, *arrays, prior)


def spatial_next(kinds, first, k, v, following, stats, own, heads):
    slots, _, count, _ = own.shape
    chunk = min(count, 256)

    def kernel(
        kind_ref, first_ref, k_in, v_in, next_in, stats_in, own_in, k_out, v_out,
        kv_ref, next_ref, stats_ref, own_ref, made_ref, in_sems, out_sems,
    ):
        def loads(slot):
            cols = head_columns(kind_ref, first_ref, heads, SPATIAL, slot)
            pairs = [
                (k_in.at[:, cols], kv_ref.at[slot, 0]),
                (v_in.at[:, cols], kv_ref.at[slot, 1]),
                (next_in.at[slot], next_ref.at[slot]),
                (stats_in.at[slot], stats_ref.at[slot]),
                (own_in.at[slot], own_ref.at[slot]),
            ]
            return [
                pltpu.make_async_copy(*pair, in_sems.at[slot, i]) for i, pair in enumerate(pairs)
            ]

        def stores(slot):
            cols = head_columns(kind_ref, first_ref, heads, SPATIAL, slot)
            return [
                pltpu.make_async_copy(made_ref.at[slot, i], out.at[:, cols], out_sems.at[slot, i])
                for i, out in enumerate((k_out, v_out))
            ]

        for slot in range(slots):
            for copy in loads(slot):
                copy.start()

        @pl.loop(0, slots)
        def _(slot):
            for copy in loads(slot):
                copy.wait()
            q, g = next_ref[slot, 0], next_ref[slot, 1]
            lse, delta = stats_ref[slot, 0:1] * math.log2(math.e), stats_ref[slot, 1:2]
            parts = [slice(start, start + chunk) for start in range(0, count, chunk)]
            scores = [dot_nt(kv_ref[slot, 0, part], q) for part in parts]
            dprobs = [dot_nt(kv_ref[slot, 1, part], g) for part in parts]
            weights = [jnp.exp2(x * SCALE_LOG2 - lse) for x in scores]
            slopes = [(w * (x - delta)).astype(BF16) for w, x in zip(weights, dprobs)]
            for part, weight, slope in zip(parts, weights, slopes):
                terms = dot_nn(slope, q) * SCALE, dot_nn(weight.astype(BF16), g)
                for i, term in enumerate(terms):
                    made_ref[slot, i, part] = (own_ref[slot, i, part] + term).astype(BF16)
            for copy in stores(slot):
                copy.start()

        for slot in range(slots):
            for copy in stores(slot):
                copy.wait()

    return pl.pallas_call(
        kernel,
        out_shape=[jax.ShapeDtypeStruct(k.shape, BF16)] * 2,
        in_specs=[pl.BlockSpec(memory_space=pltpu.SMEM)] * 2
        + [pl.BlockSpec(memory_space=pl.ANY)] * 5,
        out_specs=[pl.BlockSpec(memory_space=pl.ANY)] * 2,
        scratch_shapes=[
            pltpu.VMEM((slots, 2, count, DH), BF16),
            pltpu.VMEM((slots, 2, count, DH), BF16),
            pltpu.VMEM((slots, 2, count), F32),
            pltpu.VMEM((slots, 2, count, DH), F32),
            pltpu.VMEM((slots, 2, count, DH), BF16),
            pltpu.SemaphoreType.DMA((slots, 5)),
            pltpu.SemaphoreType.DMA((slots, 2)),
        ],
        compiler_params=pltpu.CompilerParams(vmem_limit_bytes=24 * MIB),
        cost_estimate=cost(8 * slots * count * count * DH, 20 * slots * count * DH),
        name="spatial_next",
    )(kinds, first, k, v, following, stats, own)


def unpack(kinds, first, rows_in, filled, heads):
    frames, _, slots, rows, _ = rows_in.shape
    count = frames * rows
    total = 4 * slots

    def kernel(kind_ref, first_ref, in_ref, *refs):
        outs, (stage, in_sems, out_sems) = refs[-7:-3], refs[-3:]
        triples = []
        for slot in range(slots):
            cols = head_columns(kind_ref, first_ref, heads, TEMPORAL, slot)
            for place, out in enumerate(outs):
                held = stage.at[slot, place]
                triples.append((in_ref.at[:, place, slot], held, out.at[:, :, cols]))
        staged_copies(triples, in_sems, out_sems)

    shape = (frames, rows, heads * DH)
    filled = [x.reshape(shape) for x in filled]
    outs = pl.pallas_call(
        kernel,
        out_shape=[jax.ShapeDtypeStruct(shape, BF16)] * 4,
        in_specs=[pl.BlockSpec(memory_space=pltpu.SMEM)] * 2
        + [pl.BlockSpec(memory_space=pl.ANY)] * (1 + len(filled)),
        out_specs=[pl.BlockSpec(memory_space=pl.ANY)] * 4,
        scratch_shapes=[
            pltpu.VMEM((slots, 4, frames, rows, DH), BF16),
            pltpu.SemaphoreType.DMA((total,)),
            pltpu.SemaphoreType.DMA((total,)),
        ],
        input_output_aliases={3 + place: place for place in range(len(filled))},
        compiler_params=pltpu.CompilerParams(vmem_limit_bytes=24 * MIB),
        cost_estimate=cost(0, 4 * rows_in.size),
        name="unpack",
    )(kinds, first, rows_in, *filled)
    return [x.reshape(count, heads * DH) for x in outs]


def passed_along(array, axis, by):
    length = lax.axis_size(axis)
    pairs = [(i, i + by) for i in range(length) if 0 <= i + by < length]
    return lax.ppermute(array, axis, pairs)


def behind(arrays, *others):
    return lax.optimization_barrier((tuple(arrays), others))[0]


def neighbour_rows(ahead, back, frame, results):
    length = lax.axis_size("ctx")
    even = lax.rem(frame[0], 2) == 0
    far = [(i, i - 1 if i % 2 == 0 else i + 1) for i in range(length)]
    far = [pair for pair in far if 0 <= pair[1] < length]
    near = [(i, i + 1 if i % 2 == 0 else i - 1) for i in range(length)]
    near = lax.ppermute(jnp.where(even, ahead, back), "ctx", near)
    far = lax.ppermute(jnp.where(even, back, ahead), "ctx", far)
    if results is not None:
        near, far = behind((near, far), results)
    return jnp.where(even, far, near), jnp.where(even, near, far)


def exchange_order(frames):
    half = frames // 2
    return [*range(half - 1), half, half - 1, *range(half + 1, frames)]


def branch(slots, heads, kinds, bands, first, frame, q, k, v, g):
    frames, rows, width = q.shape
    count = frames * rows
    others = heads - slots
    exchange = functools.partial(
        lax.all_to_all, axis_name="ctx", split_axis=0, concat_axis=0, tiled=True,
        axis_index_groups=[exchange_order(frames)],
    )
    flat = [x.reshape(count, width) for x in (q, k, v, g)]
    packed = []
    filled, results = (), None
    if slots > 0:
        packed = [pack_temporal(kinds, first, (q, k, v, g), slots, heads)]
        framed = exchange(*packed)
        results = temporal(kinds, first, bands, framed, heads)
        returned = exchange(results)
    if others > 0:
        ahead, back = pack_spatial(kinds, first, (k, v, q, g), others, heads, packed)
        arrived = neighbour_rows(ahead, back, frame, results)
        prior, following = (x.reshape(others, 2, count, DH) for x in arrived)
        attended, qgrad, own, stats = spatial(kinds, first, frame, flat, prior, heads)
        stats = passed_along(stats, "ctx", -1)
        grads = spatial_next(kinds, first, *flat[1:3], following, stats, own, heads)
        filled = (attended, qgrad, *grads)
    if slots > 0:
        filled = unpack(kinds, first, returned, filled, heads)
    return tuple(filled)


def body(queries, key_rows, value_rows, out_grad, head_kind, frame_band):
    frames = lax.axis_size("ctx")
    count = queries.shape[1]
    heads = queries.shape[2] // DH
    first = lax.axis_index("head").astype(jnp.int32) * heads
    frame = lax.axis_index("ctx").astype(jnp.int32)
    offset = jnp.arange(head_kind.shape[0], dtype=jnp.int32) - first
    here = jnp.logical_and(offset >= 0, offset < heads)
    slots = jnp.sum(jnp.logical_and(here, head_kind == TEMPORAL).astype(jnp.int32))
    arrays = [
        x.reshape(frames, count // frames, heads * DH)
        for x in (queries, key_rows, value_rows, out_grad)
    ]
    outs = lax.switch(
        slots,
        [functools.partial(branch, n, heads) for n in range(heads + 1)],
        head_kind, frame_band, first.reshape(1), frame.reshape(1), *arrays,
    )
    return tuple(out.reshape(queries.shape) for out in outs)


def solution(mesh):
    rows = P("ctx", None, "head")
    return jax.shard_map(
        body,
        mesh=mesh,
        in_specs=(rows, rows, rows, rows, P(), P()),
        out_specs=(rows, rows, rows, rows),
        check_vma=False,
    )
```

```python
import functools
import math

import jax
import jax.numpy as jnp
from jax import lax
from jax.experimental import pallas as pl
from jax.experimental.pallas import tpu as pltpu
from jax.sharding import PartitionSpec as P

DH = 128
SCALE = DH ** (-0.5)
SPATIAL, TEMPORAL = 1, 0
MASKED = -1e30
SCALE_LOG2 = SCALE * math.log2(math.e)
F32 = jnp.float32
BF16 = jnp.bfloat16
MIB = 1024 * 1024


def head_at(kind_ref, first_ref, heads, kind, slot):
    found, seen = jnp.int32(0), jnp.int32(0)
    for head in range(heads):
        hit = kind_ref[first_ref[0] + head] == kind
        found = jnp.where(jnp.logical_and(hit, seen == slot), jnp.int32(head), found)
        seen = seen + hit.astype(jnp.int32)
    return found


def dot_nt(a, b):
    return lax.dot_general(a, b, (((1,), (1,)), ((), ())), preferred_element_type=F32)


def dot_nn(a, b):
    return lax.dot_general(a, b, (((1,), (0,)), ((), ())), preferred_element_type=F32)


def dot_tn(a, b):
    return lax.dot_general(a, b, (((0,), (0,)), ((), ())), preferred_element_type=F32)


def params(mib=32):
    return pltpu.CompilerParams(
        dimension_semantics=("arbitrary",), vmem_limit_bytes=mib * MIB
    )


def cost(flops, moved):
    return pl.CostEstimate(flops=int(flops), bytes_accessed=int(moved), transcendentals=0)


def column_spec(count, heads, kind):
    return pl.BlockSpec((count, DH), lambda i, *refs: (0, head_at(*refs[:2], heads, kind, i)))


def head_columns(kind_ref, first_ref, heads, kind, slot):
    return pl.ds(pl.multiple_of(head_at(kind_ref, first_ref, heads, kind, slot) * DH, DH), DH)


def staged_copies(triples, in_sems, out_sems):
    loads = [pltpu.make_async_copy(x, y, in_sems.at[i]) for i, (x, y, _) in enumerate(triples)]
    stores = [pltpu.make_async_copy(y, z, out_sems.at[i]) for i, (_, y, z) in enumerate(triples)]
    for load in loads:
        load.start()
    for load, store in zip(loads, stores):
        load.wait()
        store.start()
    for store in stores:
        store.wait()


def whole_params():
    return pltpu.CompilerParams(vmem_limit_bytes=62 * MIB)


def pack_spatial(kinds, first, arrays, slots, heads, after):
    frames, rows, _ = arrays[0].shape
    count = len(arrays)
    total = slots * count

    def kernel(kind_ref, first_ref, *refs):
        ins, outs = refs[:count], refs[-3 - count // 2 : -3]
        stage, in_sems, out_sems = refs[-3:]
        triples = []
        for slot in range(slots):
            cols = head_columns(kind_ref, first_ref, heads, SPATIAL, slot)
            for place, ref in enumerate(ins):
                target = outs[place // 2].at[slot, place % 2]
                triples.append((ref.at[:, :, cols], stage.at[slot, place], target))
        staged_copies(triples, in_sems, out_sems)

    return pl.pallas_call(
        kernel,
        out_shape=[jax.ShapeDtypeStruct((slots, 2, frames, rows, DH), BF16)] * (count // 2),
        in_specs=[pl.BlockSpec(memory_space=pltpu.SMEM)] * 2
        + [pl.BlockSpec(memory_space=pl.ANY)] * (count + len(after)),
        out_specs=[pl.BlockSpec(memory_space=pl.ANY)] * (count // 2),
        scratch_shapes=[
            pltpu.VMEM((slots, count, frames, rows, DH), BF16),
            pltpu.SemaphoreType.DMA((total,)),
            pltpu.SemaphoreType.DMA((total,)),
        ],
        compiler_params=whole_params(),
        cost_estimate=cost(0, 4 * total * frames * rows * DH),
        name="pack_spatial",
    )(kinds, first, *arrays, *after)


def pack_temporal(kinds, first, arrays, slots, heads):
    frames, rows, _ = arrays[0].shape
    total = 4 * slots

    def kernel(kind_ref, first_ref, *refs):
        ins, (out, stage, in_sems, out_sems) = refs[:4], refs[4:]
        triples = []
        for slot in range(slots):
            cols = head_columns(kind_ref, first_ref, heads, TEMPORAL, slot)
            for place, ref in enumerate(ins):
                triples.append(
                    (ref.at[:, :, cols], stage.at[slot, place], out.at[:, place, slot])
                )
        staged_copies(triples, in_sems, out_sems)

    return pl.pallas_call(
        kernel,
        out_shape=jax.ShapeDtypeStruct((frames, 4, slots, rows, DH), BF16),
        in_specs=[pl.BlockSpec(memory_space=pltpu.SMEM)] * 2
        + [pl.BlockSpec(memory_space=pl.ANY)] * 4,
        out_specs=pl.BlockSpec(memory_space=pl.ANY),
        scratch_shapes=[
            pltpu.VMEM((slots, 4, frames, rows, DH), BF16),
            pltpu.SemaphoreType.DMA((total,)),
            pltpu.SemaphoreType.DMA((total,)),
        ],
        compiler_params=whole_params(),
        cost_estimate=cost(0, 4 * total * frames * rows * DH),
        name="pack_temporal",
    )(kinds, first, *arrays)


def temporal(kinds, first, bands, rows_in, heads):
    frames, _, slots, rows, _ = rows_in.shape
    group = 16
    size = frames * group

    def frame_at(place):
        half = frames // 2
        return place + (place == half - 1).astype(jnp.int32) - (place == half).astype(jnp.int32)

    def kernel(kind_ref, first_ref, band_ref, rows_ref, result_ref, held, made, in_sems, out_sems):
        def load(slot):
            return pltpu.make_async_copy(rows_ref.at[:, :, slot], held.at[slot], in_sems.at[slot])

        def store(slot):
            return pltpu.make_async_copy(
                made.at[slot], result_ref.at[:, :, slot], out_sems.at[slot]
            )

        for slot in range(slots):
            load(slot).start()

        def work(members):
            for slot in members:
                load(slot).wait()
            some_heads(
                kind_ref, first_ref, band_ref,
                [(slot, held.at[slot], made.at[slot]) for slot in members],
            )
            for slot in members:
                store(slot).start()

        if slots > 1:

            @pl.loop(0, slots // 2)
            def _(pair):
                work([2 * pair, 2 * pair + 1])

        if slots % 2:
            work([slots - 1])
        for slot in range(slots):
            store(slot).wait()

    def some_heads(kind_ref, first_ref, band_ref, members):
        row = lax.broadcasted_iota(jnp.int32, (size, size), 0)
        col = lax.broadcasted_iota(jnp.int32, (size, size), 1)
        same = lax.rem(row, group) == lax.rem(col, group)
        apart = jnp.abs(frame_at(lax.div(row, group)) - frame_at(lax.div(col, group)))
        distance = jnp.where(same, apart, frames)
        parts = [slice(start, start + group) for start in range(0, rows, group)]
        allowed, qs, ks, vs, gs = [], [], [], [], []
        for slot, in_ref, _ in members:
            head = head_at(kind_ref, first_ref, heads, TEMPORAL, slot)
            band = jnp.minimum(band_ref[first_ref[0] + head], frames - 1)
            allowed += [distance <= band] * len(parts)
            for place, rows_of in enumerate((qs, ks, vs, gs)):
                rows_of += [in_ref[:, place, part].reshape(size, DH) for part in parts]
        scores = [
            jnp.where(ok, dot_nt(k, q), MASKED) for ok, q, k in zip(allowed, qs, ks)
        ]
        dprobs = [dot_nt(v, g) for g, v in zip(gs, vs)]
        raised = [
            jnp.exp2((x - jnp.max(x, axis=0, keepdims=True)) * SCALE_LOG2) for x in scores
        ]
        weights = [x * (1.0 / jnp.sum(x, axis=0, keepdims=True)) for x in raised]
        probs = [x.astype(BF16) for x in weights]
        deltas = [jnp.sum(w * dp, axis=0, keepdims=True) for w, dp in zip(weights, dprobs)]
        dscores = [
            (w * (dp - delta) * SCALE).astype(BF16)
            for w, dp, delta in zip(weights, dprobs, deltas)
        ]
        results = (
            [dot_tn(x, v).astype(BF16) for x, v in zip(probs, vs)],
            [dot_tn(x, k).astype(BF16) for x, k in zip(dscores, ks)],
            [dot_nn(x, q).astype(BF16) for x, q in zip(dscores, qs)],
            [dot_nn(x, g).astype(BF16) for x, g in zip(probs, gs)],
        )
        for place, result in enumerate(results):
            targets = [(out_ref, part) for _, _, out_ref in members for part in parts]
            for (out_ref, part), value in zip(targets, result):
                out_ref[:, place, part] = value.reshape(frames, group, DH)

    block = (slots, frames, 4, rows, DH)
    return pl.pallas_call(
        kernel,
        out_shape=jax.ShapeDtypeStruct(rows_in.shape, BF16),
        in_specs=[pl.BlockSpec(memory_space=pltpu.SMEM)] * 3
        + [pl.BlockSpec(memory_space=pl.ANY)],
        out_specs=pl.BlockSpec(memory_space=pl.ANY),
        scratch_shapes=[
            pltpu.VMEM(block, BF16),
            pltpu.VMEM(block, BF16),
            pltpu.SemaphoreType.DMA((slots,)),
            pltpu.SemaphoreType.DMA((slots,)),
        ],
        compiler_params=whole_params(),
        cost_estimate=cost(1e10, 4 * rows_in.size),
        name="temporal",
    )(kinds, first, bands, rows_in)


def spatial(kinds, first, frame, arrays, prior, heads):
    count = arrays[0].shape[0]
    slots = prior.shape[0]
    chunk = min(count, 128)

    def kernel(
        kind_ref, first_ref, frame_ref, q_ref, k_ref, v_ref, g_ref, prior_ref,
        out_ref, qgrad_ref, own_ref, stats_ref,
    ):
        has_prior = frame_ref[0] > 0
        k, v = k_ref[...], v_ref[...]
        k_prior, v_prior = prior_ref[0, 0], prior_ref[0, 1]
        own_ref[...] = jnp.zeros_like(own_ref)

        @pl.loop(0, count // chunk)
        def _(step):
            part = pl.ds(pl.multiple_of(step * chunk, chunk), chunk)
            q, g = q_ref[part], g_ref[part]
            own = dot_nt(k, q)
            before = jnp.where(has_prior, dot_nt(k_prior, q), MASKED)
            top = jnp.maximum(
                jnp.max(own, axis=0, keepdims=True), jnp.max(before, axis=0, keepdims=True)
            )
            own, before = (jnp.exp2((x - top) * SCALE_LOG2) for x in (own, before))
            total = jnp.sum(own, axis=0, keepdims=True) + jnp.sum(before, axis=0, keepdims=True)
            inverse = 1.0 / total
            own, before = own * inverse, before * inverse
            own_dp, before_dp = dot_nt(v, g), dot_nt(v_prior, g)
            delta = jnp.sum(own * own_dp, axis=0, keepdims=True) + jnp.sum(
                before * before_dp, axis=0, keepdims=True
            )
            own_prob, before_prob = own.astype(BF16), before.astype(BF16)
            own_ds = (own * (own_dp - delta) * SCALE).astype(BF16)
            before_ds = (before * (before_dp - delta) * SCALE).astype(BF16)
            out_ref[part] = (dot_tn(own_prob, v) + dot_tn(before_prob, v_prior)).astype(BF16)
            qgrad_ref[part] = (dot_tn(own_ds, k) + dot_tn(before_ds, k_prior)).astype(BF16)
            own_ref[0, 0] += dot_nn(own_ds, q)
            own_ref[0, 1] += dot_nn(own_prob, g)
            stats_ref[0, 0:1, part] = top * SCALE + jnp.log(total)
            stats_ref[0, 1:2, part] = delta

    columns = column_spec(count, heads, SPATIAL)
    pair = pl.BlockSpec((1, 2, count, DH), lambda i, *refs: (i, 0, 0, 0))
    whole = jax.ShapeDtypeStruct((count, heads * DH), BF16)
    return pl.pallas_call(
        kernel,
        out_shape=[
            whole,
            whole,
            jax.ShapeDtypeStruct(prior.shape, F32),
            jax.ShapeDtypeStruct((slots, 2, count), F32),
        ],
        grid_spec=pltpu.PrefetchScalarGridSpec(
            num_scalar_prefetch=3,
            grid=(slots,),
            in_specs=[columns] * 4 + [pair],
            out_specs=[
                columns, columns, pair, pl.BlockSpec((1, 2, count), lambda i, *refs: (i, 0, 0))
            ],
        ),
        compiler_params=params(24),
        cost_estimate=cost(2e11, 16 * slots * count * DH),
        name="spatial",
    )(kinds, first, frame, *arrays, prior)


def spatial_next(kinds, first, k, v, following, stats, own, heads):
    slots, _, count, _ = own.shape
    chunk = min(count, 256)

    def kernel(
        kind_ref, first_ref, k_in, v_in, next_in, stats_in, own_in, k_out, v_out,
        kv_ref, next_ref, stats_ref, own_ref, made_ref, in_sems, out_sems,
    ):
        def loads(slot):
            cols = head_columns(kind_ref, first_ref, heads, SPATIAL, slot)
            pairs = [
                (k_in.at[:, cols], kv_ref.at[slot, 0]),
                (v_in.at[:, cols], kv_ref.at[slot, 1]),
                (next_in.at[slot], next_ref.at[slot]),
                (stats_in.at[slot], stats_ref.at[slot]),
                (own_in.at[slot], own_ref.at[slot]),
            ]
            return [
                pltpu.make_async_copy(*pair, in_sems.at[slot, i]) for i, pair in enumerate(pairs)
            ]

        def stores(slot):
            cols = head_columns(kind_ref, first_ref, heads, SPATIAL, slot)
            return [
                pltpu.make_async_copy(made_ref.at[slot, i], out.at[:, cols], out_sems.at[slot, i])
                for i, out in enumerate((k_out, v_out))
            ]

        for slot in range(slots):
            for copy in loads(slot):
                copy.start()

        @pl.loop(0, slots)
        def _(slot):
            for copy in loads(slot):
                copy.wait()
            q, g = next_ref[slot, 0], next_ref[slot, 1]
            lse, delta = stats_ref[slot, 0:1] * math.log2(math.e), stats_ref[slot, 1:2]
            parts = [slice(start, start + chunk) for start in range(0, count, chunk)]
            scores = [dot_nt(kv_ref[slot, 0, part], q) for part in parts]
            dprobs = [dot_nt(kv_ref[slot, 1, part], g) for part in parts]
            weights = [jnp.exp2(x * SCALE_LOG2 - lse) for x in scores]
            slopes = [(w * (x - delta)).astype(BF16) for w, x in zip(weights, dprobs)]
            for part, weight, slope in zip(parts, weights, slopes):
                terms = dot_nn(slope, q) * SCALE, dot_nn(weight.astype(BF16), g)
                for i, term in enumerate(terms):
                    made_ref[slot, i, part] = (own_ref[slot, i, part] + term).astype(BF16)
            for copy in stores(slot):
                copy.start()

        for slot in range(slots):
            for copy in stores(slot):
                copy.wait()

    return pl.pallas_call(
        kernel,
        out_shape=[jax.ShapeDtypeStruct(k.shape, BF16)] * 2,
        in_specs=[pl.BlockSpec(memory_space=pltpu.SMEM)] * 2
        + [pl.BlockSpec(memory_space=pl.ANY)] * 5,
        out_specs=[pl.BlockSpec(memory_space=pl.ANY)] * 2,
        scratch_shapes=[
            pltpu.VMEM((slots, 2, count, DH), BF16),
            pltpu.VMEM((slots, 2, count, DH), BF16),
            pltpu.VMEM((slots, 2, count), F32),
            pltpu.VMEM((slots, 2, count, DH), F32),
            pltpu.VMEM((slots, 2, count, DH), BF16),
            pltpu.SemaphoreType.DMA((slots, 5)),
            pltpu.SemaphoreType.DMA((slots, 2)),
        ],
        compiler_params=pltpu.CompilerParams(vmem_limit_bytes=24 * MIB),
        cost_estimate=cost(8 * slots * count * count * DH, 20 * slots * count * DH),
        name="spatial_next",
    )(kinds, first, k, v, following, stats, own)


def unpack(kinds, first, rows_in, filled, heads):
    frames, _, slots, rows, _ = rows_in.shape
    count = frames * rows
    total = 4 * slots

    def kernel(kind_ref, first_ref, in_ref, *refs):
        outs, (stage, in_sems, out_sems) = refs[-7:-3], refs[-3:]
        triples = []
        for slot in range(slots):
            cols = head_columns(kind_ref, first_ref, heads, TEMPORAL, slot)
            for place, out in enumerate(outs):
                held = stage.at[slot, place]
                triples.append((in_ref.at[:, place, slot], held, out.at[:, :, cols]))
        staged_copies(triples, in_sems, out_sems)

    shape = (frames, rows, heads * DH)
    filled = [x.reshape(shape) for x in filled]
    outs = pl.pallas_call(
        kernel,
        out_shape=[jax.ShapeDtypeStruct(shape, BF16)] * 4,
        in_specs=[pl.BlockSpec(memory_space=pltpu.SMEM)] * 2
        + [pl.BlockSpec(memory_space=pl.ANY)] * (1 + len(filled)),
        out_specs=[pl.BlockSpec(memory_space=pl.ANY)] * 4,
        scratch_shapes=[
            pltpu.VMEM((slots, 4, frames, rows, DH), BF16),
            pltpu.SemaphoreType.DMA((total,)),
            pltpu.SemaphoreType.DMA((total,)),
        ],
        input_output_aliases={3 + place: place for place in range(len(filled))},
        compiler_params=pltpu.CompilerParams(vmem_limit_bytes=24 * MIB),
        cost_estimate=cost(0, 4 * rows_in.size),
        name="unpack",
    )(kinds, first, rows_in, *filled)
    return [x.reshape(count, heads * DH) for x in outs]


def passed_along(array, axis, by):
    length = lax.axis_size(axis)
    pairs = [(i, i + by) for i in range(length) if 0 <= i + by < length]
    return lax.ppermute(array, axis, pairs)


def behind(arrays, *others):
    return lax.optimization_barrier((tuple(arrays), others))[0]


def neighbour_rows(ahead, back, frame, results):
    length = lax.axis_size("ctx")
    even = lax.rem(frame[0], 2) == 0
    far = [(i, i - 1 if i % 2 == 0 else i + 1) for i in range(length)]
    far = [pair for pair in far if 0 <= pair[1] < length]
    near = [(i, i + 1 if i % 2 == 0 else i - 1) for i in range(length)]
    near = lax.ppermute(jnp.where(even, ahead, back), "ctx", near)
    far = lax.ppermute(jnp.where(even, back, ahead), "ctx", far)
    if results is not None:
        near, far = behind((near, far), results)
    return jnp.where(even, far, near), jnp.where(even, near, far)


def exchange_order(frames):
    half = frames // 2
    return [*range(half - 1), half, half - 1, *range(half + 1, frames)][::-1]


def branch(slots, heads, kinds, bands, first, frame, q, k, v, g):
    frames, rows, width = q.shape
    count = frames * rows
    others = heads - slots
    exchange = functools.partial(
        lax.all_to_all, axis_name="ctx", split_axis=0, concat_axis=0, tiled=True,
        axis_index_groups=[exchange_order(frames)],
    )
    flat = [x.reshape(count, width) for x in (q, k, v, g)]
    packed = []
    filled, results = (), None
    if slots > 0:
        packed = [pack_temporal(kinds, first, (q, k, v, g), slots, heads)]
        framed = exchange(*packed)
        results = temporal(kinds, first, bands, framed, heads)
        returned = exchange(results)
    if others > 0:
        ahead, back = pack_spatial(kinds, first, (k, v, q, g), others, heads, packed)
        arrived = neighbour_rows(ahead, back, frame, results)
        prior, following = (x.reshape(others, 2, count, DH) for x in arrived)
        attended, qgrad, own, stats = spatial(kinds, first, frame, flat, prior, heads)
        stats = passed_along(stats, "ctx", -1)
        grads = spatial_next(kinds, first, *flat[1:3], following, stats, own, heads)
        filled = (attended, qgrad, *grads)
    if slots > 0:
        filled = unpack(kinds, first, returned, filled, heads)
    return tuple(filled)


def body(queries, key_rows, value_rows, out_grad, head_kind, frame_band):
    frames = lax.axis_size("ctx")
    count = queries.shape[1]
    heads = queries.shape[2] // DH
    first = lax.axis_index("head").astype(jnp.int32) * heads
    frame = lax.axis_index("ctx").astype(jnp.int32)
    offset = jnp.arange(head_kind.shape[0], dtype=jnp.int32) - first
    here = jnp.logical_and(offset >= 0, offset < heads)
    slots = jnp.sum(jnp.logical_and(here, head_kind == TEMPORAL).astype(jnp.int32))
    arrays = [
        x.reshape(frames, count // frames, heads * DH)
        for x in (queries, key_rows, value_rows, out_grad)
    ]
    outs = lax.switch(
        slots,
        [functools.partial(branch, n, heads) for n in range(heads + 1)],
        head_kind, frame_band, first.reshape(1), frame.reshape(1), *arrays,
    )
    return tuple(out.reshape(queries.shape) for out in outs)


def solution(mesh):
    rows = P("ctx", None, "head")
    return jax.shard_map(
        body,
        mesh=mesh,
        in_specs=(rows, rows, rows, rows, P(), P()),
        out_specs=(rows, rows, rows, rows),
        check_vma=False,
    )
```

```python
import functools
import math

import jax
import jax.numpy as jnp
from jax import lax
from jax.experimental import pallas as pl
from jax.experimental.pallas import tpu as pltpu
from jax.sharding import PartitionSpec as P

DH = 128
SCALE = DH ** (-0.5)
SPATIAL, TEMPORAL = 1, 0
MASKED = -1e30
SCALE_LOG2 = SCALE * math.log2(math.e)
F32 = jnp.float32
BF16 = jnp.bfloat16
MIB = 1024 * 1024


def head_at(kind_ref, first_ref, heads, kind, slot):
    found, seen = jnp.int32(0), jnp.int32(0)
    for head in range(heads):
        hit = kind_ref[first_ref[0] + head] == kind
        found = jnp.where(jnp.logical_and(hit, seen == slot), jnp.int32(head), found)
        seen = seen + hit.astype(jnp.int32)
    return found


def dot_nt(a, b):
    return lax.dot_general(a, b, (((1,), (1,)), ((), ())), preferred_element_type=F32)


def dot_nn(a, b):
    return lax.dot_general(a, b, (((1,), (0,)), ((), ())), preferred_element_type=F32)


def dot_tn(a, b):
    return lax.dot_general(a, b, (((0,), (0,)), ((), ())), preferred_element_type=F32)


def params(mib=32):
    return pltpu.CompilerParams(
        dimension_semantics=("arbitrary",), vmem_limit_bytes=mib * MIB
    )


def cost(flops, moved):
    return pl.CostEstimate(flops=int(flops), bytes_accessed=int(moved), transcendentals=0)


def column_spec(count, heads, kind):
    return pl.BlockSpec((count, DH), lambda i, *refs: (0, head_at(*refs[:2], heads, kind, i)))


def head_columns(kind_ref, first_ref, heads, kind, slot):
    return pl.ds(pl.multiple_of(head_at(kind_ref, first_ref, heads, kind, slot) * DH, DH), DH)


def staged_copies(triples, in_sems, out_sems):
    loads = [pltpu.make_async_copy(x, y, in_sems.at[i]) for i, (x, y, _) in enumerate(triples)]
    stores = [pltpu.make_async_copy(y, z, out_sems.at[i]) for i, (_, y, z) in enumerate(triples)]
    for load in loads:
        load.start()
    for load, store in zip(loads, stores):
        load.wait()
        store.start()
    for store in stores:
        store.wait()


def whole_params():
    return pltpu.CompilerParams(vmem_limit_bytes=62 * MIB)


def pack_spatial(kinds, first, arrays, slots, heads, after):
    frames, rows, _ = arrays[0].shape
    count = len(arrays)
    total = slots * count

    def kernel(kind_ref, first_ref, *refs):
        ins, outs = refs[:count], refs[-3 - count // 2 : -3]
        stage, in_sems, out_sems = refs[-3:]
        triples = []
        for slot in range(slots):
            cols = head_columns(kind_ref, first_ref, heads, SPATIAL, slot)
            for place, ref in enumerate(ins):
                target = outs[place // 2].at[slot, place % 2]
                triples.append((ref.at[:, :, cols], stage.at[slot, place], target))
        staged_copies(triples, in_sems, out_sems)

    return pl.pallas_call(
        kernel,
        out_shape=[jax.ShapeDtypeStruct((slots, 2, frames, rows, DH), BF16)] * (count // 2),
        in_specs=[pl.BlockSpec(memory_space=pltpu.SMEM)] * 2
        + [pl.BlockSpec(memory_space=pl.ANY)] * (count + len(after)),
        out_specs=[pl.BlockSpec(memory_space=pl.ANY)] * (count // 2),
        scratch_shapes=[
            pltpu.VMEM((slots, count, frames, rows, DH), BF16),
            pltpu.SemaphoreType.DMA((total,)),
            pltpu.SemaphoreType.DMA((total,)),
        ],
        compiler_params=whole_params(),
        cost_estimate=cost(0, 4 * total * frames * rows * DH),
        name="pack_spatial",
    )(kinds, first, *arrays, *after)


def pack_temporal(kinds, first, arrays, slots, heads):
    frames, rows, _ = arrays[0].shape
    total = 4 * slots

    def kernel(kind_ref, first_ref, *refs):
        ins, (out, stage, in_sems, out_sems) = refs[:4], refs[4:]
        triples = []
        for slot in range(slots):
            cols = head_columns(kind_ref, first_ref, heads, TEMPORAL, slot)
            for place, ref in enumerate(ins):
                triples.append(
                    (ref.at[:, :, cols], stage.at[slot, place], out.at[:, place, slot])
                )
        staged_copies(triples, in_sems, out_sems)

    return pl.pallas_call(
        kernel,
        out_shape=jax.ShapeDtypeStruct((frames, 4, slots, rows, DH), BF16),
        in_specs=[pl.BlockSpec(memory_space=pltpu.SMEM)] * 2
        + [pl.BlockSpec(memory_space=pl.ANY)] * 4,
        out_specs=pl.BlockSpec(memory_space=pl.ANY),
        scratch_shapes=[
            pltpu.VMEM((slots, 4, frames, rows, DH), BF16),
            pltpu.SemaphoreType.DMA((total,)),
            pltpu.SemaphoreType.DMA((total,)),
        ],
        compiler_params=whole_params(),
        cost_estimate=cost(0, 4 * total * frames * rows * DH),
        name="pack_temporal",
    )(kinds, first, *arrays)


def temporal(kinds, first, bands, rows_in, heads):
    frames, _, slots, rows, _ = rows_in.shape
    group = 16
    size = frames * group

    def frame_at(place):
        half = frames // 2
        return place + (place == half - 1).astype(jnp.int32) - (place == half).astype(jnp.int32)

    def kernel(kind_ref, first_ref, band_ref, rows_ref, result_ref, held, made, in_sems, out_sems):
        def load(slot, place):
            return pltpu.make_async_copy(
                rows_ref.at[:, place, slot], held.at[slot, place], in_sems.at[slot, place]
            )

        def store(slot, place):
            return pltpu.make_async_copy(
                made.at[slot, place], result_ref.at[:, place, slot], out_sems.at[slot, place]
            )

        for slot in range(slots):
            for place in range(4):
                load(slot, place).start()

        def work(members):
            some_heads(
                kind_ref, first_ref, band_ref,
                [(slot, held.at[slot], made.at[slot]) for slot in members],
                lambda place: [load(slot, place).wait() for slot in members],
                lambda place: [store(slot, place).start() for slot in members],
            )

        if slots > 1:

            @pl.loop(0, slots // 2)
            def _(pair):
                work([2 * pair, 2 * pair + 1])

        if slots % 2:
            work([slots - 1])
        for slot in range(slots):
            for place in range(4):
                store(slot, place).wait()

    def some_heads(kind_ref, first_ref, band_ref, members, arrived, leave):
        row = lax.broadcasted_iota(jnp.int32, (size, size), 0)
        col = lax.broadcasted_iota(jnp.int32, (size, size), 1)
        same = lax.rem(row, group) == lax.rem(col, group)
        apart = jnp.abs(frame_at(lax.div(row, group)) - frame_at(lax.div(col, group)))
        distance = jnp.where(same, apart, frames)
        parts = [slice(start, start + group) for start in range(0, rows, group)]
        allowed = []
        for slot, _, _ in members:
            head = head_at(kind_ref, first_ref, heads, TEMPORAL, slot)
            band = jnp.minimum(band_ref[first_ref[0] + head], frames - 1)
            allowed += [distance <= band] * len(parts)

        def rows_of(place):
            arrived(place)
            return [
                in_ref[place, :, part].reshape(size, DH) for _, in_ref, _ in members for part in parts
            ]

        def give(place, result):
            targets = [(out_ref, part) for _, _, out_ref in members for part in parts]
            for (out_ref, part), value in zip(targets, result):
                out_ref[place, :, part] = value.astype(BF16).reshape(frames, group, DH)
            leave(place)

        qs, ks = rows_of(0), rows_of(1)
        scores = [
            jnp.where(ok, dot_nt(k, q), MASKED) for ok, q, k in zip(allowed, qs, ks)
        ]
        vs, gs = rows_of(2), rows_of(3)
        dprobs = [dot_nt(v, g) for g, v in zip(gs, vs)]
        raised = [
            jnp.exp2((x - jnp.max(x, axis=0, keepdims=True)) * SCALE_LOG2) for x in scores
        ]
        weights = [x * (1.0 / jnp.sum(x, axis=0, keepdims=True)) for x in raised]
        probs = [x.astype(BF16) for x in weights]
        deltas = [jnp.sum(w * dp, axis=0, keepdims=True) for w, dp in zip(weights, dprobs)]
        dscores = [
            (w * (dp - delta) * SCALE).astype(BF16)
            for w, dp, delta in zip(weights, dprobs, deltas)
        ]
        give(0, [dot_tn(x, v) for x, v in zip(probs, vs)])
        give(3, [dot_nn(x, g) for x, g in zip(probs, gs)])
        give(1, [dot_tn(x, k) for x, k in zip(dscores, ks)])
        give(2, [dot_nn(x, q) for x, q in zip(dscores, qs)])

    block = (slots, 4, frames, rows, DH)
    return pl.pallas_call(
        kernel,
        out_shape=jax.ShapeDtypeStruct(rows_in.shape, BF16),
        in_specs=[pl.BlockSpec(memory_space=pltpu.SMEM)] * 3
        + [pl.BlockSpec(memory_space=pl.ANY)],
        out_specs=pl.BlockSpec(memory_space=pl.ANY),
        scratch_shapes=[
            pltpu.VMEM(block, BF16),
            pltpu.VMEM(block, BF16),
            pltpu.SemaphoreType.DMA((slots, 4)),
            pltpu.SemaphoreType.DMA((slots, 4)),
        ],
        compiler_params=whole_params(),
        cost_estimate=cost(1e10, 4 * rows_in.size),
        name="temporal",
    )(kinds, first, bands, rows_in)


def spatial(kinds, first, frame, arrays, prior, heads):
    count = arrays[0].shape[0]
    slots = prior.shape[0]
    chunk = min(count, 128)

    def kernel(
        kind_ref, first_ref, frame_ref, q_ref, k_ref, v_ref, g_ref, prior_ref,
        out_ref, qgrad_ref, own_ref, stats_ref,
    ):
        has_prior = frame_ref[0] > 0
        k, v = k_ref[...], v_ref[...]
        k_prior, v_prior = prior_ref[0, 0], prior_ref[0, 1]
        own_ref[...] = jnp.zeros_like(own_ref)

        @pl.loop(0, count // chunk)
        def _(step):
            part = pl.ds(pl.multiple_of(step * chunk, chunk), chunk)
            q, g = q_ref[part], g_ref[part]
            own = dot_nt(k, q)
            before = jnp.where(has_prior, dot_nt(k_prior, q), MASKED)
            top = jnp.maximum(
                jnp.max(own, axis=0, keepdims=True), jnp.max(before, axis=0, keepdims=True)
            )
            own, before = (jnp.exp2((x - top) * SCALE_LOG2) for x in (own, before))
            total = jnp.sum(own, axis=0, keepdims=True) + jnp.sum(before, axis=0, keepdims=True)
            inverse = 1.0 / total
            own, before = own * inverse, before * inverse
            own_dp, before_dp = dot_nt(v, g), dot_nt(v_prior, g)
            delta = jnp.sum(own * own_dp, axis=0, keepdims=True) + jnp.sum(
                before * before_dp, axis=0, keepdims=True
            )
            own_prob, before_prob = own.astype(BF16), before.astype(BF16)
            own_ds = (own * (own_dp - delta) * SCALE).astype(BF16)
            before_ds = (before * (before_dp - delta) * SCALE).astype(BF16)
            out_ref[part] = (dot_tn(own_prob, v) + dot_tn(before_prob, v_prior)).astype(BF16)
            qgrad_ref[part] = (dot_tn(own_ds, k) + dot_tn(before_ds, k_prior)).astype(BF16)
            own_ref[0, 0] += dot_nn(own_ds, q)
            own_ref[0, 1] += dot_nn(own_prob, g)
            stats_ref[0, 0:1, part] = top * SCALE + jnp.log(total)
            stats_ref[0, 1:2, part] = delta

    columns = column_spec(count, heads, SPATIAL)
    pair = pl.BlockSpec((1, 2, count, DH), lambda i, *refs: (i, 0, 0, 0))
    whole = jax.ShapeDtypeStruct((count, heads * DH), BF16)
    return pl.pallas_call(
        kernel,
        out_shape=[
            whole,
            whole,
            jax.ShapeDtypeStruct(prior.shape, F32),
            jax.ShapeDtypeStruct((slots, 2, count), F32),
        ],
        grid_spec=pltpu.PrefetchScalarGridSpec(
            num_scalar_prefetch=3,
            grid=(slots,),
            in_specs=[columns] * 4 + [pair],
            out_specs=[
                columns, columns, pair, pl.BlockSpec((1, 2, count), lambda i, *refs: (i, 0, 0))
            ],
        ),
        compiler_params=params(24),
        cost_estimate=cost(2e11, 16 * slots * count * DH),
        name="spatial",
    )(kinds, first, frame, *arrays, prior)


def spatial_next(kinds, first, k, v, following, stats, own, heads):
    slots, _, count, _ = own.shape
    chunk = min(count, 256)

    def kernel(
        kind_ref, first_ref, k_in, v_in, next_in, stats_in, own_in, k_out, v_out,
        kv_ref, next_ref, stats_ref, own_ref, made_ref, in_sems, out_sems,
    ):
        def loads(slot):
            cols = head_columns(kind_ref, first_ref, heads, SPATIAL, slot)
            pairs = [
                (k_in.at[:, cols], kv_ref.at[slot, 0]),
                (v_in.at[:, cols], kv_ref.at[slot, 1]),
                (next_in.at[slot], next_ref.at[slot]),
                (stats_in.at[slot], stats_ref.at[slot]),
                (own_in.at[slot], own_ref.at[slot]),
            ]
            return [
                pltpu.make_async_copy(*pair, in_sems.at[slot, i]) for i, pair in enumerate(pairs)
            ]

        def stores(slot):
            cols = head_columns(kind_ref, first_ref, heads, SPATIAL, slot)
            return [
                pltpu.make_async_copy(made_ref.at[slot, i], out.at[:, cols], out_sems.at[slot, i])
                for i, out in enumerate((k_out, v_out))
            ]

        for slot in range(slots):
            for copy in loads(slot):
                copy.start()

        @pl.loop(0, slots)
        def _(slot):
            for copy in loads(slot):
                copy.wait()
            q, g = next_ref[slot, 0], next_ref[slot, 1]
            lse, delta = stats_ref[slot, 0:1] * math.log2(math.e), stats_ref[slot, 1:2]
            parts = [slice(start, start + chunk) for start in range(0, count, chunk)]
            scores = [dot_nt(kv_ref[slot, 0, part], q) for part in parts]
            dprobs = [dot_nt(kv_ref[slot, 1, part], g) for part in parts]
            weights = [jnp.exp2(x * SCALE_LOG2 - lse) for x in scores]
            slopes = [(w * (x - delta)).astype(BF16) for w, x in zip(weights, dprobs)]
            for part, weight, slope in zip(parts, weights, slopes):
                terms = dot_nn(slope, q) * SCALE, dot_nn(weight.astype(BF16), g)
                for i, term in enumerate(terms):
                    made_ref[slot, i, part] = (own_ref[slot, i, part] + term).astype(BF16)
            for copy in stores(slot):
                copy.start()

        for slot in range(slots):
            for copy in stores(slot):
                copy.wait()

    return pl.pallas_call(
        kernel,
        out_shape=[jax.ShapeDtypeStruct(k.shape, BF16)] * 2,
        in_specs=[pl.BlockSpec(memory_space=pltpu.SMEM)] * 2
        + [pl.BlockSpec(memory_space=pl.ANY)] * 5,
        out_specs=[pl.BlockSpec(memory_space=pl.ANY)] * 2,
        scratch_shapes=[
            pltpu.VMEM((slots, 2, count, DH), BF16),
            pltpu.VMEM((slots, 2, count, DH), BF16),
            pltpu.VMEM((slots, 2, count), F32),
            pltpu.VMEM((slots, 2, count, DH), F32),
            pltpu.VMEM((slots, 2, count, DH), BF16),
            pltpu.SemaphoreType.DMA((slots, 5)),
            pltpu.SemaphoreType.DMA((slots, 2)),
        ],
        compiler_params=pltpu.CompilerParams(vmem_limit_bytes=24 * MIB),
        cost_estimate=cost(8 * slots * count * count * DH, 20 * slots * count * DH),
        name="spatial_next",
    )(kinds, first, k, v, following, stats, own)


def unpack(kinds, first, rows_in, filled, heads):
    frames, _, slots, rows, _ = rows_in.shape
    count = frames * rows
    total = 4 * slots

    def kernel(kind_ref, first_ref, in_ref, *refs):
        outs, (stage, in_sems, out_sems) = refs[-7:-3], refs[-3:]
        triples = []
        for slot in range(slots):
            cols = head_columns(kind_ref, first_ref, heads, TEMPORAL, slot)
            for place, out in enumerate(outs):
                held = stage.at[slot, place]
                triples.append((in_ref.at[:, place, slot], held, out.at[:, :, cols]))
        staged_copies(triples, in_sems, out_sems)

    shape = (frames, rows, heads * DH)
    filled = [x.reshape(shape) for x in filled]
    outs = pl.pallas_call(
        kernel,
        out_shape=[jax.ShapeDtypeStruct(shape, BF16)] * 4,
        in_specs=[pl.BlockSpec(memory_space=pltpu.SMEM)] * 2
        + [pl.BlockSpec(memory_space=pl.ANY)] * (1 + len(filled)),
        out_specs=[pl.BlockSpec(memory_space=pl.ANY)] * 4,
        scratch_shapes=[
            pltpu.VMEM((slots, 4, frames, rows, DH), BF16),
            pltpu.SemaphoreType.DMA((total,)),
            pltpu.SemaphoreType.DMA((total,)),
        ],
        input_output_aliases={3 + place: place for place in range(len(filled))},
        compiler_params=pltpu.CompilerParams(vmem_limit_bytes=24 * MIB),
        cost_estimate=cost(0, 4 * rows_in.size),
        name="unpack",
    )(kinds, first, rows_in, *filled)
    return [x.reshape(count, heads * DH) for x in outs]


def passed_along(array, axis, by):
    length = lax.axis_size(axis)
    pairs = [(i, i + by) for i in range(length) if 0 <= i + by < length]
    return lax.ppermute(array, axis, pairs)


def behind(arrays, *others):
    return lax.optimization_barrier((tuple(arrays), others))[0]


def neighbour_rows(ahead, back, frame, results):
    length = lax.axis_size("ctx")
    even = lax.rem(frame[0], 2) == 0
    far = [(i, i - 1 if i % 2 == 0 else i + 1) for i in range(length)]
    far = [pair for pair in far if 0 <= pair[1] < length]
    near = [(i, i + 1 if i % 2 == 0 else i - 1) for i in range(length)]
    near = lax.ppermute(jnp.where(even, ahead, back), "ctx", near)
    far = lax.ppermute(jnp.where(even, back, ahead), "ctx", far)
    if results is not None:
        near, far = behind((near, far), results)
    return jnp.where(even, far, near), jnp.where(even, near, far)


def exchange_order(frames):
    half = frames // 2
    return [*range(half - 1), half, half - 1, *range(half + 1, frames)]


def branch(slots, heads, kinds, bands, first, frame, q, k, v, g):
    frames, rows, width = q.shape
    count = frames * rows
    others = heads - slots
    exchange = functools.partial(
        lax.all_to_all, axis_name="ctx", split_axis=0, concat_axis=0, tiled=True,
        axis_index_groups=[exchange_order(frames)],
    )
    flat = [x.reshape(count, width) for x in (q, k, v, g)]
    packed = []
    filled, results = (), None
    if slots > 0:
        packed = [pack_temporal(kinds, first, (q, k, v, g), slots, heads)]
        framed = exchange(*packed)
        results = temporal(kinds, first, bands, framed, heads)
        returned = exchange(results)
    if others > 0:
        ahead, back = pack_spatial(kinds, first, (k, v, q, g), others, heads, packed)
        arrived = neighbour_rows(ahead, back, frame, results)
        prior, following = (x.reshape(others, 2, count, DH) for x in arrived)
        attended, qgrad, own, stats = spatial(kinds, first, frame, flat, prior, heads)
        stats = passed_along(stats, "ctx", -1)
        grads = spatial_next(kinds, first, *flat[1:3], following, stats, own, heads)
        filled = (attended, qgrad, *grads)
    if slots > 0:
        filled = unpack(kinds, first, returned, filled, heads)
    return tuple(filled)


def body(queries, key_rows, value_rows, out_grad, head_kind, frame_band):
    frames = lax.axis_size("ctx")
    count = queries.shape[1]
    heads = queries.shape[2] // DH
    first = lax.axis_index("head").astype(jnp.int32) * heads
    frame = lax.axis_index("ctx").astype(jnp.int32)
    offset = jnp.arange(head_kind.shape[0], dtype=jnp.int32) - first
    here = jnp.logical_and(offset >= 0, offset < heads)
    slots = jnp.sum(jnp.logical_and(here, head_kind == TEMPORAL).astype(jnp.int32))
    arrays = [
        x.reshape(frames, count // frames, heads * DH)
        for x in (queries, key_rows, value_rows, out_grad)
    ]
    outs = lax.switch(
        slots,
        [functools.partial(branch, n, heads) for n in range(heads + 1)],
        head_kind, frame_band, first.reshape(1), frame.reshape(1), *arrays,
    )
    return tuple(out.reshape(queries.shape) for out in outs)


def solution(mesh):
    rows = P("ctx", None, "head")
    return jax.shard_map(
        body,
        mesh=mesh,
        in_specs=(rows, rows, rows, rows, P(), P()),
        out_specs=(rows, rows, rows, rows),
        check_vma=False,
    )
```

```python
import functools
import math

import jax
import jax.numpy as jnp
from jax import lax
from jax.experimental import pallas as pl
from jax.experimental.pallas import tpu as pltpu
from jax.sharding import PartitionSpec as P

DH = 128
SCALE = DH ** (-0.5)
SPATIAL, TEMPORAL = 1, 0
MASKED = -1e30
SCALE_LOG2 = SCALE * math.log2(math.e)
F32 = jnp.float32
BF16 = jnp.bfloat16
MIB = 1024 * 1024


def head_at(kind_ref, first_ref, heads, kind, slot):
    found, seen = jnp.int32(0), jnp.int32(0)
    for head in range(heads):
        hit = kind_ref[first_ref[0] + head] == kind
        found = jnp.where(jnp.logical_and(hit, seen == slot), jnp.int32(head), found)
        seen = seen + hit.astype(jnp.int32)
    return found


def dot_nt(a, b):
    return lax.dot_general(a, b, (((1,), (1,)), ((), ())), preferred_element_type=F32)


def dot_nn(a, b):
    return lax.dot_general(a, b, (((1,), (0,)), ((), ())), preferred_element_type=F32)


def dot_tn(a, b):
    return lax.dot_general(a, b, (((0,), (0,)), ((), ())), preferred_element_type=F32)


def params(mib=32):
    return pltpu.CompilerParams(
        dimension_semantics=("arbitrary",), vmem_limit_bytes=mib * MIB
    )


def cost(flops, moved):
    return pl.CostEstimate(flops=int(flops), bytes_accessed=int(moved), transcendentals=0)


def column_spec(count, heads, kind):
    return pl.BlockSpec((count, DH), lambda i, *refs: (0, head_at(*refs[:2], heads, kind, i)))


def head_columns(kind_ref, first_ref, heads, kind, slot):
    return pl.ds(pl.multiple_of(head_at(kind_ref, first_ref, heads, kind, slot) * DH, DH), DH)


def staged_copies(triples, in_sems, out_sems):
    loads = [pltpu.make_async_copy(x, y, in_sems.at[i]) for i, (x, y, _) in enumerate(triples)]
    stores = [pltpu.make_async_copy(y, z, out_sems.at[i]) for i, (_, y, z) in enumerate(triples)]
    for load in loads:
        load.start()
    for load, store in zip(loads, stores):
        load.wait()
        store.start()
    for store in stores:
        store.wait()


def whole_params():
    return pltpu.CompilerParams(vmem_limit_bytes=62 * MIB)


def pack_spatial(kinds, first, arrays, slots, heads, after):
    frames, rows, _ = arrays[0].shape
    count = len(arrays)
    total = slots * count

    def kernel(kind_ref, first_ref, *refs):
        ins, outs = refs[:count], refs[-3 - count // 2 : -3]
        stage, in_sems, out_sems = refs[-3:]
        triples = []
        for slot in range(slots):
            cols = head_columns(kind_ref, first_ref, heads, SPATIAL, slot)
            for place, ref in enumerate(ins):
                target = outs[place // 2].at[slot, place % 2]
                triples.append((ref.at[:, :, cols], stage.at[slot, place], target))
        staged_copies(triples, in_sems, out_sems)

    return pl.pallas_call(
        kernel,
        out_shape=[jax.ShapeDtypeStruct((slots, 2, frames, rows, DH), BF16)] * (count // 2),
        in_specs=[pl.BlockSpec(memory_space=pltpu.SMEM)] * 2
        + [pl.BlockSpec(memory_space=pl.ANY)] * (count + len(after)),
        out_specs=[pl.BlockSpec(memory_space=pl.ANY)] * (count // 2),
        scratch_shapes=[
            pltpu.VMEM((slots, count, frames, rows, DH), BF16),
            pltpu.SemaphoreType.DMA((total,)),
            pltpu.SemaphoreType.DMA((total,)),
        ],
        compiler_params=whole_params(),
        cost_estimate=cost(0, 4 * total * frames * rows * DH),
        name="pack_spatial",
    )(kinds, first, *arrays, *after)


def pack_temporal(kinds, first, arrays, slots, heads):
    frames, rows, _ = arrays[0].shape
    total = 4 * slots

    def kernel(kind_ref, first_ref, *refs):
        ins, (out, stage, in_sems, out_sems) = refs[:4], refs[4:]
        triples = []
        for slot in range(slots):
            cols = head_columns(kind_ref, first_ref, heads, TEMPORAL, slot)
            for place, ref in enumerate(ins):
                triples.append(
                    (ref.at[:, :, cols], stage.at[slot, place], out.at[:, place, slot])
                )
        staged_copies(triples, in_sems, out_sems)

    return pl.pallas_call(
        kernel,
        out_shape=jax.ShapeDtypeStruct((frames, 4, slots, rows, DH), BF16),
        in_specs=[pl.BlockSpec(memory_space=pltpu.SMEM)] * 2
        + [pl.BlockSpec(memory_space=pl.ANY)] * 4,
        out_specs=pl.BlockSpec(memory_space=pl.ANY),
        scratch_shapes=[
            pltpu.VMEM((slots, 4, frames, rows, DH), BF16),
            pltpu.SemaphoreType.DMA((total,)),
            pltpu.SemaphoreType.DMA((total,)),
        ],
        compiler_params=whole_params(),
        cost_estimate=cost(0, 4 * total * frames * rows * DH),
        name="pack_temporal",
    )(kinds, first, *arrays)


def temporal(kinds, first, bands, rows_in, heads):
    frames, _, slots, rows, _ = rows_in.shape
    group = 16
    size = frames * group

    def frame_at(place):
        half = frames // 2
        return place + (place == half - 1).astype(jnp.int32) - (place == half).astype(jnp.int32)

    def kernel(kind_ref, first_ref, band_ref, rows_ref, result_ref, held, made, in_sems, out_sems):
        load = pltpu.make_async_copy(rows_ref, held, in_sems.at[0])

        def store(slot):
            return pltpu.make_async_copy(
                made.at[slot], result_ref.at[:, :, slot], out_sems.at[slot]
            )

        load.start()
        load.wait()

        def work(members):
            some_heads(
                kind_ref, first_ref, band_ref,
                [(slot, held.at[:, :, slot], made.at[slot]) for slot in members],
            )
            for slot in members:
                store(slot).start()

        if slots > 1:

            @pl.loop(0, slots // 2)
            def _(pair):
                work([2 * pair, 2 * pair + 1])

        if slots % 2:
            work([slots - 1])
        for slot in range(slots):
            store(slot).wait()

    def some_heads(kind_ref, first_ref, band_ref, members):
        row = lax.broadcasted_iota(jnp.int32, (size, size), 0)
        col = lax.broadcasted_iota(jnp.int32, (size, size), 1)
        same = lax.rem(row, group) == lax.rem(col, group)
        apart = jnp.abs(frame_at(lax.div(row, group)) - frame_at(lax.div(col, group)))
        distance = jnp.where(same, apart, frames)
        parts = [slice(start, start + group) for start in range(0, rows, group)]
        allowed, qs, ks, vs, gs = [], [], [], [], []
        for slot, in_ref, _ in members:
            head = head_at(kind_ref, first_ref, heads, TEMPORAL, slot)
            band = jnp.minimum(band_ref[first_ref[0] + head], frames - 1)
            allowed += [distance <= band] * len(parts)
            for place, rows_of in enumerate((qs, ks, vs, gs)):
                rows_of += [in_ref[:, place, part].reshape(size, DH) for part in parts]
        scores = [
            jnp.where(ok, dot_nt(k, q), MASKED) for ok, q, k in zip(allowed, qs, ks)
        ]
        dprobs = [dot_nt(v, g) for g, v in zip(gs, vs)]
        raised = [
            jnp.exp2((x - jnp.max(x, axis=0, keepdims=True)) * SCALE_LOG2) for x in scores
        ]
        weights = [x * (1.0 / jnp.sum(x, axis=0, keepdims=True)) for x in raised]
        probs = [x.astype(BF16) for x in weights]
        deltas = [jnp.sum(w * dp, axis=0, keepdims=True) for w, dp in zip(weights, dprobs)]
        dscores = [
            (w * (dp - delta) * SCALE).astype(BF16)
            for w, dp, delta in zip(weights, dprobs, deltas)
        ]
        results = (
            [dot_tn(x, v).astype(BF16) for x, v in zip(probs, vs)],
            [dot_tn(x, k).astype(BF16) for x, k in zip(dscores, ks)],
            [dot_nn(x, q).astype(BF16) for x, q in zip(dscores, qs)],
            [dot_nn(x, g).astype(BF16) for x, g in zip(probs, gs)],
        )
        for place, result in enumerate(results):
            targets = [(out_ref, part) for _, _, out_ref in members for part in parts]
            for (out_ref, part), value in zip(targets, result):
                out_ref[:, place, part] = value.reshape(frames, group, DH)

    block = (slots, frames, 4, rows, DH)
    return pl.pallas_call(
        kernel,
        out_shape=jax.ShapeDtypeStruct(rows_in.shape, BF16),
        in_specs=[pl.BlockSpec(memory_space=pltpu.SMEM)] * 3
        + [pl.BlockSpec(memory_space=pl.ANY)],
        out_specs=pl.BlockSpec(memory_space=pl.ANY),
        scratch_shapes=[
            pltpu.VMEM(rows_in.shape, BF16),
            pltpu.VMEM(block, BF16),
            pltpu.SemaphoreType.DMA((1,)),
            pltpu.SemaphoreType.DMA((slots,)),
        ],
        compiler_params=whole_params(),
        cost_estimate=cost(1e10, 4 * rows_in.size),
        name="temporal",
    )(kinds, first, bands, rows_in)


def spatial(kinds, first, frame, arrays, prior, heads):
    count = arrays[0].shape[0]
    slots = prior.shape[0]
    chunk = min(count, 128)

    def kernel(
        kind_ref, first_ref, frame_ref, q_ref, k_ref, v_ref, g_ref, prior_ref,
        out_ref, qgrad_ref, own_ref, stats_ref,
    ):
        has_prior = frame_ref[0] > 0
        k, v = k_ref[...], v_ref[...]
        k_prior, v_prior = prior_ref[0, 0], prior_ref[0, 1]
        own_ref[...] = jnp.zeros_like(own_ref)

        @pl.loop(0, count // chunk)
        def _(step):
            part = pl.ds(pl.multiple_of(step * chunk, chunk), chunk)
            q, g = q_ref[part], g_ref[part]
            own = dot_nt(k, q)
            before = jnp.where(has_prior, dot_nt(k_prior, q), MASKED)
            top = jnp.maximum(
                jnp.max(own, axis=0, keepdims=True), jnp.max(before, axis=0, keepdims=True)
            )
            own, before = (jnp.exp2((x - top) * SCALE_LOG2) for x in (own, before))
            total = jnp.sum(own, axis=0, keepdims=True) + jnp.sum(before, axis=0, keepdims=True)
            inverse = 1.0 / total
            own, before = own * inverse, before * inverse
            own_dp, before_dp = dot_nt(v, g), dot_nt(v_prior, g)
            delta = jnp.sum(own * own_dp, axis=0, keepdims=True) + jnp.sum(
                before * before_dp, axis=0, keepdims=True
            )
            own_prob, before_prob = own.astype(BF16), before.astype(BF16)
            own_ds = (own * (own_dp - delta) * SCALE).astype(BF16)
            before_ds = (before * (before_dp - delta) * SCALE).astype(BF16)
            out_ref[part] = (dot_tn(own_prob, v) + dot_tn(before_prob, v_prior)).astype(BF16)
            qgrad_ref[part] = (dot_tn(own_ds, k) + dot_tn(before_ds, k_prior)).astype(BF16)
            own_ref[0, 0] += dot_nn(own_ds, q)
            own_ref[0, 1] += dot_nn(own_prob, g)
            stats_ref[0, 0:1, part] = top * SCALE + jnp.log(total)
            stats_ref[0, 1:2, part] = delta

    columns = column_spec(count, heads, SPATIAL)
    pair = pl.BlockSpec((1, 2, count, DH), lambda i, *refs: (i, 0, 0, 0))
    whole = jax.ShapeDtypeStruct((count, heads * DH), BF16)
    return pl.pallas_call(
        kernel,
        out_shape=[
            whole,
            whole,
            jax.ShapeDtypeStruct(prior.shape, F32),
            jax.ShapeDtypeStruct((slots, 2, count), F32),
        ],
        grid_spec=pltpu.PrefetchScalarGridSpec(
            num_scalar_prefetch=3,
            grid=(slots,),
            in_specs=[columns] * 4 + [pair],
            out_specs=[
                columns, columns, pair, pl.BlockSpec((1, 2, count), lambda i, *refs: (i, 0, 0))
            ],
        ),
        compiler_params=params(24),
        cost_estimate=cost(2e11, 16 * slots * count * DH),
        name="spatial",
    )(kinds, first, frame, *arrays, prior)


def spatial_next(kinds, first, k, v, following, stats, own, heads):
    slots, _, count, _ = own.shape
    chunk = min(count, 256)

    def kernel(
        kind_ref, first_ref, k_in, v_in, next_in, stats_in, own_in, k_out, v_out,
        kv_ref, next_ref, stats_ref, own_ref, made_ref, in_sems, out_sems,
    ):
        def loads(slot):
            cols = head_columns(kind_ref, first_ref, heads, SPATIAL, slot)
            pairs = [
                (k_in.at[:, cols], kv_ref.at[slot, 0]),
                (v_in.at[:, cols], kv_ref.at[slot, 1]),
                (next_in.at[slot], next_ref.at[slot]),
                (stats_in.at[slot], stats_ref.at[slot]),
                (own_in.at[slot], own_ref.at[slot]),
            ]
            return [
                pltpu.make_async_copy(*pair, in_sems.at[slot, i]) for i, pair in enumerate(pairs)
            ]

        def stores(slot):
            cols = head_columns(kind_ref, first_ref, heads, SPATIAL, slot)
            return [
                pltpu.make_async_copy(made_ref.at[slot, i], out.at[:, cols], out_sems.at[slot, i])
                for i, out in enumerate((k_out, v_out))
            ]

        for slot in range(slots):
            for copy in loads(slot):
                copy.start()

        @pl.loop(0, slots)
        def _(slot):
            for copy in loads(slot):
                copy.wait()
            q, g = next_ref[slot, 0], next_ref[slot, 1]
            lse, delta = stats_ref[slot, 0:1] * math.log2(math.e), stats_ref[slot, 1:2]
            parts = [slice(start, start + chunk) for start in range(0, count, chunk)]
            scores = [dot_nt(kv_ref[slot, 0, part], q) for part in parts]
            dprobs = [dot_nt(kv_ref[slot, 1, part], g) for part in parts]
            weights = [jnp.exp2(x * SCALE_LOG2 - lse) for x in scores]
            slopes = [(w * (x - delta)).astype(BF16) for w, x in zip(weights, dprobs)]
            for part, weight, slope in zip(parts, weights, slopes):
                terms = dot_nn(slope, q) * SCALE, dot_nn(weight.astype(BF16), g)
                for i, term in enumerate(terms):
                    made_ref[slot, i, part] = (own_ref[slot, i, part] + term).astype(BF16)
            for copy in stores(slot):
                copy.start()

        for slot in range(slots):
            for copy in stores(slot):
                copy.wait()

    return pl.pallas_call(
        kernel,
        out_shape=[jax.ShapeDtypeStruct(k.shape, BF16)] * 2,
        in_specs=[pl.BlockSpec(memory_space=pltpu.SMEM)] * 2
        + [pl.BlockSpec(memory_space=pl.ANY)] * 5,
        out_specs=[pl.BlockSpec(memory_space=pl.ANY)] * 2,
        scratch_shapes=[
            pltpu.VMEM((slots, 2, count, DH), BF16),
            pltpu.VMEM((slots, 2, count, DH), BF16),
            pltpu.VMEM((slots, 2, count), F32),
            pltpu.VMEM((slots, 2, count, DH), F32),
            pltpu.VMEM((slots, 2, count, DH), BF16),
            pltpu.SemaphoreType.DMA((slots, 5)),
            pltpu.SemaphoreType.DMA((slots, 2)),
        ],
        compiler_params=pltpu.CompilerParams(vmem_limit_bytes=24 * MIB),
        cost_estimate=cost(8 * slots * count * count * DH, 20 * slots * count * DH),
        name="spatial_next",
    )(kinds, first, k, v, following, stats, own)


def unpack(kinds, first, rows_in, filled, heads):
    frames, _, slots, rows, _ = rows_in.shape
    count = frames * rows
    total = 4 * slots

    def kernel(kind_ref, first_ref, in_ref, *refs):
        outs, (stage, in_sems, out_sems) = refs[-7:-3], refs[-3:]
        triples = []
        for slot in range(slots):
            cols = head_columns(kind_ref, first_ref, heads, TEMPORAL, slot)
            for place, out in enumerate(outs):
                held = stage.at[slot, place]
                triples.append((in_ref.at[:, place, slot], held, out.at[:, :, cols]))
        staged_copies(triples, in_sems, out_sems)

    shape = (frames, rows, heads * DH)
    filled = [x.reshape(shape) for x in filled]
    outs = pl.pallas_call(
        kernel,
        out_shape=[jax.ShapeDtypeStruct(shape, BF16)] * 4,
        in_specs=[pl.BlockSpec(memory_space=pltpu.SMEM)] * 2
        + [pl.BlockSpec(memory_space=pl.ANY)] * (1 + len(filled)),
        out_specs=[pl.BlockSpec(memory_space=pl.ANY)] * 4,
        scratch_shapes=[
            pltpu.VMEM((slots, 4, frames, rows, DH), BF16),
            pltpu.SemaphoreType.DMA((total,)),
            pltpu.SemaphoreType.DMA((total,)),
        ],
        input_output_aliases={3 + place: place for place in range(len(filled))},
        compiler_params=pltpu.CompilerParams(vmem_limit_bytes=24 * MIB),
        cost_estimate=cost(0, 4 * rows_in.size),
        name="unpack",
    )(kinds, first, rows_in, *filled)
    return [x.reshape(count, heads * DH) for x in outs]


def passed_along(array, axis, by):
    length = lax.axis_size(axis)
    pairs = [(i, i + by) for i in range(length) if 0 <= i + by < length]
    return lax.ppermute(array, axis, pairs)


def behind(arrays, *others):
    return lax.optimization_barrier((tuple(arrays), others))[0]


def neighbour_rows(ahead, back, frame, results):
    length = lax.axis_size("ctx")
    even = lax.rem(frame[0], 2) == 0
    far = [(i, i - 1 if i % 2 == 0 else i + 1) for i in range(length)]
    far = [pair for pair in far if 0 <= pair[1] < length]
    near = [(i, i + 1 if i % 2 == 0 else i - 1) for i in range(length)]
    near = lax.ppermute(jnp.where(even, ahead, back), "ctx", near)
    far = lax.ppermute(jnp.where(even, back, ahead), "ctx", far)
    if results is not None:
        near, far = behind((near, far), results)
    return jnp.where(even, far, near), jnp.where(even, near, far)


def exchange_order(frames):
    half = frames // 2
    return [*range(half - 1), half, half - 1, *range(half + 1, frames)]


def branch(slots, heads, kinds, bands, first, frame, q, k, v, g):
    frames, rows, width = q.shape
    count = frames * rows
    others = heads - slots
    exchange = functools.partial(
        lax.all_to_all, axis_name="ctx", split_axis=0, concat_axis=0, tiled=True,
        axis_index_groups=[exchange_order(frames)],
    )
    flat = [x.reshape(count, width) for x in (q, k, v, g)]
    packed = []
    filled, results = (), None
    if slots > 0:
        packed = [pack_temporal(kinds, first, (q, k, v, g), slots, heads)]
        framed = exchange(*packed)
        results = temporal(kinds, first, bands, framed, heads)
        returned = exchange(results)
    if others > 0:
        ahead, back = pack_spatial(kinds, first, (k, v, q, g), others, heads, packed)
        arrived = neighbour_rows(ahead, back, frame, results)
        prior, following = (x.reshape(others, 2, count, DH) for x in arrived)
        attended, qgrad, own, stats = spatial(kinds, first, frame, flat, prior, heads)
        stats = passed_along(stats, "ctx", -1)
        grads = spatial_next(kinds, first, *flat[1:3], following, stats, own, heads)
        filled = (attended, qgrad, *grads)
    if slots > 0:
        filled = unpack(kinds, first, returned, filled, heads)
    return tuple(filled)


def body(queries, key_rows, value_rows, out_grad, head_kind, frame_band):
    frames = lax.axis_size("ctx")
    count = queries.shape[1]
    heads = queries.shape[2] // DH
    first = lax.axis_index("head").astype(jnp.int32) * heads
    frame = lax.axis_index("ctx").astype(jnp.int32)
    offset = jnp.arange(head_kind.shape[0], dtype=jnp.int32) - first
    here = jnp.logical_and(offset >= 0, offset < heads)
    slots = jnp.sum(jnp.logical_and(here, head_kind == TEMPORAL).astype(jnp.int32))
    arrays = [
        x.reshape(frames, count // frames, heads * DH)
        for x in (queries, key_rows, value_rows, out_grad)
    ]
    outs = lax.switch(
        slots,
        [functools.partial(branch, n, heads) for n in range(heads + 1)],
        head_kind, frame_band, first.reshape(1), frame.reshape(1), *arrays,
    )
    return tuple(out.reshape(queries.shape) for out in outs)


def solution(mesh):
    rows = P("ctx", None, "head")
    return jax.shard_map(
        body,
        mesh=mesh,
        in_specs=(rows, rows, rows, rows, P(), P()),
        out_specs=(rows, rows, rows, rows),
        check_vma=False,
    )
```
